32 devices in a mesh: ctx: 8 (over z, core), head: 4 (over y, x).
Axes of the slice: x: 2, y: 2, z: 4, core: 2. Of those that a mesh axis runs over, the one named last changes fastest.
Arguments:
- activations: bfloat16 [2048, 4096], P('ctx', 'head'), may hold values from -40 to 40
- positions: int32 [2048], P('ctx'), may hold values from 0 to 6143, as said below
- w_query: bfloat16 [4096, 4096], P('ctx', 'head'), may hold values from -0.09375 to 0.09375
- w_key: bfloat16 [4096, 4096], P('ctx', 'head'), may hold values from -0.09375 to 0.09375
- w_value: bfloat16 [4096, 4096], P('ctx', 'head'), may hold values from -0.09375 to 0.09375
- conv_kernel: float32 [32, 66], P('head'), may hold values from -0.6 to 0.6
- head_mix: float32 [32, 4], P('head'), may hold values from -0.45 to 1.45
- out_gain: float32 [4096], P('head'), may hold values from 0.1 to 1.9
- w_out: bfloat16 [4096, 4096], P('head', 'ctx'), may hold values from -0.09375 to 0.09375
Outputs:
- attended: bfloat16 [2048, 4096], P('ctx', 'head')
The draws below stay inside these ranges and needn't reach their ends.
Inputs may be any that keep to these rules, and one draw needn't show every extreme that they name: `positions`: strictly increasing along the tokens; the first token's is 0 and the last token's is 6143.
All inputs are finite; a program needn't handle non-finite values.
Results may differ from the reference program's by a relative error of at most 0.018.
Values may be sent and summed in bfloat16 or wider, within the bound.
No kernel may reach another device: no remote copies, remote signals or barrier semaphores. Data moves between devices by JAX's collectives and lax.ppermute only.
A program may use at most 128 MiB of HBM per device.

```python
import math
import jax
import jax.numpy as jnp
from jax import lax

D = 4096
HEADS = 32
HD = 128
GROUP = 4
CQ = 6
CK = 11
KB = 512
TOKEN_COUNT = 2048


def draw_activations(key, part):
    key_base = jax.random.fold_in(key, 0)
    values = jnp.clip(jax.random.normal(key_base, (TOKEN_COUNT, D), jnp.float32), -5.0, 5.0)
    return values.astype(jnp.bfloat16)


def draw_positions(key, part):
    steps_drawn = jax.random.randint(key, (TOKEN_COUNT,), 1, 4)
    walked = (jnp.cumsum(steps_drawn) - 1).astype(jnp.int32)
    walked = walked.at[0].set(0)
    return walked.at[TOKEN_COUNT - 1].set(3 * TOKEN_COUNT - 1)


def draw_head_mix(key, part):
    diagonal = ((jnp.arange(HEADS) % GROUP)[:, None] == jnp.arange(GROUP)[None, :]).astype(jnp.float32)
    noise = jax.random.uniform(key, (HEADS, GROUP), jnp.float32, -0.3, 0.3)
    return diagonal + noise


def block_levels(own_key, shape, pieces, least, high):
    loudness, own = 1.0, jax.random.fold_in(own_key, 6)
    for position, parts in pieces:
        draws = jnp.exp(jax.random.uniform(jax.random.fold_in(own, position), (parts,), jnp.float32, least / len(pieces), high / len(pieces)))
        loudness = loudness * jnp.repeat(draws, shape[position] // parts).reshape([-1 if axis == position else 1 for axis in range(len(shape))])
    return loudness


def gaussian(own_key, extent, scale, bound, shards=(), held_as=jnp.bfloat16):
    drawn = scale * jax.random.normal(own_key, extent, jnp.float32)
    if shards:
        drawn = drawn * block_levels(own_key, extent, shards, -0.22, 0.18)
    return jnp.clip(drawn, -bound, bound).astype(held_as)


def setup_inputs(seed: int = 0) -> dict:
    splits = jax.random.split(jax.random.key(seed), 10)
    activations = draw_activations(jax.random.fold_in(splits[9], 71), 0)
    positions = draw_positions(jax.random.fold_in(splits[9], 71), 0)
    w_query = gaussian(splits[2], (D, HEADS * HD), D ** -0.5, 0.09375, ((0, 8), (1, 4)))
    w_key = gaussian(splits[3], (D, HEADS * HD), D ** -0.5, 0.09375, ((0, 8), (1, 4)))
    w_value = gaussian(splits[4], (D, HEADS * HD), D ** -0.5, 0.09375, ((0, 8), (1, 4)))
    conv_kernel = gaussian(splits[5], (HEADS, CQ * CK), 0.15, 0.6, ((0, 4),), jnp.float32)
    head_mix = draw_head_mix(jax.random.fold_in(splits[9], 71), 0)
    out_gain = jnp.clip(1.0 + 0.18 * jax.random.normal(splits[7], (HEADS * HD,), jnp.float32), 0.1, 1.9)
    w_out = gaussian(splits[8], (HEADS * HD, D), (HEADS * HD) ** -0.5, 0.09375, ((0, 4), (1, 8)))
    return dict(activations=activations, positions=positions, w_query=w_query, w_key=w_key, w_value=w_value, conv_kernel=conv_kernel, head_mix=head_mix, out_gain=out_gain, w_out=w_out)


def rope(projected, positions):
    row_count = projected.shape[0]
    head_count = projected.shape[1] // HD
    shaped = projected.reshape(row_count, head_count, HD)
    half_size = HD // 2
    exponents = jnp.arange(half_size, dtype=jnp.float32) * (2.0 / HD)
    inverse = jnp.exp(-exponents * math.log(500000.0))
    angle = (positions.astype(jnp.float32) * 0.25)[:, None, None] * inverse[None, None, :]
    cosine = jnp.cos(angle)
    sine = jnp.sin(angle)
    lower_half = shaped[..., :half_size]
    upper_half = shaped[..., half_size:]
    rotated_rows = jnp.concatenate([lower_half * cosine - upper_half * sine, upper_half * cosine + lower_half * sine], -1)
    return rotated_rows.reshape(row_count, head_count * HD)

def convolve(masked, kernel, row_count, col_count):
    summed = jnp.zeros((masked.shape[0], row_count, col_count), jnp.float32)
    for lag_q in range(CQ):
        for lag_k in range(CK):
            weight = kernel[:, lag_q * CK + lag_k][:, None, None]
            window = masked[:, CQ - 1 - lag_q:CQ - 1 - lag_q + row_count, CK - 1 - lag_k:CK - 1 - lag_k + col_count]
            summed = summed + weight * window
    return summed

def reference(activations, positions, w_query, w_key, w_value, conv_kernel, head_mix, out_gain, w_out):
    length = TOKEN_COUNT
    groups = HEADS // GROUP
    scale = 1.0 / math.sqrt(HD)
    query = rope(jnp.dot(activations, w_query, preferred_element_type=jnp.float32), positions).astype(jnp.bfloat16)
    key = rope(jnp.dot(activations, w_key, preferred_element_type=jnp.float32), positions).astype(jnp.bfloat16)
    value = jnp.dot(activations, w_value, preferred_element_type=jnp.float32).astype(jnp.bfloat16)
    query_groups = query.reshape(length, groups, GROUP, HD).transpose(1, 0, 2, 3)
    query_groups = jnp.pad(query_groups, ((0, 0), (CQ - 1, 0), (0, 0), (0, 0)))
    key_groups = key.reshape(length, groups, GROUP, HD).transpose(1, 0, 2, 3)
    key_groups = jnp.pad(key_groups, ((0, 0), (CK // 2, CK // 2), (0, 0), (0, 0)))
    value_groups = value.reshape(length, groups, GROUP, HD).transpose(1, 0, 2, 3)
    kernels = conv_kernel.reshape(groups, GROUP, CQ * CK)
    mixes = head_mix.reshape(groups, GROUP, GROUP)

    def one_group(packed):
        query_pad, key_pad, value_cluster, kernel, mixing = packed

        def one_block(start):
            query_ext = lax.dynamic_slice_in_dim(query_pad, start, KB + CQ - 1, 0)
            scores = jnp.einsum('rhd,khd->hrk', query_ext.astype(jnp.float32), key_pad.astype(jnp.float32)) * scale
            prow = start - (CQ - 1) + jnp.arange(KB + CQ - 1, dtype=jnp.int32)
            kcol = jnp.arange(length + CK - 1, dtype=jnp.int32) - CK // 2
            valid = (kcol[None, :] <= prow[:, None]) & (prow[:, None] >= 0)
            masked = jnp.where(valid[None], scores, 0.0)
            conv = convolve(masked, kernel, KB, length)
            irow = start + jnp.arange(KB, dtype=jnp.int32)
            jcol = jnp.arange(length, dtype=jnp.int32)
            logits = jnp.where((jcol[None, :] <= irow[:, None])[None], conv, -jnp.inf)
            probs = jax.nn.softmax(logits, axis=-1)
            mixed_scores = jnp.einsum('ab,bik->aik', mixing, probs).astype(jnp.bfloat16)
            return jnp.einsum('gup,pgb->ugb', mixed_scores.astype(jnp.float32), value_cluster.astype(jnp.float32))
        starts = jnp.arange(length // KB, dtype=jnp.int32) * KB
        return lax.map(one_block, starts)
    outputs = lax.map(one_group, (query_groups, key_groups, value_groups, kernels, mixes))
    head_output = outputs.transpose(1, 2, 0, 3, 4).reshape(length, HEADS, HD)
    rms = jnp.sqrt(lax.optimization_barrier(jnp.mean(head_output * head_output, axis=-1, keepdims=True)) + 1e-05)
    normed = (head_output / rms * out_gain.reshape(HEADS, HD)).astype(jnp.bfloat16).reshape(length, HEADS * HD)
    return jnp.dot(normed, w_out, preferred_element_type=jnp.float32).astype(jnp.bfloat16)
```

```python
import math

import jax
import jax.numpy as jnp
from jax import lax
from jax.experimental import pallas as pl
from jax.experimental.pallas import tpu as pltpu
from jax.sharding import PartitionSpec as P

HD = 128
GROUP = 4
CQ = 6
CK = 11
KB = 512


def passed_along(value, axis, steps):
    count = lax.axis_size(axis)
    leading, last = (max(0, -steps), min(count, count - steps))
    return lax.ppermute(value, axis, [(source, source + steps) for source in range(leading, last)])


def rope(projected, positions):
    row_count = projected.shape[0]
    head_count = projected.shape[1] // HD
    shaped = projected.reshape(row_count, head_count, HD)
    half_size = HD // 2
    exponents = jnp.arange(half_size, dtype=jnp.float32) * (2.0 / HD)
    inverse = jnp.exp(-exponents * math.log(500000.0))
    angle = (positions.astype(jnp.float32) * 0.25)[:, None, None] * inverse[None, None, :]
    cosine = jnp.cos(angle)
    sine = jnp.sin(angle)
    lower_half = shaped[..., :half_size]
    upper_half = shaped[..., half_size:]
    rotated_rows = jnp.concatenate(
        [lower_half * cosine - upper_half * sine, upper_half * cosine + lower_half * sine], -1
    )
    return rotated_rows.reshape(row_count, head_count * HD)


def convolve(masked, kernel, row_count, col_count):
    summed = jnp.zeros((masked.shape[0], row_count, col_count), jnp.float32)
    for lag_q in range(CQ):
        for lag_k in range(CK):
            weight = kernel[:, lag_q * CK + lag_k][:, None, None]
            window = masked[
                :,
                CQ - 1 - lag_q : CQ - 1 - lag_q + row_count,
                CK - 1 - lag_k : CK - 1 - lag_k + col_count,
            ]
            summed = summed + weight * window
    return summed


def add_rows(left, piece):
    return jnp.dot(left, piece, preferred_element_type=jnp.float32)


def share_keys(key, value):
    return (
        lax.all_gather(key, "ctx", axis=0, tiled=True),
        lax.all_gather(value, "ctx", axis=0, tiled=True),
    )


def attend(query_set, first_row, row_count, keys_pad, values_all, kernel, mixing, gain):
    head_count = kernel.shape[0]
    ext_rows = row_count + CQ - 1
    query_heads = query_set.reshape(ext_rows, head_count, HD)
    token_total = values_all.shape[0]
    block_count = token_total // KB
    last_row = first_row + row_count - 1
    scale = 1.0 / math.sqrt(HD)
    prow = first_row - (CQ - 1) + jnp.arange(ext_rows, dtype=jnp.int32)
    irow = first_row + jnp.arange(row_count, dtype=jnp.int32)

    def logits_of(block):
        key_start = block * KB
        key_block = lax.dynamic_slice_in_dim(keys_pad, key_start, KB + CK - 1, 0).reshape(
            KB + CK - 1, head_count, HD
        )
        scores = (
            jnp.einsum("rhd,khd->hrk", query_heads, key_block, preferred_element_type=jnp.float32)
            * scale
        )
        kcol = key_start - CK // 2 + jnp.arange(KB + CK - 1, dtype=jnp.int32)
        valid = (kcol[None, :] <= prow[:, None]) & (prow[:, None] >= 0)
        masked = jnp.where(valid[None], scores, 0.0)
        conv = convolve(masked, kernel, row_count, KB)
        jcol = key_start + jnp.arange(KB, dtype=jnp.int32)
        return jnp.where((jcol[None, :] <= irow[:, None])[None], conv, -jnp.inf)

    def first_pass(block, carry_in):

        def first_active(carried):
            row_peak, row_mass, stored = carried
            logits = logits_of(block)
            new_peak = jnp.maximum(row_peak, jnp.max(logits, axis=-1))
            new_mass = row_mass * jnp.exp(row_peak - new_peak) + jnp.sum(
                jnp.exp(logits - new_peak[..., None]), axis=-1
            )
            stored = lax.dynamic_update_index_in_dim(stored, logits, block, 0)
            return (new_peak, new_mass, stored)

        return lax.cond(block * KB <= last_row, first_active, lambda carried: carried, carry_in)

    peak_start = jnp.full((head_count, row_count), -jnp.inf, jnp.float32)
    mass_start = jnp.zeros((head_count, row_count), jnp.float32)
    store_start = jnp.zeros((block_count, head_count, row_count, KB), jnp.float32)
    row_peak, row_mass, stored = lax.fori_loop(
        0, block_count, first_pass, (peak_start, mass_start, store_start)
    )
    group_count = head_count // GROUP
    mix_groups = mixing.reshape(group_count, GROUP, GROUP)

    def second_pass(block, carry_in):

        def second_active(summed):
            logits = lax.dynamic_index_in_dim(stored, block, 0, keepdims=False)
            probs = jnp.exp(logits - row_peak[..., None]) / row_mass[..., None]
            grouped = probs.reshape(group_count, GROUP, row_count, KB)
            mixed_scores = (
                jnp.einsum("gab,gbrk->gark", mix_groups, grouped)
                .reshape(head_count, row_count, KB)
                .astype(jnp.bfloat16)
            )
            value_block = lax.dynamic_slice_in_dim(values_all, block * KB, KB, 0).reshape(
                KB, head_count, HD
            )
            return summed + jnp.einsum(
                "hrk,khd->rhd", mixed_scores, value_block, preferred_element_type=jnp.float32
            )

        return lax.cond(block * KB <= last_row, second_active, lambda summed: summed, carry_in)

    summed = lax.fori_loop(
        0, block_count, second_pass, jnp.zeros((row_count, head_count, HD), jnp.float32)
    )
    rms = jnp.sqrt(jnp.mean(summed * summed, axis=-1, keepdims=True) + 1e-05)
    normed = (summed / rms * gain.reshape(head_count, HD)).astype(jnp.bfloat16)
    return normed.reshape(row_count, head_count * HD)


def per_device(
    activations, positions, w_query, w_key, w_value, conv_kernel, head_mix, out_gain, w_out
):
    row_count = activations.shape[0]
    ctx_place = lax.axis_index("ctx")
    features = lax.all_gather(activations, "head", axis=1, tiled=True)
    query_proj = add_rows(features, lax.all_gather(w_query, "ctx", axis=0, tiled=True))
    key_proj = add_rows(features, lax.all_gather(w_key, "ctx", axis=0, tiled=True))
    value_proj = add_rows(features, lax.all_gather(w_value, "ctx", axis=0, tiled=True))
    key = rope(key_proj, positions).astype(jnp.bfloat16)
    value = value_proj.astype(jnp.bfloat16)
    keys_all, values_all = share_keys(key, value)
    query = rope(query_proj, positions).astype(jnp.bfloat16)
    rim_rows = passed_along(query[row_count - (CQ - 1) :], "ctx", 1)
    query_ext = jnp.concatenate([rim_rows, query], 0)
    keys_pad = jnp.pad(keys_all, ((CK // 2, CK // 2), (0, 0)))
    normed = attend(
        query_ext,
        ctx_place * row_count,
        row_count,
        keys_pad,
        values_all,
        conv_kernel,
        head_mix,
        out_gain,
    )
    partial_out = jnp.dot(
        normed, lax.all_gather(w_out, "ctx", axis=1, tiled=True), preferred_element_type=jnp.float32
    )
    return lax.psum_scatter(
        partial_out.astype(jnp.bfloat16), "head", scatter_dimension=1, tiled=True
    )


ROWS = 256
BAND = 128
LANES = 128
SUB = 64
VMEM_BYTES = 56 * 1024 * 1024


def kernel_params():
    return pltpu.CompilerParams(vmem_limit_bytes=VMEM_BYTES)


def whole(memory_space):
    return pl.BlockSpec(memory_space=memory_space)


def project_kernel(place, *refs):
    a_parts = refs[:16]
    w_same, w_swap = refs[16:20], refs[20:24]
    cos_ref, sin_ref = refs[24:26]
    mine, theirs, v_out = refs[26:29]
    abuf, wbuf, acc, sem_a, sem_w = refs[29:]
    turn, core = place[0], place[1]
    half = w_same[0].shape[0]
    own_rows = pl.ds(pl.multiple_of(core * half, half), half)
    swap_rows = pl.ds(pl.multiple_of((1 - core) * half, half), half)

    def copy_a(t, b):
        return pltpu.make_async_copy(a_parts[4 * t + b], abuf.at[t, b], sem_a.at[t, b])

    def copies_w(t, s):
        return [
            pltpu.make_async_copy(w_same[s], wbuf.at[t, own_rows], sem_w.at[t, 0]),
            pltpu.make_async_copy(w_swap[s], wbuf.at[t, swap_rows], sem_w.at[t, 1]),
        ]

    for t in range(4):
        for s in range(4):

            @pl.when(s == lax.bitwise_xor(turn, t))
            def _():
                for copy in copies_w(t, s):
                    copy.start()

        for b in range(4):
            copy_a(t, b).start()

    for t in range(4):
        for copy in copies_w(t, 0):
            copy.wait()
        for b in range(4):
            copy_a(t, b).wait()
            part = jnp.dot(abuf[t, b], wbuf[t], preferred_element_type=jnp.float32)
            if t == 0:
                acc[b] = part
            elif t < 3:
                acc[b] += part
            else:
                total = acc[b] + part
                cosine, sine = cos_ref[b], sin_ref[b]

                def turned(x):
                    return x * cosine + pltpu.roll(x, HD // 2, 1) * sine

                first = core == 0
                at = place[5 + b]
                for col, out in ((0, 0), (2 * HD, HD)):
                    h0 = turned(total[:, col : col + HD]).astype(jnp.bfloat16)
                    h1 = turned(total[:, col + HD : col + 2 * HD]).astype(jnp.bfloat16)
                    mine[at, :, out : out + HD] = jnp.where(first, h0, h1)
                    theirs[at, :, out : out + HD] = jnp.where(first, h1, h0)
                v_out[at] = total[:, 4 * HD :].astype(jnp.bfloat16)


def project(place, a_parts, w_same, w_swap, cosine, sine):
    rows, depth = a_parts[0].shape
    width = w_same[0].shape[1]
    out = jax.ShapeDtypeStruct((4, rows, 2 * HD), jnp.bfloat16)
    return pl.pallas_call(
        project_kernel,
        out_shape=(out, out, out),
        in_specs=[whole(pltpu.SMEM)] + [whole(pl.ANY)] * 24 + [whole(pltpu.VMEM)] * 2,
        out_specs=[whole(pltpu.VMEM)] * 3,
        scratch_shapes=[
            pltpu.VMEM((4, 4, rows, depth), jnp.bfloat16),
            pltpu.VMEM((4, depth, width), jnp.bfloat16),
            pltpu.VMEM((4, rows, width), jnp.float32),
            pltpu.SemaphoreType.DMA((4, 4)),
            pltpu.SemaphoreType.DMA((4, 2)),
        ],
        compiler_params=kernel_params(),
        cost_estimate=pl.CostEstimate(
            flops=8 * rows * 4 * depth * width, bytes_accessed=16 * 2**20, transcendentals=0
        ),
    )(place, *a_parts, *w_same, *w_swap, cosine, sine)


def prepare_kernel(place, weights, mine, other, even_ref, odd_ref, q_out, k_out, corr, qf, kf):
    core = place[1]
    total = q_out.shape[0]
    qf[0:8] = jnp.zeros((8, HD), jnp.float32)
    kf[0:8] = jnp.zeros((8, HD), jnp.float32)
    kf[8 + total :] = jnp.zeros((kf.shape[0] - 8 - total, HD), jnp.float32)
    for i in range(total // (2 * ROWS)):
        for ref, parity in ((mine, core), (other, 1 - core)):
            start = pl.multiple_of(8 + (2 * i + parity) * ROWS, 8)
            block = ref[i].astype(jnp.float32)
            qf[pl.ds(start, ROWS)] = block[:, :HD]
            kf[pl.ds(start, ROWS)] = block[:, HD:]

    ahead = lax.broadcasted_iota(jnp.int32, (SUB + 8, LANES), 1) - lax.broadcasted_iota(
        jnp.int32, (SUB + 8, LANES), 0
    )
    near = (ahead >= 1) & (ahead < CQ + CK // 2)

    def block_step(b, carry):
        corr[b] = jnp.zeros(corr.shape[1:], jnp.float32)
        for m in range(ROWS // SUB):
            base = pl.multiple_of(b * ROWS + m * SUB, SUB)
            qwin = qf[pl.ds(base, SUB + 8)]
            kwin = kf[pl.ds(base, LANES)]
            scores = lax.dot_general(
                qwin.astype(jnp.bfloat16),
                kwin.astype(jnp.bfloat16),
                (((1,), (1,)), ((), ())),
                preferred_element_type=jnp.float32,
            )
            future = jnp.where(near, scores, 0.0)
            lagged = jnp.concatenate(
                [future[8 - a : 8 - a + SUB].astype(jnp.bfloat16) for a in range(CQ)], 1
            )
            taps = odd_ref if m % 2 else even_ref
            col = LANES * ((m + 1) // 2)
            corr[b, m * SUB : (m + 1) * SUB, col : col + taps.shape[1]] = jnp.dot(
                lagged, taps[...], preferred_element_type=jnp.float32
            )
            for a in range(CQ):
                q_out[pl.ds(base, SUB), a * HD : (a + 1) * HD] = qwin[8 - a : 8 - a + SUB].astype(
                    jnp.bfloat16
                )
            sums = [None] * CQ
            for c in range(CK):
                off = 8 + CK // 2 - c
                window = kwin[off : off + SUB]
                for a in range(CQ):
                    term = weights[a * CK + c] * window
                    sums[a] = term if c == 0 else sums[a] + term
            for a in range(CQ):
                k_out[pl.ds(base, SUB), a * HD : (a + 1) * HD] = sums[a].astype(jnp.bfloat16)
        return carry

    lax.fori_loop(0, total // ROWS, block_step, 0)


def prepare(place, weights, mine, other, even, odd):
    total = mine.shape[0] * 2 * ROWS
    return pl.pallas_call(
        prepare_kernel,
        out_shape=(
            jax.ShapeDtypeStruct((total, CQ * HD), jnp.bfloat16),
            jax.ShapeDtypeStruct((total, CQ * HD), jnp.bfloat16),
            jax.ShapeDtypeStruct((total // ROWS, ROWS, BAND + ROWS), jnp.float32),
        ),
        in_specs=[whole(pltpu.SMEM)] * 2 + [whole(pltpu.VMEM)] * 4,
        out_specs=[whole(pltpu.VMEM)] * 3,
        scratch_shapes=[
            pltpu.VMEM((8 + total, HD), jnp.float32),
            pltpu.VMEM((8 + total + LANES, HD), jnp.float32),
        ],
        compiler_params=kernel_params(),
        cost_estimate=pl.CostEstimate(flops=2**31, bytes_accessed=12 * 2**20, transcendentals=0),
    )(place, weights, mine, other, even, odd)


def band_taps(weights, first, lanes):
    lag = jnp.arange(CQ)[:, None, None]
    tap = (first + jnp.arange(lanes))[None, None, :] + CK // 2 + 8 - jnp.arange(LANES)[None, :, None]
    band = jnp.zeros((CQ, LANES, lanes), jnp.float32)
    for c in range(CK):
        band = band + jnp.where(tap == c, weights[:, c][:, None, None], 0.0)
    return band.astype(jnp.bfloat16).reshape(CQ * LANES, lanes)


def attend_kernel(place, mix, q_ref, k_ref, corr, va, vb, vc, vd, mine, theirs, v_all):
    side, core = place[2], place[1]
    b = pl.program_id(0)
    count = k_ref.shape[0] // ROWS

    @pl.when(b == 0)
    def _():
        for i in range(count // 2):
            for parity, near, far in ((core, va, vb), (1 - core, vc, vd)):
                rows = pl.ds(pl.multiple_of((2 * i + parity) * ROWS, ROWS), ROWS)
                first, last = near[i], far[i]
                v_all[rows, : 2 * HD] = jnp.where(side == 0, first, last)
                v_all[rows, 2 * HD :] = jnp.where(side == 0, last, first)

    row = lax.broadcasted_iota(jnp.int32, (ROWS, ROWS), 0)
    col = lax.broadcasted_iota(jnp.int32, (ROWS, ROWS), 1)
    seen = col <= row

    for step in range(count):

        @pl.when(b == step)
        def _():
            pieces = []
            for j in range(step + 1):
                part = lax.dot_general(
                    q_ref[...],
                    k_ref[j * ROWS : (j + 1) * ROWS],
                    (((1,), (1,)), ((), ())),
                    preferred_element_type=jnp.float32,
                )
                if j == step:
                    part = jnp.where(seen, part - corr[0, :, BAND:], -jnp.inf)
                elif j == step - 1:
                    part = jnp.concatenate(
                        [part[:, : ROWS - BAND], part[:, ROWS - BAND :] - corr[0, :, :BAND]], 1
                    )
                pieces.append(part)
            peak = pieces[0]
            for part in pieces[1:]:
                peak = jnp.maximum(peak, part)
            peak = jnp.max(peak, axis=1, keepdims=True)
            mass = jnp.zeros((ROWS, ROWS), jnp.float32)
            summed = jnp.zeros((ROWS, GROUP * HD), jnp.float32)
            for j, part in enumerate(pieces):
                probs = jnp.exp2(part - peak)
                mass = mass + probs
                summed = summed + jnp.dot(
                    probs.astype(jnp.bfloat16),
                    v_all[j * ROWS : (j + 1) * ROWS],
                    preferred_element_type=jnp.float32,
                )
            inverse = 1.0 / jnp.sum(mass, axis=1, keepdims=True)
            out = jnp.concatenate(
                [summed[:, g * HD : (g + 1) * HD] * (inverse * mix[g]) for g in range(GROUP)], 1
            ).astype(jnp.bfloat16)

            @pl.when(core == step % 2)
            def _():
                mine[0] = out

            @pl.when(core != step % 2)
            def _():
                theirs[0] = out


def attend_head(place, mix, q_wide, k_wide, corr, va, vb, vc, vd):
    total, depth = k_wide.shape
    count = total // ROWS
    out = jax.ShapeDtypeStruct((count // 2, ROWS, GROUP * HD), jnp.bfloat16)
    out_spec = pl.BlockSpec((1, ROWS, GROUP * HD), lambda b: (b // 2, 0, 0))
    v_spec = pl.BlockSpec(va.shape, lambda b: (0, 0, 0))
    return pl.pallas_call(
        attend_kernel,
        grid=(count,),
        out_shape=(out, out),
        in_specs=[
            whole(pltpu.SMEM),
            whole(pltpu.SMEM),
            pl.BlockSpec((ROWS, depth), lambda b: (b, 0)),
            pl.BlockSpec((total, depth), lambda b: (0, 0)),
            pl.BlockSpec((1, ROWS, BAND + ROWS), lambda b: (b, 0, 0)),
        ]
        + [v_spec] * 4,
        out_specs=[out_spec, out_spec],
        scratch_shapes=[pltpu.VMEM((total, GROUP * HD), jnp.bfloat16)],
        compiler_params=kernel_params(),
        cost_estimate=pl.CostEstimate(
            flops=total * total * (depth + GROUP * HD),
            bytes_accessed=16 * 2**20,
            transcendentals=total * total // 2,
        ),
    )(place, mix, q_wide, k_wide, corr, va, vb, vc, vd)


def finish_kernel(place, own, r1, r2, r3, gain, w_ref, out, normed):
    @pl.when(pl.program_id(0) == 0)
    def _():
        near = own[...] + r1[...].astype(jnp.float32)
        far = r2[...].astype(jnp.float32) + r3[...].astype(jnp.float32)
        low = place[3] == 0
        for g in range(2 * GROUP):
            cols = slice((g % GROUP) * HD, (g % GROUP + 1) * HD)
            first = low if g < GROUP else jnp.logical_not(low)
            x = jnp.where(first, near[:, cols], far[:, cols])
            scale = lax.rsqrt(jnp.mean(x * x, axis=1, keepdims=True) + 1e-05)
            normed[:, g * HD : (g + 1) * HD] = (
                x * scale * gain[:, g * HD : (g + 1) * HD]
            ).astype(jnp.bfloat16)

    out[0] = jnp.dot(normed[...], w_ref[0], preferred_element_type=jnp.float32).astype(jnp.bfloat16)


def finish(place, own, r1, r2, r3, gain, w_all):
    rows = own.shape[0]
    blocks, depth, width = w_all.shape
    per = blocks // 4
    fixed = pl.BlockSpec((rows, own.shape[1]), lambda c, place: (0, 0))
    return pl.pallas_call(
        finish_kernel,
        grid_spec=pltpu.PrefetchScalarGridSpec(
            num_scalar_prefetch=1,
            grid=(blocks,),
            in_specs=[fixed] * 4
            + [
                pl.BlockSpec((1, depth), lambda c, place: (0, 0)),
                pl.BlockSpec((1, depth, width), lambda c, place: (c, 0, 0)),
            ],
            out_specs=pl.BlockSpec(
                (1, rows, width), lambda c, place: (lax.bitwise_xor(c // per, place[4]), 0, c % per)
            ),
            scratch_shapes=[pltpu.VMEM((rows, depth), jnp.bfloat16)],
        ),
        out_shape=jax.ShapeDtypeStruct((4, rows, per * width), jnp.bfloat16),
        compiler_params=kernel_params(),
        cost_estimate=pl.CostEstimate(
            flops=2 * rows * depth * blocks * width, bytes_accessed=11 * 2**20, transcendentals=0
        ),
    )(place, own, r1, r2, r3, gain, w_all)


def swapped(value, axis, mask):
    count = lax.axis_size(axis)
    return lax.ppermute(value, axis, [(i, i ^ mask) for i in range(count)])


def per_device_one_head(
    activations, positions, w_query, w_key, w_value, conv_kernel, head_mix, out_gain, w_out
):
    ctx, head = lax.axis_index("ctx"), lax.axis_index("head")
    z, core = ctx // 2, ctx % 2
    pair = 2 * HD

    def columns(target):
        return jnp.concatenate(
            [
                lax.dynamic_slice_in_dim(w, target * pair, pair, 1)
                for w in (w_query, w_key, w_value)
            ],
            1,
        )

    inner = (z == 1) | (z == 2)
    near = swapped(activations, "ctx", 2)
    across = lax.ppermute(activations, "ctx", [(2, 4), (3, 5), (4, 2), (5, 3)])
    across_next = lax.ppermute(near, "ctx", [(2, 4), (3, 5), (4, 2), (5, 3)])
    outward = [(2, 0), (3, 1), (4, 6), (5, 7)]
    far_a = across + lax.ppermute(across, "ctx", outward)
    far_b = across_next + lax.ppermute(across_next, "ctx", outward)
    tokens = [activations, near, far_a, far_b]
    from_x = [swapped(a, "head", 1) for a in tokens]
    from_y = [swapped(a, "head", 2) for a in tokens]
    corner = [
        swapped(from_y[b], "head", 1) if b % 2 else swapped(from_x[b], "head", 2) for b in range(4)
    ]
    place_near = swapped(positions, "ctx", 2)
    place_far = swapped(jnp.stack([positions, place_near]), "ctx", 4)
    place_far = jnp.where(inner, place_far[::-1], place_far)
    place_of = jnp.concatenate([jnp.stack([positions, place_near]), place_far])
    order = jnp.where(inner, z ^ 3, z ^ 2), jnp.where(inner, z ^ 2, z ^ 3)
    place = jnp.stack([z ^ head, core, z % 2, z // 2, head, z, z ^ 1, *order]).astype(jnp.int32)

    w_same = [columns(z)] + [swapped(columns(z ^ s), "ctx", 2 * s) for s in (1, 2, 3)]
    w_swap = [swapped(w, "ctx", 1) for w in w_same]

    exponents = jnp.arange(HD // 2, dtype=jnp.float32) * (2.0 / HD)
    inverse = jnp.exp(-exponents * math.log(500000.0))
    angle = (place_of.astype(jnp.float32) * 0.25)[:, :, None] * inverse
    cosine, sine = jnp.cos(angle), jnp.sin(angle)
    mine, theirs, v_pair = project(
        place,
        tokens + from_x + from_y + corner,
        w_same,
        w_swap,
        jnp.concatenate([cosine, cosine], -1),
        jnp.concatenate([-sine, sine], -1),
    )
    other = swapped(theirs, "ctx", 1)
    v_next = swapped(v_pair, "ctx", 2)
    v_pair_other = swapped(v_pair, "ctx", 1)
    v_next_other = swapped(v_next, "ctx", 1)

    weights = lax.dynamic_index_in_dim(conv_kernel, ctx, 0, keepdims=False)
    weights = weights * (math.log2(math.e) / math.sqrt(HD))
    taps = weights.reshape(CQ, CK)
    even, odd = band_taps(taps, -BAND, 2 * LANES), band_taps(taps, -SUB, LANES)
    even, odd, _ = lax.optimization_barrier((even, odd, positions))
    q_wide, k_wide, corr = prepare(place, weights, mine, other, even, odd)
    group_rows = lax.dynamic_slice_in_dim(head_mix, GROUP * (ctx // GROUP), GROUP, 0)
    mix = lax.dynamic_index_in_dim(group_rows, ctx % GROUP, 1, keepdims=False)
    out_mine, out_theirs = attend_head(
        place, mix, q_wide, k_wide, corr, v_pair, v_next, v_pair_other, v_next_other
    )
    summed = out_mine.astype(jnp.float32) + swapped(out_theirs, "ctx", 1).astype(jnp.float32)
    own = lax.dynamic_index_in_dim(summed, z, 0, keepdims=False)
    r1, r2, r3 = [
        swapped(
            lax.dynamic_index_in_dim(summed, z ^ s, 0, keepdims=False).astype(jnp.bfloat16),
            "ctx",
            2 * s,
        )
        for s in (1, 2, 3)
    ]

    w_out, *_ = lax.optimization_barrier((w_out, far_b, w_same[2], w_same[3]))
    w_all = lax.all_gather(w_out, "ctx", axis=0)
    shares = finish(place, own, r1, r2, r3, out_gain.reshape(1, -1), w_all)
    total = shares[0].astype(jnp.float32)
    for t in (1, 2, 3):
        total = total + swapped(shares[t], "head", t).astype(jnp.float32)
    return total.astype(jnp.bfloat16)


def solution(mesh):
    one_head_each = mesh.shape["ctx"] == 8 and mesh.shape["head"] == 4
    body = per_device_one_head if one_head_each else per_device
    return jax.shard_map(
        body,
        mesh=mesh,
        in_specs=(
            P("ctx", "head"),
            P("ctx"),
            P("ctx", "head"),
            P("ctx", "head"),
            P("ctx", "head"),
            P("head", None),
            P("head", None),
            P("head"),
            P("head", "ctx"),
        ),
        out_specs=P("ctx", "head"),
        check_vma=False,
    )
```

```python
import math

import jax
import jax.numpy as jnp
from jax import lax
from jax.experimental import pallas as pl
from jax.experimental.pallas import tpu as pltpu
from jax.sharding import PartitionSpec as P

HD = 128
GROUP = 4
CQ = 6
CK = 11
KB = 512


def passed_along(value, axis, steps):
    count = lax.axis_size(axis)
    leading, last = (max(0, -steps), min(count, count - steps))
    return lax.ppermute(value, axis, [(source, source + steps) for source in range(leading, last)])


def rope(projected, positions):
    row_count = projected.shape[0]
    head_count = projected.shape[1] // HD
    shaped = projected.reshape(row_count, head_count, HD)
    half_size = HD // 2
    exponents = jnp.arange(half_size, dtype=jnp.float32) * (2.0 / HD)
    inverse = jnp.exp(-exponents * math.log(500000.0))
    angle = (positions.astype(jnp.float32) * 0.25)[:, None, None] * inverse[None, None, :]
    cosine = jnp.cos(angle)
    sine = jnp.sin(angle)
    lower_half = shaped[..., :half_size]
    upper_half = shaped[..., half_size:]
    rotated_rows = jnp.concatenate(
        [lower_half * cosine - upper_half * sine, upper_half * cosine + lower_half * sine], -1
    )
    return rotated_rows.reshape(row_count, head_count * HD)


def convolve(masked, kernel, row_count, col_count):
    summed = jnp.zeros((masked.shape[0], row_count, col_count), jnp.float32)
    for lag_q in range(CQ):
        for lag_k in range(CK):
            weight = kernel[:, lag_q * CK + lag_k][:, None, None]
            window = masked[
                :,
                CQ - 1 - lag_q : CQ - 1 - lag_q + row_count,
                CK - 1 - lag_k : CK - 1 - lag_k + col_count,
            ]
            summed = summed + weight * window
    return summed


def add_rows(left, piece):
    return jnp.dot(left, piece, preferred_element_type=jnp.float32)


def share_keys(key, value):
    return (
        lax.all_gather(key, "ctx", axis=0, tiled=True),
        lax.all_gather(value, "ctx", axis=0, tiled=True),
    )


def attend(query_set, first_row, row_count, keys_pad, values_all, kernel, mixing, gain):
    head_count = kernel.shape[0]
    ext_rows = row_count + CQ - 1
    query_heads = query_set.reshape(ext_rows, head_count, HD)
    token_total = values_all.shape[0]
    block_count = token_total // KB
    last_row = first_row + row_count - 1
    scale = 1.0 / math.sqrt(HD)
    prow = first_row - (CQ - 1) + jnp.arange(ext_rows, dtype=jnp.int32)
    irow = first_row + jnp.arange(row_count, dtype=jnp.int32)

    def logits_of(block):
        key_start = block * KB
        key_block = lax.dynamic_slice_in_dim(keys_pad, key_start, KB + CK - 1, 0).reshape(
            KB + CK - 1, head_count, HD
        )
        scores = (
            jnp.einsum("rhd,khd->hrk", query_heads, key_block, preferred_element_type=jnp.float32)
            * scale
        )
        kcol = key_start - CK // 2 + jnp.arange(KB + CK - 1, dtype=jnp.int32)
        valid = (kcol[None, :] <= prow[:, None]) & (prow[:, None] >= 0)
        masked = jnp.where(valid[None], scores, 0.0)
        conv = convolve(masked, kernel, row_count, KB)
        jcol = key_start + jnp.arange(KB, dtype=jnp.int32)
        return jnp.where((jcol[None, :] <= irow[:, None])[None], conv, -jnp.inf)

    def first_pass(block, carry_in):

        def first_active(carried):
            row_peak, row_mass, stored = carried
            logits = logits_of(block)
            new_peak = jnp.maximum(row_peak, jnp.max(logits, axis=-1))
            new_mass = row_mass * jnp.exp(row_peak - new_peak) + jnp.sum(
                jnp.exp(logits - new_peak[..., None]), axis=-1
            )
            stored = lax.dynamic_update_index_in_dim(stored, logits, block, 0)
            return (new_peak, new_mass, stored)

        return lax.cond(block * KB <= last_row, first_active, lambda carried: carried, carry_in)

    peak_start = jnp.full((head_count, row_count), -jnp.inf, jnp.float32)
    mass_start = jnp.zeros((head_count, row_count), jnp.float32)
    store_start = jnp.zeros((block_count, head_count, row_count, KB), jnp.float32)
    row_peak, row_mass, stored = lax.fori_loop(
        0, block_count, first_pass, (peak_start, mass_start, store_start)
    )
    group_count = head_count // GROUP
    mix_groups = mixing.reshape(group_count, GROUP, GROUP)

    def second_pass(block, carry_in):

        def second_active(summed):
            logits = lax.dynamic_index_in_dim(stored, block, 0, keepdims=False)
            probs = jnp.exp(logits - row_peak[..., None]) / row_mass[..., None]
            grouped = probs.reshape(group_count, GROUP, row_count, KB)
            mixed_scores = (
                jnp.einsum("gab,gbrk->gark", mix_groups, grouped)
                .reshape(head_count, row_count, KB)
                .astype(jnp.bfloat16)
            )
            value_block = lax.dynamic_slice_in_dim(values_all, block * KB, KB, 0).reshape(
                KB, head_count, HD
            )
            return summed + jnp.einsum(
                "hrk,khd->rhd", mixed_scores, value_block, preferred_element_type=jnp.float32
            )

        return lax.cond(block * KB <= last_row, second_active, lambda summed: summed, carry_in)

    summed = lax.fori_loop(
        0, block_count, second_pass, jnp.zeros((row_count, head_count, HD), jnp.float32)
    )
    rms = jnp.sqrt(jnp.mean(summed * summed, axis=-1, keepdims=True) + 1e-05)
    normed = (summed / rms * gain.reshape(head_count, HD)).astype(jnp.bfloat16)
    return normed.reshape(row_count, head_count * HD)


def per_device(
    activations, positions, w_query, w_key, w_value, conv_kernel, head_mix, out_gain, w_out
):
    row_count = activations.shape[0]
    ctx_place = lax.axis_index("ctx")
    features = lax.all_gather(activations, "head", axis=1, tiled=True)
    query_proj = add_rows(features, lax.all_gather(w_query, "ctx", axis=0, tiled=True))
    key_proj = add_rows(features, lax.all_gather(w_key, "ctx", axis=0, tiled=True))
    value_proj = add_rows(features, lax.all_gather(w_value, "ctx", axis=0, tiled=True))
    key = rope(key_proj, positions).astype(jnp.bfloat16)
    value = value_proj.astype(jnp.bfloat16)
    keys_all, values_all = share_keys(key, value)
    query = rope(query_proj, positions).astype(jnp.bfloat16)
    rim_rows = passed_along(query[row_count - (CQ - 1) :], "ctx", 1)
    query_ext = jnp.concatenate([rim_rows, query], 0)
    keys_pad = jnp.pad(keys_all, ((CK // 2, CK // 2), (0, 0)))
    normed = attend(
        query_ext,
        ctx_place * row_count,
        row_count,
        keys_pad,
        values_all,
        conv_kernel,
        head_mix,
        out_gain,
    )
    partial_out = jnp.dot(
        normed, lax.all_gather(w_out, "ctx", axis=1, tiled=True), preferred_element_type=jnp.float32
    )
    return lax.psum_scatter(
        partial_out.astype(jnp.bfloat16), "head", scatter_dimension=1, tiled=True
    )


ROWS = 256
BAND = 128
LANES = 128
SUB = 64
VMEM_BYTES = 56 * 1024 * 1024


def kernel_params():
    return pltpu.CompilerParams(vmem_limit_bytes=VMEM_BYTES)


def whole(memory_space):
    return pl.BlockSpec(memory_space=memory_space)


def project_kernel(place, *refs):
    a_own, a_x, a_y = refs[:4], refs[4:9], refs[9:14]
    weights = refs[14:20]
    cos_ref, sin_ref = refs[20:22]
    mine, theirs, v_out = refs[22:25]
    abuf, wbuf, sem_a, sem_w = refs[25:]
    turn, core = place[0], place[1]
    rows, depth = a_own[0].shape
    half, pair = weights[0].shape[1:]
    first_rows, last_rows = pl.ds(0, rows // 2), pl.ds(rows // 2, rows // 2)

    def copies_a(t, b):
        cols = pl.ds(t * depth, depth)
        if t < 3:
            source = (a_own, a_x, a_y)[t][b].at[pl.ds(0, rows)]
            return [pltpu.make_async_copy(source, abuf.at[b, :, cols], sem_a.at[t, b])]
        late = pl.ds(rows if b < 3 else 0, rows // 2)
        return [
            pltpu.make_async_copy(
                a_y[b + 1].at[late], abuf.at[b, first_rows, cols], sem_a.at[3, b]
            ),
            pltpu.make_async_copy(
                a_x[b + 1].at[late], abuf.at[b, last_rows, cols], sem_a.at[4, b]
            ),
        ]

    def copy_w(t, i):
        side = core if i % 2 == 0 else 1 - core
        start = pl.multiple_of(t * depth + side * half, half)
        return pltpu.make_async_copy(
            weights[i].at[lax.bitwise_xor(turn, t)],
            wbuf.at[pl.ds(start, half), pl.ds((i // 2) * pair, pair)],
            sem_w.at[t, i],
        )

    for t in range(4):
        for copy in copies_a(t, 0):
            copy.start()
        for i in range(6):
            copy_w(t, i).start()
    for b in range(1, 4):
        for t in range(4):
            for copy in copies_a(t, b):
                copy.start()
    for t in range(4):
        for i in range(6):
            copy_w(t, i).wait()
    first = core == 0
    for b in range(4):
        for t in range(4):
            for copy in copies_a(t, b):
                copy.wait()
        total = jnp.dot(abuf[b], wbuf[...], preferred_element_type=jnp.float32)
        cosine, sine = cos_ref[b], sin_ref[b]
        at = place[5 + b]
        for col, out in ((0, 0), (2 * HD, HD)):
            heads = []
            for start in (col, col + HD):
                x = total[:, start : start + HD]
                x = x * cosine + pltpu.roll(x, HD // 2, 1) * sine
                heads.append(x.astype(jnp.bfloat16))
            mine[at, :, out : out + HD] = jnp.where(first, heads[0], heads[1])
            theirs[at, :, out : out + HD] = jnp.where(first, heads[1], heads[0])
        v_out[at] = total[:, 4 * HD :].astype(jnp.bfloat16)


def project(place, a_own, a_x, a_y, weights, cosine, sine):
    rows, depth = a_own[0].shape
    width = 3 * weights[0].shape[2]
    out = jax.ShapeDtypeStruct((4, rows, 2 * HD), jnp.bfloat16)
    return pl.pallas_call(
        project_kernel,
        out_shape=(out, out, out),
        in_specs=[whole(pltpu.SMEM)] + [whole(pl.ANY)] * 20 + [whole(pltpu.VMEM)] * 2,
        out_specs=[whole(pltpu.VMEM)] * 3,
        scratch_shapes=[
            pltpu.VMEM((4, rows, 4 * depth), jnp.bfloat16),
            pltpu.VMEM((4 * depth, width), jnp.bfloat16),
            pltpu.SemaphoreType.DMA((5, 4)),
            pltpu.SemaphoreType.DMA((4, 6)),
        ],
        compiler_params=kernel_params(),
        cost_estimate=pl.CostEstimate(
            flops=8 * rows * 4 * depth * width, bytes_accessed=16 * 2**20, transcendentals=0
        ),
    )(place, *a_own, *a_x, *a_y, *weights, cosine, sine)


def prepare_kernel(place, weights, mine, other, even_ref, odd_ref, q_out, k_out, corr, qf, kf, lags):
    core = place[1]
    total = q_out.shape[0]
    qf[0:8] = jnp.zeros((8, HD), jnp.float32)
    kf[0:8] = jnp.zeros((8, HD), jnp.float32)
    kf[8 + total :] = jnp.zeros((kf.shape[0] - 8 - total, HD), jnp.float32)
    for i in range(total // (2 * ROWS)):
        for ref, parity in ((mine, core), (other, 1 - core)):
            start = pl.multiple_of(8 + (2 * i + parity) * ROWS, 8)
            block = ref[i].astype(jnp.float32)
            qf[pl.ds(start, ROWS)] = block[:, :HD]
            kf[pl.ds(start, ROWS)] = block[:, HD:]

    ahead = lax.broadcasted_iota(jnp.int32, (SUB + 8, LANES), 1) - lax.broadcasted_iota(
        jnp.int32, (SUB + 8, LANES), 0
    )
    near = (ahead >= 1) & (ahead < CQ + CK // 2)

    def block_step(b, carry):
        corr[b] = jnp.zeros(corr.shape[1:], jnp.float32)
        for m in range(ROWS // SUB):
            base = pl.multiple_of(b * ROWS + m * SUB, SUB)
            qwin = qf[pl.ds(base, SUB + 8)]
            kwin = kf[pl.ds(base, LANES)]
            scores = lax.dot_general(
                qwin.astype(jnp.bfloat16),
                kwin.astype(jnp.bfloat16),
                (((1,), (1,)), ((), ())),
                preferred_element_type=jnp.float32,
            )
            future = jnp.where(near, scores, 0.0)
            rows = pl.ds(pl.multiple_of((2 * b + m // 2) * SUB, SUB), SUB)
            for a in range(CQ):
                lags[m % 2, rows, a * LANES : (a + 1) * LANES] = future[
                    8 - a : 8 - a + SUB
                ].astype(jnp.bfloat16)
            for a in range(CQ):
                q_out[pl.ds(base, SUB), a * HD : (a + 1) * HD] = qwin[8 - a : 8 - a + SUB].astype(
                    jnp.bfloat16
                )
            sums = [None] * CQ
            for c in range(CK):
                off = 8 + CK // 2 - c
                window = kwin[off : off + SUB]
                for a in range(CQ):
                    term = weights[a * CK + c] * window
                    sums[a] = term if c == 0 else sums[a] + term
            for a in range(CQ):
                k_out[pl.ds(base, SUB), a * HD : (a + 1) * HD] = sums[a].astype(jnp.bfloat16)
        return carry

    lax.fori_loop(0, total // ROWS, block_step, 0)
    for odd, taps in enumerate((even_ref, odd_ref)):
        for b in range(0, total // ROWS, 2):
            fix = jnp.dot(
                lags[odd, 2 * b * SUB : (2 * b + 4) * SUB],
                taps[...],
                preferred_element_type=jnp.float32,
            )
            for n in range(4):
                m = 2 * (n % 2) + odd
                col = LANES * ((m + 1) // 2)
                corr[b + n // 2, m * SUB : (m + 1) * SUB, col : col + taps.shape[1]] = fix[
                    n * SUB : (n + 1) * SUB
                ]


def prepare(place, weights, mine, other, even, odd):
    total = mine.shape[0] * 2 * ROWS
    return pl.pallas_call(
        prepare_kernel,
        out_shape=(
            jax.ShapeDtypeStruct((total, CQ * HD), jnp.bfloat16),
            jax.ShapeDtypeStruct((total, CQ * HD), jnp.bfloat16),
            jax.ShapeDtypeStruct((total // ROWS, ROWS, BAND + ROWS), jnp.float32),
        ),
        in_specs=[whole(pltpu.SMEM)] * 2 + [whole(pltpu.VMEM)] * 4,
        out_specs=[whole(pltpu.VMEM)] * 3,
        scratch_shapes=[
            pltpu.VMEM((8 + total, HD), jnp.float32),
            pltpu.VMEM((8 + total + LANES, HD), jnp.float32),
            pltpu.VMEM((2, total // 2, CQ * LANES), jnp.bfloat16),
        ],
        compiler_params=kernel_params(),
        cost_estimate=pl.CostEstimate(flops=2**31, bytes_accessed=12 * 2**20, transcendentals=0),
    )(place, weights, mine, other, even, odd)


def band_taps(weights, first, lanes):
    lag = jnp.arange(CQ)[:, None, None]
    tap = (first + jnp.arange(lanes))[None, None, :] + CK // 2 + 8 - jnp.arange(LANES)[None, :, None]
    band = jnp.zeros((CQ, LANES, lanes), jnp.float32)
    for c in range(CK):
        band = band + jnp.where(tap == c, weights[:, c][:, None, None], 0.0)
    return band.astype(jnp.bfloat16).reshape(CQ * LANES, lanes)


def attend_kernel(place, mix, q_ref, k_ref, corr, va, vb, vc, vd, mine, theirs, v_all):
    side, core = place[2], place[1]
    b = pl.program_id(0)
    count = k_ref.shape[0] // ROWS

    @pl.when(b == 0)
    def _():
        for i in range(count // 2):
            for parity, near, far in ((core, va, vb), (1 - core, vc, vd)):
                rows = pl.ds(pl.multiple_of((2 * i + parity) * ROWS, ROWS), ROWS)
                first, last = near[i], far[i]
                v_all[rows, : 2 * HD] = jnp.where(side == 0, first, last)
                v_all[rows, 2 * HD :] = jnp.where(side == 0, last, first)

    row = lax.broadcasted_iota(jnp.int32, (ROWS, ROWS), 0)
    col = lax.broadcasted_iota(jnp.int32, (ROWS, ROWS), 1)
    seen = col <= row

    for step in range(count):

        @pl.when(b == step)
        def _():
            pieces = []
            for j in range(step + 1):
                part = lax.dot_general(
                    q_ref[...],
                    k_ref[j * ROWS : (j + 1) * ROWS],
                    (((1,), (1,)), ((), ())),
                    preferred_element_type=jnp.float32,
                )
                if j == step:
                    part = jnp.where(seen, part - corr[0, :, BAND:], -jnp.inf)
                elif j == step - 1:
                    part = jnp.concatenate(
                        [part[:, : ROWS - BAND], part[:, ROWS - BAND :] - corr[0, :, :BAND]], 1
                    )
                pieces.append(part)
            peak = pieces[0]
            for part in pieces[1:]:
                peak = jnp.maximum(peak, part)
            peak = jnp.max(peak, axis=1, keepdims=True)
            mass = jnp.zeros((ROWS, ROWS), jnp.float32)
            probs = []
            for part in pieces:
                part = jnp.exp2(part - peak)
                mass = mass + part
                probs.append(part.astype(jnp.bfloat16))
            summed = jnp.dot(
                jnp.concatenate(probs, 1),
                v_all[: (step + 1) * ROWS],
                preferred_element_type=jnp.float32,
            )
            inverse = 1.0 / jnp.sum(mass, axis=1, keepdims=True)
            out = jnp.concatenate(
                [summed[:, g * HD : (g + 1) * HD] * (inverse * mix[g]) for g in range(GROUP)], 1
            ).astype(jnp.bfloat16)

            @pl.when(core == step % 2)
            def _():
                mine[0] = out

            @pl.when(core != step % 2)
            def _():
                theirs[0] = out


def attend_head(place, mix, q_wide, k_wide, corr, va, vb, vc, vd):
    total, depth = k_wide.shape
    count = total // ROWS
    out = jax.ShapeDtypeStruct((count // 2, ROWS, GROUP * HD), jnp.bfloat16)
    out_spec = pl.BlockSpec((1, ROWS, GROUP * HD), lambda b: (b // 2, 0, 0))
    v_spec = pl.BlockSpec(va.shape, lambda b: (0, 0, 0))
    return pl.pallas_call(
        attend_kernel,
        grid=(count,),
        out_shape=(out, out),
        in_specs=[
            whole(pltpu.SMEM),
            whole(pltpu.SMEM),
            pl.BlockSpec((ROWS, depth), lambda b: (b, 0)),
            pl.BlockSpec((total, depth), lambda b: (0, 0)),
            pl.BlockSpec((1, ROWS, BAND + ROWS), lambda b: (b, 0, 0)),
        ]
        + [v_spec] * 4,
        out_specs=[out_spec, out_spec],
        scratch_shapes=[pltpu.VMEM((total, GROUP * HD), jnp.bfloat16)],
        compiler_params=kernel_params(),
        cost_estimate=pl.CostEstimate(
            flops=total * total * (depth + GROUP * HD),
            bytes_accessed=16 * 2**20,
            transcendentals=total * total // 2,
        ),
    )(place, mix, q_wide, k_wide, corr, va, vb, vc, vd)


def finish_kernel(place, own, r1, r2, r3, gain, w_any, out, normed, w_buf, sem):
    blocks, _, width = w_buf.shape
    per = blocks // 4
    order = [(t, i) for t in (3, 2, 1, 0) for i in range(per)]

    def copy_w(n):
        t, i = order[n]
        source = per * lax.bitwise_xor(place[4], t) + i
        return pltpu.make_async_copy(w_any.at[source], w_buf.at[n], sem.at[n])

    for n in range(blocks):
        copy_w(n).start()
    near = own[...] + r1[...].astype(jnp.float32)
    far = r2[...].astype(jnp.float32) + r3[...].astype(jnp.float32)
    low = place[3] == 0
    for g in range(2 * GROUP):
        cols = slice((g % GROUP) * HD, (g % GROUP + 1) * HD)
        first = low if g < GROUP else jnp.logical_not(low)
        x = jnp.where(first, near[:, cols], far[:, cols])
        scale = lax.rsqrt(jnp.mean(x * x, axis=1, keepdims=True) + 1e-05)
        normed[:, g * HD : (g + 1) * HD] = (
            x * scale * gain[:, g * HD : (g + 1) * HD]
        ).astype(jnp.bfloat16)
    for n in range(blocks):
        t, i = order[n]
        copy_w(n).wait()
        out[t, :, i * width : (i + 1) * width] = jnp.dot(
            normed[...], w_buf[n], preferred_element_type=jnp.float32
        ).astype(jnp.bfloat16)


def finish(place, own, r1, r2, r3, gain, w_all):
    rows = own.shape[0]
    blocks, depth, width = w_all.shape
    return pl.pallas_call(
        finish_kernel,
        in_specs=[whole(pltpu.SMEM)] + [whole(pltpu.VMEM)] * 5 + [whole(pl.ANY)],
        out_specs=whole(pltpu.VMEM),
        out_shape=jax.ShapeDtypeStruct((4, rows, blocks // 4 * width), jnp.bfloat16),
        scratch_shapes=[
            pltpu.VMEM((rows, depth), jnp.bfloat16),
            pltpu.VMEM((blocks, depth, width), jnp.bfloat16),
            pltpu.SemaphoreType.DMA((blocks,)),
        ],
        compiler_params=kernel_params(),
        cost_estimate=pl.CostEstimate(
            flops=2 * rows * depth * blocks * width, bytes_accessed=11 * 2**20, transcendentals=0
        ),
    )(place, own, r1, r2, r3, gain, w_all)


def swapped(value, axis, mask):
    count = lax.axis_size(axis)
    return lax.ppermute(value, axis, [(i, i ^ mask) for i in range(count)])


def per_device_one_head(
    activations, positions, w_query, w_key, w_value, conv_kernel, head_mix, out_gain, w_out
):
    ctx, head = lax.axis_index("ctx"), lax.axis_index("head")
    z, core = ctx // 2, ctx % 2
    pair = 2 * HD
    same_core = [[i for i in range(8) if i % 2 == k] for k in range(2)]

    def columns(w):
        return lax.all_to_all(
            w.reshape(w.shape[0], 4, pair).transpose(1, 0, 2),
            "ctx",
            0,
            0,
            axis_index_groups=same_core,
        )

    middle = [(2, 4), (3, 5), (4, 2), (5, 3)]
    outward = [(2, 0), (3, 1), (4, 6), (5, 7)]
    inner = (z == 1) | (z == 2)
    rows = activations.shape[0]
    half = rows // 2

    def plane(block, x_before, y_before):
        to_x = jnp.concatenate([block, y_before[half:rows]])
        to_y = jnp.concatenate([block, x_before[:half]])
        return swapped(to_x, "head", 1), swapped(to_y, "head", 2)

    barrier = lax.optimization_barrier
    near = swapped(activations, "ctx", 2)
    across = lax.ppermute(activations, "ctx", middle)
    x0, y0 = swapped(activations, "head", 1), swapped(activations, "head", 2)
    place_near = swapped(positions, "ctx", 2)
    near, across, x0, y0, place_near, w_value, w_key, w_query = barrier(
        (near, across, x0, y0, place_near, w_value, w_key, w_query)
    )
    across_next = lax.ppermute(near, "ctx", middle)
    passed = lax.ppermute(across, "ctx", outward)
    x1, y1 = plane(near, x0, y0)
    place_far = swapped(jnp.stack([positions, place_near]), "ctx", 4)
    v_same = columns(w_value)
    across_next, passed, x1, y1, place_far, v_same, w_key, w_query = barrier(
        (across_next, passed, x1, y1, place_far, v_same, w_key, w_query)
    )
    far_a = across + passed
    passed_next = lax.ppermute(across_next, "ctx", outward)
    x2, y2 = plane(far_a, x1, y1)
    k_same = columns(w_key)
    v_swap = swapped(v_same, "ctx", 1)
    passed_next, x2, y2, k_same, v_swap, w_query, w_out = barrier(
        (passed_next, x2, y2, k_same, v_swap, w_query, w_out)
    )
    far_b = across_next + passed_next
    x3, y3 = plane(far_b, x2, y2)
    q_same = columns(w_query)
    k_swap = swapped(k_same, "ctx", 1)
    x3, y3, q_same, k_swap = barrier((x3, y3, q_same, k_swap))
    x4, y4 = swapped(y3[half:rows], "head", 1), swapped(x3[:half], "head", 2)
    q_swap = swapped(q_same, "ctx", 1)

    place_far = jnp.where(inner, place_far[::-1], place_far)
    place_of = jnp.concatenate([jnp.stack([positions, place_near]), place_far])
    order = jnp.where(inner, z ^ 3, z ^ 2), jnp.where(inner, z ^ 2, z ^ 3)
    place = jnp.stack([head, core, z % 2, z // 2, head, z, z ^ 1, *order]).astype(jnp.int32)

    exponents = jnp.arange(HD // 2, dtype=jnp.float32) * (2.0 / HD)
    inverse = jnp.exp(-exponents * math.log(500000.0))
    angle = (place_of.astype(jnp.float32) * 0.25)[:, :, None] * inverse
    cosine, sine = jnp.cos(angle), jnp.sin(angle)
    mine, theirs, v_pair = project(
        place,
        (activations, near, far_a, far_b),
        (x0, x1, x2, x3, x4),
        (y0, y1, y2, y3, y4),
        (q_same, q_swap, k_same, k_swap, v_same, v_swap),
        jnp.concatenate([cosine, cosine], -1),
        jnp.concatenate([-sine, sine], -1),
    )
    other = swapped(theirs, "ctx", 1)
    v_next = swapped(v_pair, "ctx", 2)
    v_pair_other = swapped(v_pair, "ctx", 1)
    v_next_other = swapped(v_next, "ctx", 1)

    weights = lax.dynamic_index_in_dim(conv_kernel, ctx, 0, keepdims=False)
    weights = weights * (math.log2(math.e) / math.sqrt(HD))
    taps = weights.reshape(CQ, CK)
    even, odd = band_taps(taps, -BAND, 2 * LANES), band_taps(taps, -SUB, LANES)
    even, odd, _ = lax.optimization_barrier((even, odd, positions))
    q_wide, k_wide, corr = prepare(place, weights, mine, other, even, odd)
    group_rows = lax.dynamic_slice_in_dim(head_mix, GROUP * (ctx // GROUP), GROUP, 0)
    mix = lax.dynamic_index_in_dim(group_rows, ctx % GROUP, 1, keepdims=False)
    out_mine, out_theirs = attend_head(
        place, mix, q_wide, k_wide, corr, v_pair, v_next, v_pair_other, v_next_other
    )
    summed = out_mine.astype(jnp.float32) + swapped(out_theirs, "ctx", 1).astype(jnp.float32)
    own = lax.dynamic_index_in_dim(summed, z, 0, keepdims=False)
    r1, r2, r3 = [
        swapped(
            lax.dynamic_index_in_dim(summed, z ^ s, 0, keepdims=False).astype(jnp.bfloat16),
            "ctx",
            2 * s,
        )
        for s in (1, 2, 3)
    ]

    w_all = lax.all_gather(w_out, "ctx", axis=0)
    shares = finish(place, own, r1, r2, r3, out_gain.reshape(1, -1), w_all)
    total = shares[0].astype(jnp.float32)
    for t in (1, 2, 3):
        total = total + swapped(shares[t], "head", t).astype(jnp.float32)
    return total.astype(jnp.bfloat16)


def solution(mesh):
    one_head_each = mesh.shape["ctx"] == 8 and mesh.shape["head"] == 4
    body = per_device_one_head if one_head_each else per_device
    return jax.shard_map(
        body,
        mesh=mesh,
        in_specs=(
            P("ctx", "head"),
            P("ctx"),
            P("ctx", "head"),
            P("ctx", "head"),
            P("ctx", "head"),
            P("head", None),
            P("head", None),
            P("head"),
            P("head", "ctx"),
        ),
        out_specs=P("ctx", "head"),
        check_vma=False,
    )
```

```python
import math

import jax
import jax.numpy as jnp
from jax import lax
from jax.experimental import pallas as pl
from jax.experimental.pallas import tpu as pltpu
from jax.sharding import PartitionSpec as P

HD = 128
GROUP = 4
CQ = 6
CK = 11
KB = 512


def passed_along(value, axis, steps):
    count = lax.axis_size(axis)
    leading, last = (max(0, -steps), min(count, count - steps))
    return lax.ppermute(value, axis, [(source, source + steps) for source in range(leading, last)])


def rope(projected, positions):
    row_count = projected.shape[0]
    head_count = projected.shape[1] // HD
    shaped = projected.reshape(row_count, head_count, HD)
    half_size = HD // 2
    exponents = jnp.arange(half_size, dtype=jnp.float32) * (2.0 / HD)
    inverse = jnp.exp(-exponents * math.log(500000.0))
    angle = (positions.astype(jnp.float32) * 0.25)[:, None, None] * inverse[None, None, :]
    cosine = jnp.cos(angle)
    sine = jnp.sin(angle)
    lower_half = shaped[..., :half_size]
    upper_half = shaped[..., half_size:]
    rotated_rows = jnp.concatenate(
        [lower_half * cosine - upper_half * sine, upper_half * cosine + lower_half * sine], -1
    )
    return rotated_rows.reshape(row_count, head_count * HD)


def convolve(masked, kernel, row_count, col_count):
    summed = jnp.zeros((masked.shape[0], row_count, col_count), jnp.float32)
    for lag_q in range(CQ):
        for lag_k in range(CK):
            weight = kernel[:, lag_q * CK + lag_k][:, None, None]
            window = masked[
                :,
                CQ - 1 - lag_q : CQ - 1 - lag_q + row_count,
                CK - 1 - lag_k : CK - 1 - lag_k + col_count,
            ]
            summed = summed + weight * window
    return summed


def add_rows(left, piece):
    return jnp.dot(left, piece, preferred_element_type=jnp.float32)


def share_keys(key, value):
    return (
        lax.all_gather(key, "ctx", axis=0, tiled=True),
        lax.all_gather(value, "ctx", axis=0, tiled=True),
    )


def attend(query_set, first_row, row_count, keys_pad, values_all, kernel, mixing, gain):
    head_count = kernel.shape[0]
    ext_rows = row_count + CQ - 1
    query_heads = query_set.reshape(ext_rows, head_count, HD)
    token_total = values_all.shape[0]
    block_count = token_total // KB
    last_row = first_row + row_count - 1
    scale = 1.0 / math.sqrt(HD)
    prow = first_row - (CQ - 1) + jnp.arange(ext_rows, dtype=jnp.int32)
    irow = first_row + jnp.arange(row_count, dtype=jnp.int32)

    def logits_of(block):
        key_start = block * KB
        key_block = lax.dynamic_slice_in_dim(keys_pad, key_start, KB + CK - 1, 0).reshape(
            KB + CK - 1, head_count, HD
        )
        scores = (
            jnp.einsum("rhd,khd->hrk", query_heads, key_block, preferred_element_type=jnp.float32)
            * scale
        )
        kcol = key_start - CK // 2 + jnp.arange(KB + CK - 1, dtype=jnp.int32)
        valid = (kcol[None, :] <= prow[:, None]) & (prow[:, None] >= 0)
        masked = jnp.where(valid[None], scores, 0.0)
        conv = convolve(masked, kernel, row_count, KB)
        jcol = key_start + jnp.arange(KB, dtype=jnp.int32)
        return jnp.where((jcol[None, :] <= irow[:, None])[None], conv, -jnp.inf)

    def first_pass(block, carry_in):

        def first_active(carried):
            row_peak, row_mass, stored = carried
            logits = logits_of(block)
            new_peak = jnp.maximum(row_peak, jnp.max(logits, axis=-1))
            new_mass = row_mass * jnp.exp(row_peak - new_peak) + jnp.sum(
                jnp.exp(logits - new_peak[..., None]), axis=-1
            )
            stored = lax.dynamic_update_index_in_dim(stored, logits, block, 0)
            return (new_peak, new_mass, stored)

        return lax.cond(block * KB <= last_row, first_active, lambda carried: carried, carry_in)

    peak_start = jnp.full((head_count, row_count), -jnp.inf, jnp.float32)
    mass_start = jnp.zeros((head_count, row_count), jnp.float32)
    store_start = jnp.zeros((block_count, head_count, row_count, KB), jnp.float32)
    row_peak, row_mass, stored = lax.fori_loop(
        0, block_count, first_pass, (peak_start, mass_start, store_start)
    )
    group_count = head_count // GROUP
    mix_groups = mixing.reshape(group_count, GROUP, GROUP)

    def second_pass(block, carry_in):

        def second_active(summed):
            logits = lax.dynamic_index_in_dim(stored, block, 0, keepdims=False)
            probs = jnp.exp(logits - row_peak[..., None]) / row_mass[..., None]
            grouped = probs.reshape(group_count, GROUP, row_count, KB)
            mixed_scores = (
                jnp.einsum("gab,gbrk->gark", mix_groups, grouped)
                .reshape(head_count, row_count, KB)
                .astype(jnp.bfloat16)
            )
            value_block = lax.dynamic_slice_in_dim(values_all, block * KB, KB, 0).reshape(
                KB, head_count, HD
            )
            return summed + jnp.einsum(
                "hrk,khd->rhd", mixed_scores, value_block, preferred_element_type=jnp.float32
            )

        return lax.cond(block * KB <= last_row, second_active, lambda summed: summed, carry_in)

    summed = lax.fori_loop(
        0, block_count, second_pass, jnp.zeros((row_count, head_count, HD), jnp.float32)
    )
    rms = jnp.sqrt(jnp.mean(summed * summed, axis=-1, keepdims=True) + 1e-05)
    normed = (summed / rms * gain.reshape(head_count, HD)).astype(jnp.bfloat16)
    return normed.reshape(row_count, head_count * HD)


def per_device(
    activations, positions, w_query, w_key, w_value, conv_kernel, head_mix, out_gain, w_out
):
    row_count = activations.shape[0]
    ctx_place = lax.axis_index("ctx")
    features = lax.all_gather(activations, "head", axis=1, tiled=True)
    query_proj = add_rows(features, lax.all_gather(w_query, "ctx", axis=0, tiled=True))
    key_proj = add_rows(features, lax.all_gather(w_key, "ctx", axis=0, tiled=True))
    value_proj = add_rows(features, lax.all_gather(w_value, "ctx", axis=0, tiled=True))
    key = rope(key_proj, positions).astype(jnp.bfloat16)
    value = value_proj.astype(jnp.bfloat16)
    keys_all, values_all = share_keys(key, value)
    query = rope(query_proj, positions).astype(jnp.bfloat16)
    rim_rows = passed_along(query[row_count - (CQ - 1) :], "ctx", 1)
    query_ext = jnp.concatenate([rim_rows, query], 0)
    keys_pad = jnp.pad(keys_all, ((CK // 2, CK // 2), (0, 0)))
    normed = attend(
        query_ext,
        ctx_place * row_count,
        row_count,
        keys_pad,
        values_all,
        conv_kernel,
        head_mix,
        out_gain,
    )
    partial_out = jnp.dot(
        normed, lax.all_gather(w_out, "ctx", axis=1, tiled=True), preferred_element_type=jnp.float32
    )
    return lax.psum_scatter(
        partial_out.astype(jnp.bfloat16), "head", scatter_dimension=1, tiled=True
    )


ROWS = 256
BAND = 128
LANES = 128
SUB = 64
AHEAD = 16
VMEM_BYTES = 56 * 1024 * 1024


def kernel_params():
    return pltpu.CompilerParams(vmem_limit_bytes=VMEM_BYTES)


def whole(memory_space):
    return pl.BlockSpec(memory_space=memory_space)


def project_kernel(place, *refs):
    a_own, a_x, a_y = refs[:4], refs[4:9], refs[9:14]
    weights = refs[14:18]
    cos_ref, sin_ref = refs[18:20]
    mine, theirs, v_out = refs[20:23]
    abuf, wbuf, acc, sem_a, sem_w = refs[23:]
    turn, core = place[0], place[1]
    rows, depth = a_own[0].shape
    half = weights[0].shape[1]

    def copies(t):
        out = []
        start = 0
        for i in range(4):
            width = weights[i].shape[2]
            side = core if i % 2 == 0 else 1 - core
            out.append(
                pltpu.make_async_copy(
                    weights[i].at[lax.bitwise_xor(turn, t)],
                    wbuf.at[
                        t, pl.ds(pl.multiple_of(side * half, half), half), pl.ds(start, width)
                    ],
                    sem_w.at[t, i],
                )
            )
            start += width * (i % 2)
        for b in range(4):
            if t < 3:
                source = (a_own, a_x, a_y)[t][b].at[pl.ds(0, rows)]
                target = abuf.at[t, pl.ds(b * rows, rows)]
                out.append(pltpu.make_async_copy(source, target, sem_a.at[t, b]))
                continue
            late = pl.ds(rows if b < 3 else 0, rows // 2)
            for n, part in enumerate((a_y, a_x)):
                target = abuf.at[t, pl.ds(b * rows + n * (rows // 2), rows // 2)]
                out.append(
                    pltpu.make_async_copy(part[b + 1].at[late], target, sem_a.at[t + n, b])
                )
        return out

    for t in range(4):
        for copy in copies(t):
            copy.start()
    for t in range(4):
        for copy in copies(t):
            copy.wait()
        part = jnp.dot(abuf[t], wbuf[t], preferred_element_type=jnp.float32)
        acc[...] = part if t == 0 else acc[...] + part
    first = core == 0
    for b in range(4):
        total = acc[b * rows : (b + 1) * rows]
        cosine, sine = cos_ref[b], sin_ref[b]
        at = place[5 + b]
        for col, out in ((0, 0), (4 * HD, HD)):
            heads = []
            for start in (col, col + HD):
                x = total[:, start : start + HD]
                x = x * cosine + pltpu.roll(x, HD // 2, 1) * sine
                heads.append(x.astype(jnp.bfloat16))
            mine[at, :, out : out + HD] = jnp.where(first, heads[0], heads[1])
            theirs[at, :, out : out + HD] = jnp.where(first, heads[1], heads[0])
        v_out[at] = total[:, 2 * HD : 4 * HD].astype(jnp.bfloat16)


def project(place, a_own, a_x, a_y, weights, cosine, sine):
    rows, depth = a_own[0].shape
    width = weights[0].shape[2] + weights[2].shape[2]
    out = jax.ShapeDtypeStruct((4, rows, 2 * HD), jnp.bfloat16)
    return pl.pallas_call(
        project_kernel,
        out_shape=(out, out, out),
        in_specs=[whole(pltpu.SMEM)] + [whole(pl.ANY)] * 18 + [whole(pltpu.VMEM)] * 2,
        out_specs=[whole(pltpu.VMEM)] * 3,
        scratch_shapes=[
            pltpu.VMEM((4, 4 * rows, depth), jnp.bfloat16),
            pltpu.VMEM((4, depth, width), jnp.bfloat16),
            pltpu.VMEM((4 * rows, width), jnp.float32),
            pltpu.SemaphoreType.DMA((5, 4)),
            pltpu.SemaphoreType.DMA((4, 4)),
        ],
        compiler_params=kernel_params(),
        cost_estimate=pl.CostEstimate(
            flops=8 * rows * 4 * depth * width, bytes_accessed=16 * 2**20, transcendentals=0
        ),
    )(place, *a_own, *a_x, *a_y, *weights, cosine, sine)


def prepare_kernel(place, mine, other, key_ref, even_ref, odd_ref, q_out, k_out, corr, *scratch):
    qf, kf, lags, turned = scratch
    core = place[1]
    total = q_out.shape[0]
    qf[0:8] = jnp.zeros((8, HD), jnp.float32)
    kf[0:AHEAD] = jnp.zeros((AHEAD, HD), jnp.float32)
    kf[AHEAD + total :] = jnp.zeros((kf.shape[0] - AHEAD - total, HD), jnp.float32)
    corr[...] = jnp.zeros(corr.shape, jnp.float32)
    for i in range(total // (2 * ROWS)):
        for ref, parity in ((mine, core), (other, 1 - core)):
            start = pl.multiple_of((2 * i + parity) * ROWS, ROWS)
            block = ref[i].astype(jnp.float32)
            qf[pl.ds(8 + start, ROWS)] = block[:, :HD]
            kf[pl.ds(AHEAD + start, ROWS)] = block[:, HD:]

    ahead = lax.broadcasted_iota(jnp.int32, (SUB + 8, LANES), 1) - lax.broadcasted_iota(
        jnp.int32, (SUB + 8, LANES), 0
    )
    near = (ahead >= 1) & (ahead < CQ + CK // 2)
    steps = total // LANES
    for w in range(steps):
        base = w * LANES
        window = kf[base : base + 2 * LANES].T
        turned[base : base + LANES] = window.astype(jnp.bfloat16)
        for odd in range(2):
            at = base + odd * SUB
            qwin = qf[at : at + SUB + 8]
            kwin = kf[at + AHEAD - 8 : at + AHEAD - 8 + LANES]
            scores = lax.dot_general(
                qwin.astype(jnp.bfloat16),
                kwin.astype(jnp.bfloat16),
                (((1,), (1,)), ((), ())),
                preferred_element_type=jnp.float32,
            )
            future = jnp.where(near, scores, 0.0)
            for a in range(CQ):
                cols = slice(a * LANES, (a + 1) * LANES)
                lags[odd, w * SUB : (w + 1) * SUB, cols] = future[8 - a : 8 - a + SUB].astype(
                    jnp.bfloat16
                )
                q_out[at : at + SUB, cols] = qwin[8 - a : 8 - a + SUB].astype(jnp.bfloat16)
    for w in range(0, steps, 4):
        wide = jnp.dot(
            turned[w * LANES : (w + 4) * LANES], key_ref[...], preferred_element_type=jnp.float32
        )
        for n in range(4):
            cols = slice((w + n) * LANES, (w + n + 1) * LANES)
            for a in range(CQ):
                k_out[a * HD : (a + 1) * HD, cols] = wide[
                    n * LANES : (n + 1) * LANES, a * LANES : (a + 1) * LANES
                ].astype(jnp.bfloat16)
    for odd, taps in enumerate((even_ref, odd_ref)):
        for w in range(0, steps, 8):
            fix = jnp.dot(
                lags[odd, w * SUB : (w + 8) * SUB], taps[...], preferred_element_type=jnp.float32
            )
            for n in range(8):
                m = 2 * ((w + n) % 2) + odd
                col = LANES * ((m + 1) // 2)
                corr[(w + n) // 2, m * SUB : (m + 1) * SUB, col : col + taps.shape[1]] = fix[
                    n * SUB : (n + 1) * SUB
                ]


def prepare(place, mine, other, key_taps, even, odd):
    total = mine.shape[0] * 2 * ROWS
    return pl.pallas_call(
        prepare_kernel,
        out_shape=(
            jax.ShapeDtypeStruct((total, CQ * HD), jnp.bfloat16),
            jax.ShapeDtypeStruct((CQ * HD, total), jnp.bfloat16),
            jax.ShapeDtypeStruct((total // ROWS, ROWS, BAND + ROWS), jnp.float32),
        ),
        in_specs=[whole(pltpu.SMEM)] + [whole(pltpu.VMEM)] * 5,
        out_specs=[whole(pltpu.VMEM)] * 3,
        scratch_shapes=[
            pltpu.VMEM((8 + total, HD), jnp.float32),
            pltpu.VMEM((AHEAD + total + LANES, HD), jnp.float32),
            pltpu.VMEM((2, total // 2, CQ * LANES), jnp.bfloat16),
            pltpu.VMEM((total, 2 * LANES), jnp.bfloat16),
        ],
        compiler_params=kernel_params(),
        cost_estimate=pl.CostEstimate(flops=2**31, bytes_accessed=12 * 2**20, transcendentals=0),
    )(place, mine, other, key_taps, even, odd)


def key_taps_of(weights):
    tap = jnp.arange(LANES)[None, None, :] + CK // 2 + AHEAD - jnp.arange(2 * LANES)[:, None, None]
    out = jnp.zeros((2 * LANES, CQ, LANES), jnp.float32)
    for c in range(CK):
        out = out + jnp.where(tap == c, weights[:, c][None, :, None], 0.0)
    return out.astype(jnp.bfloat16).reshape(2 * LANES, CQ * LANES)


def band_taps(weights, first, lanes):
    lag = jnp.arange(CQ)[:, None, None]
    tap = (first + jnp.arange(lanes))[None, None, :] + CK // 2 + 8 - jnp.arange(LANES)[None, :, None]
    band = jnp.zeros((CQ, LANES, lanes), jnp.float32)
    for c in range(CK):
        band = band + jnp.where(tap == c, weights[:, c][:, None, None], 0.0)
    return band.astype(jnp.bfloat16).reshape(CQ * LANES, lanes)


def attend_kernel(place, mix, q_ref, k_ref, corr, va, vb, vc, vd, mine, theirs, v_all):
    side, core = place[2], place[1]
    b = pl.program_id(0)
    count = k_ref.shape[1] // (2 * ROWS)

    @pl.when(b == 0)
    def _():
        for i in range(count):
            for parity, near, far in ((core, va, vb), (1 - core, vc, vd)):
                rows = pl.ds(pl.multiple_of((2 * i + parity) * ROWS, ROWS), ROWS)
                first, last = near[i], far[i]
                v_all[rows, : 2 * HD] = jnp.where(side == 0, first, last)
                v_all[rows, 2 * HD :] = jnp.where(side == 0, last, first)

    row = lax.broadcasted_iota(jnp.int32, (ROWS, ROWS), 0)
    col = lax.broadcasted_iota(jnp.int32, (ROWS, ROWS), 1)
    seen = col <= row
    top, low = slice(0, ROWS), slice(ROWS, 2 * ROWS)

    def fixed(part, n):
        return jnp.concatenate([part[:, :BAND], part[:, BAND:] - corr[n, :, :BAND]], 1)

    def rows_of(upper, lower):
        return jnp.concatenate([upper, lower], 0)

    def block(step):
        parts = []
        for j in range(2 * step + 1):
            part = jnp.dot(
                q_ref[...],
                k_ref[:, j * ROWS : (j + 1) * ROWS],
                preferred_element_type=jnp.float32,
            )
            if j == 2 * step:
                diagonal = jnp.where(seen, part[top] - corr[0, :, BAND:], -jnp.inf)
                part = rows_of(diagonal, fixed(part[low], 1))
            elif j == 2 * step - 1:
                part = rows_of(fixed(part[top], 0), part[low])
            parts.append(part)
        start = (2 * step + 1) * ROWS
        last = jnp.dot(
            q_ref[low], k_ref[:, start : start + ROWS], preferred_element_type=jnp.float32
        )
        last = jnp.where(seen, last - corr[1, :, BAND:], -jnp.inf)
        peak = parts[0]
        for part in parts[1:]:
            peak = jnp.maximum(peak, part)
        peak = rows_of(peak[top], jnp.maximum(peak[low], last))
        peak = jnp.max(peak, axis=1, keepdims=True)
        mass = jnp.zeros((2 * ROWS, ROWS), jnp.float32)
        probs = []
        for part in parts:
            part = jnp.exp2(part - peak)
            mass = mass + part
            probs.append(part.astype(jnp.bfloat16))
        last = jnp.exp2(last - peak[low])
        mass = rows_of(mass[top], mass[low] + last)
        summed = jnp.dot(
            jnp.concatenate(probs, 1), v_all[:start], preferred_element_type=jnp.float32
        )
        extra = jnp.dot(
            last.astype(jnp.bfloat16),
            v_all[start : start + ROWS],
            preferred_element_type=jnp.float32,
        )
        inverse = 1.0 / jnp.sum(mass, axis=1, keepdims=True)
        halves = []
        for rows, total in ((top, summed[top]), (low, summed[low] + extra)):
            halves.append(
                jnp.concatenate(
                    [
                        total[:, g * HD : (g + 1) * HD] * (inverse[rows] * mix[g])
                        for g in range(GROUP)
                    ],
                    1,
                ).astype(jnp.bfloat16)
            )
        mine[0] = jnp.where(core == 0, halves[0], halves[1])
        theirs[0] = jnp.where(core == 0, halves[1], halves[0])

    for step in range(count):
        pl.when(b == step)(lambda step=step: block(step))


def attend_head(place, mix, q_wide, k_wide, corr, va, vb, vc, vd):
    depth, total = k_wide.shape
    rows = 2 * ROWS
    count = total // rows
    out = jax.ShapeDtypeStruct((count, ROWS, GROUP * HD), jnp.bfloat16)
    out_spec = pl.BlockSpec((1, ROWS, GROUP * HD), lambda b: (b, 0, 0))
    v_spec = pl.BlockSpec(va.shape, lambda b: (0, 0, 0))
    return pl.pallas_call(
        attend_kernel,
        grid=(count,),
        out_shape=(out, out),
        in_specs=[
            whole(pltpu.SMEM),
            whole(pltpu.SMEM),
            pl.BlockSpec((rows, depth), lambda b: (b, 0)),
            pl.BlockSpec((depth, total), lambda b: (0, 0)),
            pl.BlockSpec((2, ROWS, BAND + ROWS), lambda b: (b, 0, 0)),
        ]
        + [v_spec] * 4,
        out_specs=[out_spec, out_spec],
        scratch_shapes=[pltpu.VMEM((total, GROUP * HD), jnp.bfloat16)],
        compiler_params=kernel_params(),
        cost_estimate=pl.CostEstimate(
            flops=total * total * (depth + GROUP * HD),
            bytes_accessed=16 * 2**20,
            transcendentals=total * total // 2,
        ),
    )(place, mix, q_wide, k_wide, corr, va, vb, vc, vd)


def finish_kernel(place, own, r1, r2, r3, gain, w_any, o0, o1, o2, o3, normed, w_buf, sem):
    blocks, _, width = w_buf.shape
    per = blocks // 4
    order = [(t, i) for t in (3, 2, 1, 0) for i in range(per)]

    def copy_w(n):
        t, i = order[n]
        source = per * lax.bitwise_xor(place[4], t) + i
        return pltpu.make_async_copy(w_any.at[source], w_buf.at[n], sem.at[n])

    for n in range(blocks):
        copy_w(n).start()
    near = own[...] + r1[...].astype(jnp.float32)
    far = r2[...].astype(jnp.float32) + r3[...].astype(jnp.float32)
    low = place[3] == 0
    for g in range(2 * GROUP):
        cols = slice((g % GROUP) * HD, (g % GROUP + 1) * HD)
        first = low if g < GROUP else jnp.logical_not(low)
        x = jnp.where(first, near[:, cols], far[:, cols])
        scale = lax.rsqrt(jnp.mean(x * x, axis=1, keepdims=True) + 1e-05)
        normed[:, g * HD : (g + 1) * HD] = (
            x * scale * gain[:, g * HD : (g + 1) * HD]
        ).astype(jnp.bfloat16)
    for n in range(blocks):
        t, i = order[n]
        copy_w(n).wait()
        (o0, o1, o2, o3)[t][:, i * width : (i + 1) * width] = jnp.dot(
            normed[...], w_buf[n], preferred_element_type=jnp.float32
        ).astype(jnp.bfloat16)


def finish(place, own, r1, r2, r3, gain, w_all):
    rows = own.shape[0]
    blocks, depth, width = w_all.shape
    return pl.pallas_call(
        finish_kernel,
        in_specs=[whole(pltpu.SMEM)] + [whole(pltpu.VMEM)] * 5 + [whole(pl.ANY)],
        out_specs=[whole(pltpu.VMEM)] * 4,
        out_shape=[jax.ShapeDtypeStruct((rows, blocks // 4 * width), jnp.bfloat16)] * 4,
        scratch_shapes=[
            pltpu.VMEM((rows, depth), jnp.bfloat16),
            pltpu.VMEM((blocks, depth, width), jnp.bfloat16),
            pltpu.SemaphoreType.DMA((blocks,)),
        ],
        compiler_params=kernel_params(),
        cost_estimate=pl.CostEstimate(
            flops=2 * rows * depth * blocks * width, bytes_accessed=11 * 2**20, transcendentals=0
        ),
    )(place, own, r1, r2, r3, gain, w_all)


def swapped(value, axis, mask):
    count = lax.axis_size(axis)
    return lax.ppermute(value, axis, [(i, i ^ mask) for i in range(count)])


def per_device_one_head(
    activations, positions, w_query, w_key, w_value, conv_kernel, head_mix, out_gain, w_out
):
    ctx, head = lax.axis_index("ctx"), lax.axis_index("head")
    z, core = ctx // 2, ctx % 2
    pair = 2 * HD
    same_core = [[i for i in range(8) if i % 2 == k] for k in range(2)]

    def columns(*weights):
        shaped = [w.reshape(w.shape[0], 4, pair) for w in weights]
        return lax.all_to_all(
            jnp.concatenate(shaped, -1).transpose(1, 0, 2),
            "ctx",
            0,
            0,
            axis_index_groups=same_core,
        )

    middle = [(2, 4), (3, 5), (4, 2), (5, 3)]
    outward = [(2, 0), (3, 1), (4, 6), (5, 7)]
    inner = (z == 1) | (z == 2)
    rows = activations.shape[0]
    half = rows // 2

    def plane(block, x_before, y_before):
        to_x = jnp.concatenate([block, y_before[half:rows]])
        to_y = jnp.concatenate([block, x_before[:half]])
        return swapped(to_x, "head", 1), swapped(to_y, "head", 2)

    barrier = lax.optimization_barrier
    near = swapped(activations, "ctx", 2)
    across = lax.ppermute(activations, "ctx", middle)
    x0, y0 = swapped(activations, "head", 1), swapped(activations, "head", 2)
    place_near = swapped(positions, "ctx", 2)
    vk_same, q_same = columns(w_value, w_key), columns(w_query)
    near, across, x0, y0 = barrier((near, across, x0, y0))
    across_next = lax.ppermute(near, "ctx", middle)
    passed = lax.ppermute(across, "ctx", outward)
    x1, y1 = plane(near, x0, y0)
    across_next, passed, x1, y1, place_near = barrier((across_next, passed, x1, y1, place_near))
    far_a = across + passed
    passed_next = lax.ppermute(across_next, "ctx", outward)
    x2, y2 = plane(far_a, x1, y1)
    place_far = swapped(jnp.stack([positions, place_near]), "ctx", 4)
    passed_next, x2, y2, place_far, vk_same = barrier((passed_next, x2, y2, place_far, vk_same))
    far_b = across_next + passed_next
    x3, y3 = plane(far_b, x2, y2)
    vk_swap = swapped(vk_same, "ctx", 1)
    x3, y3, vk_swap, q_same, w_out = barrier((x3, y3, vk_swap, q_same, w_out))
    x4, y4 = swapped(y3[half:rows], "head", 1), swapped(x3[:half], "head", 2)
    q_swap = swapped(q_same, "ctx", 1)

    place_far = jnp.where(inner, place_far[::-1], place_far)
    place_of = jnp.concatenate([jnp.stack([positions, place_near]), place_far])
    order = jnp.where(inner, z ^ 3, z ^ 2), jnp.where(inner, z ^ 2, z ^ 3)
    place = jnp.stack([head, core, z % 2, z // 2, head, z, z ^ 1, *order]).astype(jnp.int32)

    exponents = jnp.arange(HD // 2, dtype=jnp.float32) * (2.0 / HD)
    inverse = jnp.exp(-exponents * math.log(500000.0))
    angle = (place_of.astype(jnp.float32) * 0.25)[:, :, None] * inverse
    cosine, sine = jnp.cos(angle), jnp.sin(angle)
    mine, theirs, v_pair = project(
        place,
        (activations, near, far_a, far_b),
        (x0, x1, x2, x3, x4),
        (y0, y1, y2, y3, y4),
        (q_same, q_swap, vk_same, vk_swap),
        jnp.concatenate([cosine, cosine], -1),
        jnp.concatenate([-sine, sine], -1),
    )
    other = swapped(theirs, "ctx", 1)
    v_next = swapped(v_pair, "ctx", 2)
    v_pair_other = swapped(v_pair, "ctx", 1)

    weights = lax.dynamic_index_in_dim(conv_kernel, ctx, 0, keepdims=False)
    weights = weights * (math.log2(math.e) / math.sqrt(HD))
    taps = weights.reshape(CQ, CK)
    tables = key_taps_of(taps), band_taps(taps, -BAND, 2 * LANES), band_taps(taps, -SUB, LANES)
    q_wide, k_wide, corr = prepare(place, mine, other, *tables)
    v_next, q_wide = barrier((v_next, q_wide))
    v_next_other = swapped(v_next, "ctx", 1)
    group_rows = lax.dynamic_slice_in_dim(head_mix, GROUP * (ctx // GROUP), GROUP, 0)
    mix = lax.dynamic_index_in_dim(group_rows, ctx % GROUP, 1, keepdims=False)
    out_mine, out_theirs = attend_head(
        place, mix, q_wide, k_wide, corr, v_pair, v_next, v_pair_other, v_next_other
    )
    summed = out_mine.astype(jnp.float32) + swapped(out_theirs, "ctx", 1).astype(jnp.float32)
    own = lax.dynamic_index_in_dim(summed, z, 0, keepdims=False)
    r1, r2, r3 = [
        swapped(
            lax.dynamic_index_in_dim(summed, z ^ s, 0, keepdims=False).astype(jnp.bfloat16),
            "ctx",
            2 * s,
        )
        for s in (1, 2, 3)
    ]

    w_all = lax.all_gather(w_out, "ctx", axis=0)
    shares = finish(place, own, r1, r2, r3, out_gain.reshape(1, -1), w_all)
    total = shares[0].astype(jnp.float32)
    for t in (1, 2, 3):
        total = total + swapped(shares[t], "head", t).astype(jnp.float32)
    return total.astype(jnp.bfloat16)


def solution(mesh):
    one_head_each = mesh.shape["ctx"] == 8 and mesh.shape["head"] == 4
    body = per_device_one_head if one_head_each else per_device
    return jax.shard_map(
        body,
        mesh=mesh,
        in_specs=(
            P("ctx", "head"),
            P("ctx"),
            P("ctx", "head"),
            P("ctx", "head"),
            P("ctx", "head"),
            P("head", None),
            P("head", None),
            P("head"),
            P("head", "ctx"),
        ),
        out_specs=P("ctx", "head"),
        check_vma=False,
    )
```

```python
import functools
import math

import jax
import jax.numpy as jnp
from jax import lax
from jax.experimental import pallas as pl
from jax.experimental.pallas import tpu as pltpu
from jax.sharding import PartitionSpec as P

HD = 128
GROUP = 4
CQ = 6
CK = 11
KB = 512


def passed_along(value, axis, steps):
    count = lax.axis_size(axis)
    leading, last = (max(0, -steps), min(count, count - steps))
    return lax.ppermute(value, axis, [(source, source + steps) for source in range(leading, last)])


def rope(projected, positions):
    row_count = projected.shape[0]
    head_count = projected.shape[1] // HD
    shaped = projected.reshape(row_count, head_count, HD)
    half_size = HD // 2
    exponents = jnp.arange(half_size, dtype=jnp.float32) * (2.0 / HD)
    inverse = jnp.exp(-exponents * math.log(500000.0))
    angle = (positions.astype(jnp.float32) * 0.25)[:, None, None] * inverse[None, None, :]
    cosine = jnp.cos(angle)
    sine = jnp.sin(angle)
    lower_half = shaped[..., :half_size]
    upper_half = shaped[..., half_size:]
    rotated_rows = jnp.concatenate(
        [lower_half * cosine - upper_half * sine, upper_half * cosine + lower_half * sine], -1
    )
    return rotated_rows.reshape(row_count, head_count * HD)


def convolve(masked, kernel, row_count, col_count):
    summed = jnp.zeros((masked.shape[0], row_count, col_count), jnp.float32)
    for lag_q in range(CQ):
        for lag_k in range(CK):
            weight = kernel[:, lag_q * CK + lag_k][:, None, None]
            window = masked[
                :,
                CQ - 1 - lag_q : CQ - 1 - lag_q + row_count,
                CK - 1 - lag_k : CK - 1 - lag_k + col_count,
            ]
            summed = summed + weight * window
    return summed


def add_rows(left, piece):
    return jnp.dot(left, piece, preferred_element_type=jnp.float32)


def share_keys(key, value):
    return (
        lax.all_gather(key, "ctx", axis=0, tiled=True),
        lax.all_gather(value, "ctx", axis=0, tiled=True),
    )


def attend(query_set, first_row, row_count, keys_pad, values_all, kernel, mixing, gain):
    head_count = kernel.shape[0]
    ext_rows = row_count + CQ - 1
    query_heads = query_set.reshape(ext_rows, head_count, HD)
    token_total = values_all.shape[0]
    block_count = token_total // KB
    last_row = first_row + row_count - 1
    scale = 1.0 / math.sqrt(HD)
    prow = first_row - (CQ - 1) + jnp.arange(ext_rows, dtype=jnp.int32)
    irow = first_row + jnp.arange(row_count, dtype=jnp.int32)

    def logits_of(block):
        key_start = block * KB
        key_block = lax.dynamic_slice_in_dim(keys_pad, key_start, KB + CK - 1, 0).reshape(
            KB + CK - 1, head_count, HD
        )
        scores = (
            jnp.einsum("rhd,khd->hrk", query_heads, key_block, preferred_element_type=jnp.float32)
            * scale
        )
        kcol = key_start - CK // 2 + jnp.arange(KB + CK - 1, dtype=jnp.int32)
        valid = (kcol[None, :] <= prow[:, None]) & (prow[:, None] >= 0)
        masked = jnp.where(valid[None], scores, 0.0)
        conv = convolve(masked, kernel, row_count, KB)
        jcol = key_start + jnp.arange(KB, dtype=jnp.int32)
        return jnp.where((jcol[None, :] <= irow[:, None])[None], conv, -jnp.inf)

    def first_pass(block, carry_in):

        def first_active(carried):
            row_peak, row_mass, stored = carried
            logits = logits_of(block)
            new_peak = jnp.maximum(row_peak, jnp.max(logits, axis=-1))
            new_mass = row_mass * jnp.exp(row_peak - new_peak) + jnp.sum(
                jnp.exp(logits - new_peak[..., None]), axis=-1
            )
            stored = lax.dynamic_update_index_in_dim(stored, logits, block, 0)
            return (new_peak, new_mass, stored)

        return lax.cond(block * KB <= last_row, first_active, lambda carried: carried, carry_in)

    peak_start = jnp.full((head_count, row_count), -jnp.inf, jnp.float32)
    mass_start = jnp.zeros((head_count, row_count), jnp.float32)
    store_start = jnp.zeros((block_count, head_count, row_count, KB), jnp.float32)
    row_peak, row_mass, stored = lax.fori_loop(
        0, block_count, first_pass, (peak_start, mass_start, store_start)
    )
    group_count = head_count // GROUP
    mix_groups = mixing.reshape(group_count, GROUP, GROUP)

    def second_pass(block, carry_in):

        def second_active(summed):
            logits = lax.dynamic_index_in_dim(stored, block, 0, keepdims=False)
            probs = jnp.exp(logits - row_peak[..., None]) / row_mass[..., None]
            grouped = probs.reshape(group_count, GROUP, row_count, KB)
            mixed_scores = (
                jnp.einsum("gab,gbrk->gark", mix_groups, grouped)
                .reshape(head_count, row_count, KB)
                .astype(jnp.bfloat16)
            )
            value_block = lax.dynamic_slice_in_dim(values_all, block * KB, KB, 0).reshape(
                KB, head_count, HD
            )
            return summed + jnp.einsum(
                "hrk,khd->rhd", mixed_scores, value_block, preferred_element_type=jnp.float32
            )

        return lax.cond(block * KB <= last_row, second_active, lambda summed: summed, carry_in)

    summed = lax.fori_loop(
        0, block_count, second_pass, jnp.zeros((row_count, head_count, HD), jnp.float32)
    )
    rms = jnp.sqrt(jnp.mean(summed * summed, axis=-1, keepdims=True) + 1e-05)
    normed = (summed / rms * gain.reshape(head_count, HD)).astype(jnp.bfloat16)
    return normed.reshape(row_count, head_count * HD)


def per_device(
    activations, positions, w_query, w_key, w_value, conv_kernel, head_mix, out_gain, w_out
):
    row_count = activations.shape[0]
    ctx_place = lax.axis_index("ctx")
    features = lax.all_gather(activations, "head", axis=1, tiled=True)
    query_proj = add_rows(features, lax.all_gather(w_query, "ctx", axis=0, tiled=True))
    key_proj = add_rows(features, lax.all_gather(w_key, "ctx", axis=0, tiled=True))
    value_proj = add_rows(features, lax.all_gather(w_value, "ctx", axis=0, tiled=True))
    key = rope(key_proj, positions).astype(jnp.bfloat16)
    value = value_proj.astype(jnp.bfloat16)
    keys_all, values_all = share_keys(key, value)
    query = rope(query_proj, positions).astype(jnp.bfloat16)
    rim_rows = passed_along(query[row_count - (CQ - 1) :], "ctx", 1)
    query_ext = jnp.concatenate([rim_rows, query], 0)
    keys_pad = jnp.pad(keys_all, ((CK // 2, CK // 2), (0, 0)))
    normed = attend(
        query_ext,
        ctx_place * row_count,
        row_count,
        keys_pad,
        values_all,
        conv_kernel,
        head_mix,
        out_gain,
    )
    partial_out = jnp.dot(
        normed, lax.all_gather(w_out, "ctx", axis=1, tiled=True), preferred_element_type=jnp.float32
    )
    return lax.psum_scatter(
        partial_out.astype(jnp.bfloat16), "head", scatter_dimension=1, tiled=True
    )


ROWS = 256
BAND = 128
LANES = 128
SUB = 64
AHEAD = 16
VMEM_BYTES = 56 * 1024 * 1024


def kernel_params():
    return pltpu.CompilerParams(vmem_limit_bytes=VMEM_BYTES)


def whole(memory_space):
    return pl.BlockSpec(memory_space=memory_space)


def project_kernel(rows, place, *refs):
    a_own, a_x, a_y = refs[:4], refs[4:9], refs[9:14]
    weights = refs[14:18]
    cos_ref, sin_ref = refs[18:20]
    mine, theirs, v_out = refs[20:23]
    abuf, wbuf, acc, sem_a, sem_w = refs[23:]
    turn, core = place[0], place[1]
    depth = a_own[0].shape[1]
    half = weights[0].shape[1]

    def copies(t):
        out = []
        start = 0
        for i in range(4):
            width = weights[i].shape[2]
            side = core if i % 2 == 0 else 1 - core
            out.append(
                pltpu.make_async_copy(
                    weights[i].at[lax.bitwise_xor(turn, t)],
                    wbuf.at[
                        t, pl.ds(pl.multiple_of(side * half, half), half), pl.ds(start, width)
                    ],
                    sem_w.at[t, i],
                )
            )
            start += width * (i % 2)
        for b in range(4):
            if t < 3:
                source = (a_own, a_x, a_y)[t][b].at[pl.ds(0, rows)]
                target = abuf.at[t, pl.ds(b * rows, rows)]
                out.append(pltpu.make_async_copy(source, target, sem_a.at[t, b]))
                continue
            late = pl.ds(rows if b < 3 else 0, rows // 2)
            for n, part in enumerate((a_y, a_x)):
                target = abuf.at[t, pl.ds(b * rows + n * (rows // 2), rows // 2)]
                out.append(
                    pltpu.make_async_copy(part[b + 1].at[late], target, sem_a.at[t + n, b])
                )
        return out

    for t in range(4):
        for copy in copies(t):
            copy.start()
    for t in range(4):
        for copy in copies(t):
            copy.wait()
        part = jnp.dot(abuf[t], wbuf[t], preferred_element_type=jnp.float32)
        acc[...] = part if t == 0 else acc[...] + part
    first = core == 0
    for b in range(4):
        total = acc[b * rows : (b + 1) * rows]
        cosine, sine = cos_ref[b], sin_ref[b]
        at = place[5 + b]
        for col, out in ((4 * HD, 0), (2 * HD, HD)):
            heads = []
            for start in (col, col + HD):
                x = total[:, start : start + HD]
                x = x * cosine + pltpu.roll(x, HD // 2, 1) * sine
                heads.append(x.astype(jnp.bfloat16))
            mine[at, :, out : out + HD] = jnp.where(first, heads[0], heads[1])
            theirs[at, :, out : out + HD] = jnp.where(first, heads[1], heads[0])
        v_out[at] = total[:, : 2 * HD].astype(jnp.bfloat16)


def project(place, a_own, a_x, a_y, weights, cosine, sine):
    rows, depth = a_own[0].shape
    width = weights[0].shape[2] + weights[2].shape[2]
    out = jax.ShapeDtypeStruct((4, rows, 2 * HD), jnp.bfloat16)
    return pl.pallas_call(
        functools.partial(project_kernel, rows),
        out_shape=(out, out, out),
        in_specs=[whole(pltpu.SMEM)] + [whole(pl.ANY)] * 18 + [whole(pltpu.VMEM)] * 2,
        out_specs=[whole(pltpu.VMEM)] * 3,
        scratch_shapes=[
            pltpu.VMEM((4, 4 * rows, depth), jnp.bfloat16),
            pltpu.VMEM((4, depth, width), jnp.bfloat16),
            pltpu.VMEM((4 * rows, width), jnp.float32),
            pltpu.SemaphoreType.DMA((5, 4)),
            pltpu.SemaphoreType.DMA((4, 4)),
        ],
        compiler_params=kernel_params(),
        cost_estimate=pl.CostEstimate(
            flops=8 * rows * 4 * depth * width, bytes_accessed=16 * 2**20, transcendentals=0
        ),
    )(place, *a_own, *a_x, *a_y, *weights, cosine, sine)


def prepare_kernel(place, mine, other, key_ref, even_ref, odd_ref, q_out, k_out, corr, *scratch):
    qf, kf, lags, turned = scratch
    core = place[1]
    total = q_out.shape[0]
    qf[0:8] = jnp.zeros((8, HD), jnp.float32)
    kf[0:AHEAD] = jnp.zeros((AHEAD, HD), jnp.float32)
    kf[AHEAD + total :] = jnp.zeros((kf.shape[0] - AHEAD - total, HD), jnp.float32)
    corr[...] = jnp.zeros(corr.shape, jnp.float32)
    for i in range(total // (2 * ROWS)):
        for ref, parity in ((mine, core), (other, 1 - core)):
            start = pl.multiple_of((2 * i + parity) * ROWS, ROWS)
            block = ref[i].astype(jnp.float32)
            qf[pl.ds(8 + start, ROWS)] = block[:, :HD]
            kf[pl.ds(AHEAD + start, ROWS)] = block[:, HD:]

    ahead = lax.broadcasted_iota(jnp.int32, (SUB + 8, LANES), 1) - lax.broadcasted_iota(
        jnp.int32, (SUB + 8, LANES), 0
    )
    near = (ahead >= 1) & (ahead < CQ + CK // 2)
    steps = total // LANES
    for w in range(steps):
        base = w * LANES
        window = kf[base : base + 2 * LANES].T
        turned[base : base + LANES] = window.astype(jnp.bfloat16)
        for odd in range(2):
            at = base + odd * SUB
            qwin = qf[at : at + SUB + 8]
            kwin = kf[at + AHEAD - 8 : at + AHEAD - 8 + LANES]
            scores = lax.dot_general(
                qwin.astype(jnp.bfloat16),
                kwin.astype(jnp.bfloat16),
                (((1,), (1,)), ((), ())),
                preferred_element_type=jnp.float32,
            )
            future = jnp.where(near, scores, 0.0)
            for a in range(CQ):
                cols = slice(a * LANES, (a + 1) * LANES)
                lags[odd, w * SUB : (w + 1) * SUB, cols] = future[8 - a : 8 - a + SUB].astype(
                    jnp.bfloat16
                )
                q_out[at : at + SUB, cols] = qwin[8 - a : 8 - a + SUB].astype(jnp.bfloat16)
    for w in range(0, steps, 4):
        wide = jnp.dot(
            turned[w * LANES : (w + 4) * LANES], key_ref[...], preferred_element_type=jnp.float32
        )
        for n in range(4):
            cols = slice((w + n) * LANES, (w + n + 1) * LANES)
            for a in range(CQ):
                k_out[a * HD : (a + 1) * HD, cols] = wide[
                    n * LANES : (n + 1) * LANES, a * LANES : (a + 1) * LANES
                ].astype(jnp.bfloat16)
    for odd, taps in enumerate((even_ref, odd_ref)):
        for w in range(0, steps, 8):
            fix = jnp.dot(
                lags[odd, w * SUB : (w + 8) * SUB], taps[...], preferred_element_type=jnp.float32
            )
            for n in range(8):
                m = 2 * ((w + n) % 2) + odd
                col = LANES * ((m + 1) // 2)
                corr[(w + n) // 2, m * SUB : (m + 1) * SUB, col : col + taps.shape[1]] = fix[
                    n * SUB : (n + 1) * SUB
                ]


def prepare(place, mine, other, key_taps, even, odd):
    total = mine.shape[0] * 2 * ROWS
    return pl.pallas_call(
        prepare_kernel,
        out_shape=(
            jax.ShapeDtypeStruct((total, CQ * HD), jnp.bfloat16),
            jax.ShapeDtypeStruct((CQ * HD, total), jnp.bfloat16),
            jax.ShapeDtypeStruct((total // ROWS, ROWS, BAND + ROWS), jnp.float32),
        ),
        in_specs=[whole(pltpu.SMEM)] + [whole(pltpu.VMEM)] * 5,
        out_specs=[whole(pltpu.VMEM)] * 3,
        scratch_shapes=[
            pltpu.VMEM((8 + total, HD), jnp.float32),
            pltpu.VMEM((AHEAD + total + LANES, HD), jnp.float32),
            pltpu.VMEM((2, total // 2, CQ * LANES), jnp.bfloat16),
            pltpu.VMEM((total, 2 * LANES), jnp.bfloat16),
        ],
        compiler_params=kernel_params(),
        cost_estimate=pl.CostEstimate(flops=2**31, bytes_accessed=12 * 2**20, transcendentals=0),
    )(place, mine, other, key_taps, even, odd)


def key_taps_of(weights):
    tap = jnp.arange(LANES)[None, None, :] + CK // 2 + AHEAD - jnp.arange(2 * LANES)[:, None, None]
    out = jnp.zeros((2 * LANES, CQ, LANES), jnp.float32)
    for c in range(CK):
        out = out + jnp.where(tap == c, weights[:, c][None, :, None], 0.0)
    return out.astype(jnp.bfloat16).reshape(2 * LANES, CQ * LANES)


def band_taps(weights, first, lanes):
    lag = jnp.arange(CQ)[:, None, None]
    tap = (first + jnp.arange(lanes))[None, None, :] + CK // 2 + 8 - jnp.arange(LANES)[None, :, None]
    band = jnp.zeros((CQ, LANES, lanes), jnp.float32)
    for c in range(CK):
        band = band + jnp.where(tap == c, weights[:, c][:, None, None], 0.0)
    return band.astype(jnp.bfloat16).reshape(CQ * LANES, lanes)


def attend_kernel(place, mix, q_ref, k_ref, corr, va, vb, vc, vd, mine, theirs, v_all):
    side, core = place[2], place[1]
    b = pl.program_id(0)
    count = k_ref.shape[1] // (2 * ROWS)

    @pl.when(b == 0)
    def _():
        for i in range(count):
            for parity, near, far in ((core, va, vb), (1 - core, vc, vd)):
                rows = pl.ds(pl.multiple_of((2 * i + parity) * ROWS, ROWS), ROWS)
                first, last = near[i], far[i]
                v_all[rows, : 2 * HD] = jnp.where(side == 0, first, last)
                v_all[rows, 2 * HD :] = jnp.where(side == 0, last, first)

    row = lax.broadcasted_iota(jnp.int32, (ROWS, ROWS), 0)
    col = lax.broadcasted_iota(jnp.int32, (ROWS, ROWS), 1)
    seen = col <= row
    top, low = slice(0, ROWS), slice(ROWS, 2 * ROWS)

    def fixed(part, n):
        return jnp.concatenate([part[:, :BAND], part[:, BAND:] - corr[n, :, :BAND]], 1)

    def rows_of(upper, lower):
        return jnp.concatenate([upper, lower], 0)

    def block(step):
        parts = []
        for j in range(2 * step + 1):
            part = jnp.dot(
                q_ref[...],
                k_ref[:, j * ROWS : (j + 1) * ROWS],
                preferred_element_type=jnp.float32,
            )
            if j == 2 * step:
                diagonal = jnp.where(seen, part[top] - corr[0, :, BAND:], -jnp.inf)
                part = rows_of(diagonal, fixed(part[low], 1))
            elif j == 2 * step - 1:
                part = rows_of(fixed(part[top], 0), part[low])
            parts.append(part)
        start = (2 * step + 1) * ROWS
        last = jnp.dot(
            q_ref[low], k_ref[:, start : start + ROWS], preferred_element_type=jnp.float32
        )
        last = jnp.where(seen, last - corr[1, :, BAND:], -jnp.inf)
        peak = parts[0]
        for part in parts[1:]:
            peak = jnp.maximum(peak, part)
        peak = rows_of(peak[top], jnp.maximum(peak[low], last))
        peak = jnp.max(peak, axis=1, keepdims=True)
        mass = jnp.zeros((2 * ROWS, ROWS), jnp.float32)
        probs = []
        for part in parts:
            part = jnp.exp2(part - peak)
            mass = mass + part
            probs.append(part.astype(jnp.bfloat16))
        last = jnp.exp2(last - peak[low])
        mass = rows_of(mass[top], mass[low] + last)
        summed = jnp.dot(
            jnp.concatenate(probs, 1), v_all[:start], preferred_element_type=jnp.float32
        )
        extra = jnp.dot(
            last.astype(jnp.bfloat16),
            v_all[start : start + ROWS],
            preferred_element_type=jnp.float32,
        )
        inverse = 1.0 / jnp.sum(mass, axis=1, keepdims=True)
        halves = []
        for rows, total in ((top, summed[top]), (low, summed[low] + extra)):
            halves.append(
                jnp.concatenate(
                    [
                        total[:, g * HD : (g + 1) * HD] * (inverse[rows] * mix[g])
                        for g in range(GROUP)
                    ],
                    1,
                ).astype(jnp.bfloat16)
            )
        mine[0] = jnp.where(core == 0, halves[0], halves[1])
        theirs[0] = jnp.where(core == 0, halves[1], halves[0])

    for step in range(count):
        pl.when(b == step)(lambda step=step: block(step))


def attend_head(place, mix, q_wide, k_wide, corr, va, vb, vc, vd):
    depth, total = k_wide.shape
    rows = 2 * ROWS
    count = total // rows
    out = jax.ShapeDtypeStruct((count, ROWS, GROUP * HD), jnp.bfloat16)
    out_spec = pl.BlockSpec((1, ROWS, GROUP * HD), lambda b: (b, 0, 0))
    v_spec = pl.BlockSpec(va.shape, lambda b: (0, 0, 0))
    return pl.pallas_call(
        attend_kernel,
        grid=(count,),
        out_shape=(out, out),
        in_specs=[
            whole(pltpu.SMEM),
            whole(pltpu.SMEM),
            pl.BlockSpec((rows, depth), lambda b: (b, 0)),
            pl.BlockSpec((depth, total), lambda b: (0, 0)),
            pl.BlockSpec((2, ROWS, BAND + ROWS), lambda b: (b, 0, 0)),
        ]
        + [v_spec] * 4,
        out_specs=[out_spec, out_spec],
        scratch_shapes=[pltpu.VMEM((total, GROUP * HD), jnp.bfloat16)],
        compiler_params=kernel_params(),
        cost_estimate=pl.CostEstimate(
            flops=total * total * (depth + GROUP * HD),
            bytes_accessed=16 * 2**20,
            transcendentals=total * total // 2,
        ),
    )(place, mix, q_wide, k_wide, corr, va, vb, vc, vd)


def finish_kernel(place, own, r1, r2, r3, gain, *refs):
    w_parts, outs = refs[:8], refs[8:12]
    normed, w_buf, sem = refs[12:]
    width = w_parts[0].shape[1]
    core, head = place[1], place[0]

    def copy_w(n):
        side = core if n % 2 == 0 else 1 - core
        cols = pl.ds(pl.multiple_of(side * width, width), width)
        target = w_buf.at[lax.bitwise_xor(place[5 + n // 2], head), :, cols]
        return pltpu.make_async_copy(w_parts[n], target, sem.at[n])

    for n in range(8):
        copy_w(n).start()
    near = own[...] + r1[...].astype(jnp.float32)
    far = r2[...].astype(jnp.float32) + r3[...].astype(jnp.float32)
    low = place[3] == 0
    for g in range(2 * GROUP):
        cols = slice((g % GROUP) * HD, (g % GROUP + 1) * HD)
        first = low if g < GROUP else jnp.logical_not(low)
        x = jnp.where(first, near[:, cols], far[:, cols])
        scale = lax.rsqrt(jnp.mean(x * x, axis=1, keepdims=True) + 1e-05)
        normed[:, g * HD : (g + 1) * HD] = (
            x * scale * gain[:, g * HD : (g + 1) * HD]
        ).astype(jnp.bfloat16)
    for n in range(8):
        copy_w(n).wait()
    for t in (3, 2, 1, 0):
        outs[t][...] = jnp.dot(
            normed[...], w_buf[t], preferred_element_type=jnp.float32
        ).astype(jnp.bfloat16)


def finish(place, own, r1, r2, r3, gain, w_parts):
    rows = own.shape[0]
    depth, width = w_parts[0].shape
    return pl.pallas_call(
        finish_kernel,
        in_specs=[whole(pltpu.SMEM)] + [whole(pltpu.VMEM)] * 5 + [whole(pl.ANY)] * 8,
        out_specs=[whole(pltpu.VMEM)] * 4,
        out_shape=[jax.ShapeDtypeStruct((rows, 2 * width), jnp.bfloat16)] * 4,
        scratch_shapes=[
            pltpu.VMEM((rows, depth), jnp.bfloat16),
            pltpu.VMEM((4, depth, 2 * width), jnp.bfloat16),
            pltpu.SemaphoreType.DMA((8,)),
        ],
        compiler_params=kernel_params(),
        cost_estimate=pl.CostEstimate(
            flops=2 * rows * depth * 8 * width, bytes_accessed=11 * 2**20, transcendentals=0
        ),
    )(place, own, r1, r2, r3, gain, *w_parts)


def swapped(value, axis, mask):
    count = lax.axis_size(axis)
    return lax.ppermute(value, axis, [(i, i ^ mask) for i in range(count)])


def per_device_one_head(
    activations, positions, w_query, w_key, w_value, conv_kernel, head_mix, out_gain, w_out
):
    ctx, head = lax.axis_index("ctx"), lax.axis_index("head")
    z, core = ctx // 2, ctx % 2
    pair = 2 * HD
    same_core = [[i for i in range(8) if i % 2 == k] for k in range(2)]

    def columns(*weights):
        shaped = [w.reshape(w.shape[0], 4, pair) for w in weights]
        return lax.all_to_all(
            jnp.concatenate(shaped, -1).transpose(1, 0, 2),
            "ctx",
            0,
            0,
            axis_index_groups=same_core,
        )

    middle = [(2, 4), (3, 5), (4, 2), (5, 3)]
    outward = [(2, 0), (3, 1), (4, 6), (5, 7)]
    inner = (z == 1) | (z == 2)
    rows = activations.shape[0]
    half = rows // 2
    barrier = lax.optimization_barrier

    def plane(block, x_before, y_before):
        to_x = jnp.concatenate([block[:rows], y_before[half:rows]])
        to_y = jnp.concatenate([block[:rows], x_before[:half]])
        return swapped(to_x, "head", 1), swapped(to_y, "head", 2)

    digits = jnp.stack([positions // 256, positions % 256]).astype(jnp.bfloat16)
    digits = jnp.pad(digits, ((0, 14), (0, activations.shape[1] - rows)))
    block = jnp.concatenate([activations, digits])
    near = swapped(block, "ctx", 2)
    across = lax.ppermute(block, "ctx", middle)
    x0, y0 = swapped(activations, "head", 1), swapped(activations, "head", 2)
    near, across, x0, y0, w_value, w_key, w_query = barrier(
        (near, across, x0, y0, w_value, w_key, w_query)
    )
    v_same, kq_same = columns(w_value), columns(w_key, w_query)
    across_next = lax.ppermute(near, "ctx", middle)
    passed = lax.ppermute(across, "ctx", outward)
    x1, y1 = plane(near, x0, y0)
    across_next, passed, x1, y1 = barrier((across_next, passed, x1, y1))
    far_a = across + passed
    passed_next = lax.ppermute(across_next, "ctx", outward)
    x2, y2 = plane(far_a, x1, y1)
    weights = lax.dynamic_index_in_dim(conv_kernel, ctx, 0, keepdims=False)
    weights = weights * (math.log2(math.e) / math.sqrt(HD))
    taps = weights.reshape(CQ, CK)
    tables = key_taps_of(taps), band_taps(taps, -BAND, 2 * LANES), band_taps(taps, -SUB, LANES)
    passed_next, x2, y2, v_same, tables = barrier((passed_next, x2, y2, v_same, tables))
    far_b = across_next + passed_next
    x3, y3 = plane(far_b, x2, y2)
    v_swap = swapped(v_same, "ctx", 1)
    x3, y3, v_swap, kq_same, w_out = barrier((x3, y3, v_swap, kq_same, w_out))
    x4, y4 = swapped(y3[half:rows], "head", 1), swapped(x3[:half], "head", 2)
    kq_swap = swapped(kq_same, "ctx", 1)
    w_near = swapped(w_out, "ctx", 2)
    w_across = lax.ppermute(w_out, "ctx", middle)
    x4, y4, kq_swap, w_near, w_across = barrier((x4, y4, kq_swap, w_near, w_across))
    w_across_next = lax.ppermute(w_near, "ctx", middle)
    w_passed = lax.ppermute(w_across, "ctx", outward)

    tokens = (block, near, far_a, far_b)
    place_of = jnp.stack(
        [a[rows, :rows].astype(jnp.float32) * 256.0 + a[rows + 1, :rows].astype(jnp.float32) for a in tokens]
    )
    order = jnp.where(inner, z ^ 3, z ^ 2), jnp.where(inner, z ^ 2, z ^ 3)
    place = jnp.stack([head, core, z % 2, z // 2, head, z, z ^ 1, *order]).astype(jnp.int32)

    exponents = jnp.arange(HD // 2, dtype=jnp.float32) * (2.0 / HD)
    inverse = jnp.exp(-exponents * math.log(500000.0))
    angle = (place_of * 0.25)[:, :, None] * inverse
    cosine, sine = jnp.cos(angle), jnp.sin(angle)
    mine, theirs, v_pair = project(
        place,
        (activations, near, far_a, far_b),
        (x0, x1, x2, x3, x4),
        (y0, y1, y2, y3, y4),
        (v_same, v_swap, kq_same, kq_swap),
        jnp.concatenate([cosine, cosine], -1),
        jnp.concatenate([-sine, sine], -1),
    )
    mine, theirs, v_pair, w_across_next, w_passed = barrier(
        (mine, theirs, v_pair, w_across_next, w_passed)
    )
    other = swapped(theirs, "ctx", 1)
    v_next = swapped(v_pair, "ctx", 2)
    v_pair_other = swapped(v_pair, "ctx", 1)
    w_passed_next = lax.ppermute(w_across_next, "ctx", outward)
    q_wide, k_wide, corr = prepare(place, mine, other, *tables)
    v_next, q_wide = barrier((v_next, q_wide))
    v_next_other = swapped(v_next, "ctx", 1)
    w_own_swap, w_near_swap = swapped(w_out, "ctx", 1), swapped(w_near, "ctx", 1)
    w_far_a = w_across + w_passed
    group_rows = lax.dynamic_slice_in_dim(head_mix, GROUP * (ctx // GROUP), GROUP, 0)
    mix = lax.dynamic_index_in_dim(group_rows, ctx % GROUP, 1, keepdims=False)
    out_mine, out_theirs = attend_head(
        place, mix, q_wide, k_wide, corr, v_pair, v_next, v_pair_other, v_next_other
    )
    out_mine, out_theirs, w_own_swap, w_near_swap, w_passed_next = barrier(
        (out_mine, out_theirs, w_own_swap, w_near_swap, w_passed_next)
    )
    w_far_b = w_across_next + w_passed_next
    w_far_a_swap, w_far_b_swap = swapped(w_far_a, "ctx", 1), swapped(w_far_b, "ctx", 1)
    summed = out_mine.astype(jnp.float32) + swapped(out_theirs, "ctx", 1).astype(jnp.float32)
    own = lax.dynamic_index_in_dim(summed, z, 0, keepdims=False)
    r1, r2, r3 = [
        swapped(
            lax.dynamic_index_in_dim(summed, z ^ s, 0, keepdims=False).astype(jnp.bfloat16),
            "ctx",
            2 * s,
        )
        for s in (1, 2, 3)
    ]

    w_parts = (w_out, w_own_swap, w_near, w_near_swap)
    w_parts += (w_far_a, w_far_a_swap, w_far_b, w_far_b_swap)
    shares = finish(place, own, r1, r2, r3, out_gain.reshape(1, -1), w_parts)
    total = shares[0].astype(jnp.float32)
    for t in (1, 2, 3):
        total = total + swapped(shares[t], "head", t).astype(jnp.float32)
    return total.astype(jnp.bfloat16)


def solution(mesh):
    one_head_each = mesh.shape["ctx"] == 8 and mesh.shape["head"] == 4
    body = per_device_one_head if one_head_each else per_device
    return jax.shard_map(
        body,
        mesh=mesh,
        in_specs=(
            P("ctx", "head"),
            P("ctx"),
            P("ctx", "head"),
            P("ctx", "head"),
            P("ctx", "head"),
            P("head", None),
            P("head", None),
            P("head"),
            P("head", "ctx"),
        ),
        out_specs=P("ctx", "head"),
        check_vma=False,
    )
```

```python
import functools
import math

import jax
import jax.numpy as jnp
from jax import lax
from jax.experimental import pallas as pl
from jax.experimental.pallas import tpu as pltpu
from jax.sharding import PartitionSpec as P

HD = 128
GROUP = 4
CQ = 6
CK = 11
KB = 512


def passed_along(value, axis, steps):
    count = lax.axis_size(axis)
    leading, last = (max(0, -steps), min(count, count - steps))
    return lax.ppermute(value, axis, [(source, source + steps) for source in range(leading, last)])


def rope(projected, positions):
    row_count = projected.shape[0]
    head_count = projected.shape[1] // HD
    shaped = projected.reshape(row_count, head_count, HD)
    half_size = HD // 2
    exponents = jnp.arange(half_size, dtype=jnp.float32) * (2.0 / HD)
    inverse = jnp.exp(-exponents * math.log(500000.0))
    angle = (positions.astype(jnp.float32) * 0.25)[:, None, None] * inverse[None, None, :]
    cosine = jnp.cos(angle)
    sine = jnp.sin(angle)
    lower_half = shaped[..., :half_size]
    upper_half = shaped[..., half_size:]
    rotated_rows = jnp.concatenate(
        [lower_half * cosine - upper_half * sine, upper_half * cosine + lower_half * sine], -1
    )
    return rotated_rows.reshape(row_count, head_count * HD)


def convolve(masked, kernel, row_count, col_count):
    summed = jnp.zeros((masked.shape[0], row_count, col_count), jnp.float32)
    for lag_q in range(CQ):
        for lag_k in range(CK):
            weight = kernel[:, lag_q * CK + lag_k][:, None, None]
            window = masked[
                :,
                CQ - 1 - lag_q : CQ - 1 - lag_q + row_count,
                CK - 1 - lag_k : CK - 1 - lag_k + col_count,
            ]
            summed = summed + weight * window
    return summed


def add_rows(left, piece):
    return jnp.dot(left, piece, preferred_element_type=jnp.float32)


def share_keys(key, value):
    return (
        lax.all_gather(key, "ctx", axis=0, tiled=True),
        lax.all_gather(value, "ctx", axis=0, tiled=True),
    )


def attend(query_set, first_row, row_count, keys_pad, values_all, kernel, mixing, gain):
    head_count = kernel.shape[0]
    ext_rows = row_count + CQ - 1
    query_heads = query_set.reshape(ext_rows, head_count, HD)
    token_total = values_all.shape[0]
    block_count = token_total // KB
    last_row = first_row + row_count - 1
    scale = 1.0 / math.sqrt(HD)
    prow = first_row - (CQ - 1) + jnp.arange(ext_rows, dtype=jnp.int32)
    irow = first_row + jnp.arange(row_count, dtype=jnp.int32)

    def logits_of(block):
        key_start = block * KB
        key_block = lax.dynamic_slice_in_dim(keys_pad, key_start, KB + CK - 1, 0).reshape(
            KB + CK - 1, head_count, HD
        )
        scores = (
            jnp.einsum("rhd,khd->hrk", query_heads, key_block, preferred_element_type=jnp.float32)
            * scale
        )
        kcol = key_start - CK // 2 + jnp.arange(KB + CK - 1, dtype=jnp.int32)
        valid = (kcol[None, :] <= prow[:, None]) & (prow[:, None] >= 0)
        masked = jnp.where(valid[None], scores, 0.0)
        conv = convolve(masked, kernel, row_count, KB)
        jcol = key_start + jnp.arange(KB, dtype=jnp.int32)
        return jnp.where((jcol[None, :] <= irow[:, None])[None], conv, -jnp.inf)

    def first_pass(block, carry_in):

        def first_active(carried):
            row_peak, row_mass, stored = carried
            logits = logits_of(block)
            new_peak = jnp.maximum(row_peak, jnp.max(logits, axis=-1))
            new_mass = row_mass * jnp.exp(row_peak - new_peak) + jnp.sum(
                jnp.exp(logits - new_peak[..., None]), axis=-1
            )
            stored = lax.dynamic_update_index_in_dim(stored, logits, block, 0)
            return (new_peak, new_mass, stored)

        return lax.cond(block * KB <= last_row, first_active, lambda carried: carried, carry_in)

    peak_start = jnp.full((head_count, row_count), -jnp.inf, jnp.float32)
    mass_start = jnp.zeros((head_count, row_count), jnp.float32)
    store_start = jnp.zeros((block_count, head_count, row_count, KB), jnp.float32)
    row_peak, row_mass, stored = lax.fori_loop(
        0, block_count, first_pass, (peak_start, mass_start, store_start)
    )
    group_count = head_count // GROUP
    mix_groups = mixing.reshape(group_count, GROUP, GROUP)

    def second_pass(block, carry_in):

        def second_active(summed):
            logits = lax.dynamic_index_in_dim(stored, block, 0, keepdims=False)
            probs = jnp.exp(logits - row_peak[..., None]) / row_mass[..., None]
            grouped = probs.reshape(group_count, GROUP, row_count, KB)
            mixed_scores = (
                jnp.einsum("gab,gbrk->gark", mix_groups, grouped)
                .reshape(head_count, row_count, KB)
                .astype(jnp.bfloat16)
            )
            value_block = lax.dynamic_slice_in_dim(values_all, block * KB, KB, 0).reshape(
                KB, head_count, HD
            )
            return summed + jnp.einsum(
                "hrk,khd->rhd", mixed_scores, value_block, preferred_element_type=jnp.float32
            )

        return lax.cond(block * KB <= last_row, second_active, lambda summed: summed, carry_in)

    summed = lax.fori_loop(
        0, block_count, second_pass, jnp.zeros((row_count, head_count, HD), jnp.float32)
    )
    rms = jnp.sqrt(jnp.mean(summed * summed, axis=-1, keepdims=True) + 1e-05)
    normed = (summed / rms * gain.reshape(head_count, HD)).astype(jnp.bfloat16)
    return normed.reshape(row_count, head_count * HD)


def per_device(
    activations, positions, w_query, w_key, w_value, conv_kernel, head_mix, out_gain, w_out
):
    row_count = activations.shape[0]
    ctx_place = lax.axis_index("ctx")
    features = lax.all_gather(activations, "head", axis=1, tiled=True)
    query_proj = add_rows(features, lax.all_gather(w_query, "ctx", axis=0, tiled=True))
    key_proj = add_rows(features, lax.all_gather(w_key, "ctx", axis=0, tiled=True))
    value_proj = add_rows(features, lax.all_gather(w_value, "ctx", axis=0, tiled=True))
    key = rope(key_proj, positions).astype(jnp.bfloat16)
    value = value_proj.astype(jnp.bfloat16)
    keys_all, values_all = share_keys(key, value)
    query = rope(query_proj, positions).astype(jnp.bfloat16)
    rim_rows = passed_along(query[row_count - (CQ - 1) :], "ctx", 1)
    query_ext = jnp.concatenate([rim_rows, query], 0)
    keys_pad = jnp.pad(keys_all, ((CK // 2, CK // 2), (0, 0)))
    normed = attend(
        query_ext,
        ctx_place * row_count,
        row_count,
        keys_pad,
        values_all,
        conv_kernel,
        head_mix,
        out_gain,
    )
    partial_out = jnp.dot(
        normed, lax.all_gather(w_out, "ctx", axis=1, tiled=True), preferred_element_type=jnp.float32
    )
    return lax.psum_scatter(
        partial_out.astype(jnp.bfloat16), "head", scatter_dimension=1, tiled=True
    )


ROWS = 256
BAND = 128
LANES = 128
SUB = 64
AHEAD = 16
VMEM_BYTES = 56 * 1024 * 1024


def kernel_params():
    return pltpu.CompilerParams(vmem_limit_bytes=VMEM_BYTES)


def whole(memory_space):
    return pl.BlockSpec(memory_space=memory_space)


def project_kernel(rows, place, *refs):
    a_own, (x0, x_rest, y0, y_rest, d_rest) = refs[:4], refs[4:9]
    w_same, w_swap = refs[9:13], refs[13:17]
    cos_ref, sin_ref = refs[17:19]
    mine, theirs, v_out = refs[19:22]
    abuf, wbuf, acc, sem_a, sem_w = refs[22:]
    turn, core = place[4], place[1]
    half = w_same[0].shape[0]
    rest = pl.ds(rows, 3 * rows)

    def copies_a(t):
        if t == 0:
            pairs = [(a_own[b], 0, b * rows, rows) for b in range(4)]
        elif t < 3:
            first, others = ((x0, x_rest), (y0, y_rest))[t - 1]
            pairs = [(first, 0, 0, rows), (others, 0, rows, 3 * rows)]
        else:
            late, mid = 3 * rows, rows // 2
            pairs = [(y_rest, late, 0, mid), (x_rest, late, mid, mid), (d_rest, 0, rows, 3 * rows)]
        return [
            pltpu.make_async_copy(
                ref.at[pl.ds(source, size)], abuf.at[t, pl.ds(target, size)], sem_a.at[t, n]
            )
            for n, (ref, source, target, size) in enumerate(pairs)
        ]

    def copies_w(t, s):
        out = []
        for n, (ref, side) in enumerate(((w_same[s], core), (w_swap[s], 1 - core))):
            target = wbuf.at[t, pl.ds(pl.multiple_of(side * half, half), half)]
            out.append(pltpu.make_async_copy(ref, target, sem_w.at[t, n]))
        return out

    for t in range(4):
        for s in range(4):

            @pl.when(s == lax.bitwise_xor(turn, t))
            def _():
                for copy in copies_w(t, s):
                    copy.start()

        for copy in copies_a(t):
            copy.start()

    def copies(t):
        return copies_w(t, 0) + copies_a(t)

    for t in range(4):
        for copy in copies(t):
            copy.wait()
        part = jnp.dot(abuf[t], wbuf[t], preferred_element_type=jnp.float32)
        acc[...] = part if t == 0 else acc[...] + part
    first = core == 0
    for b in range(4):
        total = acc[b * rows : (b + 1) * rows]
        cosine, sine = cos_ref[b], sin_ref[b]
        at = place[5 + b]
        for col, out in ((0, 0), (2 * HD, HD)):
            heads = []
            for start in (col, col + HD):
                x = total[:, start : start + HD]
                x = x * cosine + pltpu.roll(x, HD // 2, 1) * sine
                heads.append(x.astype(jnp.bfloat16))
            mine[at, :, out : out + HD] = jnp.where(first, heads[0], heads[1])
            theirs[at, :, out : out + HD] = jnp.where(first, heads[1], heads[0])
        v_out[at] = total[:, 4 * HD :].astype(jnp.bfloat16)


def project(place, a_own, a_plane, w_same, w_swap, cosine, sine):
    rows, depth = a_own[0].shape
    width = w_same[0].shape[1]
    out = jax.ShapeDtypeStruct((4, rows, 2 * HD), jnp.bfloat16)
    return pl.pallas_call(
        functools.partial(project_kernel, rows),
        out_shape=(out, out, out),
        in_specs=[whole(pltpu.SMEM)] + [whole(pl.ANY)] * 17 + [whole(pltpu.VMEM)] * 2,
        out_specs=[whole(pltpu.VMEM)] * 3,
        scratch_shapes=[
            pltpu.VMEM((4, 4 * rows, depth), jnp.bfloat16),
            pltpu.VMEM((4, depth, width), jnp.bfloat16),
            pltpu.VMEM((4 * rows, width), jnp.float32),
            pltpu.SemaphoreType.DMA((4, 4)),
            pltpu.SemaphoreType.DMA((4, 2)),
        ],
        compiler_params=kernel_params(),
        cost_estimate=pl.CostEstimate(
            flops=8 * rows * 4 * depth * width, bytes_accessed=16 * 2**20, transcendentals=0
        ),
    )(place, *a_own, *a_plane, *w_same, *w_swap, cosine, sine)


def prepare_kernel(place, mine, other, key_ref, even_ref, odd_ref, q_out, k_out, corr, *scratch):
    qf, kf, lags, turned = scratch
    core = place[1]
    total = q_out.shape[0]
    qf[0:8] = jnp.zeros((8, HD), jnp.float32)
    kf[0:AHEAD] = jnp.zeros((AHEAD, HD), jnp.float32)
    kf[AHEAD + total :] = jnp.zeros((kf.shape[0] - AHEAD - total, HD), jnp.float32)
    corr[...] = jnp.zeros(corr.shape, jnp.float32)
    for i in range(total // (2 * ROWS)):
        for ref, parity in ((mine, core), (other, 1 - core)):
            start = pl.multiple_of((2 * i + parity) * ROWS, ROWS)
            block = ref[i].astype(jnp.float32)
            qf[pl.ds(8 + start, ROWS)] = block[:, :HD]
            kf[pl.ds(AHEAD + start, ROWS)] = block[:, HD:]

    ahead = lax.broadcasted_iota(jnp.int32, (SUB + 8, LANES), 1) - lax.broadcasted_iota(
        jnp.int32, (SUB + 8, LANES), 0
    )
    near = (ahead >= 1) & (ahead < CQ + CK // 2)
    steps = total // LANES
    for w in range(steps):
        base = w * LANES
        window = kf[base : base + 2 * LANES].T
        turned[base : base + LANES] = window.astype(jnp.bfloat16)
        for odd in range(2):
            at = base + odd * SUB
            qwin = qf[at : at + SUB + 8]
            kwin = kf[at + AHEAD - 8 : at + AHEAD - 8 + LANES]
            scores = lax.dot_general(
                qwin.astype(jnp.bfloat16),
                kwin.astype(jnp.bfloat16),
                (((1,), (1,)), ((), ())),
                preferred_element_type=jnp.float32,
            )
            future = jnp.where(near, scores, 0.0)
            for a in range(CQ):
                cols = slice(a * LANES, (a + 1) * LANES)
                lags[odd, w * SUB : (w + 1) * SUB, cols] = future[8 - a : 8 - a + SUB].astype(
                    jnp.bfloat16
                )
                q_out[at : at + SUB, cols] = qwin[8 - a : 8 - a + SUB].astype(jnp.bfloat16)
    for w in range(0, steps, 4):
        wide = jnp.dot(
            turned[w * LANES : (w + 4) * LANES], key_ref[...], preferred_element_type=jnp.float32
        )
        for n in range(4):
            cols = slice((w + n) * LANES, (w + n + 1) * LANES)
            for a in range(CQ):
                k_out[a * HD : (a + 1) * HD, cols] = wide[
                    n * LANES : (n + 1) * LANES, a * LANES : (a + 1) * LANES
                ].astype(jnp.bfloat16)
    for odd, taps in enumerate((even_ref, odd_ref)):
        for w in range(0, steps, 8):
            fix = jnp.dot(
                lags[odd, w * SUB : (w + 8) * SUB], taps[...], preferred_element_type=jnp.float32
            )
            for n in range(8):
                m = 2 * ((w + n) % 2) + odd
                col = LANES * ((m + 1) // 2)
                corr[(w + n) // 2, m * SUB : (m + 1) * SUB, col : col + taps.shape[1]] = fix[
                    n * SUB : (n + 1) * SUB
                ]


def prepare(place, mine, other, key_taps, even, odd):
    total = mine.shape[0] * 2 * ROWS
    return pl.pallas_call(
        prepare_kernel,
        out_shape=(
            jax.ShapeDtypeStruct((total, CQ * HD), jnp.bfloat16),
            jax.ShapeDtypeStruct((CQ * HD, total), jnp.bfloat16),
            jax.ShapeDtypeStruct((total // ROWS, ROWS, BAND + ROWS), jnp.float32),
        ),
        in_specs=[whole(pltpu.SMEM)] + [whole(pltpu.VMEM)] * 5,
        out_specs=[whole(pltpu.VMEM)] * 3,
        scratch_shapes=[
            pltpu.VMEM((8 + total, HD), jnp.float32),
            pltpu.VMEM((AHEAD + total + LANES, HD), jnp.float32),
            pltpu.VMEM((2, total // 2, CQ * LANES), jnp.bfloat16),
            pltpu.VMEM((total, 2 * LANES), jnp.bfloat16),
        ],
        compiler_params=kernel_params(),
        cost_estimate=pl.CostEstimate(flops=2**31, bytes_accessed=12 * 2**20, transcendentals=0),
    )(place, mine, other, key_taps, even, odd)


def tables_kernel(weights, key_ref, even_ref, odd_ref):
    def fill(ref, origin, swap):
        height = ref.shape[0] if swap else ref.shape[0] // CQ
        width = ref.shape[1] // CQ if swap else ref.shape[1]
        shape = (height, width)
        tap = lax.broadcasted_iota(jnp.int32, shape, 1) - lax.broadcasted_iota(jnp.int32, shape, 0)
        for a in range(CQ):
            value = jnp.zeros(shape, jnp.float32)
            for c in range(CK):
                value = jnp.where(tap == c - origin, weights[a * CK + c], value)
            value = value.astype(jnp.bfloat16)
            if swap:
                ref[:, a * width : (a + 1) * width] = value
            else:
                ref[a * height : (a + 1) * height, :] = value

    fill(key_ref, CK // 2 + AHEAD, True)
    fill(even_ref, CK // 2 + 8 - BAND, False)
    fill(odd_ref, CK // 2 + 8 - SUB, False)


def tables_of(weights):
    return pl.pallas_call(
        tables_kernel,
        out_shape=(
            jax.ShapeDtypeStruct((2 * LANES, CQ * LANES), jnp.bfloat16),
            jax.ShapeDtypeStruct((CQ * LANES, 2 * LANES), jnp.bfloat16),
            jax.ShapeDtypeStruct((CQ * LANES, LANES), jnp.bfloat16),
        ),
        in_specs=[whole(pltpu.SMEM)],
        out_specs=[whole(pltpu.VMEM)] * 3,
        compiler_params=pltpu.CompilerParams(vmem_limit_bytes=8 * 1024 * 1024),
        cost_estimate=pl.CostEstimate(flops=2**23, bytes_accessed=2**20, transcendentals=0),
    )(weights)


def attend_kernel(place, mix, q_ref, k_ref, corr, va, vb, vc, vd, mine, theirs, v_all):
    side, core = place[2], place[1]
    b = pl.program_id(0)
    count = k_ref.shape[1] // (2 * ROWS)

    @pl.when(b == 0)
    def _():
        for i in range(count):
            for parity, near, far in ((core, va, vb), (1 - core, vc, vd)):
                rows = pl.ds(pl.multiple_of((2 * i + parity) * ROWS, ROWS), ROWS)
                first, last = near[i], far[i]
                v_all[rows, : 2 * HD] = jnp.where(side == 0, first, last)
                v_all[rows, 2 * HD :] = jnp.where(side == 0, last, first)

    row = lax.broadcasted_iota(jnp.int32, (ROWS, ROWS), 0)
    col = lax.broadcasted_iota(jnp.int32, (ROWS, ROWS), 1)
    seen = col <= row
    top, low = slice(0, ROWS), slice(ROWS, 2 * ROWS)

    def fixed(part, n):
        return jnp.concatenate([part[:, :BAND], part[:, BAND:] - corr[n, :, :BAND]], 1)

    def rows_of(upper, lower):
        return jnp.concatenate([upper, lower], 0)

    def block(step):
        parts = []
        for j in range(2 * step + 1):
            part = jnp.dot(
                q_ref[...],
                k_ref[:, j * ROWS : (j + 1) * ROWS],
                preferred_element_type=jnp.float32,
            )
            if j == 2 * step:
                diagonal = jnp.where(seen, part[top] - corr[0, :, BAND:], -jnp.inf)
                part = rows_of(diagonal, fixed(part[low], 1))
            elif j == 2 * step - 1:
                part = rows_of(fixed(part[top], 0), part[low])
            parts.append(part)
        start = (2 * step + 1) * ROWS
        last = jnp.dot(
            q_ref[low], k_ref[:, start : start + ROWS], preferred_element_type=jnp.float32
        )
        last = jnp.where(seen, last - corr[1, :, BAND:], -jnp.inf)
        peak = parts[0]
        for part in parts[1:]:
            peak = jnp.maximum(peak, part)
        peak = rows_of(peak[top], jnp.maximum(peak[low], last))
        peak = jnp.max(peak, axis=1, keepdims=True)
        mass = jnp.zeros((2 * ROWS, ROWS), jnp.float32)
        probs = []
        for part in parts:
            part = jnp.exp2(part - peak)
            mass = mass + part
            probs.append(part.astype(jnp.bfloat16))
        last = jnp.exp2(last - peak[low])
        mass = rows_of(mass[top], mass[low] + last)
        summed = jnp.dot(
            jnp.concatenate(probs, 1), v_all[:start], preferred_element_type=jnp.float32
        )
        extra = jnp.dot(
            last.astype(jnp.bfloat16),
            v_all[start : start + ROWS],
            preferred_element_type=jnp.float32,
        )
        inverse = 1.0 / jnp.sum(mass, axis=1, keepdims=True)
        halves = []
        for rows, total in ((top, summed[top]), (low, summed[low] + extra)):
            halves.append(
                jnp.concatenate(
                    [
                        total[:, g * HD : (g + 1) * HD] * (inverse[rows] * mix[g])
                        for g in range(GROUP)
                    ],
                    1,
                ).astype(jnp.bfloat16)
            )
        mine[0] = jnp.where(core == 0, halves[0], halves[1])
        theirs[0] = jnp.where(core == 0, halves[1], halves[0])

    for step in range(count):
        pl.when(b == step)(lambda step=step: block(step))


def attend_head(place, mix, q_wide, k_wide, corr, va, vb, vc, vd):
    depth, total = k_wide.shape
    rows = 2 * ROWS
    count = total // rows
    out = jax.ShapeDtypeStruct((count, ROWS, GROUP * HD), jnp.bfloat16)
    out_spec = pl.BlockSpec((1, ROWS, GROUP * HD), lambda b: (b, 0, 0))
    v_spec = pl.BlockSpec(va.shape, lambda b: (0, 0, 0))
    return pl.pallas_call(
        attend_kernel,
        grid=(count,),
        out_shape=(out, out),
        in_specs=[
            whole(pltpu.SMEM),
            whole(pltpu.SMEM),
            pl.BlockSpec((rows, depth), lambda b: (b, 0)),
            pl.BlockSpec((depth, total), lambda b: (0, 0)),
            pl.BlockSpec((2, ROWS, BAND + ROWS), lambda b: (b, 0, 0)),
        ]
        + [v_spec] * 4,
        out_specs=[out_spec, out_spec],
        scratch_shapes=[pltpu.VMEM((total, GROUP * HD), jnp.bfloat16)],
        compiler_params=kernel_params(),
        cost_estimate=pl.CostEstimate(
            flops=total * total * (depth + GROUP * HD),
            bytes_accessed=16 * 2**20,
            transcendentals=total * total // 2,
        ),
    )(place, mix, q_wide, k_wide, corr, va, vb, vc, vd)


def finish_kernel(place, own, r1, r2, r3, gain, w_any, o0, o1, o2, o3, normed, w_buf, sem):
    blocks, _, width = w_buf.shape
    per = blocks // 4
    order = [(t, i) for t in (3, 2, 1, 0) for i in range(per)]

    def copy_w(n):
        t, i = order[n]
        source = per * lax.bitwise_xor(place[0], t) + i
        return pltpu.make_async_copy(w_any.at[source], w_buf.at[n], sem.at[n])

    for n in range(blocks):
        copy_w(n).start()
    near = own[...] + r1[...].astype(jnp.float32)
    far = r2[...].astype(jnp.float32) + r3[...].astype(jnp.float32)
    low = place[3] == 0
    for g in range(2 * GROUP):
        cols = slice((g % GROUP) * HD, (g % GROUP + 1) * HD)
        first = low if g < GROUP else jnp.logical_not(low)
        x = jnp.where(first, near[:, cols], far[:, cols])
        scale = lax.rsqrt(jnp.mean(x * x, axis=1, keepdims=True) + 1e-05)
        normed[:, g * HD : (g + 1) * HD] = (
            x * scale * gain[:, g * HD : (g + 1) * HD]
        ).astype(jnp.bfloat16)
    for n in range(blocks):
        t, i = order[n]
        copy_w(n).wait()
        (o0, o1, o2, o3)[t][:, i * width : (i + 1) * width] = jnp.dot(
            normed[...], w_buf[n], preferred_element_type=jnp.float32
        ).astype(jnp.bfloat16)


def finish(place, own, r1, r2, r3, gain, w_all):
    rows = own.shape[0]
    blocks, depth, width = w_all.shape
    return pl.pallas_call(
        finish_kernel,
        in_specs=[whole(pltpu.SMEM)] + [whole(pltpu.VMEM)] * 5 + [whole(pl.ANY)],
        out_specs=[whole(pltpu.VMEM)] * 4,
        out_shape=[jax.ShapeDtypeStruct((rows, blocks // 4 * width), jnp.bfloat16)] * 4,
        scratch_shapes=[
            pltpu.VMEM((rows, depth), jnp.bfloat16),
            pltpu.VMEM((blocks, depth, width), jnp.bfloat16),
            pltpu.SemaphoreType.DMA((blocks,)),
        ],
        compiler_params=kernel_params(),
        cost_estimate=pl.CostEstimate(
            flops=2 * rows * depth * blocks * width, bytes_accessed=11 * 2**20, transcendentals=0
        ),
    )(place, own, r1, r2, r3, gain, w_all)


def swapped(value, axis, mask):
    count = lax.axis_size(axis)
    return lax.ppermute(value, axis, [(i, i ^ mask) for i in range(count)])


def per_device_one_head(
    activations, positions, w_query, w_key, w_value, conv_kernel, head_mix, out_gain, w_out
):
    ctx, head = lax.axis_index("ctx"), lax.axis_index("head")
    z, core = ctx // 2, ctx % 2
    rows = activations.shape[0]
    half = rows // 2
    barrier = lax.optimization_barrier
    pair = 2 * HD

    def columns(target):
        parts = [
            lax.dynamic_slice_in_dim(w, target * pair, pair, 1) for w in (w_query, w_key, w_value)
        ]
        return jnp.concatenate(parts, 1)

    digits = jnp.stack([positions // 256, positions % 256]).astype(jnp.bfloat16)
    digits = jnp.pad(digits, ((0, 14), (0, activations.shape[1] - rows)))
    block = jnp.concatenate([activations, digits])
    w_pieces = [columns(z ^ s) for s in range(4)]
    w_near = swapped(w_pieces[1], "ctx", 2)
    far = [swapped(block, "ctx", 2 * s) for s in (1, 2, 3)]
    x0, y0 = swapped(activations, "head", 1), swapped(activations, "head", 2)
    far, x0, y0, w_near, w_pieces = barrier((far, x0, y0, w_near, w_pieces))

    w_far = [swapped(w_pieces[s], "ctx", 2 * s) for s in (2, 3)]
    inner = [a[:rows] for a in far]
    x_rest = swapped(jnp.concatenate(inner + [y0[half:]]), "head", 1)
    y_rest = swapped(jnp.concatenate(inner + [x0[:half]]), "head", 2)
    d_rest = swapped(jnp.concatenate(inner), "head", 3)
    place_of = jnp.stack(
        [
            a[rows, :rows].astype(jnp.float32) * 256.0 + a[rows + 1, :rows].astype(jnp.float32)
            for a in [block] + far
        ]
    )
    exponents = jnp.arange(HD // 2, dtype=jnp.float32) * (2.0 / HD)
    inverse = jnp.exp(-exponents * math.log(500000.0))
    angle = (place_of * 0.25)[:, :, None] * inverse
    cosine, sine = jnp.cos(angle), jnp.sin(angle)
    cosine = jnp.concatenate([cosine, cosine], -1)
    sine = jnp.concatenate([-sine, sine], -1)
    weights = lax.dynamic_index_in_dim(conv_kernel, ctx, 0, keepdims=False)
    tables = tables_of(weights * (math.log2(math.e) / math.sqrt(HD)))
    place = jnp.stack([head, core, z % 2, z // 2, z ^ head, z, z ^ 1, z ^ 2, z ^ 3])
    place = place.astype(jnp.int32)
    w_far, x_rest, y_rest, d_rest, cosine, sine, tables, place = barrier(
        (w_far, x_rest, y_rest, d_rest, cosine, sine, tables, place)
    )
    w_same = [w_pieces[0], w_near] + list(w_far)
    w_swap = [swapped(w, "ctx", 1) for w in w_same]
    w_all = lax.all_gather(w_out, "ctx", axis=0)

    mine, theirs, v_pair = project(
        place,
        [activations] + list(far),
        (x0, x_rest, y0, y_rest, d_rest),
        w_same,
        w_swap,
        cosine,
        sine,
    )
    mine, theirs, v_pair, w_all = barrier((mine, theirs, v_pair, w_all))
    other = swapped(theirs, "ctx", 1)
    v_next = swapped(v_pair, "ctx", 2)
    v_pair_other = swapped(v_pair, "ctx", 1)
    q_wide, k_wide, corr = prepare(place, mine, other, *tables)
    v_next, q_wide = barrier((v_next, q_wide))
    v_next_other = swapped(v_next, "ctx", 1)
    group_rows = lax.dynamic_slice_in_dim(head_mix, GROUP * (ctx // GROUP), GROUP, 0)
    mix = lax.dynamic_index_in_dim(group_rows, ctx % GROUP, 1, keepdims=False)
    out_mine, out_theirs = attend_head(
        place, mix, q_wide, k_wide, corr, v_pair, v_next, v_pair_other, v_next_other
    )
    summed = out_mine.astype(jnp.float32) + swapped(out_theirs, "ctx", 1).astype(jnp.float32)
    own = lax.dynamic_index_in_dim(summed, z, 0, keepdims=False)
    r1, r2, r3 = [
        swapped(
            lax.dynamic_index_in_dim(summed, z ^ s, 0, keepdims=False).astype(jnp.bfloat16),
            "ctx",
            2 * s,
        )
        for s in (1, 2, 3)
    ]

    shares = finish(place, own, r1, r2, r3, out_gain.reshape(1, -1), w_all)
    total = shares[0].astype(jnp.float32)
    for t in (1, 2, 3):
        total = total + swapped(shares[t], "head", t).astype(jnp.float32)
    return total.astype(jnp.bfloat16)


def solution(mesh):
    one_head_each = mesh.shape["ctx"] == 8 and mesh.shape["head"] == 4
    body = per_device_one_head if one_head_each else per_device
    return jax.shard_map(
        body,
        mesh=mesh,
        in_specs=(
            P("ctx", "head"),
            P("ctx"),
            P("ctx", "head"),
            P("ctx", "head"),
            P("ctx", "head"),
            P("head", None),
            P("head", None),
            P("head"),
            P("head", "ctx"),
        ),
        out_specs=P("ctx", "head"),
        check_vma=False,
    )
```

```python
import functools
import math

import jax
import jax.numpy as jnp
from jax import lax
from jax.experimental import pallas as pl
from jax.experimental.pallas import tpu as pltpu
from jax.sharding import PartitionSpec as P

HD = 128
GROUP = 4
CQ = 6
CK = 11
KB = 512


def passed_along(value, axis, steps):
    count = lax.axis_size(axis)
    leading, last = (max(0, -steps), min(count, count - steps))
    return lax.ppermute(value, axis, [(source, source + steps) for source in range(leading, last)])


def rope(projected, positions):
    row_count = projected.shape[0]
    head_count = projected.shape[1] // HD
    shaped = projected.reshape(row_count, head_count, HD)
    half_size = HD // 2
    exponents = jnp.arange(half_size, dtype=jnp.float32) * (2.0 / HD)
    inverse = jnp.exp(-exponents * math.log(500000.0))
    angle = (positions.astype(jnp.float32) * 0.25)[:, None, None] * inverse[None, None, :]
    cosine = jnp.cos(angle)
    sine = jnp.sin(angle)
    lower_half = shaped[..., :half_size]
    upper_half = shaped[..., half_size:]
    rotated_rows = jnp.concatenate(
        [lower_half * cosine - upper_half * sine, upper_half * cosine + lower_half * sine], -1
    )
    return rotated_rows.reshape(row_count, head_count * HD)


def convolve(masked, kernel, row_count, col_count):
    summed = jnp.zeros((masked.shape[0], row_count, col_count), jnp.float32)
    for lag_q in range(CQ):
        for lag_k in range(CK):
            weight = kernel[:, lag_q * CK + lag_k][:, None, None]
            window = masked[
                :,
                CQ - 1 - lag_q : CQ - 1 - lag_q + row_count,
                CK - 1 - lag_k : CK - 1 - lag_k + col_count,
            ]
            summed = summed + weight * window
    return summed


def add_rows(left, piece):
    return jnp.dot(left, piece, preferred_element_type=jnp.float32)


def share_keys(key, value):
    return (
        lax.all_gather(key, "ctx", axis=0, tiled=True),
        lax.all_gather(value, "ctx", axis=0, tiled=True),
    )


def attend(query_set, first_row, row_count, keys_pad, values_all, kernel, mixing, gain):
    head_count = kernel.shape[0]
    ext_rows = row_count + CQ - 1
    query_heads = query_set.reshape(ext_rows, head_count, HD)
    token_total = values_all.shape[0]
    block_count = token_total // KB
    last_row = first_row + row_count - 1
    scale = 1.0 / math.sqrt(HD)
    prow = first_row - (CQ - 1) + jnp.arange(ext_rows, dtype=jnp.int32)
    irow = first_row + jnp.arange(row_count, dtype=jnp.int32)

    def logits_of(block):
        key_start = block * KB
        key_block = lax.dynamic_slice_in_dim(keys_pad, key_start, KB + CK - 1, 0).reshape(
            KB + CK - 1, head_count, HD
        )
        scores = (
            jnp.einsum("rhd,khd->hrk", query_heads, key_block, preferred_element_type=jnp.float32)
            * scale
        )
        kcol = key_start - CK // 2 + jnp.arange(KB + CK - 1, dtype=jnp.int32)
        valid = (kcol[None, :] <= prow[:, None]) & (prow[:, None] >= 0)
        masked = jnp.where(valid[None], scores, 0.0)
        conv = convolve(masked, kernel, row_count, KB)
        jcol = key_start + jnp.arange(KB, dtype=jnp.int32)
        return jnp.where((jcol[None, :] <= irow[:, None])[None], conv, -jnp.inf)

    def first_pass(block, carry_in):

        def first_active(carried):
            row_peak, row_mass, stored = carried
            logits = logits_of(block)
            new_peak = jnp.maximum(row_peak, jnp.max(logits, axis=-1))
            new_mass = row_mass * jnp.exp(row_peak - new_peak) + jnp.sum(
                jnp.exp(logits - new_peak[..., None]), axis=-1
            )
            stored = lax.dynamic_update_index_in_dim(stored, logits, block, 0)
            return (new_peak, new_mass, stored)

        return lax.cond(block * KB <= last_row, first_active, lambda carried: carried, carry_in)

    peak_start = jnp.full((head_count, row_count), -jnp.inf, jnp.float32)
    mass_start = jnp.zeros((head_count, row_count), jnp.float32)
    store_start = jnp.zeros((block_count, head_count, row_count, KB), jnp.float32)
    row_peak, row_mass, stored = lax.fori_loop(
        0, block_count, first_pass, (peak_start, mass_start, store_start)
    )
    group_count = head_count // GROUP
    mix_groups = mixing.reshape(group_count, GROUP, GROUP)

    def second_pass(block, carry_in):

        def second_active(summed):
            logits = lax.dynamic_index_in_dim(stored, block, 0, keepdims=False)
            probs = jnp.exp(logits - row_peak[..., None]) / row_mass[..., None]
            grouped = probs.reshape(group_count, GROUP, row_count, KB)
            mixed_scores = (
                jnp.einsum("gab,gbrk->gark", mix_groups, grouped)
                .reshape(head_count, row_count, KB)
                .astype(jnp.bfloat16)
            )
            value_block = lax.dynamic_slice_in_dim(values_all, block * KB, KB, 0).reshape(
                KB, head_count, HD
            )
            return summed + jnp.einsum(
                "hrk,khd->rhd", mixed_scores, value_block, preferred_element_type=jnp.float32
            )

        return lax.cond(block * KB <= last_row, second_active, lambda summed: summed, carry_in)

    summed = lax.fori_loop(
        0, block_count, second_pass, jnp.zeros((row_count, head_count, HD), jnp.float32)
    )
    rms = jnp.sqrt(jnp.mean(summed * summed, axis=-1, keepdims=True) + 1e-05)
    normed = (summed / rms * gain.reshape(head_count, HD)).astype(jnp.bfloat16)
    return normed.reshape(row_count, head_count * HD)


def per_device(
    activations, positions, w_query, w_key, w_value, conv_kernel, head_mix, out_gain, w_out
):
    row_count = activations.shape[0]
    ctx_place = lax.axis_index("ctx")
    features = lax.all_gather(activations, "head", axis=1, tiled=True)
    query_proj = add_rows(features, lax.all_gather(w_query, "ctx", axis=0, tiled=True))
    key_proj = add_rows(features, lax.all_gather(w_key, "ctx", axis=0, tiled=True))
    value_proj = add_rows(features, lax.all_gather(w_value, "ctx", axis=0, tiled=True))
    key = rope(key_proj, positions).astype(jnp.bfloat16)
    value = value_proj.astype(jnp.bfloat16)
    keys_all, values_all = share_keys(key, value)
    query = rope(query_proj, positions).astype(jnp.bfloat16)
    rim_rows = passed_along(query[row_count - (CQ - 1) :], "ctx", 1)
    query_ext = jnp.concatenate([rim_rows, query], 0)
    keys_pad = jnp.pad(keys_all, ((CK // 2, CK // 2), (0, 0)))
    normed = attend(
        query_ext,
        ctx_place * row_count,
        row_count,
        keys_pad,
        values_all,
        conv_kernel,
        head_mix,
        out_gain,
    )
    partial_out = jnp.dot(
        normed, lax.all_gather(w_out, "ctx", axis=1, tiled=True), preferred_element_type=jnp.float32
    )
    return lax.psum_scatter(
        partial_out.astype(jnp.bfloat16), "head", scatter_dimension=1, tiled=True
    )


ROWS = 256
BAND = 128
LANES = 128
SUB = 64
AHEAD = 16


def kernel_params(mebibytes):
    return pltpu.CompilerParams(vmem_limit_bytes=mebibytes * 1024 * 1024)


def whole(memory_space):
    return pl.BlockSpec(memory_space=memory_space)


def project_kernel(rows, place, *refs):
    a_own, (x0, x_rest, y0, y_rest, d_rest) = refs[:4], refs[4:9]
    w_same, w_swap = refs[9:13], refs[13:17]
    cos_ref, sin_ref = refs[17:19]
    mine, theirs, v_out = refs[19:22]
    abuf, wbuf, acc, sem_a, sem_w = refs[22:]
    turn, core = place[4], place[1]
    half = w_same[0].shape[0]
    rest = pl.ds(rows, 3 * rows)

    def copies_a(t):
        if t == 0:
            pairs = [(a_own[b], 0, b * rows, rows) for b in range(4)]
        elif t < 3:
            first, others = ((x0, x_rest), (y0, y_rest))[t - 1]
            pairs = [(first, 0, 0, rows), (others, 0, rows, 3 * rows)]
        else:
            late, mid = 3 * rows, rows // 2
            pairs = [(y_rest, late, 0, mid), (x_rest, late, mid, mid), (d_rest, 0, rows, 3 * rows)]
        return [
            pltpu.make_async_copy(
                ref.at[pl.ds(source, size)], abuf.at[t, pl.ds(target, size)], sem_a.at[t, n]
            )
            for n, (ref, source, target, size) in enumerate(pairs)
        ]

    def copies_w(t, s):
        out = []
        for n, (ref, side) in enumerate(((w_same[s], core), (w_swap[s], 1 - core))):
            target = wbuf.at[t, pl.ds(pl.multiple_of(side * half, half), half)]
            out.append(pltpu.make_async_copy(ref, target, sem_w.at[t, n]))
        return out

    for t in range(4):
        for s in range(4):

            @pl.when(s == lax.bitwise_xor(turn, t))
            def _():
                for copy in copies_w(t, s):
                    copy.start()

        for copy in copies_a(t):
            copy.start()

    def copies(t):
        return copies_w(t, 0) + copies_a(t)

    for t in range(4):
        for copy in copies(t):
            copy.wait()
        part = jnp.dot(abuf[t], wbuf[t], preferred_element_type=jnp.float32)
        acc[...] = part if t == 0 else acc[...] + part
    first = core == 0
    for b in range(4):
        total = acc[b * rows : (b + 1) * rows]
        cosine, sine = cos_ref[b], sin_ref[b]
        at = place[5 + b]
        for col, out in ((0, 0), (2 * HD, HD)):
            heads = []
            for start in (col, col + HD):
                x = total[:, start : start + HD]
                x = x * cosine + pltpu.roll(x, HD // 2, 1) * sine
                heads.append(x.astype(jnp.bfloat16))
            mine[at, :, out : out + HD] = jnp.where(first, heads[0], heads[1])
            theirs[at, :, out : out + HD] = jnp.where(first, heads[1], heads[0])
        v_out[at] = total[:, 4 * HD :].astype(jnp.bfloat16)


def project(place, a_own, a_plane, w_same, w_swap, cosine, sine):
    rows, depth = a_own[0].shape
    width = w_same[0].shape[1]
    out = jax.ShapeDtypeStruct((4, rows, 2 * HD), jnp.bfloat16)
    return pl.pallas_call(
        functools.partial(project_kernel, rows),
        out_shape=(out, out, out),
        in_specs=[whole(pltpu.SMEM)] + [whole(pl.ANY)] * 17 + [whole(pltpu.VMEM)] * 2,
        out_specs=[whole(pltpu.VMEM)] * 3,
        scratch_shapes=[
            pltpu.VMEM((4, 4 * rows, depth), jnp.bfloat16),
            pltpu.VMEM((4, depth, width), jnp.bfloat16),
            pltpu.VMEM((4 * rows, width), jnp.float32),
            pltpu.SemaphoreType.DMA((4, 4)),
            pltpu.SemaphoreType.DMA((4, 2)),
        ],
        compiler_params=kernel_params(24),
        cost_estimate=pl.CostEstimate(
            flops=8 * rows * 4 * depth * width, bytes_accessed=16 * 2**20, transcendentals=0
        ),
    )(place, *a_own, *a_plane, *w_same, *w_swap, cosine, sine)


def prepare_kernel(place, mine, other, key_ref, even_ref, odd_ref, q_out, k_out, corr, *scratch):
    qf, kf, lags, turned = scratch
    core = place[1]
    total = q_out.shape[0]
    qf[0:8] = jnp.zeros((8, HD), jnp.float32)
    kf[0:AHEAD] = jnp.zeros((AHEAD, HD), jnp.float32)
    kf[AHEAD + total :] = jnp.zeros((kf.shape[0] - AHEAD - total, HD), jnp.float32)
    corr[...] = jnp.zeros(corr.shape, jnp.float32)
    for i in range(total // (2 * ROWS)):
        for ref, parity in ((mine, core), (other, 1 - core)):
            start = pl.multiple_of((2 * i + parity) * ROWS, ROWS)
            block = ref[i].astype(jnp.float32)
            qf[pl.ds(8 + start, ROWS)] = block[:, :HD]
            kf[pl.ds(AHEAD + start, ROWS)] = block[:, HD:]

    ahead = lax.broadcasted_iota(jnp.int32, (SUB + 8, LANES), 1) - lax.broadcasted_iota(
        jnp.int32, (SUB + 8, LANES), 0
    )
    near = (ahead >= 1) & (ahead < CQ + CK // 2)
    steps = total // LANES
    for w in range(steps):
        base = w * LANES
        window = kf[base : base + 2 * LANES].T
        turned[base : base + LANES] = window.astype(jnp.bfloat16)
        for odd in range(2):
            at = base + odd * SUB
            qwin = qf[at : at + SUB + 8]
            kwin = kf[at + AHEAD - 8 : at + AHEAD - 8 + LANES]
            scores = lax.dot_general(
                qwin.astype(jnp.bfloat16),
                kwin.astype(jnp.bfloat16),
                (((1,), (1,)), ((), ())),
                preferred_element_type=jnp.float32,
            )
            future = jnp.where(near, scores, 0.0)
            for a in range(CQ):
                cols = slice(a * LANES, (a + 1) * LANES)
                lags[odd, w * SUB : (w + 1) * SUB, cols] = future[8 - a : 8 - a + SUB].astype(
                    jnp.bfloat16
                )
                q_out[at : at + SUB, cols] = qwin[8 - a : 8 - a + SUB].astype(jnp.bfloat16)
    for w in range(0, steps, 4):
        wide = jnp.dot(
            turned[w * LANES : (w + 4) * LANES], key_ref[...], preferred_element_type=jnp.float32
        )
        for n in range(4):
            cols = slice((w + n) * LANES, (w + n + 1) * LANES)
            for a in range(CQ):
                k_out[a * HD : (a + 1) * HD, cols] = wide[
                    n * LANES : (n + 1) * LANES, a * LANES : (a + 1) * LANES
                ].astype(jnp.bfloat16)
    for odd, taps in enumerate((even_ref, odd_ref)):
        for w in range(0, steps, 8):
            fix = jnp.dot(
                lags[odd, w * SUB : (w + 8) * SUB], taps[...], preferred_element_type=jnp.float32
            )
            for n in range(8):
                m = 2 * ((w + n) % 2) + odd
                col = LANES * ((m + 1) // 2)
                corr[(w + n) // 2, m * SUB : (m + 1) * SUB, col : col + taps.shape[1]] = fix[
                    n * SUB : (n + 1) * SUB
                ]


def prepare(place, mine, other, key_taps, even, odd):
    total = mine.shape[0] * 2 * ROWS
    return pl.pallas_call(
        prepare_kernel,
        out_shape=(
            jax.ShapeDtypeStruct((total, CQ * HD), jnp.bfloat16),
            jax.ShapeDtypeStruct((CQ * HD, total), jnp.bfloat16),
            jax.ShapeDtypeStruct((total // ROWS, ROWS, BAND + ROWS), jnp.float32),
        ),
        in_specs=[whole(pltpu.SMEM)] + [whole(pltpu.VMEM)] * 5,
        out_specs=[whole(pltpu.VMEM)] * 3,
        scratch_shapes=[
            pltpu.VMEM((8 + total, HD), jnp.float32),
            pltpu.VMEM((AHEAD + total + LANES, HD), jnp.float32),
            pltpu.VMEM((2, total // 2, CQ * LANES), jnp.bfloat16),
            pltpu.VMEM((total, 2 * LANES), jnp.bfloat16),
        ],
        compiler_params=kernel_params(22),
        cost_estimate=pl.CostEstimate(flops=2**31, bytes_accessed=12 * 2**20, transcendentals=0),
    )(place, mine, other, key_taps, even, odd)


def tables_kernel(weights, key_ref, even_ref, odd_ref):
    def fill(ref, origin, swap):
        height = ref.shape[0] if swap else ref.shape[0] // CQ
        width = ref.shape[1] // CQ if swap else ref.shape[1]
        shape = (height, width)
        tap = lax.broadcasted_iota(jnp.int32, shape, 1) - lax.broadcasted_iota(jnp.int32, shape, 0)
        for a in range(CQ):
            value = jnp.zeros(shape, jnp.float32)
            for c in range(CK):
                value = jnp.where(tap == c - origin, weights[a * CK + c], value)
            value = value.astype(jnp.bfloat16)
            if swap:
                ref[:, a * width : (a + 1) * width] = value
            else:
                ref[a * height : (a + 1) * height, :] = value

    fill(key_ref, CK // 2 + AHEAD, True)
    fill(even_ref, CK // 2 + 8 - BAND, False)
    fill(odd_ref, CK // 2 + 8 - SUB, False)


def tables_of(weights):
    return pl.pallas_call(
        tables_kernel,
        out_shape=(
            jax.ShapeDtypeStruct((2 * LANES, CQ * LANES), jnp.bfloat16),
            jax.ShapeDtypeStruct((CQ * LANES, 2 * LANES), jnp.bfloat16),
            jax.ShapeDtypeStruct((CQ * LANES, LANES), jnp.bfloat16),
        ),
        in_specs=[whole(pltpu.SMEM)],
        out_specs=[whole(pltpu.VMEM)] * 3,
        compiler_params=kernel_params(8),
        cost_estimate=pl.CostEstimate(flops=2**23, bytes_accessed=2**20, transcendentals=0),
    )(weights)


def attend_kernel(place, mix, q_ref, k_ref, corr, va, vb, vc, vd, mine, theirs, v_all):
    side, core = place[2], place[1]
    b = pl.program_id(0)
    count = k_ref.shape[1] // (2 * ROWS)

    @pl.when(b == 0)
    def _():
        for i in range(count):
            for parity, near, far in ((core, va, vb), (1 - core, vc, vd)):
                rows = pl.ds(pl.multiple_of((2 * i + parity) * ROWS, ROWS), ROWS)
                first, last = near[i], far[i]
                v_all[rows, : 2 * HD] = jnp.where(side == 0, first, last)
                v_all[rows, 2 * HD :] = jnp.where(side == 0, last, first)

    row = lax.broadcasted_iota(jnp.int32, (ROWS, ROWS), 0)
    col = lax.broadcasted_iota(jnp.int32, (ROWS, ROWS), 1)
    seen = col <= row
    top, low = slice(0, ROWS), slice(ROWS, 2 * ROWS)

    def fixed(part, n):
        return jnp.concatenate([part[:, :BAND], part[:, BAND:] - corr[n, :, :BAND]], 1)

    def rows_of(upper, lower):
        return jnp.concatenate([upper, lower], 0)

    def block(step):
        parts = []
        for j in range(2 * step + 1):
            part = jnp.dot(
                q_ref[...],
                k_ref[:, j * ROWS : (j + 1) * ROWS],
                preferred_element_type=jnp.float32,
            )
            if j == 2 * step:
                diagonal = jnp.where(seen, part[top] - corr[0, :, BAND:], -jnp.inf)
                part = rows_of(diagonal, fixed(part[low], 1))
            elif j == 2 * step - 1:
                part = rows_of(fixed(part[top], 0), part[low])
            parts.append(part)
        start = (2 * step + 1) * ROWS
        last = jnp.dot(
            q_ref[low], k_ref[:, start : start + ROWS], preferred_element_type=jnp.float32
        )
        last = jnp.where(seen, last - corr[1, :, BAND:], -jnp.inf)
        peak = parts[0]
        for part in parts[1:]:
            peak = jnp.maximum(peak, part)
        peak = rows_of(peak[top], jnp.maximum(peak[low], last))
        peak = jnp.max(peak, axis=1, keepdims=True)
        mass = jnp.zeros((2 * ROWS, ROWS), jnp.float32)
        probs = []
        for part in parts:
            part = jnp.exp2(part - peak)
            mass = mass + part
            probs.append(part.astype(jnp.bfloat16))
        last = jnp.exp2(last - peak[low])
        mass = rows_of(mass[top], mass[low] + last)
        summed = jnp.dot(
            jnp.concatenate(probs, 1), v_all[:start], preferred_element_type=jnp.float32
        )
        extra = jnp.dot(
            last.astype(jnp.bfloat16),
            v_all[start : start + ROWS],
            preferred_element_type=jnp.float32,
        )
        inverse = 1.0 / jnp.sum(mass, axis=1, keepdims=True)
        halves = []
        for rows, total in ((top, summed[top]), (low, summed[low] + extra)):
            halves.append(
                jnp.concatenate(
                    [
                        total[:, g * HD : (g + 1) * HD] * (inverse[rows] * mix[g])
                        for g in range(GROUP)
                    ],
                    1,
                ).astype(jnp.bfloat16)
            )
        mine[0] = jnp.where(core == 0, halves[0], halves[1])
        theirs[0] = jnp.where(core == 0, halves[1], halves[0])

    for step in range(count):
        pl.when(b == step)(lambda step=step: block(step))


def attend_head(place, mix, q_wide, k_wide, corr, va, vb, vc, vd):
    depth, total = k_wide.shape
    rows = 2 * ROWS
    count = total // rows
    out = jax.ShapeDtypeStruct((count, ROWS, GROUP * HD), jnp.bfloat16)
    out_spec = pl.BlockSpec((1, ROWS, GROUP * HD), lambda b: (b, 0, 0))
    v_spec = pl.BlockSpec(va.shape, lambda b: (0, 0, 0))
    return pl.pallas_call(
        attend_kernel,
        grid=(count,),
        out_shape=(out, out),
        in_specs=[
            whole(pltpu.SMEM),
            whole(pltpu.SMEM),
            pl.BlockSpec((rows, depth), lambda b: (b, 0)),
            pl.BlockSpec((depth, total), lambda b: (0, 0)),
            pl.BlockSpec((2, ROWS, BAND + ROWS), lambda b: (b, 0, 0)),
        ]
        + [v_spec] * 4,
        out_specs=[out_spec, out_spec],
        scratch_shapes=[pltpu.VMEM((total, GROUP * HD), jnp.bfloat16)],
        compiler_params=kernel_params(30),
        cost_estimate=pl.CostEstimate(
            flops=total * total * (depth + GROUP * HD),
            bytes_accessed=16 * 2**20,
            transcendentals=total * total // 2,
        ),
    )(place, mix, q_wide, k_wide, corr, va, vb, vc, vd)


def finish_kernel(place, own, r1, r2, r3, gain, w_any, o0, o1, o2, o3, normed, w_buf, sem):
    blocks, _, width = w_buf.shape
    per = blocks // 4
    order = [(t, i) for t in (3, 2, 1, 0) for i in range(per)]

    def copy_w(n):
        t, i = order[n]
        source = per * lax.bitwise_xor(place[0], t) + i
        return pltpu.make_async_copy(w_any.at[source], w_buf.at[n], sem.at[n])

    for n in range(blocks):
        copy_w(n).start()
    near = own[...] + r1[...].astype(jnp.float32)
    far = r2[...].astype(jnp.float32) + r3[...].astype(jnp.float32)
    low = place[3] == 0
    for g in range(2 * GROUP):
        cols = slice((g % GROUP) * HD, (g % GROUP + 1) * HD)
        first = low if g < GROUP else jnp.logical_not(low)
        x = jnp.where(first, near[:, cols], far[:, cols])
        scale = lax.rsqrt(jnp.mean(x * x, axis=1, keepdims=True) + 1e-05)
        normed[:, g * HD : (g + 1) * HD] = (
            x * scale * gain[:, g * HD : (g + 1) * HD]
        ).astype(jnp.bfloat16)
    for n in range(blocks):
        t, i = order[n]
        copy_w(n).wait()
        (o0, o1, o2, o3)[t][:, i * width : (i + 1) * width] = jnp.dot(
            normed[...], w_buf[n], preferred_element_type=jnp.float32
        ).astype(jnp.bfloat16)


def finish(place, own, r1, r2, r3, gain, w_all):
    rows = own.shape[0]
    blocks, depth, width = w_all.shape
    return pl.pallas_call(
        finish_kernel,
        in_specs=[whole(pltpu.SMEM)] + [whole(pltpu.VMEM)] * 5 + [whole(pl.ANY)],
        out_specs=[whole(pltpu.VMEM)] * 4,
        out_shape=[jax.ShapeDtypeStruct((rows, blocks // 4 * width), jnp.bfloat16)] * 4,
        scratch_shapes=[
            pltpu.VMEM((rows, depth), jnp.bfloat16),
            pltpu.VMEM((blocks, depth, width), jnp.bfloat16),
            pltpu.SemaphoreType.DMA((blocks,)),
        ],
        compiler_params=kernel_params(14),
        cost_estimate=pl.CostEstimate(
            flops=2 * rows * depth * blocks * width, bytes_accessed=11 * 2**20, transcendentals=0
        ),
    )(place, own, r1, r2, r3, gain, w_all)


def swapped(value, axis, mask):
    count = lax.axis_size(axis)
    return lax.ppermute(value, axis, [(i, i ^ mask) for i in range(count)])


def per_device_one_head(
    activations, positions, w_query, w_key, w_value, conv_kernel, head_mix, out_gain, w_out
):
    ctx, head = lax.axis_index("ctx"), lax.axis_index("head")
    z, core = ctx // 2, ctx % 2
    rows = activations.shape[0]
    half = rows // 2
    barrier = lax.optimization_barrier
    pair = 2 * HD

    def columns(target):
        parts = [
            lax.dynamic_slice_in_dim(w, target * pair, pair, 1) for w in (w_query, w_key, w_value)
        ]
        return jnp.concatenate(parts, 1)

    digits = jnp.stack([positions // 256, positions % 256]).astype(jnp.bfloat16)
    digits = jnp.pad(digits, ((0, 14), (0, activations.shape[1] - rows)))
    block = jnp.concatenate([activations, digits])
    w_pieces = [columns(z ^ s) for s in range(4)]
    w_near = swapped(w_pieces[1], "ctx", 2)
    far = [swapped(block, "ctx", 2 * s) for s in (1, 2, 3)]
    x0, y0 = swapped(activations, "head", 1), swapped(activations, "head", 2)
    weights = lax.dynamic_index_in_dim(conv_kernel, ctx, 0, keepdims=False)
    tables = tables_of(weights * (math.log2(math.e) / math.sqrt(HD)))
    place = jnp.stack([head, core, z % 2, z // 2, z ^ head, z, z ^ 1, z ^ 2, z ^ 3])
    place = place.astype(jnp.int32)
    far, x0, y0, w_near, w_pieces, tables, place, w_out = barrier(
        (far, x0, y0, w_near, w_pieces, tables, place, w_out)
    )

    w_far = [swapped(w_pieces[s], "ctx", 2 * s) for s in (2, 3)]
    inner = [a[:rows] for a in far]
    x_rest = swapped(jnp.concatenate(inner + [y0[half:]]), "head", 1)
    y_rest = swapped(jnp.concatenate(inner + [x0[:half]]), "head", 2)
    d_rest = swapped(jnp.concatenate(inner), "head", 3)
    place_of = jnp.stack(
        [
            a[rows, :rows].astype(jnp.float32) * 256.0 + a[rows + 1, :rows].astype(jnp.float32)
            for a in [block] + far
        ]
    )
    exponents = jnp.arange(HD // 2, dtype=jnp.float32) * (2.0 / HD)
    inverse = jnp.exp(-exponents * math.log(500000.0))
    angle = (place_of * 0.25)[:, :, None] * inverse
    cosine, sine = jnp.cos(angle), jnp.sin(angle)
    cosine = jnp.concatenate([cosine, cosine], -1)
    sine = jnp.concatenate([-sine, sine], -1)
    w_far, x_rest, y_rest, d_rest, cosine, sine = barrier(
        (w_far, x_rest, y_rest, d_rest, cosine, sine)
    )
    w_same = [w_pieces[0], w_near] + list(w_far)
    w_swap = [swapped(w, "ctx", 1) for w in w_same]
    w_all = lax.all_gather(w_out, "ctx", axis=0)

    mine, theirs, v_pair = project(
        place,
        [activations] + list(far),
        (x0, x_rest, y0, y_rest, d_rest),
        w_same,
        w_swap,
        cosine,
        sine,
    )
    mine, theirs, v_pair, w_all = barrier((mine, theirs, v_pair, w_all))
    other = swapped(theirs, "ctx", 1)
    v_next = swapped(v_pair, "ctx", 2)
    v_pair_other = swapped(v_pair, "ctx", 1)
    q_wide, k_wide, corr = prepare(place, mine, other, *tables)
    v_next, q_wide = barrier((v_next, q_wide))
    v_next_other = swapped(v_next, "ctx", 1)
    group_rows = lax.dynamic_slice_in_dim(head_mix, GROUP * (ctx // GROUP), GROUP, 0)
    mix = lax.dynamic_index_in_dim(group_rows, ctx % GROUP, 1, keepdims=False)
    out_mine, out_theirs = attend_head(
        place, mix, q_wide, k_wide, corr, v_pair, v_next, v_pair_other, v_next_other
    )
    summed = out_mine.astype(jnp.float32) + swapped(out_theirs, "ctx", 1).astype(jnp.float32)
    own = lax.dynamic_index_in_dim(summed, z, 0, keepdims=False)
    r1, r2, r3 = [
        swapped(
            lax.dynamic_index_in_dim(summed, z ^ s, 0, keepdims=False).astype(jnp.bfloat16),
            "ctx",
            2 * s,
        )
        for s in (1, 2, 3)
    ]

    shares = finish(place, own, r1, r2, r3, out_gain.reshape(1, -1), w_all)
    total = shares[0].astype(jnp.float32)
    for t in (1, 2, 3):
        total = total + swapped(shares[t], "head", t).astype(jnp.float32)
    return total.astype(jnp.bfloat16)


def solution(mesh):
    one_head_each = mesh.shape["ctx"] == 8 and mesh.shape["head"] == 4
    body = per_device_one_head if one_head_each else per_device
    return jax.shard_map(
        body,
        mesh=mesh,
        in_specs=(
            P("ctx", "head"),
            P("ctx"),
            P("ctx", "head"),
            P("ctx", "head"),
            P("ctx", "head"),
            P("head", None),
            P("head", None),
            P("head"),
            P("head", "ctx"),
        ),
        out_specs=P("ctx", "head"),
        check_vma=False,
    )
```

```python
import functools
import math

import jax
import jax.numpy as jnp
from jax import lax
from jax.experimental import pallas as pl
from jax.experimental.pallas import tpu as pltpu
from jax.sharding import PartitionSpec as P

HD = 128
GROUP = 4
CQ = 6
CK = 11
KB = 512


def passed_along(value, axis, steps):
    count = lax.axis_size(axis)
    leading, last = (max(0, -steps), min(count, count - steps))
    return lax.ppermute(value, axis, [(source, source + steps) for source in range(leading, last)])


def rope(projected, positions):
    row_count = projected.shape[0]
    head_count = projected.shape[1] // HD
    shaped = projected.reshape(row_count, head_count, HD)
    half_size = HD // 2
    exponents = jnp.arange(half_size, dtype=jnp.float32) * (2.0 / HD)
    inverse = jnp.exp(-exponents * math.log(500000.0))
    angle = (positions.astype(jnp.float32) * 0.25)[:, None, None] * inverse[None, None, :]
    cosine = jnp.cos(angle)
    sine = jnp.sin(angle)
    lower_half = shaped[..., :half_size]
    upper_half = shaped[..., half_size:]
    rotated_rows = jnp.concatenate(
        [lower_half * cosine - upper_half * sine, upper_half * cosine + lower_half * sine], -1
    )
    return rotated_rows.reshape(row_count, head_count * HD)


def convolve(masked, kernel, row_count, col_count):
    summed = jnp.zeros((masked.shape[0], row_count, col_count), jnp.float32)
    for lag_q in range(CQ):
        for lag_k in range(CK):
            weight = kernel[:, lag_q * CK + lag_k][:, None, None]
            window = masked[
                :,
                CQ - 1 - lag_q : CQ - 1 - lag_q + row_count,
                CK - 1 - lag_k : CK - 1 - lag_k + col_count,
            ]
            summed = summed + weight * window
    return summed


def add_rows(left, piece):
    return jnp.dot(left, piece, preferred_element_type=jnp.float32)


def share_keys(key, value):
    return (
        lax.all_gather(key, "ctx", axis=0, tiled=True),
        lax.all_gather(value, "ctx", axis=0, tiled=True),
    )


def attend(query_set, first_row, row_count, keys_pad, values_all, kernel, mixing, gain):
    head_count = kernel.shape[0]
    ext_rows = row_count + CQ - 1
    query_heads = query_set.reshape(ext_rows, head_count, HD)
    token_total = values_all.shape[0]
    block_count = token_total // KB
    last_row = first_row + row_count - 1
    scale = 1.0 / math.sqrt(HD)
    prow = first_row - (CQ - 1) + jnp.arange(ext_rows, dtype=jnp.int32)
    irow = first_row + jnp.arange(row_count, dtype=jnp.int32)

    def logits_of(block):
        key_start = block * KB
        key_block = lax.dynamic_slice_in_dim(keys_pad, key_start, KB + CK - 1, 0).reshape(
            KB + CK - 1, head_count, HD
        )
        scores = (
            jnp.einsum("rhd,khd->hrk", query_heads, key_block, preferred_element_type=jnp.float32)
            * scale
        )
        kcol = key_start - CK // 2 + jnp.arange(KB + CK - 1, dtype=jnp.int32)
        valid = (kcol[None, :] <= prow[:, None]) & (prow[:, None] >= 0)
        masked = jnp.where(valid[None], scores, 0.0)
        conv = convolve(masked, kernel, row_count, KB)
        jcol = key_start + jnp.arange(KB, dtype=jnp.int32)
        return jnp.where((jcol[None, :] <= irow[:, None])[None], conv, -jnp.inf)

    def first_pass(block, carry_in):

        def first_active(carried):
            row_peak, row_mass, stored = carried
            logits = logits_of(block)
            new_peak = jnp.maximum(row_peak, jnp.max(logits, axis=-1))
            new_mass = row_mass * jnp.exp(row_peak - new_peak) + jnp.sum(
                jnp.exp(logits - new_peak[..., None]), axis=-1
            )
            stored = lax.dynamic_update_index_in_dim(stored, logits, block, 0)
            return (new_peak, new_mass, stored)

        return lax.cond(block * KB <= last_row, first_active, lambda carried: carried, carry_in)

    peak_start = jnp.full((head_count, row_count), -jnp.inf, jnp.float32)
    mass_start = jnp.zeros((head_count, row_count), jnp.float32)
    store_start = jnp.zeros((block_count, head_count, row_count, KB), jnp.float32)
    row_peak, row_mass, stored = lax.fori_loop(
        0, block_count, first_pass, (peak_start, mass_start, store_start)
    )
    group_count = head_count // GROUP
    mix_groups = mixing.reshape(group_count, GROUP, GROUP)

    def second_pass(block, carry_in):

        def second_active(summed):
            logits = lax.dynamic_index_in_dim(stored, block, 0, keepdims=False)
            probs = jnp.exp(logits - row_peak[..., None]) / row_mass[..., None]
            grouped = probs.reshape(group_count, GROUP, row_count, KB)
            mixed_scores = (
                jnp.einsum("gab,gbrk->gark", mix_groups, grouped)
                .reshape(head_count, row_count, KB)
                .astype(jnp.bfloat16)
            )
            value_block = lax.dynamic_slice_in_dim(values_all, block * KB, KB, 0).reshape(
                KB, head_count, HD
            )
            return summed + jnp.einsum(
                "hrk,khd->rhd", mixed_scores, value_block, preferred_element_type=jnp.float32
            )

        return lax.cond(block * KB <= last_row, second_active, lambda summed: summed, carry_in)

    summed = lax.fori_loop(
        0, block_count, second_pass, jnp.zeros((row_count, head_count, HD), jnp.float32)
    )
    rms = jnp.sqrt(jnp.mean(summed * summed, axis=-1, keepdims=True) + 1e-05)
    normed = (summed / rms * gain.reshape(head_count, HD)).astype(jnp.bfloat16)
    return normed.reshape(row_count, head_count * HD)


def per_device(
    activations, positions, w_query, w_key, w_value, conv_kernel, head_mix, out_gain, w_out
):
    row_count = activations.shape[0]
    ctx_place = lax.axis_index("ctx")
    features = lax.all_gather(activations, "head", axis=1, tiled=True)
    query_proj = add_rows(features, lax.all_gather(w_query, "ctx", axis=0, tiled=True))
    key_proj = add_rows(features, lax.all_gather(w_key, "ctx", axis=0, tiled=True))
    value_proj = add_rows(features, lax.all_gather(w_value, "ctx", axis=0, tiled=True))
    key = rope(key_proj, positions).astype(jnp.bfloat16)
    value = value_proj.astype(jnp.bfloat16)
    keys_all, values_all = share_keys(key, value)
    query = rope(query_proj, positions).astype(jnp.bfloat16)
    rim_rows = passed_along(query[row_count - (CQ - 1) :], "ctx", 1)
    query_ext = jnp.concatenate([rim_rows, query], 0)
    keys_pad = jnp.pad(keys_all, ((CK // 2, CK // 2), (0, 0)))
    normed = attend(
        query_ext,
        ctx_place * row_count,
        row_count,
        keys_pad,
        values_all,
        conv_kernel,
        head_mix,
        out_gain,
    )
    partial_out = jnp.dot(
        normed, lax.all_gather(w_out, "ctx", axis=1, tiled=True), preferred_element_type=jnp.float32
    )
    return lax.psum_scatter(
        partial_out.astype(jnp.bfloat16), "head", scatter_dimension=1, tiled=True
    )


ROWS = 256
BAND = 128
LANES = 128
SUB = 64
AHEAD = 16


def kernel_params(mebibytes):
    return pltpu.CompilerParams(vmem_limit_bytes=mebibytes * 1024 * 1024)


def whole(memory_space):
    return pl.BlockSpec(memory_space=memory_space)


def project_kernel(rows, first_col, place, *refs):
    a_own, (x0, x_rest, y0, y_rest, d_rest) = refs[:4], refs[4:9]
    w_same, w_swap = refs[9:13], refs[13:17]
    abuf, wbuf, acc, sem_a, sem_w = refs[-5:]
    turn, core = place[4], place[1]
    half = w_same[0].shape[0]
    width = wbuf.shape[2]

    def copies_a(t):
        if t == 0:
            pairs = [(a_own[b], 0, b * rows, rows) for b in range(4)]
        elif t < 3:
            first, others = ((x0, x_rest), (y0, y_rest))[t - 1]
            pairs = [(first, 0, 0, rows), (others, 0, rows, 3 * rows)]
        else:
            late, mid = 3 * rows, rows // 2
            pairs = [(y_rest, late, 0, mid), (x_rest, late, mid, mid), (d_rest, 0, rows, 3 * rows)]
        return [
            pltpu.make_async_copy(
                ref.at[pl.ds(source, size)], abuf.at[t, pl.ds(target, size)], sem_a.at[t, n]
            )
            for n, (ref, source, target, size) in enumerate(pairs)
        ]

    def copies_w(t, s):
        out = []
        for n, (ref, side) in enumerate(((w_same[s], core), (w_swap[s], 1 - core))):
            source = ref.at[:, pl.ds(first_col, width)]
            target = wbuf.at[t, pl.ds(pl.multiple_of(side * half, half), half)]
            out.append(pltpu.make_async_copy(source, target, sem_w.at[t, n]))
        return out

    for t in range(4):
        for s in range(4):

            @pl.when(s == lax.bitwise_xor(turn, t))
            def _():
                for copy in copies_w(t, s):
                    copy.start()

        for copy in copies_a(t):
            copy.start()
    for t in range(4):
        for copy in copies_w(t, 0) + copies_a(t):
            copy.wait()
        part = jnp.dot(abuf[t], wbuf[t], preferred_element_type=jnp.float32)
        acc[...] = part if t == 0 else acc[...] + part
    if first_col:
        v_out = refs[17]
        for b in range(4):
            v_out[place[5 + b]] = acc[b * rows : (b + 1) * rows].astype(jnp.bfloat16)
        return
    cos_ref, sin_ref, mine, theirs = refs[17:21]
    first = core == 0
    for b in range(4):
        total = acc[b * rows : (b + 1) * rows]
        cosine, sine = cos_ref[b], sin_ref[b]
        at = place[5 + b]
        for col, out in ((0, 0), (2 * HD, HD)):
            heads = []
            for start in (col, col + HD):
                x = total[:, start : start + HD]
                x = x * cosine + pltpu.roll(x, HD // 2, 1) * sine
                heads.append(x.astype(jnp.bfloat16))
            mine[at, :, out : out + HD] = jnp.where(first, heads[0], heads[1])
            theirs[at, :, out : out + HD] = jnp.where(first, heads[1], heads[0])


def project(place, a_own, a_plane, w_same, w_swap, angles=()):
    rows, depth = a_own[0].shape
    first_col, width = (0, 4 * HD) if angles else (4 * HD, 2 * HD)
    out = jax.ShapeDtypeStruct((4, rows, 2 * HD), jnp.bfloat16)
    count = 2 if angles else 1
    return pl.pallas_call(
        functools.partial(project_kernel, rows, first_col),
        out_shape=[out] * count,
        in_specs=[whole(pltpu.SMEM)]
        + [whole(pl.ANY)] * 17
        + [whole(pltpu.VMEM)] * len(angles),
        out_specs=[whole(pltpu.VMEM)] * count,
        scratch_shapes=[
            pltpu.VMEM((4, 4 * rows, depth), jnp.bfloat16),
            pltpu.VMEM((4, depth, width), jnp.bfloat16),
            pltpu.VMEM((4 * rows, width), jnp.float32),
            pltpu.SemaphoreType.DMA((4, 4)),
            pltpu.SemaphoreType.DMA((4, 2)),
        ],
        compiler_params=kernel_params(20),
        cost_estimate=pl.CostEstimate(
            flops=8 * rows * 4 * depth * width, bytes_accessed=16 * 2**20, transcendentals=0
        ),
    )(place, *a_own, *a_plane, *w_same, *w_swap, *angles)


def prepare(core, mine, other, key_ref, even_ref, odd_ref, q_out, k_out, corr, *scratch):
    qf, kf, lags, turned = scratch
    total = q_out.shape[0]
    qf[0:8] = jnp.zeros((8, HD), jnp.float32)
    kf[0:AHEAD] = jnp.zeros((AHEAD, HD), jnp.float32)
    kf[AHEAD + total :] = jnp.zeros((kf.shape[0] - AHEAD - total, HD), jnp.float32)
    corr[...] = jnp.zeros(corr.shape, jnp.float32)
    for i in range(total // (2 * ROWS)):
        for ref, parity in ((mine, core), (other, 1 - core)):
            start = pl.multiple_of((2 * i + parity) * ROWS, ROWS)
            block = ref[i].astype(jnp.float32)
            qf[pl.ds(8 + start, ROWS)] = block[:, :HD]
            kf[pl.ds(AHEAD + start, ROWS)] = block[:, HD:]

    ahead = lax.broadcasted_iota(jnp.int32, (SUB + 8, LANES), 1) - lax.broadcasted_iota(
        jnp.int32, (SUB + 8, LANES), 0
    )
    near = (ahead >= 1) & (ahead < CQ + CK // 2)
    steps = total // LANES
    for w in range(steps):
        base = w * LANES
        window = kf[base : base + 2 * LANES].T
        turned[base : base + LANES] = window.astype(jnp.bfloat16)
        for odd in range(2):
            at = base + odd * SUB
            qwin = qf[at : at + SUB + 8]
            kwin = kf[at + AHEAD - 8 : at + AHEAD - 8 + LANES]
            scores = lax.dot_general(
                qwin.astype(jnp.bfloat16),
                kwin.astype(jnp.bfloat16),
                (((1,), (1,)), ((), ())),
                preferred_element_type=jnp.float32,
            )
            future = jnp.where(near, scores, 0.0)
            for a in range(CQ):
                cols = slice(a * LANES, (a + 1) * LANES)
                lags[odd, w * SUB : (w + 1) * SUB, cols] = future[8 - a : 8 - a + SUB].astype(
                    jnp.bfloat16
                )
                q_out[at : at + SUB, cols] = qwin[8 - a : 8 - a + SUB].astype(jnp.bfloat16)
    for w in range(0, steps, 4):
        wide = jnp.dot(
            turned[w * LANES : (w + 4) * LANES], key_ref[...], preferred_element_type=jnp.float32
        )
        for n in range(4):
            cols = slice((w + n) * LANES, (w + n + 1) * LANES)
            for a in range(CQ):
                k_out[a * HD : (a + 1) * HD, cols] = wide[
                    n * LANES : (n + 1) * LANES, a * LANES : (a + 1) * LANES
                ].astype(jnp.bfloat16)
    for odd, taps in enumerate((even_ref, odd_ref)):
        for w in range(0, steps, 8):
            fix = jnp.dot(
                lags[odd, w * SUB : (w + 8) * SUB], taps[...], preferred_element_type=jnp.float32
            )
            for n in range(8):
                m = 2 * ((w + n) % 2) + odd
                col = LANES * ((m + 1) // 2)
                corr[(w + n) // 2, m * SUB : (m + 1) * SUB, col : col + taps.shape[1]] = fix[
                    n * SUB : (n + 1) * SUB
                ]


def tables_kernel(weights, key_ref, even_ref, odd_ref):
    def fill(ref, origin, swap):
        height = ref.shape[0] if swap else ref.shape[0] // CQ
        width = ref.shape[1] // CQ if swap else ref.shape[1]
        shape = (height, width)
        tap = lax.broadcasted_iota(jnp.int32, shape, 1) - lax.broadcasted_iota(jnp.int32, shape, 0)
        for a in range(CQ):
            value = jnp.zeros(shape, jnp.float32)
            for c in range(CK):
                value = jnp.where(tap == c - origin, weights[a * CK + c], value)
            value = value.astype(jnp.bfloat16)
            if swap:
                ref[:, a * width : (a + 1) * width] = value
            else:
                ref[a * height : (a + 1) * height, :] = value

    fill(key_ref, CK // 2 + AHEAD, True)
    fill(even_ref, CK // 2 + 8 - BAND, False)
    fill(odd_ref, CK // 2 + 8 - SUB, False)


def tables_of(weights):
    return pl.pallas_call(
        tables_kernel,
        out_shape=(
            jax.ShapeDtypeStruct((2 * LANES, CQ * LANES), jnp.bfloat16),
            jax.ShapeDtypeStruct((CQ * LANES, 2 * LANES), jnp.bfloat16),
            jax.ShapeDtypeStruct((CQ * LANES, LANES), jnp.bfloat16),
        ),
        in_specs=[whole(pltpu.SMEM)],
        out_specs=[whole(pltpu.VMEM)] * 3,
        compiler_params=kernel_params(8),
        cost_estimate=pl.CostEstimate(flops=2**23, bytes_accessed=2**20, transcendentals=0),
    )(weights)


def attend_kernel(place, mix, *refs):
    qk_refs, (va, vb, vc, vd), (mine, theirs) = refs[:5], refs[5:9], refs[9:11]
    v_all, q_wide, k_ref, corr = refs[11:15]
    side, core = place[2], place[1]
    b = pl.program_id(0)
    count = k_ref.shape[1] // (2 * ROWS)

    @pl.when(b == 0)
    def _():
        prepare(core, *qk_refs, q_wide, k_ref, corr, *refs[15:])
        for i in range(count):
            for parity, near, far in ((core, va, vb), (1 - core, vc, vd)):
                rows = pl.ds(pl.multiple_of((2 * i + parity) * ROWS, ROWS), ROWS)
                first, last = near[i], far[i]
                v_all[rows, : 2 * HD] = jnp.where(side == 0, first, last)
                v_all[rows, 2 * HD :] = jnp.where(side == 0, last, first)

    row = lax.broadcasted_iota(jnp.int32, (ROWS, ROWS), 0)
    col = lax.broadcasted_iota(jnp.int32, (ROWS, ROWS), 1)
    seen = col <= row
    top, low = slice(0, ROWS), slice(ROWS, 2 * ROWS)

    def fixed(part, n):
        return jnp.concatenate([part[:, :BAND], part[:, BAND:] - corr[n, :, :BAND]], 1)

    def rows_of(upper, lower):
        return jnp.concatenate([upper, lower], 0)

    def block(step):
        q_rows = q_wide[2 * step * ROWS : (2 * step + 2) * ROWS]
        parts = []
        for j in range(2 * step + 1):
            part = jnp.dot(
                q_rows,
                k_ref[:, j * ROWS : (j + 1) * ROWS],
                preferred_element_type=jnp.float32,
            )
            if j == 2 * step:
                diagonal = jnp.where(seen, part[top] - corr[2 * step, :, BAND:], -jnp.inf)
                part = rows_of(diagonal, fixed(part[low], 2 * step + 1))
            elif j == 2 * step - 1:
                part = rows_of(fixed(part[top], 2 * step), part[low])
            parts.append(part)
        start = (2 * step + 1) * ROWS
        last = jnp.dot(
            q_rows[low], k_ref[:, start : start + ROWS], preferred_element_type=jnp.float32
        )
        last = jnp.where(seen, last - corr[2 * step + 1, :, BAND:], -jnp.inf)
        peak = parts[0]
        for part in parts[1:]:
            peak = jnp.maximum(peak, part)
        peak = rows_of(peak[top], jnp.maximum(peak[low], last))
        peak = jnp.max(peak, axis=1, keepdims=True)
        mass = jnp.zeros((2 * ROWS, ROWS), jnp.float32)
        probs = []
        for part in parts:
            part = jnp.exp2(part - peak)
            mass = mass + part
            probs.append(part.astype(jnp.bfloat16))
        last = jnp.exp2(last - peak[low])
        mass = rows_of(mass[top], mass[low] + last)
        summed = jnp.dot(
            jnp.concatenate(probs, 1), v_all[:start], preferred_element_type=jnp.float32
        )
        extra = jnp.dot(
            last.astype(jnp.bfloat16),
            v_all[start : start + ROWS],
            preferred_element_type=jnp.float32,
        )
        inverse = 1.0 / jnp.sum(mass, axis=1, keepdims=True)
        halves = []
        for rows, total in ((top, summed[top]), (low, summed[low] + extra)):
            halves.append(
                jnp.concatenate(
                    [
                        total[:, g * HD : (g + 1) * HD] * (inverse[rows] * mix[g])
                        for g in range(GROUP)
                    ],
                    1,
                ).astype(jnp.bfloat16)
            )
        mine[0] = jnp.where(core == 0, halves[0], halves[1])
        theirs[0] = jnp.where(core == 0, halves[1], halves[0])

    for step in range(count):
        pl.when(b == step)(lambda step=step: block(step))


def attend_head(place, mix, mine, other, tables, values):
    total = 2 * mine.shape[0] * ROWS
    count = total // (2 * ROWS)
    depth = CQ * HD
    out = jax.ShapeDtypeStruct((count, ROWS, GROUP * HD), jnp.bfloat16)
    out_spec = pl.BlockSpec((1, ROWS, GROUP * HD), lambda b: (b, 0, 0))
    return pl.pallas_call(
        attend_kernel,
        grid=(count,),
        out_shape=(out, out),
        in_specs=[whole(pltpu.SMEM)] * 2 + [whole(pltpu.VMEM)] * 9,
        out_specs=[out_spec, out_spec],
        scratch_shapes=[
            pltpu.VMEM((total, GROUP * HD), jnp.bfloat16),
            pltpu.VMEM((total, depth), jnp.bfloat16),
            pltpu.VMEM((depth, total), jnp.bfloat16),
            pltpu.VMEM((total // ROWS, ROWS, BAND + ROWS), jnp.float32),
            pltpu.VMEM((8 + total, HD), jnp.float32),
            pltpu.VMEM((AHEAD + total + LANES, HD), jnp.float32),
            pltpu.VMEM((2, total // 2, CQ * LANES), jnp.bfloat16),
            pltpu.VMEM((total, 2 * LANES), jnp.bfloat16),
        ],
        compiler_params=kernel_params(36),
        cost_estimate=pl.CostEstimate(
            flops=total * total * (depth + GROUP * HD),
            bytes_accessed=16 * 2**20,
            transcendentals=total * total // 2,
        ),
    )(place, mix, mine, other, *tables, *values)


def finish_kernel(place, own, r1, r2, r3, gain, *refs):
    w_parts, outs = refs[:12], refs[12:16]
    normed, w_buf, sem = refs[16:]
    width = w_parts[0].shape[1]
    core, head, inner = place[1], place[0], place[9]

    def copy_w(n, source):
        side = core if n % 2 == 0 else 1 - core
        cols = pl.ds(pl.multiple_of(side * width, width), width)
        target = w_buf.at[lax.bitwise_xor(place[5 + n // 2], head), :, cols]
        return pltpu.make_async_copy(w_parts[source], target, sem.at[n])

    for n in range(4):
        copy_w(n, n).start()
    for n in range(4, 8):
        straight = n if n < 6 else n + 2

        @pl.when(inner == 1)
        def _():
            copy_w(n, straight).start()

        @pl.when(inner == 0)
        def _():
            copy_w(n, straight + 2).start()

    near = own[...] + r1[...].astype(jnp.float32)
    far = r2[...].astype(jnp.float32) + r3[...].astype(jnp.float32)
    low = place[3] == 0
    for g in range(2 * GROUP):
        cols = slice((g % GROUP) * HD, (g % GROUP + 1) * HD)
        first = low if g < GROUP else jnp.logical_not(low)
        x = jnp.where(first, near[:, cols], far[:, cols])
        scale = lax.rsqrt(jnp.mean(x * x, axis=1, keepdims=True) + 1e-05)
        normed[:, g * HD : (g + 1) * HD] = (
            x * scale * gain[:, g * HD : (g + 1) * HD]
        ).astype(jnp.bfloat16)
    for n in range(8):
        copy_w(n, n).wait()
    for t in (3, 2, 1, 0):
        outs[t][...] = jnp.dot(
            normed[...], w_buf[t], preferred_element_type=jnp.float32
        ).astype(jnp.bfloat16)


def finish(place, own, r1, r2, r3, gain, w_parts):
    rows = own.shape[0]
    depth, width = w_parts[0].shape
    return pl.pallas_call(
        finish_kernel,
        in_specs=[whole(pltpu.SMEM)] + [whole(pltpu.VMEM)] * 5 + [whole(pl.ANY)] * 12,
        out_specs=[whole(pltpu.VMEM)] * 4,
        out_shape=[jax.ShapeDtypeStruct((rows, 2 * width), jnp.bfloat16)] * 4,
        scratch_shapes=[
            pltpu.VMEM((rows, depth), jnp.bfloat16),
            pltpu.VMEM((4, depth, 2 * width), jnp.bfloat16),
            pltpu.SemaphoreType.DMA((8,)),
        ],
        compiler_params=kernel_params(14),
        cost_estimate=pl.CostEstimate(
            flops=2 * rows * depth * 8 * width, bytes_accessed=11 * 2**20, transcendentals=0
        ),
    )(place, own, r1, r2, r3, gain, *w_parts)


def swapped(value, axis, mask):
    count = lax.axis_size(axis)
    return lax.ppermute(value, axis, [(i, i ^ mask) for i in range(count)])


def per_device_one_head(
    activations, positions, w_query, w_key, w_value, conv_kernel, head_mix, out_gain, w_out
):
    ctx, head = lax.axis_index("ctx"), lax.axis_index("head")
    z, core = ctx // 2, ctx % 2
    rows = activations.shape[0]
    half = rows // 2
    barrier = lax.optimization_barrier
    pair = 2 * HD

    def columns(target):
        parts = [
            lax.dynamic_slice_in_dim(w, target * pair, pair, 1) for w in (w_query, w_key, w_value)
        ]
        return jnp.concatenate(parts, 1)

    digits = jnp.stack([positions // 256, positions % 256]).astype(jnp.bfloat16)
    digits = jnp.pad(digits, ((0, 14), (0, activations.shape[1] - rows)))
    block = jnp.concatenate([activations, digits])
    w_pieces = [columns(z ^ s) for s in range(4)]
    far = [swapped(block, "ctx", 2 * s) for s in (1, 2, 3)]
    x0, y0 = swapped(activations, "head", 1), swapped(activations, "head", 2)
    w_near = swapped(w_pieces[1], "ctx", 2)
    weights = lax.dynamic_index_in_dim(conv_kernel, ctx, 0, keepdims=False)
    tables = tables_of(weights * (math.log2(math.e) / math.sqrt(HD)))
    place = jnp.stack([head, core, z % 2, z // 2, z ^ head, z, z ^ 1, z ^ 2, z ^ 3])
    place = place.astype(jnp.int32)
    far, x0, y0, w_near, w_pieces, tables, place, w_out = barrier(
        (far, x0, y0, w_near, w_pieces, tables, place, w_out)
    )

    w_far = [swapped(w_pieces[s], "ctx", 2 * s) for s in (2, 3)]
    inner = [a[:rows] for a in far]
    x_rest = swapped(jnp.concatenate(inner + [y0[half:]]), "head", 1)
    y_rest = swapped(jnp.concatenate(inner + [x0[:half]]), "head", 2)
    d_rest = swapped(jnp.concatenate(inner), "head", 3)
    place_of = jnp.stack(
        [
            a[rows, :rows].astype(jnp.float32) * 256.0 + a[rows + 1, :rows].astype(jnp.float32)
            for a in [block] + far
        ]
    )
    exponents = jnp.arange(HD // 2, dtype=jnp.float32) * (2.0 / HD)
    inverse = jnp.exp(-exponents * math.log(500000.0))
    angle = (place_of * 0.25)[:, :, None] * inverse
    cosine, sine = jnp.cos(angle), jnp.sin(angle)
    cosine = jnp.concatenate([cosine, cosine], -1)
    sine = jnp.concatenate([-sine, sine], -1)
    w_far, x_rest, y_rest, d_rest, cosine, sine, w_out = barrier(
        (w_far, x_rest, y_rest, d_rest, cosine, sine, w_out)
    )
    w_same = [w_pieces[0], w_near] + list(w_far)
    w_swap = [swapped(w, "ctx", 1) for w in w_same]
    middle = [(2, 4), (3, 5), (4, 2), (5, 3)]
    outward = [(2, 0), (3, 1), (4, 6), (5, 7)]
    out_near = swapped(w_out, "ctx", 2)
    out_across = lax.ppermute(w_out, "ctx", middle)
    sources = place, [activations] + list(far), (x0, x_rest, y0, y_rest, d_rest), w_same, w_swap
    (v_pair,) = project(*sources)
    v_next = swapped(v_pair, "ctx", 2)
    v_pair_other = swapped(v_pair, "ctx", 1)
    out_own_swap = swapped(w_out, "ctx", 1)
    place, v_pair = barrier((place, v_pair))
    mine, theirs = project(place, *sources[1:], (cosine, sine))
    mine, theirs, v_next, v_pair_other, out_near, out_across, out_own_swap = barrier(
        (mine, theirs, v_next, v_pair_other, out_near, out_across, out_own_swap)
    )
    out_near_swap, out_across_swap = swapped(out_near, "ctx", 1), swapped(out_across, "ctx", 1)
    other = swapped(theirs, "ctx", 1)
    v_next_other = swapped(v_next, "ctx", 1)
    out_across_next = lax.ppermute(out_near, "ctx", middle)
    out_passed = lax.ppermute(out_across, "ctx", outward)
    group_rows = lax.dynamic_slice_in_dim(head_mix, GROUP * (ctx // GROUP), GROUP, 0)
    mix = lax.dynamic_index_in_dim(group_rows, ctx % GROUP, 1, keepdims=False)
    out_mine, out_theirs = attend_head(
        place, mix, mine, other, tables, (v_pair, v_next, v_pair_other, v_next_other)
    )
    out_mine, out_theirs, out_across_next, out_passed, out_near_swap, out_across_swap = barrier(
        (out_mine, out_theirs, out_across_next, out_passed, out_near_swap, out_across_swap)
    )
    out_passed_next = lax.ppermute(out_across_next, "ctx", outward)
    out_parts = [w_out, out_own_swap, out_near, out_near_swap, out_across, out_across_swap]
    out_parts += [p for w in (out_passed, out_across_next) for p in (w, swapped(w, "ctx", 1))]
    summed = out_mine.astype(jnp.float32) + swapped(out_theirs, "ctx", 1).astype(jnp.float32)
    own = lax.dynamic_index_in_dim(summed, z, 0, keepdims=False)
    r1, r2, r3 = [
        swapped(
            lax.dynamic_index_in_dim(summed, z ^ s, 0, keepdims=False).astype(jnp.bfloat16),
            "ctx",
            2 * s,
        )
        for s in (1, 2, 3)
    ]

    r1, r2, r3, out_passed_next = barrier((r1, r2, r3, out_passed_next))
    out_parts += [out_passed_next, swapped(out_passed_next, "ctx", 1)]
    inner = (z == 1) | (z == 2)
    out_places = jnp.stack(
        [z, z ^ 1, jnp.where(inner, z ^ 3, z ^ 2), jnp.where(inner, z ^ 2, z ^ 3), inner]
    )
    where = jnp.concatenate([place[:5], out_places.astype(jnp.int32)])
    shares = finish(where, own, r1, r2, r3, out_gain.reshape(1, -1), out_parts)
    total = shares[0].astype(jnp.float32)
    for t in (1, 2, 3):
        total = total + swapped(shares[t], "head", t).astype(jnp.float32)
    return total.astype(jnp.bfloat16)


def solution(mesh):
    one_head_each = mesh.shape["ctx"] == 8 and mesh.shape["head"] == 4
    body = per_device_one_head if one_head_each else per_device
    return jax.shard_map(
        body,
        mesh=mesh,
        in_specs=(
            P("ctx", "head"),
            P("ctx"),
            P("ctx", "head"),
            P("ctx", "head"),
            P("ctx", "head"),
            P("head", None),
            P("head", None),
            P("head"),
            P("head", "ctx"),
        ),
        out_specs=P("ctx", "head"),
        check_vma=False,
    )
```

```python
import functools
import math

import jax
import jax.numpy as jnp
from jax import lax
from jax.experimental import pallas as pl
from jax.experimental.pallas import tpu as pltpu
from jax.sharding import PartitionSpec as P

HD = 128
GROUP = 4
CQ = 6
CK = 11
KB = 512


def passed_along(value, axis, steps):
    count = lax.axis_size(axis)
    leading, last = (max(0, -steps), min(count, count - steps))
    return lax.ppermute(value, axis, [(source, source + steps) for source in range(leading, last)])


def rope(projected, positions):
    row_count = projected.shape[0]
    head_count = projected.shape[1] // HD
    shaped = projected.reshape(row_count, head_count, HD)
    half_size = HD // 2
    exponents = jnp.arange(half_size, dtype=jnp.float32) * (2.0 / HD)
    inverse = jnp.exp(-exponents * math.log(500000.0))
    angle = (positions.astype(jnp.float32) * 0.25)[:, None, None] * inverse[None, None, :]
    cosine = jnp.cos(angle)
    sine = jnp.sin(angle)
    lower_half = shaped[..., :half_size]
    upper_half = shaped[..., half_size:]
    rotated_rows = jnp.concatenate(
        [lower_half * cosine - upper_half * sine, upper_half * cosine + lower_half * sine], -1
    )
    return rotated_rows.reshape(row_count, head_count * HD)


def convolve(masked, kernel, row_count, col_count):
    summed = jnp.zeros((masked.shape[0], row_count, col_count), jnp.float32)
    for lag_q in range(CQ):
        for lag_k in range(CK):
            weight = kernel[:, lag_q * CK + lag_k][:, None, None]
            window = masked[
                :,
                CQ - 1 - lag_q : CQ - 1 - lag_q + row_count,
                CK - 1 - lag_k : CK - 1 - lag_k + col_count,
            ]
            summed = summed + weight * window
    return summed


def add_rows(left, piece):
    return jnp.dot(left, piece, preferred_element_type=jnp.float32)


def share_keys(key, value):
    return (
        lax.all_gather(key, "ctx", axis=0, tiled=True),
        lax.all_gather(value, "ctx", axis=0, tiled=True),
    )


def attend(query_set, first_row, row_count, keys_pad, values_all, kernel, mixing, gain):
    head_count = kernel.shape[0]
    ext_rows = row_count + CQ - 1
    query_heads = query_set.reshape(ext_rows, head_count, HD)
    token_total = values_all.shape[0]
    block_count = token_total // KB
    last_row = first_row + row_count - 1
    scale = 1.0 / math.sqrt(HD)
    prow = first_row - (CQ - 1) + jnp.arange(ext_rows, dtype=jnp.int32)
    irow = first_row + jnp.arange(row_count, dtype=jnp.int32)

    def logits_of(block):
        key_start = block * KB
        key_block = lax.dynamic_slice_in_dim(keys_pad, key_start, KB + CK - 1, 0).reshape(
            KB + CK - 1, head_count, HD
        )
        scores = (
            jnp.einsum("rhd,khd->hrk", query_heads, key_block, preferred_element_type=jnp.float32)
            * scale
        )
        kcol = key_start - CK // 2 + jnp.arange(KB + CK - 1, dtype=jnp.int32)
        valid = (kcol[None, :] <= prow[:, None]) & (prow[:, None] >= 0)
        masked = jnp.where(valid[None], scores, 0.0)
        conv = convolve(masked, kernel, row_count, KB)
        jcol = key_start + jnp.arange(KB, dtype=jnp.int32)
        return jnp.where((jcol[None, :] <= irow[:, None])[None], conv, -jnp.inf)

    def first_pass(block, carry_in):

        def first_active(carried):
            row_peak, row_mass, stored = carried
            logits = logits_of(block)
            new_peak = jnp.maximum(row_peak, jnp.max(logits, axis=-1))
            new_mass = row_mass * jnp.exp(row_peak - new_peak) + jnp.sum(
                jnp.exp(logits - new_peak[..., None]), axis=-1
            )
            stored = lax.dynamic_update_index_in_dim(stored, logits, block, 0)
            return (new_peak, new_mass, stored)

        return lax.cond(block * KB <= last_row, first_active, lambda carried: carried, carry_in)

    peak_start = jnp.full((head_count, row_count), -jnp.inf, jnp.float32)
    mass_start = jnp.zeros((head_count, row_count), jnp.float32)
    store_start = jnp.zeros((block_count, head_count, row_count, KB), jnp.float32)
    row_peak, row_mass, stored = lax.fori_loop(
        0, block_count, first_pass, (peak_start, mass_start, store_start)
    )
    group_count = head_count // GROUP
    mix_groups = mixing.reshape(group_count, GROUP, GROUP)

    def second_pass(block, carry_in):

        def second_active(summed):
            logits = lax.dynamic_index_in_dim(stored, block, 0, keepdims=False)
            probs = jnp.exp(logits - row_peak[..., None]) / row_mass[..., None]
            grouped = probs.reshape(group_count, GROUP, row_count, KB)
            mixed_scores = (
                jnp.einsum("gab,gbrk->gark", mix_groups, grouped)
                .reshape(head_count, row_count, KB)
                .astype(jnp.bfloat16)
            )
            value_block = lax.dynamic_slice_in_dim(values_all, block * KB, KB, 0).reshape(
                KB, head_count, HD
            )
            return summed + jnp.einsum(
                "hrk,khd->rhd", mixed_scores, value_block, preferred_element_type=jnp.float32
            )

        return lax.cond(block * KB <= last_row, second_active, lambda summed: summed, carry_in)

    summed = lax.fori_loop(
        0, block_count, second_pass, jnp.zeros((row_count, head_count, HD), jnp.float32)
    )
    rms = jnp.sqrt(jnp.mean(summed * summed, axis=-1, keepdims=True) + 1e-05)
    normed = (summed / rms * gain.reshape(head_count, HD)).astype(jnp.bfloat16)
    return normed.reshape(row_count, head_count * HD)


def per_device(
    activations, positions, w_query, w_key, w_value, conv_kernel, head_mix, out_gain, w_out
):
    row_count = activations.shape[0]
    ctx_place = lax.axis_index("ctx")
    features = lax.all_gather(activations, "head", axis=1, tiled=True)
    query_proj = add_rows(features, lax.all_gather(w_query, "ctx", axis=0, tiled=True))
    key_proj = add_rows(features, lax.all_gather(w_key, "ctx", axis=0, tiled=True))
    value_proj = add_rows(features, lax.all_gather(w_value, "ctx", axis=0, tiled=True))
    key = rope(key_proj, positions).astype(jnp.bfloat16)
    value = value_proj.astype(jnp.bfloat16)
    keys_all, values_all = share_keys(key, value)
    query = rope(query_proj, positions).astype(jnp.bfloat16)
    rim_rows = passed_along(query[row_count - (CQ - 1) :], "ctx", 1)
    query_ext = jnp.concatenate([rim_rows, query], 0)
    keys_pad = jnp.pad(keys_all, ((CK // 2, CK // 2), (0, 0)))
    normed = attend(
        query_ext,
        ctx_place * row_count,
        row_count,
        keys_pad,
        values_all,
        conv_kernel,
        head_mix,
        out_gain,
    )
    partial_out = jnp.dot(
        normed, lax.all_gather(w_out, "ctx", axis=1, tiled=True), preferred_element_type=jnp.float32
    )
    return lax.psum_scatter(
        partial_out.astype(jnp.bfloat16), "head", scatter_dimension=1, tiled=True
    )


ROWS = 256
BAND = 128
LANES = 128
SUB = 64
AHEAD = 16


def kernel_params(mebibytes):
    return pltpu.CompilerParams(vmem_limit_bytes=mebibytes * 1024 * 1024)


def whole(memory_space):
    return pl.BlockSpec(memory_space=memory_space)


def project_kernel(rows, first_col, place, *refs):
    a_own, (x0, x_rest, y0, y_rest, d_rest) = refs[:4], refs[4:9]
    w_same, w_swap = refs[9:11]
    abuf, wbuf, acc, sem_a, sem_w = refs[-5:]
    turn, core = place[0], place[1]
    half = w_same.shape[1]
    width = wbuf.shape[2]

    def copies_a(t):
        if t == 0:
            pairs = [(a_own[b], 0, b * rows, rows) for b in range(4)]
        elif t < 3:
            first, others = ((x0, x_rest), (y0, y_rest))[t - 1]
            pairs = [(first, 0, 0, rows), (others, 0, rows, 3 * rows)]
        else:
            late, mid = 3 * rows, rows // 2
            pairs = [(y_rest, late, 0, mid), (x_rest, late, mid, mid), (d_rest, 0, rows, 3 * rows)]
        return [
            pltpu.make_async_copy(
                ref.at[pl.ds(source, size)], abuf.at[t, pl.ds(target, size)], sem_a.at[t, n]
            )
            for n, (ref, source, target, size) in enumerate(pairs)
        ]

    def copies_w(t):
        out = []
        for n, (ref, side) in enumerate(((w_same, core), (w_swap, 1 - core))):
            source = ref.at[lax.bitwise_xor(turn, t), :, pl.ds(first_col, width)]
            target = wbuf.at[t, pl.ds(pl.multiple_of(side * half, half), half)]
            out.append(pltpu.make_async_copy(source, target, sem_w.at[t, n]))
        return out

    for t in range(4):
        for copy in copies_w(t) + copies_a(t):
            copy.start()
    for t in range(4):
        for copy in copies_w(t) + copies_a(t):
            copy.wait()
        part = jnp.dot(abuf[t], wbuf[t], preferred_element_type=jnp.float32)
        acc[...] = part if t == 0 else acc[...] + part
    if first_col:
        v_out = refs[11]
        for b in range(4):
            v_out[place[5 + b]] = acc[b * rows : (b + 1) * rows].astype(jnp.bfloat16)
        return
    cos_ref, sin_ref, mine, theirs = refs[11:15]
    first = core == 0
    for b in range(4):
        total = acc[b * rows : (b + 1) * rows]
        cosine, sine = cos_ref[b], sin_ref[b]
        at = place[5 + b]
        for col, out in ((0, 0), (2 * HD, HD)):
            heads = []
            for start in (col, col + HD):
                x = total[:, start : start + HD]
                x = x * cosine + pltpu.roll(x, HD // 2, 1) * sine
                heads.append(x.astype(jnp.bfloat16))
            mine[at, :, out : out + HD] = jnp.where(first, heads[0], heads[1])
            theirs[at, :, out : out + HD] = jnp.where(first, heads[1], heads[0])


def project(place, a_own, a_plane, w_same, w_swap, angles=()):
    rows, depth = a_own[0].shape
    first_col, width = (0, 4 * HD) if angles else (4 * HD, 2 * HD)
    out = jax.ShapeDtypeStruct((4, rows, 2 * HD), jnp.bfloat16)
    count = 2 if angles else 1
    return pl.pallas_call(
        functools.partial(project_kernel, rows, first_col),
        out_shape=[out] * count,
        in_specs=[whole(pltpu.SMEM)]
        + [whole(pl.ANY)] * 11
        + [whole(pltpu.VMEM)] * len(angles),
        out_specs=[whole(pltpu.VMEM)] * count,
        scratch_shapes=[
            pltpu.VMEM((4, 4 * rows, depth), jnp.bfloat16),
            pltpu.VMEM((4, depth, width), jnp.bfloat16),
            pltpu.VMEM((4 * rows, width), jnp.float32),
            pltpu.SemaphoreType.DMA((4, 4)),
            pltpu.SemaphoreType.DMA((4, 2)),
        ],
        compiler_params=kernel_params(20),
        cost_estimate=pl.CostEstimate(
            flops=8 * rows * 4 * depth * width, bytes_accessed=16 * 2**20, transcendentals=0
        ),
    )(place, *a_own, *a_plane, w_same, w_swap, *angles)


def prepare(core, mine, other, key_ref, even_ref, odd_ref, q_out, k_out, corr, *scratch):
    qf, kf, lags, turned = scratch
    total = q_out.shape[0]
    qf[0:8] = jnp.zeros((8, HD), jnp.float32)
    kf[0:AHEAD] = jnp.zeros((AHEAD, HD), jnp.float32)
    kf[AHEAD + total :] = jnp.zeros((kf.shape[0] - AHEAD - total, HD), jnp.float32)
    corr[...] = jnp.zeros(corr.shape, jnp.float32)
    for i in range(total // (2 * ROWS)):
        for ref, parity in ((mine, core), (other, 1 - core)):
            start = pl.multiple_of((2 * i + parity) * ROWS, ROWS)
            block = ref[i].astype(jnp.float32)
            qf[pl.ds(8 + start, ROWS)] = block[:, :HD]
            kf[pl.ds(AHEAD + start, ROWS)] = block[:, HD:]

    ahead = lax.broadcasted_iota(jnp.int32, (SUB + 8, LANES), 1) - lax.broadcasted_iota(
        jnp.int32, (SUB + 8, LANES), 0
    )
    near = (ahead >= 1) & (ahead < CQ + CK // 2)
    steps = total // LANES
    for w in range(steps):
        base = w * LANES
        window = kf[base : base + 2 * LANES].T
        turned[base : base + LANES] = window.astype(jnp.bfloat16)
        for odd in range(2):
            at = base + odd * SUB
            qwin = qf[at : at + SUB + 8]
            kwin = kf[at + AHEAD - 8 : at + AHEAD - 8 + LANES]
            scores = lax.dot_general(
                qwin.astype(jnp.bfloat16),
                kwin.astype(jnp.bfloat16),
                (((1,), (1,)), ((), ())),
                preferred_element_type=jnp.float32,
            )
            future = jnp.where(near, scores, 0.0)
            for a in range(CQ):
                cols = slice(a * LANES, (a + 1) * LANES)
                lags[odd, w * SUB : (w + 1) * SUB, cols] = future[8 - a : 8 - a + SUB].astype(
                    jnp.bfloat16
                )
                q_out[at : at + SUB, cols] = qwin[8 - a : 8 - a + SUB].astype(jnp.bfloat16)
    for w in range(0, steps, 4):
        wide = jnp.dot(
            turned[w * LANES : (w + 4) * LANES], key_ref[...], preferred_element_type=jnp.float32
        )
        for n in range(4):
            cols = slice((w + n) * LANES, (w + n + 1) * LANES)
            for a in range(CQ):
                k_out[a * HD : (a + 1) * HD, cols] = wide[
                    n * LANES : (n + 1) * LANES, a * LANES : (a + 1) * LANES
                ].astype(jnp.bfloat16)
    for odd, taps in enumerate((even_ref, odd_ref)):
        for w in range(0, steps, 8):
            fix = jnp.dot(
                lags[odd, w * SUB : (w + 8) * SUB], taps[...], preferred_element_type=jnp.float32
            )
            for n in range(8):
                m = 2 * ((w + n) % 2) + odd
                col = LANES * ((m + 1) // 2)
                corr[(w + n) // 2, m * SUB : (m + 1) * SUB, col : col + taps.shape[1]] = fix[
                    n * SUB : (n + 1) * SUB
                ]


def tables_kernel(weights, key_ref, even_ref, odd_ref):
    def fill(ref, origin, swap):
        height = ref.shape[0] if swap else ref.shape[0] // CQ
        width = ref.shape[1] // CQ if swap else ref.shape[1]
        shape = (height, width)
        tap = lax.broadcasted_iota(jnp.int32, shape, 1) - lax.broadcasted_iota(jnp.int32, shape, 0)
        for a in range(CQ):
            value = jnp.zeros(shape, jnp.float32)
            for c in range(CK):
                value = jnp.where(tap == c - origin, weights[a * CK + c], value)
            value = value.astype(jnp.bfloat16)
            if swap:
                ref[:, a * width : (a + 1) * width] = value
            else:
                ref[a * height : (a + 1) * height, :] = value

    fill(key_ref, CK // 2 + AHEAD, True)
    fill(even_ref, CK // 2 + 8 - BAND, False)
    fill(odd_ref, CK // 2 + 8 - SUB, False)


def tables_of(weights):
    return pl.pallas_call(
        tables_kernel,
        out_shape=(
            jax.ShapeDtypeStruct((2 * LANES, CQ * LANES), jnp.bfloat16),
            jax.ShapeDtypeStruct((CQ * LANES, 2 * LANES), jnp.bfloat16),
            jax.ShapeDtypeStruct((CQ * LANES, LANES), jnp.bfloat16),
        ),
        in_specs=[whole(pltpu.SMEM)],
        out_specs=[whole(pltpu.VMEM)] * 3,
        compiler_params=kernel_params(8),
        cost_estimate=pl.CostEstimate(flops=2**23, bytes_accessed=2**20, transcendentals=0),
    )(weights)


def attend_kernel(place, mix, *refs):
    qk_refs, table_refs, (va, vb, vc, vd), (mine, theirs) = refs[:2], refs[2:5], refs[5:9], refs[9:11]
    v_all, q_wide, k_ref, corr = refs[11:15]
    tables, sem_v, sem_t = refs[19:22], refs[22], refs[23]
    side, core = place[2], place[1]
    b = pl.program_id(0)
    count = k_ref.shape[1] // (2 * ROWS)

    @pl.when(b == 0)
    def _():
        def copies_v():
            out = []
            for n, ref in enumerate((va, vb, vc, vd)):
                parity = core if n < 2 else 1 - core
                start = pl.multiple_of((side if n % 2 == 0 else 1 - side) * 2 * HD, 2 * HD)
                for i in range(count):
                    rows = pl.ds(pl.multiple_of((2 * i + parity) * ROWS, ROWS), ROWS)
                    target = v_all.at[rows, pl.ds(start, 2 * HD)]
                    out.append(pltpu.make_async_copy(ref.at[i], target, sem_v.at[n, i]))
            return out

        loads = [
            pltpu.make_async_copy(ref, table, sem_t.at[n])
            for n, (ref, table) in enumerate(zip(table_refs, tables))
        ]
        for copy in loads + copies_v():
            copy.start()
        for copy in loads:
            copy.wait()
        prepare(core, *qk_refs, *tables, q_wide, k_ref, corr, *refs[15:19])
        for copy in copies_v():
            copy.wait()

    row = lax.broadcasted_iota(jnp.int32, (ROWS, ROWS), 0)
    col = lax.broadcasted_iota(jnp.int32, (ROWS, ROWS), 1)
    seen = col <= row
    top, low = slice(0, ROWS), slice(ROWS, 2 * ROWS)

    def fixed(part, n):
        return jnp.concatenate([part[:, :BAND], part[:, BAND:] - corr[n, :, :BAND]], 1)

    def rows_of(upper, lower):
        return jnp.concatenate([upper, lower], 0)

    def block(step):
        q_rows = q_wide[2 * step * ROWS : (2 * step + 2) * ROWS]
        parts = []
        for j in range(2 * step + 1):
            part = jnp.dot(
                q_rows,
                k_ref[:, j * ROWS : (j + 1) * ROWS],
                preferred_element_type=jnp.float32,
            )
            if j == 2 * step:
                diagonal = jnp.where(seen, part[top] - corr[2 * step, :, BAND:], -jnp.inf)
                part = rows_of(diagonal, fixed(part[low], 2 * step + 1))
            elif j == 2 * step - 1:
                part = rows_of(fixed(part[top], 2 * step), part[low])
            parts.append(part)
        start = (2 * step + 1) * ROWS
        last = jnp.dot(
            q_rows[low], k_ref[:, start : start + ROWS], preferred_element_type=jnp.float32
        )
        last = jnp.where(seen, last - corr[2 * step + 1, :, BAND:], -jnp.inf)
        peak = parts[0]
        for part in parts[1:]:
            peak = jnp.maximum(peak, part)
        peak = rows_of(peak[top], jnp.maximum(peak[low], last))
        peak = jnp.max(peak, axis=1, keepdims=True)
        mass = jnp.zeros((2 * ROWS, ROWS), jnp.float32)
        probs = []
        for part in parts:
            part = jnp.exp2(part - peak)
            mass = mass + part
            probs.append(part.astype(jnp.bfloat16))
        last = jnp.exp2(last - peak[low])
        mass = rows_of(mass[top], mass[low] + last)
        summed = jnp.dot(
            jnp.concatenate(probs, 1), v_all[:start], preferred_element_type=jnp.float32
        )
        extra = jnp.dot(
            last.astype(jnp.bfloat16),
            v_all[start : start + ROWS],
            preferred_element_type=jnp.float32,
        )
        inverse = 1.0 / jnp.sum(mass, axis=1, keepdims=True)
        halves = []
        for rows, total in ((top, summed[top]), (low, summed[low] + extra)):
            halves.append(
                jnp.concatenate(
                    [
                        total[:, g * HD : (g + 1) * HD] * (inverse[rows] * mix[g])
                        for g in range(GROUP)
                    ],
                    1,
                ).astype(jnp.bfloat16)
            )
        mine[0] = jnp.where(core == 0, halves[0], halves[1])
        theirs[0] = jnp.where(core == 0, halves[1], halves[0])

    for step in range(count):
        pl.when(b == step)(lambda step=step: block(step))


def attend_head(place, mix, mine, other, tables, values):
    total = 2 * mine.shape[0] * ROWS
    count = total // (2 * ROWS)
    depth = CQ * HD
    out = jax.ShapeDtypeStruct((count, ROWS, GROUP * HD), jnp.bfloat16)
    out_spec = pl.BlockSpec((1, ROWS, GROUP * HD), lambda b: (b, 0, 0))
    return pl.pallas_call(
        attend_kernel,
        grid=(count,),
        out_shape=(out, out),
        in_specs=[whole(pltpu.SMEM)] * 2 + [whole(pltpu.VMEM)] * 2 + [whole(pl.ANY)] * 7,
        out_specs=[out_spec, out_spec],
        scratch_shapes=[
            pltpu.VMEM((total, GROUP * HD), jnp.bfloat16),
            pltpu.VMEM((total, depth), jnp.bfloat16),
            pltpu.VMEM((depth, total), jnp.bfloat16),
            pltpu.VMEM((total // ROWS, ROWS, BAND + ROWS), jnp.float32),
            pltpu.VMEM((8 + total, HD), jnp.float32),
            pltpu.VMEM((AHEAD + total + LANES, HD), jnp.float32),
            pltpu.VMEM((2, total // 2, CQ * LANES), jnp.bfloat16),
            pltpu.VMEM((total, 2 * LANES), jnp.bfloat16),
        ]
        + [pltpu.VMEM(table.shape, table.dtype) for table in tables]
        + [pltpu.SemaphoreType.DMA((4, count)), pltpu.SemaphoreType.DMA((3,))],
        compiler_params=kernel_params(36),
        cost_estimate=pl.CostEstimate(
            flops=total * total * (depth + GROUP * HD),
            bytes_accessed=16 * 2**20,
            transcendentals=total * total // 2,
        ),
    )(place, mix, mine, other, *tables, *values)


def finish_kernel(place, own, r1, r2, r3, gain, *refs):
    w_parts, outs = refs[:12], refs[12:16]
    normed, w_buf, sem = refs[16:]
    width = w_parts[0].shape[1]
    core, head, inner = place[1], place[0], place[9]

    def copy_w(n, source):
        side = core if n % 2 == 0 else 1 - core
        cols = pl.ds(pl.multiple_of(side * width, width), width)
        target = w_buf.at[lax.bitwise_xor(place[5 + n // 2], head), :, cols]
        return pltpu.make_async_copy(w_parts[source], target, sem.at[n])

    for n in range(4):
        copy_w(n, n).start()
    for n in range(4, 8):
        straight = n if n < 6 else n + 2

        @pl.when(inner == 1)
        def _():
            copy_w(n, straight).start()

        @pl.when(inner == 0)
        def _():
            copy_w(n, straight + 2).start()

    near = own[...] + r1[...].astype(jnp.float32)
    far = r2[...].astype(jnp.float32) + r3[...].astype(jnp.float32)
    low = place[3] == 0
    for g in range(2 * GROUP):
        cols = slice((g % GROUP) * HD, (g % GROUP + 1) * HD)
        first = low if g < GROUP else jnp.logical_not(low)
        x = jnp.where(first, near[:, cols], far[:, cols])
        scale = lax.rsqrt(jnp.mean(x * x, axis=1, keepdims=True) + 1e-05)
        normed[:, g * HD : (g + 1) * HD] = (
            x * scale * gain[:, g * HD : (g + 1) * HD]
        ).astype(jnp.bfloat16)
    for n in range(8):
        copy_w(n, n).wait()
    for t in (3, 2, 1, 0):
        outs[t][...] = jnp.dot(
            normed[...], w_buf[t], preferred_element_type=jnp.float32
        ).astype(jnp.bfloat16)


def finish(place, own, r1, r2, r3, gain, w_parts):
    rows = own.shape[0]
    depth, width = w_parts[0].shape
    return pl.pallas_call(
        finish_kernel,
        in_specs=[whole(pltpu.SMEM)] + [whole(pltpu.VMEM)] * 5 + [whole(pl.ANY)] * 12,
        out_specs=[whole(pltpu.VMEM)] * 4,
        out_shape=[jax.ShapeDtypeStruct((rows, 2 * width), jnp.bfloat16)] * 4,
        scratch_shapes=[
            pltpu.VMEM((rows, depth), jnp.bfloat16),
            pltpu.VMEM((4, depth, 2 * width), jnp.bfloat16),
            pltpu.SemaphoreType.DMA((8,)),
        ],
        compiler_params=kernel_params(56),
        cost_estimate=pl.CostEstimate(
            flops=2 * rows * depth * 8 * width, bytes_accessed=11 * 2**20, transcendentals=0
        ),
    )(place, own, r1, r2, r3, gain, *w_parts)


def swapped(value, axis, mask):
    count = lax.axis_size(axis)
    return lax.ppermute(value, axis, [(i, i ^ mask) for i in range(count)])


def per_device_one_head(
    activations, positions, w_query, w_key, w_value, conv_kernel, head_mix, out_gain, w_out
):
    ctx, head = lax.axis_index("ctx"), lax.axis_index("head")
    z, core = ctx // 2, ctx % 2
    rows = activations.shape[0]
    half = rows // 2
    barrier = lax.optimization_barrier
    pair = 2 * HD

    def columns(target):
        parts = [
            lax.dynamic_slice_in_dim(w, target * pair, pair, 1) for w in (w_query, w_key, w_value)
        ]
        return jnp.concatenate(parts, 1)

    digits = jnp.stack([positions // 256, positions % 256]).astype(jnp.bfloat16)
    digits = jnp.pad(digits, ((0, 14), (0, activations.shape[1] - rows)))
    block = jnp.concatenate([activations, digits])
    w_pieces = jnp.stack([columns(target) for target in range(4)])
    far = [swapped(block, "ctx", 2 * s) for s in (1, 2, 3)]
    x0, y0 = swapped(activations, "head", 1), swapped(activations, "head", 2)
    weights = lax.dynamic_index_in_dim(conv_kernel, ctx, 0, keepdims=False)
    tables = tables_of(weights * (math.log2(math.e) / math.sqrt(HD)))
    place = jnp.stack([head, core, z % 2, z // 2, head, z, z ^ 1, z ^ 2, z ^ 3])
    place = place.astype(jnp.int32)
    far, x0, y0, w_pieces, tables, place, w_out = barrier(
        (far, x0, y0, w_pieces, tables, place, w_out)
    )

    same_core = [[i for i in range(8) if i % 2 == k] for k in range(2)]
    w_same = lax.all_to_all(w_pieces, "ctx", 0, 0, axis_index_groups=same_core)
    inner = [a[:rows] for a in far]
    x_rest = swapped(jnp.concatenate(inner + [y0[half:]]), "head", 1)
    y_rest = swapped(jnp.concatenate(inner + [x0[:half]]), "head", 2)
    d_rest = swapped(jnp.concatenate(inner), "head", 3)
    place_of = jnp.stack(
        [
            a[rows, :rows].astype(jnp.float32) * 256.0 + a[rows + 1, :rows].astype(jnp.float32)
            for a in [block] + far
        ]
    )
    exponents = jnp.arange(HD // 2, dtype=jnp.float32) * (2.0 / HD)
    inverse = jnp.exp(-exponents * math.log(500000.0))
    angle = (place_of * 0.25)[:, :, None] * inverse
    cosine, sine = jnp.cos(angle), jnp.sin(angle)
    cosine = jnp.concatenate([cosine, cosine], -1)
    sine = jnp.concatenate([-sine, sine], -1)
    middle = [(2, 4), (3, 5), (4, 2), (5, 3)]
    outward = [(2, 0), (3, 1), (4, 6), (5, 7)]
    out_near = swapped(w_out, "ctx", 2)
    out_across = lax.ppermute(w_out, "ctx", middle)
    w_same, x_rest, y_rest, d_rest, cosine, sine, out_near, out_across = barrier(
        (w_same, x_rest, y_rest, d_rest, cosine, sine, out_near, out_across)
    )
    w_swap = swapped(w_same, "ctx", 1)
    out_across_next = lax.ppermute(out_near, "ctx", middle)
    out_passed = lax.ppermute(out_across, "ctx", outward)
    sources = place, [activations] + list(far), (x0, x_rest, y0, y_rest, d_rest), w_same, w_swap
    (v_pair,) = project(*sources)
    v_next = swapped(v_pair, "ctx", 2)
    v_pair_other = swapped(v_pair, "ctx", 1)
    out_own_swap = swapped(w_out, "ctx", 1)
    place, v_pair = barrier((place, v_pair))
    mine, theirs = project(place, *sources[1:], (cosine, sine))
    mine, theirs, v_next, v_pair_other, out_across_next, out_passed, out_own_swap = barrier(
        (mine, theirs, v_next, v_pair_other, out_across_next, out_passed, out_own_swap)
    )
    out_passed_next = lax.ppermute(out_across_next, "ctx", outward)
    other = swapped(theirs, "ctx", 1)
    v_next_other = swapped(v_next, "ctx", 1)
    out_near_swap, out_across_swap = swapped(out_near, "ctx", 1), swapped(out_across, "ctx", 1)
    group_rows = lax.dynamic_slice_in_dim(head_mix, GROUP * (ctx // GROUP), GROUP, 0)
    mix = lax.dynamic_index_in_dim(group_rows, ctx % GROUP, 1, keepdims=False)
    out_mine, out_theirs = attend_head(
        place, mix, mine, other, tables, (v_pair, v_next, v_pair_other, v_next_other)
    )
    out_mine, out_theirs, out_passed_next, out_near_swap, out_across_swap = barrier(
        (out_mine, out_theirs, out_passed_next, out_near_swap, out_across_swap)
    )
    out_parts = [w_out, out_own_swap, out_near, out_near_swap, out_across, out_across_swap]
    for part in (out_passed, out_across_next, out_passed_next):
        out_parts += [part, swapped(part, "ctx", 1)]
    summed = out_mine.astype(jnp.float32) + swapped(out_theirs, "ctx", 1).astype(jnp.float32)
    own = lax.dynamic_index_in_dim(summed, z, 0, keepdims=False)
    r1, r2, r3 = [
        swapped(
            lax.dynamic_index_in_dim(summed, z ^ s, 0, keepdims=False).astype(jnp.bfloat16),
            "ctx",
            2 * s,
        )
        for s in (1, 2, 3)
    ]

    inner = (z == 1) | (z == 2)
    out_places = jnp.stack(
        [z, z ^ 1, jnp.where(inner, z ^ 3, z ^ 2), jnp.where(inner, z ^ 2, z ^ 3), inner]
    )
    where = jnp.concatenate([place[:5], out_places.astype(jnp.int32)])
    shares = finish(where, own, r1, r2, r3, out_gain.reshape(1, -1), out_parts)
    total = shares[0].astype(jnp.float32)
    for t in (1, 2, 3):
        total = total + swapped(shares[t], "head", t).astype(jnp.float32)
    return total.astype(jnp.bfloat16)


def solution(mesh):
    one_head_each = mesh.shape["ctx"] == 8 and mesh.shape["head"] == 4
    body = per_device_one_head if one_head_each else per_device
    return jax.shard_map(
        body,
        mesh=mesh,
        in_specs=(
            P("ctx", "head"),
            P("ctx"),
            P("ctx", "head"),
            P("ctx", "head"),
            P("ctx", "head"),
            P("head", None),
            P("head", None),
            P("head"),
            P("head", "ctx"),
        ),
        out_specs=P("ctx", "head"),
        check_vma=False,
    )
```

```python
import functools
import math

import jax
import jax.numpy as jnp
from jax import lax
from jax.experimental import pallas as pl
from jax.experimental.pallas import tpu as pltpu
from jax.sharding import PartitionSpec as P

HD = 128
GROUP = 4
CQ = 6
CK = 11
KB = 512


def passed_along(value, axis, steps):
    count = lax.axis_size(axis)
    leading, last = (max(0, -steps), min(count, count - steps))
    return lax.ppermute(value, axis, [(source, source + steps) for source in range(leading, last)])


def rope(projected, positions):
    row_count = projected.shape[0]
    head_count = projected.shape[1] // HD
    shaped = projected.reshape(row_count, head_count, HD)
    half_size = HD // 2
    exponents = jnp.arange(half_size, dtype=jnp.float32) * (2.0 / HD)
    inverse = jnp.exp(-exponents * math.log(500000.0))
    angle = (positions.astype(jnp.float32) * 0.25)[:, None, None] * inverse[None, None, :]
    cosine = jnp.cos(angle)
    sine = jnp.sin(angle)
    lower_half = shaped[..., :half_size]
    upper_half = shaped[..., half_size:]
    rotated_rows = jnp.concatenate(
        [lower_half * cosine - upper_half * sine, upper_half * cosine + lower_half * sine], -1
    )
    return rotated_rows.reshape(row_count, head_count * HD)


def convolve(masked, kernel, row_count, col_count):
    summed = jnp.zeros((masked.shape[0], row_count, col_count), jnp.float32)
    for lag_q in range(CQ):
        for lag_k in range(CK):
            weight = kernel[:, lag_q * CK + lag_k][:, None, None]
            window = masked[
                :,
                CQ - 1 - lag_q : CQ - 1 - lag_q + row_count,
                CK - 1 - lag_k : CK - 1 - lag_k + col_count,
            ]
            summed = summed + weight * window
    return summed


def add_rows(left, piece):
    return jnp.dot(left, piece, preferred_element_type=jnp.float32)


def share_keys(key, value):
    return (
        lax.all_gather(key, "ctx", axis=0, tiled=True),
        lax.all_gather(value, "ctx", axis=0, tiled=True),
    )


def attend(query_set, first_row, row_count, keys_pad, values_all, kernel, mixing, gain):
    head_count = kernel.shape[0]
    ext_rows = row_count + CQ - 1
    query_heads = query_set.reshape(ext_rows, head_count, HD)
    token_total = values_all.shape[0]
    block_count = token_total // KB
    last_row = first_row + row_count - 1
    scale = 1.0 / math.sqrt(HD)
    prow = first_row - (CQ - 1) + jnp.arange(ext_rows, dtype=jnp.int32)
    irow = first_row + jnp.arange(row_count, dtype=jnp.int32)

    def logits_of(block):
        key_start = block * KB
        key_block = lax.dynamic_slice_in_dim(keys_pad, key_start, KB + CK - 1, 0).reshape(
            KB + CK - 1, head_count, HD
        )
        scores = (
            jnp.einsum("rhd,khd->hrk", query_heads, key_block, preferred_element_type=jnp.float32)
            * scale
        )
        kcol = key_start - CK // 2 + jnp.arange(KB + CK - 1, dtype=jnp.int32)
        valid = (kcol[None, :] <= prow[:, None]) & (prow[:, None] >= 0)
        masked = jnp.where(valid[None], scores, 0.0)
        conv = convolve(masked, kernel, row_count, KB)
        jcol = key_start + jnp.arange(KB, dtype=jnp.int32)
        return jnp.where((jcol[None, :] <= irow[:, None])[None], conv, -jnp.inf)

    def first_pass(block, carry_in):

        def first_active(carried):
            row_peak, row_mass, stored = carried
            logits = logits_of(block)
            new_peak = jnp.maximum(row_peak, jnp.max(logits, axis=-1))
            new_mass = row_mass * jnp.exp(row_peak - new_peak) + jnp.sum(
                jnp.exp(logits - new_peak[..., None]), axis=-1
            )
            stored = lax.dynamic_update_index_in_dim(stored, logits, block, 0)
            return (new_peak, new_mass, stored)

        return lax.cond(block * KB <= last_row, first_active, lambda carried: carried, carry_in)

    peak_start = jnp.full((head_count, row_count), -jnp.inf, jnp.float32)
    mass_start = jnp.zeros((head_count, row_count), jnp.float32)
    store_start = jnp.zeros((block_count, head_count, row_count, KB), jnp.float32)
    row_peak, row_mass, stored = lax.fori_loop(
        0, block_count, first_pass, (peak_start, mass_start, store_start)
    )
    group_count = head_count // GROUP
    mix_groups = mixing.reshape(group_count, GROUP, GROUP)

    def second_pass(block, carry_in):

        def second_active(summed):
            logits = lax.dynamic_index_in_dim(stored, block, 0, keepdims=False)
            probs = jnp.exp(logits - row_peak[..., None]) / row_mass[..., None]
            grouped = probs.reshape(group_count, GROUP, row_count, KB)
            mixed_scores = (
                jnp.einsum("gab,gbrk->gark", mix_groups, grouped)
                .reshape(head_count, row_count, KB)
                .astype(jnp.bfloat16)
            )
            value_block = lax.dynamic_slice_in_dim(values_all, block * KB, KB, 0).reshape(
                KB, head_count, HD
            )
            return summed + jnp.einsum(
                "hrk,khd->rhd", mixed_scores, value_block, preferred_element_type=jnp.float32
            )

        return lax.cond(block * KB <= last_row, second_active, lambda summed: summed, carry_in)

    summed = lax.fori_loop(
        0, block_count, second_pass, jnp.zeros((row_count, head_count, HD), jnp.float32)
    )
    rms = jnp.sqrt(jnp.mean(summed * summed, axis=-1, keepdims=True) + 1e-05)
    normed = (summed / rms * gain.reshape(head_count, HD)).astype(jnp.bfloat16)
    return normed.reshape(row_count, head_count * HD)


def per_device(
    activations, positions, w_query, w_key, w_value, conv_kernel, head_mix, out_gain, w_out
):
    row_count = activations.shape[0]
    ctx_place = lax.axis_index("ctx")
    features = lax.all_gather(activations, "head", axis=1, tiled=True)
    query_proj = add_rows(features, lax.all_gather(w_query, "ctx", axis=0, tiled=True))
    key_proj = add_rows(features, lax.all_gather(w_key, "ctx", axis=0, tiled=True))
    value_proj = add_rows(features, lax.all_gather(w_value, "ctx", axis=0, tiled=True))
    key = rope(key_proj, positions).astype(jnp.bfloat16)
    value = value_proj.astype(jnp.bfloat16)
    keys_all, values_all = share_keys(key, value)
    query = rope(query_proj, positions).astype(jnp.bfloat16)
    rim_rows = passed_along(query[row_count - (CQ - 1) :], "ctx", 1)
    query_ext = jnp.concatenate([rim_rows, query], 0)
    keys_pad = jnp.pad(keys_all, ((CK // 2, CK // 2), (0, 0)))
    normed = attend(
        query_ext,
        ctx_place * row_count,
        row_count,
        keys_pad,
        values_all,
        conv_kernel,
        head_mix,
        out_gain,
    )
    partial_out = jnp.dot(
        normed, lax.all_gather(w_out, "ctx", axis=1, tiled=True), preferred_element_type=jnp.float32
    )
    return lax.psum_scatter(
        partial_out.astype(jnp.bfloat16), "head", scatter_dimension=1, tiled=True
    )


ROWS = 256
BAND = 128
LANES = 128
SUB = 64
AHEAD = 16


def kernel_params(mebibytes):
    return pltpu.CompilerParams(vmem_limit_bytes=mebibytes * 1024 * 1024)


def whole(memory_space):
    return pl.BlockSpec(memory_space=memory_space)


def project_kernel(rows, first_col, place, *refs):
    a_own, (x0, x_rest, y0, y_rest, d_rest) = refs[:4], refs[4:9]
    w_same, w_swap = refs[9:11]
    abuf, wbuf, acc, sem_a, sem_w = refs[-5:]
    turn, core = place[0], place[1]
    half = w_same.shape[1]
    width = wbuf.shape[2]

    def copies_a(t):
        if t == 0:
            pairs = [(a_own[b], 0, b * rows, rows) for b in range(4)]
        elif t < 3:
            first, others = ((x0, x_rest), (y0, y_rest))[t - 1]
            pairs = [(first, 0, 0, rows), (others, 0, rows, 3 * rows)]
        else:
            late, mid = 3 * rows, rows // 2
            pairs = [(y_rest, late, 0, mid), (x_rest, late, mid, mid), (d_rest, 0, rows, 3 * rows)]
        return [
            pltpu.make_async_copy(
                ref.at[pl.ds(source, size)], abuf.at[t, pl.ds(target, size)], sem_a.at[t, n]
            )
            for n, (ref, source, target, size) in enumerate(pairs)
        ]

    def copies_w(t):
        out = []
        for n, (ref, side) in enumerate(((w_same, core), (w_swap, 1 - core))):
            source = ref.at[lax.bitwise_xor(turn, t), :, pl.ds(first_col, width)]
            target = wbuf.at[t, pl.ds(pl.multiple_of(side * half, half), half)]
            out.append(pltpu.make_async_copy(source, target, sem_w.at[t, n]))
        return out

    for t in range(4):
        for copy in copies_w(t) + copies_a(t):
            copy.start()
    for t in range(4):
        for copy in copies_w(t) + copies_a(t):
            copy.wait()
        part = jnp.dot(abuf[t], wbuf[t], preferred_element_type=jnp.float32)
        acc[...] = part if t == 0 else acc[...] + part
    if first_col:
        v_out = refs[11]
        for b in range(4):
            v_out[place[5 + b]] = acc[b * rows : (b + 1) * rows].astype(jnp.bfloat16)
        return
    cos_ref, sin_ref, mine, theirs = refs[11:15]
    first = core == 0
    for b in range(4):
        total = acc[b * rows : (b + 1) * rows]
        cosine, sine = cos_ref[b], sin_ref[b]
        at = place[5 + b]
        for col, out in ((0, 0), (2 * HD, HD)):
            heads = []
            for start in (col, col + HD):
                x = total[:, start : start + HD]
                x = x * cosine + pltpu.roll(x, HD // 2, 1) * sine
                heads.append(x.astype(jnp.bfloat16))
            mine[at, :, out : out + HD] = jnp.where(first, heads[0], heads[1])
            theirs[at, :, out : out + HD] = jnp.where(first, heads[1], heads[0])


def project(place, a_own, a_plane, w_same, w_swap, angles=()):
    rows, depth = a_own[0].shape
    first_col, width = (0, 4 * HD) if angles else (4 * HD, 2 * HD)
    out = jax.ShapeDtypeStruct((4, rows, 2 * HD), jnp.bfloat16)
    count = 2 if angles else 1
    return pl.pallas_call(
        functools.partial(project_kernel, rows, first_col),
        out_shape=[out] * count,
        in_specs=[whole(pltpu.SMEM)]
        + [whole(pl.ANY)] * 11
        + [whole(pltpu.VMEM)] * len(angles),
        out_specs=[whole(pltpu.VMEM)] * count,
        scratch_shapes=[
            pltpu.VMEM((4, 4 * rows, depth), jnp.bfloat16),
            pltpu.VMEM((4, depth, width), jnp.bfloat16),
            pltpu.VMEM((4 * rows, width), jnp.float32),
            pltpu.SemaphoreType.DMA((4, 4)),
            pltpu.SemaphoreType.DMA((4, 2)),
        ],
        compiler_params=kernel_params(56),
        cost_estimate=pl.CostEstimate(
            flops=8 * rows * 4 * depth * width, bytes_accessed=16 * 2**20, transcendentals=0
        ),
    )(place, *a_own, *a_plane, w_same, w_swap, *angles)


def prepare(core, mine, other, key_ref, even_ref, odd_ref, q_out, k_out, corr, *scratch):
    qf, kf, lags, turned = scratch
    total = q_out.shape[0]
    qf[0:8] = jnp.zeros((8, HD), jnp.float32)
    kf[0:AHEAD] = jnp.zeros((AHEAD, HD), jnp.float32)
    kf[AHEAD + total :] = jnp.zeros((kf.shape[0] - AHEAD - total, HD), jnp.float32)
    corr[...] = jnp.zeros(corr.shape, jnp.float32)
    for i in range(total // (2 * ROWS)):
        for ref, parity in ((mine, core), (other, 1 - core)):
            start = pl.multiple_of((2 * i + parity) * ROWS, ROWS)
            block = ref[i].astype(jnp.float32)
            qf[pl.ds(8 + start, ROWS)] = block[:, :HD]
            kf[pl.ds(AHEAD + start, ROWS)] = block[:, HD:]

    ahead = lax.broadcasted_iota(jnp.int32, (SUB + 8, LANES), 1) - lax.broadcasted_iota(
        jnp.int32, (SUB + 8, LANES), 0
    )
    near = (ahead >= 1) & (ahead < CQ + CK // 2)
    steps = total // LANES
    for w in range(steps):
        base = w * LANES
        window = kf[base : base + 2 * LANES].T
        turned[base : base + LANES] = window.astype(jnp.bfloat16)
        for odd in range(2):
            at = base + odd * SUB
            qwin = qf[at : at + SUB + 8]
            kwin = kf[at + AHEAD - 8 : at + AHEAD - 8 + LANES]
            scores = lax.dot_general(
                qwin.astype(jnp.bfloat16),
                kwin.astype(jnp.bfloat16),
                (((1,), (1,)), ((), ())),
                preferred_element_type=jnp.float32,
            )
            future = jnp.where(near, scores, 0.0)
            for a in range(CQ):
                cols = slice(a * LANES, (a + 1) * LANES)
                lags[odd, w * SUB : (w + 1) * SUB, cols] = future[8 - a : 8 - a + SUB].astype(
                    jnp.bfloat16
                )
                q_out[at : at + SUB, cols] = qwin[8 - a : 8 - a + SUB].astype(jnp.bfloat16)
    for w in range(0, steps, 4):
        wide = jnp.dot(
            turned[w * LANES : (w + 4) * LANES], key_ref[...], preferred_element_type=jnp.float32
        )
        for n in range(4):
            cols = slice((w + n) * LANES, (w + n + 1) * LANES)
            for a in range(CQ):
                k_out[a * HD : (a + 1) * HD, cols] = wide[
                    n * LANES : (n + 1) * LANES, a * LANES : (a + 1) * LANES
                ].astype(jnp.bfloat16)
    for odd, taps in enumerate((even_ref, odd_ref)):
        for w in range(0, steps, 8):
            fix = jnp.dot(
                lags[odd, w * SUB : (w + 8) * SUB], taps[...], preferred_element_type=jnp.float32
            )
            for n in range(8):
                m = 2 * ((w + n) % 2) + odd
                col = LANES * ((m + 1) // 2)
                corr[(w + n) // 2, m * SUB : (m + 1) * SUB, col : col + taps.shape[1]] = fix[
                    n * SUB : (n + 1) * SUB
                ]


def fill_tables(weights, key_ref, even_ref, odd_ref):
    def fill(ref, origin, swap):
        height = ref.shape[0] if swap else ref.shape[0] // CQ
        width = ref.shape[1] // CQ if swap else ref.shape[1]
        shape = (height, width)
        tap = lax.broadcasted_iota(jnp.int32, shape, 1) - lax.broadcasted_iota(jnp.int32, shape, 0)
        for a in range(CQ):
            value = jnp.zeros(shape, jnp.float32)
            for c in range(CK):
                value = jnp.where(tap == c - origin, weights[a * CK + c], value)
            value = value.astype(jnp.bfloat16)
            if swap:
                ref[:, a * width : (a + 1) * width] = value
            else:
                ref[a * height : (a + 1) * height, :] = value

    fill(key_ref, CK // 2 + AHEAD, True)
    fill(even_ref, CK // 2 + 8 - BAND, False)
    fill(odd_ref, CK // 2 + 8 - SUB, False)


def attend_kernel(place, mix, weights, *refs):
    qk_refs, (va, vb, vc, vd), (mine, theirs) = refs[:2], refs[2:6], refs[6:8]
    v_all, q_wide, k_ref, corr = refs[8:12]
    tables, sem_v = refs[16:19], refs[19]
    side, core = place[2], place[1]
    b = pl.program_id(0)
    count = k_ref.shape[1] // (2 * ROWS)

    @pl.when(b == 0)
    def _():
        def copies_v():
            out = []
            for n, ref in enumerate((va, vb, vc, vd)):
                parity = core if n < 2 else 1 - core
                start = pl.multiple_of((side if n % 2 == 0 else 1 - side) * 2 * HD, 2 * HD)
                for i in range(count):
                    rows = pl.ds(pl.multiple_of((2 * i + parity) * ROWS, ROWS), ROWS)
                    target = v_all.at[rows, pl.ds(start, 2 * HD)]
                    out.append(pltpu.make_async_copy(ref.at[i], target, sem_v.at[n, i]))
            return out

        for copy in copies_v():
            copy.start()
        fill_tables(weights, *tables)
        prepare(core, *qk_refs, *tables, q_wide, k_ref, corr, *refs[12:16])
        for copy in copies_v():
            copy.wait()

    row = lax.broadcasted_iota(jnp.int32, (ROWS, ROWS), 0)
    col = lax.broadcasted_iota(jnp.int32, (ROWS, ROWS), 1)
    seen = col <= row
    top, low = slice(0, ROWS), slice(ROWS, 2 * ROWS)

    def fixed(part, n):
        return jnp.concatenate([part[:, :BAND], part[:, BAND:] - corr[n, :, :BAND]], 1)

    def rows_of(upper, lower):
        return jnp.concatenate([upper, lower], 0)

    def block(step):
        q_rows = q_wide[2 * step * ROWS : (2 * step + 2) * ROWS]
        parts = []
        for j in range(2 * step + 1):
            part = jnp.dot(
                q_rows,
                k_ref[:, j * ROWS : (j + 1) * ROWS],
                preferred_element_type=jnp.float32,
            )
            if j == 2 * step:
                diagonal = jnp.where(seen, part[top] - corr[2 * step, :, BAND:], -jnp.inf)
                part = rows_of(diagonal, fixed(part[low], 2 * step + 1))
            elif j == 2 * step - 1:
                part = rows_of(fixed(part[top], 2 * step), part[low])
            parts.append(part)
        start = (2 * step + 1) * ROWS
        last = jnp.dot(
            q_rows[low], k_ref[:, start : start + ROWS], preferred_element_type=jnp.float32
        )
        last = jnp.where(seen, last - corr[2 * step + 1, :, BAND:], -jnp.inf)
        peak = parts[0]
        for part in parts[1:]:
            peak = jnp.maximum(peak, part)
        peak = rows_of(peak[top], jnp.maximum(peak[low], last))
        peak = jnp.max(peak, axis=1, keepdims=True)
        mass = jnp.zeros((2 * ROWS, ROWS), jnp.float32)
        probs = []
        for part in parts:
            part = jnp.exp2(part - peak)
            mass = mass + part
            probs.append(part.astype(jnp.bfloat16))
        last = jnp.exp2(last - peak[low])
        mass = rows_of(mass[top], mass[low] + last)
        summed = jnp.dot(
            jnp.concatenate(probs, 1), v_all[:start], preferred_element_type=jnp.float32
        )
        extra = jnp.dot(
            last.astype(jnp.bfloat16),
            v_all[start : start + ROWS],
            preferred_element_type=jnp.float32,
        )
        inverse = 1.0 / jnp.sum(mass, axis=1, keepdims=True)
        halves = []
        for rows, total in ((top, summed[top]), (low, summed[low] + extra)):
            halves.append(
                jnp.concatenate(
                    [
                        total[:, g * HD : (g + 1) * HD] * (inverse[rows] * mix[g])
                        for g in range(GROUP)
                    ],
                    1,
                ).astype(jnp.bfloat16)
            )
        mine[0] = jnp.where(core == 0, halves[0], halves[1])
        theirs[0] = jnp.where(core == 0, halves[1], halves[0])

    for step in range(count):
        pl.when(b == step)(lambda step=step: block(step))


def attend_head(place, mix, weights, mine, other, values):
    total = 2 * mine.shape[0] * ROWS
    count = total // (2 * ROWS)
    depth = CQ * HD
    out = jax.ShapeDtypeStruct((count, ROWS, GROUP * HD), jnp.bfloat16)
    out_spec = pl.BlockSpec((1, ROWS, GROUP * HD), lambda b: (b, 0, 0))
    return pl.pallas_call(
        attend_kernel,
        grid=(count,),
        out_shape=(out, out),
        in_specs=[whole(pltpu.SMEM)] * 3 + [whole(pltpu.VMEM)] * 2 + [whole(pl.ANY)] * 4,
        out_specs=[out_spec, out_spec],
        scratch_shapes=[
            pltpu.VMEM((total, GROUP * HD), jnp.bfloat16),
            pltpu.VMEM((total, depth), jnp.bfloat16),
            pltpu.VMEM((depth, total), jnp.bfloat16),
            pltpu.VMEM((total // ROWS, ROWS, BAND + ROWS), jnp.float32),
            pltpu.VMEM((8 + total, HD), jnp.float32),
            pltpu.VMEM((AHEAD + total + LANES, HD), jnp.float32),
            pltpu.VMEM((2, total // 2, CQ * LANES), jnp.bfloat16),
            pltpu.VMEM((total, 2 * LANES), jnp.bfloat16),
        ]
        + [
            pltpu.VMEM(shape, jnp.bfloat16)
            for shape in ((2 * LANES, depth), (CQ * LANES, 2 * LANES), (CQ * LANES, LANES))
        ]
        + [pltpu.SemaphoreType.DMA((4, count))],
        compiler_params=kernel_params(56),
        cost_estimate=pl.CostEstimate(
            flops=total * total * (depth + GROUP * HD),
            bytes_accessed=16 * 2**20,
            transcendentals=total * total // 2,
        ),
    )(place, mix, weights, mine, other, *values)


def finish_kernel(place, own, r1, r2, r3, gain, *refs):
    w_parts, outs = refs[:12], refs[12:16]
    normed, w_buf, sem = refs[16:]
    width = w_parts[0].shape[1]
    core, head, inner = place[1], place[0], place[9]

    def copy_w(n, source):
        side = core if n % 2 == 0 else 1 - core
        cols = pl.ds(pl.multiple_of(side * width, width), width)
        target = w_buf.at[lax.bitwise_xor(place[5 + n // 2], head), :, cols]
        return pltpu.make_async_copy(w_parts[source], target, sem.at[n])

    for n in range(4):
        copy_w(n, n).start()
    for n in range(4, 8):
        straight = n if n < 6 else n + 2

        @pl.when(inner == 1)
        def _():
            copy_w(n, straight).start()

        @pl.when(inner == 0)
        def _():
            copy_w(n, straight + 2).start()

    near = own[...] + r1[...].astype(jnp.float32)
    far = r2[...].astype(jnp.float32) + r3[...].astype(jnp.float32)
    low = place[3] == 0
    for g in range(2 * GROUP):
        cols = slice((g % GROUP) * HD, (g % GROUP + 1) * HD)
        first = low if g < GROUP else jnp.logical_not(low)
        x = jnp.where(first, near[:, cols], far[:, cols])
        scale = lax.rsqrt(jnp.mean(x * x, axis=1, keepdims=True) + 1e-05)
        normed[:, g * HD : (g + 1) * HD] = (
            x * scale * gain[:, g * HD : (g + 1) * HD]
        ).astype(jnp.bfloat16)
    for n in range(8):
        copy_w(n, n).wait()
    for t in (3, 2, 1, 0):
        outs[t][...] = jnp.dot(
            normed[...], w_buf[t], preferred_element_type=jnp.float32
        ).astype(jnp.bfloat16)


def finish(place, own, r1, r2, r3, gain, w_parts):
    rows = own.shape[0]
    depth, width = w_parts[0].shape
    return pl.pallas_call(
        finish_kernel,
        in_specs=[whole(pltpu.SMEM)] + [whole(pltpu.VMEM)] * 5 + [whole(pl.ANY)] * 12,
        out_specs=[whole(pltpu.VMEM)] * 4,
        out_shape=[jax.ShapeDtypeStruct((rows, 2 * width), jnp.bfloat16)] * 4,
        scratch_shapes=[
            pltpu.VMEM((rows, depth), jnp.bfloat16),
            pltpu.VMEM((4, depth, 2 * width), jnp.bfloat16),
            pltpu.SemaphoreType.DMA((8,)),
        ],
        compiler_params=kernel_params(56),
        cost_estimate=pl.CostEstimate(
            flops=2 * rows * depth * 8 * width, bytes_accessed=11 * 2**20, transcendentals=0
        ),
    )(place, own, r1, r2, r3, gain, *w_parts)


def swapped(value, axis, mask):
    count = lax.axis_size(axis)
    return lax.ppermute(value, axis, [(i, i ^ mask) for i in range(count)])


def per_device_one_head(
    activations, positions, w_query, w_key, w_value, conv_kernel, head_mix, out_gain, w_out
):
    ctx, head = lax.axis_index("ctx"), lax.axis_index("head")
    z, core = ctx // 2, ctx % 2
    rows = activations.shape[0]
    half = rows // 2
    barrier = lax.optimization_barrier
    pair = 2 * HD

    def columns(target):
        parts = [
            lax.dynamic_slice_in_dim(w, target * pair, pair, 1) for w in (w_query, w_key, w_value)
        ]
        return jnp.concatenate(parts, 1)

    digits = jnp.stack([positions // 256, positions % 256]).astype(jnp.bfloat16)
    digits = jnp.pad(digits, ((0, 14), (0, activations.shape[1] - rows)))
    block = jnp.concatenate([activations, digits])
    w_pieces = jnp.stack([columns(target) for target in range(4)])
    far = [swapped(block, "ctx", 2 * s) for s in (1, 2, 3)]
    x0, y0 = swapped(activations, "head", 1), swapped(activations, "head", 2)
    weights = lax.dynamic_index_in_dim(conv_kernel, ctx, 0, keepdims=False)
    weights = weights * (math.log2(math.e) / math.sqrt(HD))
    place = jnp.stack([head, core, z % 2, z // 2, head, z, z ^ 1, z ^ 2, z ^ 3])
    place = place.astype(jnp.int32)
    far, x0, y0, w_pieces, weights, place, w_out = barrier(
        (far, x0, y0, w_pieces, weights, place, w_out)
    )

    same_core = [[i for i in range(8) if i % 2 == k] for k in range(2)]
    w_same = lax.all_to_all(w_pieces, "ctx", 0, 0, axis_index_groups=same_core)
    inner = [a[:rows] for a in far]
    x_rest = swapped(jnp.concatenate(inner + [y0[half:]]), "head", 1)
    y_rest = swapped(jnp.concatenate(inner + [x0[:half]]), "head", 2)
    d_rest = swapped(jnp.concatenate(inner), "head", 3)
    place_of = jnp.stack(
        [
            a[rows, :rows].astype(jnp.float32) * 256.0 + a[rows + 1, :rows].astype(jnp.float32)
            for a in [block] + far
        ]
    )
    exponents = jnp.arange(HD // 2, dtype=jnp.float32) * (2.0 / HD)
    inverse = jnp.exp(-exponents * math.log(500000.0))
    angle = (place_of * 0.25)[:, :, None] * inverse
    cosine, sine = jnp.cos(angle), jnp.sin(angle)
    cosine = jnp.concatenate([cosine, cosine], -1)
    sine = jnp.concatenate([-sine, sine], -1)
    w_same, x_rest, y_rest, d_rest, cosine, sine, w_out = barrier(
        (w_same, x_rest, y_rest, d_rest, cosine, sine, w_out)
    )
    w_swap = swapped(w_same, "ctx", 1)
    middle = [(2, 4), (3, 5), (4, 2), (5, 3)]
    outward = [(2, 0), (3, 1), (4, 6), (5, 7)]
    out_near = swapped(w_out, "ctx", 2)
    out_across = lax.ppermute(w_out, "ctx", middle)
    sources = place, [activations] + list(far), (x0, x_rest, y0, y_rest, d_rest), w_same, w_swap
    (v_pair,) = project(*sources)
    place, v_pair, out_near, out_across = barrier((place, v_pair, out_near, out_across))
    v_next = swapped(v_pair, "ctx", 2)
    v_pair_other = swapped(v_pair, "ctx", 1)
    out_across_next = lax.ppermute(out_near, "ctx", middle)
    out_passed = lax.ppermute(out_across, "ctx", outward)
    mine, theirs = project(place, *sources[1:], (cosine, sine))
    mine, theirs, v_next, v_pair_other = barrier((mine, theirs, v_next, v_pair_other))
    other = swapped(theirs, "ctx", 1)
    v_next_other = swapped(v_next, "ctx", 1)
    out_own_swap = swapped(w_out, "ctx", 1)
    other, v_next_other, out_across_next, out_own_swap = barrier(
        (other, v_next_other, out_across_next, out_own_swap)
    )
    out_passed_next = lax.ppermute(out_across_next, "ctx", outward)
    out_near_swap, out_across_swap = swapped(out_near, "ctx", 1), swapped(out_across, "ctx", 1)
    group_rows = lax.dynamic_slice_in_dim(head_mix, GROUP * (ctx // GROUP), GROUP, 0)
    mix = lax.dynamic_index_in_dim(group_rows, ctx % GROUP, 1, keepdims=False)
    out_mine, out_theirs = attend_head(
        place, mix, weights, mine, other, (v_pair, v_next, v_pair_other, v_next_other)
    )
    out_mine, out_theirs, out_passed, out_passed_next, out_near_swap, out_across_swap = barrier(
        (out_mine, out_theirs, out_passed, out_passed_next, out_near_swap, out_across_swap)
    )
    out_parts = [w_out, out_own_swap, out_near, out_near_swap, out_across, out_across_swap]
    for part in (out_passed, out_across_next, out_passed_next):
        out_parts += [part, swapped(part, "ctx", 1)]
    summed = out_mine.astype(jnp.float32) + swapped(out_theirs, "ctx", 1).astype(jnp.float32)
    own = lax.dynamic_index_in_dim(summed, z, 0, keepdims=False)
    r1, r2, r3 = [
        swapped(
            lax.dynamic_index_in_dim(summed, z ^ s, 0, keepdims=False).astype(jnp.bfloat16),
            "ctx",
            2 * s,
        )
        for s in (1, 2, 3)
    ]

    inner = (z == 1) | (z == 2)
    out_places = jnp.stack(
        [z, z ^ 1, jnp.where(inner, z ^ 3, z ^ 2), jnp.where(inner, z ^ 2, z ^ 3), inner]
    )
    where = jnp.concatenate([place[:5], out_places.astype(jnp.int32)])
    shares = finish(where, own, r1, r2, r3, out_gain.reshape(1, -1), out_parts)
    total = shares[0].astype(jnp.float32)
    for t in (1, 2, 3):
        total = total + swapped(shares[t], "head", t).astype(jnp.float32)
    return total.astype(jnp.bfloat16)


def solution(mesh):
    one_head_each = mesh.shape["ctx"] == 8 and mesh.shape["head"] == 4
    body = per_device_one_head if one_head_each else per_device
    return jax.shard_map(
        body,
        mesh=mesh,
        in_specs=(
            P("ctx", "head"),
            P("ctx"),
            P("ctx", "head"),
            P("ctx", "head"),
            P("ctx", "head"),
            P("head", None),
            P("head", None),
            P("head"),
            P("head", "ctx"),
        ),
        out_specs=P("ctx", "head"),
        check_vma=False,
    )
```

```python
import functools
import math

import jax
import jax.numpy as jnp
from jax import lax
from jax.experimental import pallas as pl
from jax.experimental.pallas import tpu as pltpu
from jax.sharding import PartitionSpec as P

HD = 128
GROUP = 4
CQ = 6
CK = 11
KB = 512


def passed_along(value, axis, steps):
    count = lax.axis_size(axis)
    leading, last = (max(0, -steps), min(count, count - steps))
    return lax.ppermute(value, axis, [(source, source + steps) for source in range(leading, last)])


def rope(projected, positions):
    row_count = projected.shape[0]
    head_count = projected.shape[1] // HD
    shaped = projected.reshape(row_count, head_count, HD)
    half_size = HD // 2
    exponents = jnp.arange(half_size, dtype=jnp.float32) * (2.0 / HD)
    inverse = jnp.exp(-exponents * math.log(500000.0))
    angle = (positions.astype(jnp.float32) * 0.25)[:, None, None] * inverse[None, None, :]
    cosine = jnp.cos(angle)
    sine = jnp.sin(angle)
    lower_half = shaped[..., :half_size]
    upper_half = shaped[..., half_size:]
    rotated_rows = jnp.concatenate(
        [lower_half * cosine - upper_half * sine, upper_half * cosine + lower_half * sine], -1
    )
    return rotated_rows.reshape(row_count, head_count * HD)


def convolve(masked, kernel, row_count, col_count):
    summed = jnp.zeros((masked.shape[0], row_count, col_count), jnp.float32)
    for lag_q in range(CQ):
        for lag_k in range(CK):
            weight = kernel[:, lag_q * CK + lag_k][:, None, None]
            window = masked[
                :,
                CQ - 1 - lag_q : CQ - 1 - lag_q + row_count,
                CK - 1 - lag_k : CK - 1 - lag_k + col_count,
            ]
            summed = summed + weight * window
    return summed


def add_rows(left, piece):
    return jnp.dot(left, piece, preferred_element_type=jnp.float32)


def share_keys(key, value):
    return (
        lax.all_gather(key, "ctx", axis=0, tiled=True),
        lax.all_gather(value, "ctx", axis=0, tiled=True),
    )


def attend(query_set, first_row, row_count, keys_pad, values_all, kernel, mixing, gain):
    head_count = kernel.shape[0]
    ext_rows = row_count + CQ - 1
    query_heads = query_set.reshape(ext_rows, head_count, HD)
    token_total = values_all.shape[0]
    block_count = token_total // KB
    last_row = first_row + row_count - 1
    scale = 1.0 / math.sqrt(HD)
    prow = first_row - (CQ - 1) + jnp.arange(ext_rows, dtype=jnp.int32)
    irow = first_row + jnp.arange(row_count, dtype=jnp.int32)

    def logits_of(block):
        key_start = block * KB
        key_block = lax.dynamic_slice_in_dim(keys_pad, key_start, KB + CK - 1, 0).reshape(
            KB + CK - 1, head_count, HD
        )
        scores = (
            jnp.einsum("rhd,khd->hrk", query_heads, key_block, preferred_element_type=jnp.float32)
            * scale
        )
        kcol = key_start - CK // 2 + jnp.arange(KB + CK - 1, dtype=jnp.int32)
        valid = (kcol[None, :] <= prow[:, None]) & (prow[:, None] >= 0)
        masked = jnp.where(valid[None], scores, 0.0)
        conv = convolve(masked, kernel, row_count, KB)
        jcol = key_start + jnp.arange(KB, dtype=jnp.int32)
        return jnp.where((jcol[None, :] <= irow[:, None])[None], conv, -jnp.inf)

    def first_pass(block, carry_in):

        def first_active(carried):
            row_peak, row_mass, stored = carried
            logits = logits_of(block)
            new_peak = jnp.maximum(row_peak, jnp.max(logits, axis=-1))
            new_mass = row_mass * jnp.exp(row_peak - new_peak) + jnp.sum(
                jnp.exp(logits - new_peak[..., None]), axis=-1
            )
            stored = lax.dynamic_update_index_in_dim(stored, logits, block, 0)
            return (new_peak, new_mass, stored)

        return lax.cond(block * KB <= last_row, first_active, lambda carried: carried, carry_in)

    peak_start = jnp.full((head_count, row_count), -jnp.inf, jnp.float32)
    mass_start = jnp.zeros((head_count, row_count), jnp.float32)
    store_start = jnp.zeros((block_count, head_count, row_count, KB), jnp.float32)
    row_peak, row_mass, stored = lax.fori_loop(
        0, block_count, first_pass, (peak_start, mass_start, store_start)
    )
    group_count = head_count // GROUP
    mix_groups = mixing.reshape(group_count, GROUP, GROUP)

    def second_pass(block, carry_in):

        def second_active(summed):
            logits = lax.dynamic_index_in_dim(stored, block, 0, keepdims=False)
            probs = jnp.exp(logits - row_peak[..., None]) / row_mass[..., None]
            grouped = probs.reshape(group_count, GROUP, row_count, KB)
            mixed_scores = (
                jnp.einsum("gab,gbrk->gark", mix_groups, grouped)
                .reshape(head_count, row_count, KB)
                .astype(jnp.bfloat16)
            )
            value_block = lax.dynamic_slice_in_dim(values_all, block * KB, KB, 0).reshape(
                KB, head_count, HD
            )
            return summed + jnp.einsum(
                "hrk,khd->rhd", mixed_scores, value_block, preferred_element_type=jnp.float32
            )

        return lax.cond(block * KB <= last_row, second_active, lambda summed: summed, carry_in)

    summed = lax.fori_loop(
        0, block_count, second_pass, jnp.zeros((row_count, head_count, HD), jnp.float32)
    )
    rms = jnp.sqrt(jnp.mean(summed * summed, axis=-1, keepdims=True) + 1e-05)
    normed = (summed / rms * gain.reshape(head_count, HD)).astype(jnp.bfloat16)
    return normed.reshape(row_count, head_count * HD)


def per_device(
    activations, positions, w_query, w_key, w_value, conv_kernel, head_mix, out_gain, w_out
):
    row_count = activations.shape[0]
    ctx_place = lax.axis_index("ctx")
    features = lax.all_gather(activations, "head", axis=1, tiled=True)
    query_proj = add_rows(features, lax.all_gather(w_query, "ctx", axis=0, tiled=True))
    key_proj = add_rows(features, lax.all_gather(w_key, "ctx", axis=0, tiled=True))
    value_proj = add_rows(features, lax.all_gather(w_value, "ctx", axis=0, tiled=True))
    key = rope(key_proj, positions).astype(jnp.bfloat16)
    value = value_proj.astype(jnp.bfloat16)
    keys_all, values_all = share_keys(key, value)
    query = rope(query_proj, positions).astype(jnp.bfloat16)
    rim_rows = passed_along(query[row_count - (CQ - 1) :], "ctx", 1)
    query_ext = jnp.concatenate([rim_rows, query], 0)
    keys_pad = jnp.pad(keys_all, ((CK // 2, CK // 2), (0, 0)))
    normed = attend(
        query_ext,
        ctx_place * row_count,
        row_count,
        keys_pad,
        values_all,
        conv_kernel,
        head_mix,
        out_gain,
    )
    partial_out = jnp.dot(
        normed, lax.all_gather(w_out, "ctx", axis=1, tiled=True), preferred_element_type=jnp.float32
    )
    return lax.psum_scatter(
        partial_out.astype(jnp.bfloat16), "head", scatter_dimension=1, tiled=True
    )


ROWS = 256
BAND = 128
LANES = 128
SUB = 64
AHEAD = 16


def kernel_params(mebibytes):
    return pltpu.CompilerParams(vmem_limit_bytes=mebibytes * 1024 * 1024)


def whole(memory_space):
    return pl.BlockSpec(memory_space=memory_space)


def project_kernel(rows, first_col, place, *refs):
    a_own, (x0, x_rest, y0, y_rest, c_low, c_high) = refs[:4], refs[4:10]
    w_same, w_swap = refs[10:12]
    abuf, wbuf, acc, sem_a, sem_w = refs[-5:]
    turn, core = place[0], place[1]
    half = w_same.shape[1]
    width = wbuf.shape[2]

    def copies_a(t):
        if t == 0:
            pairs = [(a_own[b], 0, b * rows, rows) for b in range(4)]
        elif t < 3:
            first, others = ((x0, x_rest), (y0, y_rest))[t - 1]
            pairs = [(first, 0, 0, rows), (others, 0, rows, 3 * rows)]
        else:
            late, mid = 3 * rows, rows // 2
            pairs = [(y_rest, late, 0, mid), (x_rest, late, mid, mid)]
            pairs += [(c_low, 0, rows, 3 * mid), (c_high, 0, rows + 3 * mid, 3 * mid)]
        return [
            pltpu.make_async_copy(
                ref.at[pl.ds(source, size)], abuf.at[t, pl.ds(target, size)], sem_a.at[t, n]
            )
            for n, (ref, source, target, size) in enumerate(pairs)
        ]

    def copies_w(t):
        out = []
        for n, (ref, side) in enumerate(((w_same, core), (w_swap, 1 - core))):
            source = ref.at[lax.bitwise_xor(turn, t), :, pl.ds(first_col, width)]
            target = wbuf.at[t, pl.ds(pl.multiple_of(side * half, half), half)]
            out.append(pltpu.make_async_copy(source, target, sem_w.at[t, n]))
        return out

    for t in range(4):
        for copy in copies_w(t) + copies_a(t):
            copy.start()
    for t in range(4):
        for copy in copies_w(t) + copies_a(t):
            copy.wait()
        part = jnp.dot(abuf[t], wbuf[t], preferred_element_type=jnp.float32)
        acc[...] = part if t == 0 else acc[...] + part
    if first_col:
        v_out = refs[12]
        for b in range(4):
            v_out[place[5 + b]] = acc[b * rows : (b + 1) * rows].astype(jnp.bfloat16)
        return
    cos_ref, sin_ref, mine, theirs = refs[12:16]
    first = core == 0
    for b in range(4):
        total = acc[b * rows : (b + 1) * rows]
        cosine, sine = cos_ref[b], sin_ref[b]
        at = place[5 + b]
        for col, out in ((0, 0), (2 * HD, HD)):
            heads = []
            for start in (col, col + HD):
                x = total[:, start : start + HD]
                x = x * cosine + pltpu.roll(x, HD // 2, 1) * sine
                heads.append(x.astype(jnp.bfloat16))
            mine[at, :, out : out + HD] = jnp.where(first, heads[0], heads[1])
            theirs[at, :, out : out + HD] = jnp.where(first, heads[1], heads[0])


def project(place, a_own, a_plane, w_same, w_swap, angles=()):
    rows, depth = a_own[0].shape
    first_col, width = (0, 4 * HD) if angles else (4 * HD, 2 * HD)
    out = jax.ShapeDtypeStruct((4, rows, 2 * HD), jnp.bfloat16)
    count = 2 if angles else 1
    return pl.pallas_call(
        functools.partial(project_kernel, rows, first_col),
        out_shape=[out] * count,
        in_specs=[whole(pltpu.SMEM)]
        + [whole(pl.ANY)] * 12
        + [whole(pltpu.VMEM)] * len(angles),
        out_specs=[whole(pltpu.VMEM)] * count,
        scratch_shapes=[
            pltpu.VMEM((4, 4 * rows, depth), jnp.bfloat16),
            pltpu.VMEM((4, depth, width), jnp.bfloat16),
            pltpu.VMEM((4 * rows, width), jnp.float32),
            pltpu.SemaphoreType.DMA((4, 4)),
            pltpu.SemaphoreType.DMA((4, 2)),
        ],
        compiler_params=kernel_params(56),
        cost_estimate=pl.CostEstimate(
            flops=8 * rows * 4 * depth * width, bytes_accessed=16 * 2**20, transcendentals=0
        ),
    )(place, *a_own, *a_plane, w_same, w_swap, *angles)


def prepare(core, mine, other, key_ref, even_ref, odd_ref, q_out, k_out, corr, *scratch):
    qf, kf, lags, turned = scratch
    total = q_out.shape[0]
    qf[0:8] = jnp.zeros((8, HD), jnp.float32)
    kf[0:AHEAD] = jnp.zeros((AHEAD, HD), jnp.float32)
    kf[AHEAD + total :] = jnp.zeros((kf.shape[0] - AHEAD - total, HD), jnp.float32)
    corr[...] = jnp.zeros(corr.shape, jnp.float32)
    for i in range(total // (2 * ROWS)):
        for ref, parity in ((mine, core), (other, 1 - core)):
            start = pl.multiple_of((2 * i + parity) * ROWS, ROWS)
            block = ref[i].astype(jnp.float32)
            qf[pl.ds(8 + start, ROWS)] = block[:, :HD]
            kf[pl.ds(AHEAD + start, ROWS)] = block[:, HD:]

    ahead = lax.broadcasted_iota(jnp.int32, (SUB + 8, LANES), 1) - lax.broadcasted_iota(
        jnp.int32, (SUB + 8, LANES), 0
    )
    near = (ahead >= 1) & (ahead < CQ + CK // 2)
    steps = total // LANES
    for w in range(steps):
        base = w * LANES
        window = kf[base : base + 2 * LANES].T
        turned[base : base + LANES] = window.astype(jnp.bfloat16)
        for odd in range(2):
            at = base + odd * SUB
            qwin = qf[at : at + SUB + 8]
            kwin = kf[at + AHEAD - 8 : at + AHEAD - 8 + LANES]
            scores = lax.dot_general(
                qwin.astype(jnp.bfloat16),
                kwin.astype(jnp.bfloat16),
                (((1,), (1,)), ((), ())),
                preferred_element_type=jnp.float32,
            )
            future = jnp.where(near, scores, 0.0)
            for a in range(CQ):
                cols = slice(a * LANES, (a + 1) * LANES)
                lags[odd, w * SUB : (w + 1) * SUB, cols] = future[8 - a : 8 - a + SUB].astype(
                    jnp.bfloat16
                )
                q_out[at : at + SUB, cols] = qwin[8 - a : 8 - a + SUB].astype(jnp.bfloat16)
    for w in range(0, steps, 4):
        wide = jnp.dot(
            turned[w * LANES : (w + 4) * LANES], key_ref[...], preferred_element_type=jnp.float32
        )
        for n in range(4):
            cols = slice((w + n) * LANES, (w + n + 1) * LANES)
            for a in range(CQ):
                k_out[a * HD : (a + 1) * HD, cols] = wide[
                    n * LANES : (n + 1) * LANES, a * LANES : (a + 1) * LANES
                ].astype(jnp.bfloat16)
    for odd, taps in enumerate((even_ref, odd_ref)):
        for w in range(0, steps, 8):
            fix = jnp.dot(
                lags[odd, w * SUB : (w + 8) * SUB], taps[...], preferred_element_type=jnp.float32
            )
            for n in range(8):
                m = 2 * ((w + n) % 2) + odd
                col = LANES * ((m + 1) // 2)
                corr[(w + n) // 2, m * SUB : (m + 1) * SUB, col : col + taps.shape[1]] = fix[
                    n * SUB : (n + 1) * SUB
                ]


def fill_tables(weights, key_ref, even_ref, odd_ref):
    def fill(ref, origin, swap):
        height = ref.shape[0] if swap else ref.shape[0] // CQ
        width = ref.shape[1] // CQ if swap else ref.shape[1]
        shape = (height, width)
        tap = lax.broadcasted_iota(jnp.int32, shape, 1) - lax.broadcasted_iota(jnp.int32, shape, 0)
        for a in range(CQ):
            value = jnp.zeros(shape, jnp.float32)
            for c in range(CK):
                value = jnp.where(tap == c - origin, weights[a * CK + c], value)
            value = value.astype(jnp.bfloat16)
            if swap:
                ref[:, a * width : (a + 1) * width] = value
            else:
                ref[a * height : (a + 1) * height, :] = value

    fill(key_ref, CK // 2 + AHEAD, True)
    fill(even_ref, CK // 2 + 8 - BAND, False)
    fill(odd_ref, CK // 2 + 8 - SUB, False)


def attend_kernel(place, mix, weights, *refs):
    qk_refs, (va, vb, vc, vd), (mine, theirs) = refs[:2], refs[2:6], refs[6:8]
    v_all, q_wide, k_ref, corr = refs[8:12]
    tables, sem_v = refs[16:19], refs[19]
    side, core = place[2], place[1]
    b = pl.program_id(0)
    count = k_ref.shape[1] // (2 * ROWS)

    @pl.when(b == 0)
    def _():
        def copies_v():
            out = []
            for n, ref in enumerate((va, vb, vc, vd)):
                parity = core if n < 2 else 1 - core
                start = pl.multiple_of((side if n % 2 == 0 else 1 - side) * 2 * HD, 2 * HD)
                for i in range(count):
                    rows = pl.ds(pl.multiple_of((2 * i + parity) * ROWS, ROWS), ROWS)
                    target = v_all.at[rows, pl.ds(start, 2 * HD)]
                    out.append(pltpu.make_async_copy(ref.at[i], target, sem_v.at[n, i]))
            return out

        for copy in copies_v():
            copy.start()
        fill_tables(weights, *tables)
        prepare(core, *qk_refs, *tables, q_wide, k_ref, corr, *refs[12:16])
        for copy in copies_v():
            copy.wait()

    row = lax.broadcasted_iota(jnp.int32, (ROWS, ROWS), 0)
    col = lax.broadcasted_iota(jnp.int32, (ROWS, ROWS), 1)
    seen = col <= row
    top, low = slice(0, ROWS), slice(ROWS, 2 * ROWS)

    def fixed(part, n):
        return jnp.concatenate([part[:, :BAND], part[:, BAND:] - corr[n, :, :BAND]], 1)

    def rows_of(upper, lower):
        return jnp.concatenate([upper, lower], 0)

    def block(step):
        q_rows = q_wide[2 * step * ROWS : (2 * step + 2) * ROWS]
        parts = []
        for j in range(2 * step + 1):
            part = jnp.dot(
                q_rows,
                k_ref[:, j * ROWS : (j + 1) * ROWS],
                preferred_element_type=jnp.float32,
            )
            if j == 2 * step:
                diagonal = jnp.where(seen, part[top] - corr[2 * step, :, BAND:], -jnp.inf)
                part = rows_of(diagonal, fixed(part[low], 2 * step + 1))
            elif j == 2 * step - 1:
                part = rows_of(fixed(part[top], 2 * step), part[low])
            parts.append(part)
        start = (2 * step + 1) * ROWS
        last = jnp.dot(
            q_rows[low], k_ref[:, start : start + ROWS], preferred_element_type=jnp.float32
        )
        last = jnp.where(seen, last - corr[2 * step + 1, :, BAND:], -jnp.inf)
        peak = parts[0]
        for part in parts[1:]:
            peak = jnp.maximum(peak, part)
        peak = rows_of(peak[top], jnp.maximum(peak[low], last))
        peak = jnp.max(peak, axis=1, keepdims=True)
        mass = jnp.zeros((2 * ROWS, ROWS), jnp.float32)
        probs = []
        for part in parts:
            part = jnp.exp2(part - peak)
            mass = mass + part
            probs.append(part.astype(jnp.bfloat16))
        last = jnp.exp2(last - peak[low])
        mass = rows_of(mass[top], mass[low] + last)
        summed = jnp.dot(
            jnp.concatenate(probs, 1), v_all[:start], preferred_element_type=jnp.float32
        )
        extra = jnp.dot(
            last.astype(jnp.bfloat16),
            v_all[start : start + ROWS],
            preferred_element_type=jnp.float32,
        )
        inverse = 1.0 / jnp.sum(mass, axis=1, keepdims=True)
        halves = []
        for rows, total in ((top, summed[top]), (low, summed[low] + extra)):
            halves.append(
                jnp.concatenate(
                    [
                        total[:, g * HD : (g + 1) * HD] * (inverse[rows] * mix[g])
                        for g in range(GROUP)
                    ],
                    1,
                ).astype(jnp.bfloat16)
            )
        mine[0] = jnp.where(core == 0, halves[0], halves[1])
        theirs[0] = jnp.where(core == 0, halves[1], halves[0])

    for step in range(count):
        pl.when(b == step)(lambda step=step: block(step))


def attend_head(place, mix, weights, mine, other, values):
    total = 2 * mine.shape[0] * ROWS
    count = total // (2 * ROWS)
    depth = CQ * HD
    out = jax.ShapeDtypeStruct((count, ROWS, GROUP * HD), jnp.bfloat16)
    out_spec = pl.BlockSpec((1, ROWS, GROUP * HD), lambda b: (b, 0, 0))
    return pl.pallas_call(
        attend_kernel,
        grid=(count,),
        out_shape=(out, out),
        in_specs=[whole(pltpu.SMEM)] * 3 + [whole(pltpu.VMEM)] * 2 + [whole(pl.ANY)] * 4,
        out_specs=[out_spec, out_spec],
        scratch_shapes=[
            pltpu.VMEM((total, GROUP * HD), jnp.bfloat16),
            pltpu.VMEM((total, depth), jnp.bfloat16),
            pltpu.VMEM((depth, total), jnp.bfloat16),
            pltpu.VMEM((total // ROWS, ROWS, BAND + ROWS), jnp.float32),
            pltpu.VMEM((8 + total, HD), jnp.float32),
            pltpu.VMEM((AHEAD + total + LANES, HD), jnp.float32),
            pltpu.VMEM((2, total // 2, CQ * LANES), jnp.bfloat16),
            pltpu.VMEM((total, 2 * LANES), jnp.bfloat16),
        ]
        + [
            pltpu.VMEM(shape, jnp.bfloat16)
            for shape in ((2 * LANES, depth), (CQ * LANES, 2 * LANES), (CQ * LANES, LANES))
        ]
        + [pltpu.SemaphoreType.DMA((4, count))],
        compiler_params=kernel_params(56),
        cost_estimate=pl.CostEstimate(
            flops=total * total * (depth + GROUP * HD),
            bytes_accessed=16 * 2**20,
            transcendentals=total * total // 2,
        ),
    )(place, mix, weights, mine, other, *values)


def finish_kernel(place, own, r1, r2, r3, gain, *refs):
    w_parts, outs = refs[:12], refs[12:16]
    normed, w_buf, sem = refs[16:]
    width = w_parts[0].shape[1]
    core, head, inner = place[1], place[0], place[9]

    def copy_w(n, source):
        side = core if n % 2 == 0 else 1 - core
        cols = pl.ds(pl.multiple_of(side * width, width), width)
        target = w_buf.at[lax.bitwise_xor(place[5 + n // 2], head), :, cols]
        return pltpu.make_async_copy(w_parts[source], target, sem.at[n])

    for n in range(4):
        copy_w(n, n).start()
    for n in range(4, 8):
        straight = n if n < 6 else n + 2

        @pl.when(inner == 1)
        def _():
            copy_w(n, straight).start()

        @pl.when(inner == 0)
        def _():
            copy_w(n, straight + 2).start()

    near = own[...] + r1[...].astype(jnp.float32)
    far = r2[...].astype(jnp.float32) + r3[...].astype(jnp.float32)
    low = place[3] == 0
    for g in range(2 * GROUP):
        cols = slice((g % GROUP) * HD, (g % GROUP + 1) * HD)
        first = low if g < GROUP else jnp.logical_not(low)
        x = jnp.where(first, near[:, cols], far[:, cols])
        scale = lax.rsqrt(jnp.mean(x * x, axis=1, keepdims=True) + 1e-05)
        normed[:, g * HD : (g + 1) * HD] = (
            x * scale * gain[:, g * HD : (g + 1) * HD]
        ).astype(jnp.bfloat16)
    for n in range(8):
        copy_w(n, n).wait()
    for t in (3, 2, 1, 0):
        outs[t][...] = jnp.dot(
            normed[...], w_buf[t], preferred_element_type=jnp.float32
        ).astype(jnp.bfloat16)


def finish(place, own, r1, r2, r3, gain, w_parts):
    rows = own.shape[0]
    depth, width = w_parts[0].shape
    return pl.pallas_call(
        finish_kernel,
        in_specs=[whole(pltpu.SMEM)] + [whole(pltpu.VMEM)] * 5 + [whole(pl.ANY)] * 12,
        out_specs=[whole(pltpu.VMEM)] * 4,
        out_shape=[jax.ShapeDtypeStruct((rows, 2 * width), jnp.bfloat16)] * 4,
        scratch_shapes=[
            pltpu.VMEM((rows, depth), jnp.bfloat16),
            pltpu.VMEM((4, depth, 2 * width), jnp.bfloat16),
            pltpu.SemaphoreType.DMA((8,)),
        ],
        compiler_params=kernel_params(56),
        cost_estimate=pl.CostEstimate(
            flops=2 * rows * depth * 8 * width, bytes_accessed=11 * 2**20, transcendentals=0
        ),
    )(place, own, r1, r2, r3, gain, *w_parts)


def swapped(value, axis, mask):
    count = lax.axis_size(axis)
    return lax.ppermute(value, axis, [(i, i ^ mask) for i in range(count)])


def per_device_one_head(
    activations, positions, w_query, w_key, w_value, conv_kernel, head_mix, out_gain, w_out
):
    ctx, head = lax.axis_index("ctx"), lax.axis_index("head")
    z, core = ctx // 2, ctx % 2
    rows = activations.shape[0]
    half = rows // 2
    barrier = lax.optimization_barrier
    pair = 2 * HD

    def columns(target):
        parts = [
            lax.dynamic_slice_in_dim(w, target * pair, pair, 1) for w in (w_query, w_key, w_value)
        ]
        return jnp.concatenate(parts, 1)

    digits = jnp.stack([positions // 256, positions % 256]).astype(jnp.bfloat16)
    digits = jnp.pad(digits, ((0, 14), (0, activations.shape[1] - rows)))
    block = jnp.concatenate([activations, digits])
    w_pieces = jnp.stack([columns(target) for target in range(4)])
    far = [swapped(block, "ctx", 2 * s) for s in (1, 2, 3)]
    x0, y0 = swapped(activations, "head", 1), swapped(activations, "head", 2)
    weights = lax.dynamic_index_in_dim(conv_kernel, ctx, 0, keepdims=False)
    weights = weights * (math.log2(math.e) / math.sqrt(HD))
    place = jnp.stack([head, core, z % 2, z // 2, head, z, z ^ 1, z ^ 2, z ^ 3])
    place = place.astype(jnp.int32)
    far, x0, y0, w_pieces, weights, place, w_out = barrier(
        (far, x0, y0, w_pieces, weights, place, w_out)
    )

    same_core = [[i for i in range(8) if i % 2 == k] for k in range(2)]
    inside = [a[:rows] for a in far]
    to_x, to_y = jnp.concatenate(inside + [y0[half:]]), jnp.concatenate(inside + [x0[:half]])
    to_x, to_y, w_pieces = barrier((to_x, to_y, w_pieces))
    x_rest, y_rest = swapped(to_x, "head", 1), swapped(to_y, "head", 2)
    w_same = lax.all_to_all(w_pieces, "ctx", 0, 0, axis_index_groups=same_core)
    place_of = jnp.stack(
        [
            a[rows, :rows].astype(jnp.float32) * 256.0 + a[rows + 1, :rows].astype(jnp.float32)
            for a in [block] + far
        ]
    )
    exponents = jnp.arange(HD // 2, dtype=jnp.float32) * (2.0 / HD)
    inverse = jnp.exp(-exponents * math.log(500000.0))
    angle = (place_of * 0.25)[:, :, None] * inverse
    cosine, sine = jnp.cos(angle), jnp.sin(angle)
    cosine = jnp.concatenate([cosine, cosine], -1)
    sine = jnp.concatenate([-sine, sine], -1)
    x_rest, y_rest, cosine, sine, w_out = barrier((x_rest, y_rest, cosine, sine, w_out))
    c_low = swapped(x_rest[: 3 * half], "head", 2)
    c_high = swapped(y_rest[3 * half : 3 * rows], "head", 1)
    middle = [(2, 4), (3, 5), (4, 2), (5, 3)]
    outward = [(2, 0), (3, 1), (4, 6), (5, 7)]
    out_near = swapped(w_out, "ctx", 2)
    out_across = lax.ppermute(w_out, "ctx", middle)
    c_low, c_high, w_same, out_near, out_across = barrier(
        (c_low, c_high, w_same, out_near, out_across)
    )
    w_swap = swapped(w_same, "ctx", 1)
    sources = place, [activations] + list(far), (x0, x_rest, y0, y_rest, c_low, c_high), w_same, w_swap
    (v_pair,) = project(*sources)
    place, v_pair = barrier((place, v_pair))
    v_next = swapped(v_pair, "ctx", 2)
    v_pair_other = swapped(v_pair, "ctx", 1)
    out_across_next = lax.ppermute(out_near, "ctx", middle)
    out_passed = lax.ppermute(out_across, "ctx", outward)
    mine, theirs = project(place, *sources[1:], (cosine, sine))
    mine, theirs, v_next, v_pair_other = barrier((mine, theirs, v_next, v_pair_other))
    other = swapped(theirs, "ctx", 1)
    v_next_other = swapped(v_next, "ctx", 1)
    out_own_swap = swapped(w_out, "ctx", 1)
    other, v_next_other, out_across_next, out_own_swap = barrier(
        (other, v_next_other, out_across_next, out_own_swap)
    )
    out_passed_next = lax.ppermute(out_across_next, "ctx", outward)
    out_near_swap, out_across_swap = swapped(out_near, "ctx", 1), swapped(out_across, "ctx", 1)
    group_rows = lax.dynamic_slice_in_dim(head_mix, GROUP * (ctx // GROUP), GROUP, 0)
    mix = lax.dynamic_index_in_dim(group_rows, ctx % GROUP, 1, keepdims=False)
    out_mine, out_theirs = attend_head(
        place, mix, weights, mine, other, (v_pair, v_next, v_pair_other, v_next_other)
    )
    out_mine, out_theirs, out_passed, out_passed_next, out_near_swap, out_across_swap = barrier(
        (out_mine, out_theirs, out_passed, out_passed_next, out_near_swap, out_across_swap)
    )
    out_parts = [w_out, out_own_swap, out_near, out_near_swap, out_across, out_across_swap]
    for part in (out_passed, out_across_next, out_passed_next):
        out_parts += [part, swapped(part, "ctx", 1)]
    summed = out_mine.astype(jnp.float32) + swapped(out_theirs, "ctx", 1).astype(jnp.float32)
    own = lax.dynamic_index_in_dim(summed, z, 0, keepdims=False)
    r1, r2, r3 = [
        swapped(
            lax.dynamic_index_in_dim(summed, z ^ s, 0, keepdims=False).astype(jnp.bfloat16),
            "ctx",
            2 * s,
        )
        for s in (1, 2, 3)
    ]

    inner = (z == 1) | (z == 2)
    out_places = jnp.stack(
        [z, z ^ 1, jnp.where(inner, z ^ 3, z ^ 2), jnp.where(inner, z ^ 2, z ^ 3), inner]
    )
    where = jnp.concatenate([place[:5], out_places.astype(jnp.int32)])
    shares = finish(where, own, r1, r2, r3, out_gain.reshape(1, -1), out_parts)
    total = shares[0].astype(jnp.float32)
    for t in (1, 2, 3):
        total = total + swapped(shares[t], "head", t).astype(jnp.float32)
    return total.astype(jnp.bfloat16)


def solution(mesh):
    one_head_each = mesh.shape["ctx"] == 8 and mesh.shape["head"] == 4
    body = per_device_one_head if one_head_each else per_device
    return jax.shard_map(
        body,
        mesh=mesh,
        in_specs=(
            P("ctx", "head"),
            P("ctx"),
            P("ctx", "head"),
            P("ctx", "head"),
            P("ctx", "head"),
            P("head", None),
            P("head", None),
            P("head"),
            P("head", "ctx"),
        ),
        out_specs=P("ctx", "head"),
        check_vma=False,
    )
```

```python
import functools
import math

import jax
import jax.numpy as jnp
from jax import lax
from jax.experimental import pallas as pl
from jax.experimental.pallas import tpu as pltpu
from jax.sharding import PartitionSpec as P

HD = 128
GROUP = 4
CQ = 6
CK = 11
KB = 512


def passed_along(value, axis, steps):
    count = lax.axis_size(axis)
    leading, last = (max(0, -steps), min(count, count - steps))
    return lax.ppermute(value, axis, [(source, source + steps) for source in range(leading, last)])


def rope(projected, positions):
    row_count = projected.shape[0]
    head_count = projected.shape[1] // HD
    shaped = projected.reshape(row_count, head_count, HD)
    half_size = HD // 2
    exponents = jnp.arange(half_size, dtype=jnp.float32) * (2.0 / HD)
    inverse = jnp.exp(-exponents * math.log(500000.0))
    angle = (positions.astype(jnp.float32) * 0.25)[:, None, None] * inverse[None, None, :]
    cosine = jnp.cos(angle)
    sine = jnp.sin(angle)
    lower_half = shaped[..., :half_size]
    upper_half = shaped[..., half_size:]
    rotated_rows = jnp.concatenate(
        [lower_half * cosine - upper_half * sine, upper_half * cosine + lower_half * sine], -1
    )
    return rotated_rows.reshape(row_count, head_count * HD)


def convolve(masked, kernel, row_count, col_count):
    summed = jnp.zeros((masked.shape[0], row_count, col_count), jnp.float32)
    for lag_q in range(CQ):
        for lag_k in range(CK):
            weight = kernel[:, lag_q * CK + lag_k][:, None, None]
            window = masked[
                :,
                CQ - 1 - lag_q : CQ - 1 - lag_q + row_count,
                CK - 1 - lag_k : CK - 1 - lag_k + col_count,
            ]
            summed = summed + weight * window
    return summed


def add_rows(left, piece):
    return jnp.dot(left, piece, preferred_element_type=jnp.float32)


def share_keys(key, value):
    return (
        lax.all_gather(key, "ctx", axis=0, tiled=True),
        lax.all_gather(value, "ctx", axis=0, tiled=True),
    )


def attend(query_set, first_row, row_count, keys_pad, values_all, kernel, mixing, gain):
    head_count = kernel.shape[0]
    ext_rows = row_count + CQ - 1
    query_heads = query_set.reshape(ext_rows, head_count, HD)
    token_total = values_all.shape[0]
    block_count = token_total // KB
    last_row = first_row + row_count - 1
    scale = 1.0 / math.sqrt(HD)
    prow = first_row - (CQ - 1) + jnp.arange(ext_rows, dtype=jnp.int32)
    irow = first_row + jnp.arange(row_count, dtype=jnp.int32)

    def logits_of(block):
        key_start = block * KB
        key_block = lax.dynamic_slice_in_dim(keys_pad, key_start, KB + CK - 1, 0).reshape(
            KB + CK - 1, head_count, HD
        )
        scores = (
            jnp.einsum("rhd,khd->hrk", query_heads, key_block, preferred_element_type=jnp.float32)
            * scale
        )
        kcol = key_start - CK // 2 + jnp.arange(KB + CK - 1, dtype=jnp.int32)
        valid = (kcol[None, :] <= prow[:, None]) & (prow[:, None] >= 0)
        masked = jnp.where(valid[None], scores, 0.0)
        conv = convolve(masked, kernel, row_count, KB)
        jcol = key_start + jnp.arange(KB, dtype=jnp.int32)
        return jnp.where((jcol[None, :] <= irow[:, None])[None], conv, -jnp.inf)

    def first_pass(block, carry_in):

        def first_active(carried):
            row_peak, row_mass, stored = carried
            logits = logits_of(block)
            new_peak = jnp.maximum(row_peak, jnp.max(logits, axis=-1))
            new_mass = row_mass * jnp.exp(row_peak - new_peak) + jnp.sum(
                jnp.exp(logits - new_peak[..., None]), axis=-1
            )
            stored = lax.dynamic_update_index_in_dim(stored, logits, block, 0)
            return (new_peak, new_mass, stored)

        return lax.cond(block * KB <= last_row, first_active, lambda carried: carried, carry_in)

    peak_start = jnp.full((head_count, row_count), -jnp.inf, jnp.float32)
    mass_start = jnp.zeros((head_count, row_count), jnp.float32)
    store_start = jnp.zeros((block_count, head_count, row_count, KB), jnp.float32)
    row_peak, row_mass, stored = lax.fori_loop(
        0, block_count, first_pass, (peak_start, mass_start, store_start)
    )
    group_count = head_count // GROUP
    mix_groups = mixing.reshape(group_count, GROUP, GROUP)

    def second_pass(block, carry_in):

        def second_active(summed):
            logits = lax.dynamic_index_in_dim(stored, block, 0, keepdims=False)
            probs = jnp.exp(logits - row_peak[..., None]) / row_mass[..., None]
            grouped = probs.reshape(group_count, GROUP, row_count, KB)
            mixed_scores = (
                jnp.einsum("gab,gbrk->gark", mix_groups, grouped)
                .reshape(head_count, row_count, KB)
                .astype(jnp.bfloat16)
            )
            value_block = lax.dynamic_slice_in_dim(values_all, block * KB, KB, 0).reshape(
                KB, head_count, HD
            )
            return summed + jnp.einsum(
                "hrk,khd->rhd", mixed_scores, value_block, preferred_element_type=jnp.float32
            )

        return lax.cond(block * KB <= last_row, second_active, lambda summed: summed, carry_in)

    summed = lax.fori_loop(
        0, block_count, second_pass, jnp.zeros((row_count, head_count, HD), jnp.float32)
    )
    rms = jnp.sqrt(jnp.mean(summed * summed, axis=-1, keepdims=True) + 1e-05)
    normed = (summed / rms * gain.reshape(head_count, HD)).astype(jnp.bfloat16)
    return normed.reshape(row_count, head_count * HD)


def per_device(
    activations, positions, w_query, w_key, w_value, conv_kernel, head_mix, out_gain, w_out
):
    row_count = activations.shape[0]
    ctx_place = lax.axis_index("ctx")
    features = lax.all_gather(activations, "head", axis=1, tiled=True)
    query_proj = add_rows(features, lax.all_gather(w_query, "ctx", axis=0, tiled=True))
    key_proj = add_rows(features, lax.all_gather(w_key, "ctx", axis=0, tiled=True))
    value_proj = add_rows(features, lax.all_gather(w_value, "ctx", axis=0, tiled=True))
    key = rope(key_proj, positions).astype(jnp.bfloat16)
    value = value_proj.astype(jnp.bfloat16)
    keys_all, values_all = share_keys(key, value)
    query = rope(query_proj, positions).astype(jnp.bfloat16)
    rim_rows = passed_along(query[row_count - (CQ - 1) :], "ctx", 1)
    query_ext = jnp.concatenate([rim_rows, query], 0)
    keys_pad = jnp.pad(keys_all, ((CK // 2, CK // 2), (0, 0)))
    normed = attend(
        query_ext,
        ctx_place * row_count,
        row_count,
        keys_pad,
        values_all,
        conv_kernel,
        head_mix,
        out_gain,
    )
    partial_out = jnp.dot(
        normed, lax.all_gather(w_out, "ctx", axis=1, tiled=True), preferred_element_type=jnp.float32
    )
    return lax.psum_scatter(
        partial_out.astype(jnp.bfloat16), "head", scatter_dimension=1, tiled=True
    )


ROWS = 256
BAND = 128
LANES = 128
SUB = 64
AHEAD = 16


def kernel_params(mebibytes):
    return pltpu.CompilerParams(vmem_limit_bytes=mebibytes * 1024 * 1024)


def whole(memory_space):
    return pl.BlockSpec(memory_space=memory_space)


def project_kernel(rows, first_col, place, *refs):
    a_own, (x0, x_rest, y0, y_rest, c_low, c_high) = refs[:4], refs[4:10]
    w_same, w_swap = refs[10:12]
    abuf, wbuf, acc, sem_a, sem_w = refs[-5:]
    turn, core = place[0], place[1]
    half = w_same.shape[1]
    width = wbuf.shape[2]

    def copies_a(t):
        if t == 0:
            pairs = [(a_own[b], 0, b * rows, rows) for b in range(4)]
        elif t < 3:
            first, others = ((x0, x_rest), (y0, y_rest))[t - 1]
            pairs = [(first, 0, 0, rows), (others, 0, rows, 3 * rows)]
        else:
            late, mid = 3 * rows, rows // 2
            pairs = [(y_rest, late, 0, mid), (x_rest, late, mid, mid)]
            pairs += [(c_low, 0, rows, 3 * mid), (c_high, 0, rows + 3 * mid, 3 * mid)]
        return [
            pltpu.make_async_copy(
                ref.at[pl.ds(source, size)], abuf.at[t, pl.ds(target, size)], sem_a.at[t, n]
            )
            for n, (ref, source, target, size) in enumerate(pairs)
        ]

    def copies_w(t):
        out = []
        for n, (ref, side) in enumerate(((w_same, core), (w_swap, 1 - core))):
            source = ref.at[lax.bitwise_xor(turn, t), :, pl.ds(first_col, width)]
            target = wbuf.at[t, pl.ds(pl.multiple_of(side * half, half), half)]
            out.append(pltpu.make_async_copy(source, target, sem_w.at[t, n]))
        return out

    for t in range(4):
        for copy in copies_w(t) + copies_a(t):
            copy.start()
    for t in range(4):
        for copy in copies_w(t) + copies_a(t):
            copy.wait()
        part = jnp.dot(abuf[t], wbuf[t], preferred_element_type=jnp.float32)
        acc[...] = part if t == 0 else acc[...] + part
    if first_col:
        v_out = refs[12]
        for b in range(4):
            v_out[place[5 + b]] = acc[b * rows : (b + 1) * rows].astype(jnp.bfloat16)
        return
    cos_ref, sin_ref, mine, theirs = refs[12:16]
    first = core == 0
    for b in range(4):
        total = acc[b * rows : (b + 1) * rows]
        cosine, sine = cos_ref[b], sin_ref[b]
        at = place[5 + b]
        for col, out in ((0, 0), (2 * HD, HD)):
            heads = []
            for start in (col, col + HD):
                x = total[:, start : start + HD]
                x = x * cosine + pltpu.roll(x, HD // 2, 1) * sine
                heads.append(x.astype(jnp.bfloat16))
            mine[at, :, out : out + HD] = jnp.where(first, heads[0], heads[1])
            theirs[at, :, out : out + HD] = jnp.where(first, heads[1], heads[0])


def project(place, a_own, a_plane, w_same, w_swap, angles=()):
    rows, depth = a_own[0].shape
    first_col, width = (0, 4 * HD) if angles else (4 * HD, 2 * HD)
    out = jax.ShapeDtypeStruct((4, rows, 2 * HD), jnp.bfloat16)
    count = 2 if angles else 1
    return pl.pallas_call(
        functools.partial(project_kernel, rows, first_col),
        out_shape=[out] * count,
        in_specs=[whole(pltpu.SMEM)]
        + [whole(pl.ANY)] * 12
        + [whole(pltpu.VMEM)] * len(angles),
        out_specs=[whole(pltpu.VMEM)] * count,
        scratch_shapes=[
            pltpu.VMEM((4, 4 * rows, depth), jnp.bfloat16),
            pltpu.VMEM((4, depth, width), jnp.bfloat16),
            pltpu.VMEM((4 * rows, width), jnp.float32),
            pltpu.SemaphoreType.DMA((4, 4)),
            pltpu.SemaphoreType.DMA((4, 2)),
        ],
        compiler_params=kernel_params(56),
        cost_estimate=pl.CostEstimate(
            flops=8 * rows * 4 * depth * width, bytes_accessed=16 * 2**20, transcendentals=0
        ),
    )(place, *a_own, *a_plane, w_same, w_swap, *angles)


def prepare(core, mine, other, key_ref, even_ref, odd_ref, q_out, k_out, corr, *scratch):
    qf, kf, lags, turned = scratch
    total = q_out.shape[0]
    qf[0:8] = jnp.zeros((8, HD), jnp.float32)
    kf[0:AHEAD] = jnp.zeros((AHEAD, HD), jnp.float32)
    kf[AHEAD + total :] = jnp.zeros((kf.shape[0] - AHEAD - total, HD), jnp.float32)
    corr[...] = jnp.zeros(corr.shape, jnp.float32)
    for i in range(total // (2 * ROWS)):
        for ref, parity in ((mine, core), (other, 1 - core)):
            start = pl.multiple_of((2 * i + parity) * ROWS, ROWS)
            block = ref[i].astype(jnp.float32)
            qf[pl.ds(8 + start, ROWS)] = block[:, :HD]
            kf[pl.ds(AHEAD + start, ROWS)] = block[:, HD:]

    ahead = lax.broadcasted_iota(jnp.int32, (SUB + 8, LANES), 1) - lax.broadcasted_iota(
        jnp.int32, (SUB + 8, LANES), 0
    )
    near = (ahead >= 1) & (ahead < CQ + CK // 2)
    steps = total // LANES
    for w in range(steps):
        base = w * LANES
        window = kf[base : base + 2 * LANES].T
        turned[base : base + LANES] = window.astype(jnp.bfloat16)
        for odd in range(2):
            at = base + odd * SUB
            qwin = qf[at : at + SUB + 8]
            kwin = kf[at + AHEAD - 8 : at + AHEAD - 8 + LANES]
            scores = lax.dot_general(
                qwin.astype(jnp.bfloat16),
                kwin.astype(jnp.bfloat16),
                (((1,), (1,)), ((), ())),
                preferred_element_type=jnp.float32,
            )
            future = jnp.where(near, scores, 0.0)
            for a in range(CQ):
                cols = slice(a * LANES, (a + 1) * LANES)
                lags[odd, w * SUB : (w + 1) * SUB, cols] = future[8 - a : 8 - a + SUB].astype(
                    jnp.bfloat16
                )
                q_out[at : at + SUB, cols] = qwin[8 - a : 8 - a + SUB].astype(jnp.bfloat16)
    for w in range(0, steps, 4):
        wide = jnp.dot(
            turned[w * LANES : (w + 4) * LANES], key_ref[...], preferred_element_type=jnp.float32
        )
        for n in range(4):
            cols = slice((w + n) * LANES, (w + n + 1) * LANES)
            for a in range(CQ):
                k_out[a * HD : (a + 1) * HD, cols] = wide[
                    n * LANES : (n + 1) * LANES, a * LANES : (a + 1) * LANES
                ].astype(jnp.bfloat16)
    for odd, taps in enumerate((even_ref, odd_ref)):
        for w in range(0, steps, 8):
            fix = jnp.dot(
                lags[odd, w * SUB : (w + 8) * SUB], taps[...], preferred_element_type=jnp.float32
            )
            for n in range(8):
                m = 2 * ((w + n) % 2) + odd
                col = LANES * ((m + 1) // 2)
                corr[(w + n) // 2, m * SUB : (m + 1) * SUB, col : col + taps.shape[1]] = fix[
                    n * SUB : (n + 1) * SUB
                ]


def fill_tables(weights, key_ref, even_ref, odd_ref):
    def fill(ref, origin, swap):
        height = ref.shape[0] if swap else ref.shape[0] // CQ
        width = ref.shape[1] // CQ if swap else ref.shape[1]
        shape = (height, width)
        tap = lax.broadcasted_iota(jnp.int32, shape, 1) - lax.broadcasted_iota(jnp.int32, shape, 0)
        for a in range(CQ):
            value = jnp.zeros(shape, jnp.float32)
            for c in range(CK):
                value = jnp.where(tap == c - origin, weights[a * CK + c], value)
            value = value.astype(jnp.bfloat16)
            if swap:
                ref[:, a * width : (a + 1) * width] = value
            else:
                ref[a * height : (a + 1) * height, :] = value

    fill(key_ref, CK // 2 + AHEAD, True)
    fill(even_ref, CK // 2 + 8 - BAND, False)
    fill(odd_ref, CK // 2 + 8 - SUB, False)


def attend_kernel(place, mix, weights, *refs):
    qk_refs, (va, vb, vc, vd), (mine, theirs) = refs[:2], refs[2:6], refs[6:8]
    v_all, q_wide, k_ref, corr = refs[8:12]
    tables, sem_v = refs[16:19], refs[19]
    side, core = place[2], place[1]
    b = pl.program_id(0)
    count = k_ref.shape[1] // (2 * ROWS)

    @pl.when(b == 0)
    def _():
        def copies_v():
            out = []
            for n, ref in enumerate((va, vb, vc, vd)):
                parity = core if n < 2 else 1 - core
                start = pl.multiple_of((side if n % 2 == 0 else 1 - side) * 2 * HD, 2 * HD)
                for i in range(count):
                    rows = pl.ds(pl.multiple_of((2 * i + parity) * ROWS, ROWS), ROWS)
                    target = v_all.at[rows, pl.ds(start, 2 * HD)]
                    out.append(pltpu.make_async_copy(ref.at[i], target, sem_v.at[n, i]))
            return out

        for copy in copies_v():
            copy.start()
        fill_tables(weights, *tables)
        prepare(core, *qk_refs, *tables, q_wide, k_ref, corr, *refs[12:16])
        for copy in copies_v():
            copy.wait()

    row = lax.broadcasted_iota(jnp.int32, (ROWS, ROWS), 0)
    col = lax.broadcasted_iota(jnp.int32, (ROWS, ROWS), 1)
    seen = col <= row
    top, low = slice(0, ROWS), slice(ROWS, 2 * ROWS)

    def fixed(part, n):
        return jnp.concatenate([part[:, :BAND], part[:, BAND:] - corr[n, :, :BAND]], 1)

    def rows_of(upper, lower):
        return jnp.concatenate([upper, lower], 0)

    def block(step):
        q_rows = q_wide[2 * step * ROWS : (2 * step + 2) * ROWS]
        parts = []
        for j in range(2 * step + 1):
            part = jnp.dot(
                q_rows,
                k_ref[:, j * ROWS : (j + 1) * ROWS],
                preferred_element_type=jnp.float32,
            )
            if j == 2 * step:
                diagonal = jnp.where(seen, part[top] - corr[2 * step, :, BAND:], -jnp.inf)
                part = rows_of(diagonal, fixed(part[low], 2 * step + 1))
            elif j == 2 * step - 1:
                part = rows_of(fixed(part[top], 2 * step), part[low])
            parts.append(part)
        start = (2 * step + 1) * ROWS
        last = jnp.dot(
            q_rows[low], k_ref[:, start : start + ROWS], preferred_element_type=jnp.float32
        )
        last = jnp.where(seen, last - corr[2 * step + 1, :, BAND:], -jnp.inf)
        peak = parts[0]
        for part in parts[1:]:
            peak = jnp.maximum(peak, part)
        peak = rows_of(peak[top], jnp.maximum(peak[low], last))
        peak = jnp.max(peak, axis=1, keepdims=True)
        mass = jnp.zeros((2 * ROWS, ROWS), jnp.float32)
        probs = []
        for part in parts:
            part = jnp.exp2(part - peak)
            mass = mass + part
            probs.append(part.astype(jnp.bfloat16))
        last = jnp.exp2(last - peak[low])
        mass = rows_of(mass[top], mass[low] + last)
        summed = jnp.dot(
            jnp.concatenate(probs, 1), v_all[:start], preferred_element_type=jnp.float32
        )
        extra = jnp.dot(
            last.astype(jnp.bfloat16),
            v_all[start : start + ROWS],
            preferred_element_type=jnp.float32,
        )
        inverse = 1.0 / jnp.sum(mass, axis=1, keepdims=True)
        halves = []
        for rows, total in ((top, summed[top]), (low, summed[low] + extra)):
            halves.append(
                jnp.concatenate(
                    [
                        total[:, g * HD : (g + 1) * HD] * (inverse[rows] * mix[g])
                        for g in range(GROUP)
                    ],
                    1,
                ).astype(jnp.bfloat16)
            )
        mine[0] = jnp.where(core == 0, halves[0], halves[1])
        theirs[0] = jnp.where(core == 0, halves[1], halves[0])

    for step in range(count):
        pl.when(b == step)(lambda step=step: block(step))


def attend_head(place, mix, weights, mine, other, values):
    total = 2 * mine.shape[0] * ROWS
    count = total // (2 * ROWS)
    depth = CQ * HD
    out = jax.ShapeDtypeStruct((count, ROWS, GROUP * HD), jnp.bfloat16)
    out_spec = pl.BlockSpec((1, ROWS, GROUP * HD), lambda b: (b, 0, 0))
    return pl.pallas_call(
        attend_kernel,
        grid=(count,),
        out_shape=(out, out),
        in_specs=[whole(pltpu.SMEM)] * 3 + [whole(pltpu.VMEM)] * 2 + [whole(pl.ANY)] * 4,
        out_specs=[out_spec, out_spec],
        scratch_shapes=[
            pltpu.VMEM((total, GROUP * HD), jnp.bfloat16),
            pltpu.VMEM((total, depth), jnp.bfloat16),
            pltpu.VMEM((depth, total), jnp.bfloat16),
            pltpu.VMEM((total // ROWS, ROWS, BAND + ROWS), jnp.float32),
            pltpu.VMEM((8 + total, HD), jnp.float32),
            pltpu.VMEM((AHEAD + total + LANES, HD), jnp.float32),
            pltpu.VMEM((2, total // 2, CQ * LANES), jnp.bfloat16),
            pltpu.VMEM((total, 2 * LANES), jnp.bfloat16),
        ]
        + [
            pltpu.VMEM(shape, jnp.bfloat16)
            for shape in ((2 * LANES, depth), (CQ * LANES, 2 * LANES), (CQ * LANES, LANES))
        ]
        + [pltpu.SemaphoreType.DMA((4, count))],
        compiler_params=kernel_params(56),
        cost_estimate=pl.CostEstimate(
            flops=total * total * (depth + GROUP * HD),
            bytes_accessed=16 * 2**20,
            transcendentals=total * total // 2,
        ),
    )(place, mix, weights, mine, other, *values)


def finish_kernel(place, own, r1, r2, r3, gain, *refs):
    w_parts, outs = refs[:12], refs[12:16]
    normed, w_buf, sem = refs[16:]
    width = w_parts[0].shape[1]
    core, head, inner = place[1], place[0], place[9]

    def copy_w(n, source):
        side = core if n % 2 == 0 else 1 - core
        cols = pl.ds(pl.multiple_of(side * width, width), width)
        target = w_buf.at[lax.bitwise_xor(place[5 + n // 2], head), :, cols]
        return pltpu.make_async_copy(w_parts[source], target, sem.at[n])

    for n in range(4):
        copy_w(n, n).start()
    for n in range(4, 8):
        straight = n if n < 6 else n + 2

        @pl.when(inner == 1)
        def _():
            copy_w(n, straight).start()

        @pl.when(inner == 0)
        def _():
            copy_w(n, straight + 2).start()

    near = own[...] + r1[...].astype(jnp.float32)
    far = r2[...].astype(jnp.float32) + r3[...].astype(jnp.float32)
    low = place[3] == 0
    for g in range(2 * GROUP):
        cols = slice((g % GROUP) * HD, (g % GROUP + 1) * HD)
        first = low if g < GROUP else jnp.logical_not(low)
        x = jnp.where(first, near[:, cols], far[:, cols])
        scale = lax.rsqrt(jnp.mean(x * x, axis=1, keepdims=True) + 1e-05)
        normed[:, g * HD : (g + 1) * HD] = (
            x * scale * gain[:, g * HD : (g + 1) * HD]
        ).astype(jnp.bfloat16)
    for n in range(8):
        copy_w(n, n).wait()
    for t in (3, 2, 1, 0):
        outs[t][...] = jnp.dot(
            normed[...], w_buf[t], preferred_element_type=jnp.float32
        ).astype(jnp.bfloat16)


def finish(place, own, r1, r2, r3, gain, w_parts):
    rows = own.shape[0]
    depth, width = w_parts[0].shape
    return pl.pallas_call(
        finish_kernel,
        in_specs=[whole(pltpu.SMEM)] + [whole(pltpu.VMEM)] * 5 + [whole(pl.ANY)] * 12,
        out_specs=[whole(pltpu.VMEM)] * 4,
        out_shape=[jax.ShapeDtypeStruct((rows, 2 * width), jnp.bfloat16)] * 4,
        scratch_shapes=[
            pltpu.VMEM((rows, depth), jnp.bfloat16),
            pltpu.VMEM((4, depth, 2 * width), jnp.bfloat16),
            pltpu.SemaphoreType.DMA((8,)),
        ],
        compiler_params=kernel_params(56),
        cost_estimate=pl.CostEstimate(
            flops=2 * rows * depth * 8 * width, bytes_accessed=11 * 2**20, transcendentals=0
        ),
    )(place, own, r1, r2, r3, gain, *w_parts)


def swapped(value, axis, mask):
    count = lax.axis_size(axis)
    return lax.ppermute(value, axis, [(i, i ^ mask) for i in range(count)])


def per_device_one_head(
    activations, positions, w_query, w_key, w_value, conv_kernel, head_mix, out_gain, w_out
):
    ctx, head = lax.axis_index("ctx"), lax.axis_index("head")
    z, core = ctx // 2, ctx % 2
    rows = activations.shape[0]
    half = rows // 2
    barrier = lax.optimization_barrier
    pair = 2 * HD

    def columns(target):
        parts = [
            lax.dynamic_slice_in_dim(w, target * pair, pair, 1) for w in (w_query, w_key, w_value)
        ]
        return jnp.concatenate(parts, 1)

    digits = jnp.stack([positions // 256, positions % 256]).astype(jnp.bfloat16)
    digits = jnp.pad(digits, ((0, 14), (0, activations.shape[1] - rows)))
    block = jnp.concatenate([activations, digits])
    w_pieces = jnp.stack([columns(target) for target in range(4)])
    far = [swapped(block, "ctx", 2 * s) for s in (1, 2, 3)]
    x0, y0 = swapped(activations, "head", 1), swapped(activations, "head", 2)
    weights = lax.dynamic_index_in_dim(conv_kernel, ctx, 0, keepdims=False)
    weights = weights * (math.log2(math.e) / math.sqrt(HD))
    place = jnp.stack([head, core, z % 2, z // 2, head, z, z ^ 1, z ^ 2, z ^ 3])
    place = place.astype(jnp.int32)
    far, x0, y0, w_pieces, weights, place, w_out = barrier(
        (far, x0, y0, w_pieces, weights, place, w_out)
    )

    same_core = [[i for i in range(8) if i % 2 == k] for k in range(2)]
    inside = [a[:rows] for a in far]
    to_x, to_y = jnp.concatenate(inside + [y0[half:]]), jnp.concatenate(inside + [x0[:half]])
    to_x, to_y, w_pieces = barrier((to_x, to_y, w_pieces))
    x_rest, y_rest = swapped(to_x, "head", 1), swapped(to_y, "head", 2)
    w_same = lax.all_to_all(w_pieces, "ctx", 0, 0, axis_index_groups=same_core)
    place_of = jnp.stack(
        [
            a[rows, :rows].astype(jnp.float32) * 256.0 + a[rows + 1, :rows].astype(jnp.float32)
            for a in [block] + far
        ]
    )
    exponents = jnp.arange(HD // 2, dtype=jnp.float32) * (2.0 / HD)
    inverse = jnp.exp(-exponents * math.log(500000.0))
    angle = (place_of * 0.25)[:, :, None] * inverse
    cosine, sine = jnp.cos(angle), jnp.sin(angle)
    cosine = jnp.concatenate([cosine, cosine], -1)
    sine = jnp.concatenate([-sine, sine], -1)
    x_rest, y_rest, cosine, sine, w_out = barrier((x_rest, y_rest, cosine, sine, w_out))
    c_low = swapped(x_rest[: 3 * half], "head", 2)
    c_high = swapped(y_rest[3 * half : 3 * rows], "head", 1)
    middle = [(2, 4), (3, 5), (4, 2), (5, 3)]
    outward = [(2, 0), (3, 1), (4, 6), (5, 7)]
    out_near = swapped(w_out, "ctx", 2)
    out_across = lax.ppermute(w_out, "ctx", middle)
    c_low, c_high, w_same = barrier((c_low, c_high, w_same))
    w_swap = swapped(w_same, "ctx", 1)
    sources = place, [activations] + list(far), (x0, x_rest, y0, y_rest, c_low, c_high), w_same, w_swap
    (v_pair,) = project(*sources)
    place, v_pair, out_near, out_across = barrier((place, v_pair, out_near, out_across))
    v_next = swapped(v_pair, "ctx", 2)
    v_pair_other = swapped(v_pair, "ctx", 1)
    out_across_next = lax.ppermute(out_near, "ctx", middle)
    out_passed = lax.ppermute(out_across, "ctx", outward)
    mine, theirs = project(place, *sources[1:], (cosine, sine))
    mine, theirs, v_next, v_pair_other = barrier((mine, theirs, v_next, v_pair_other))
    other = swapped(theirs, "ctx", 1)
    v_next_other = swapped(v_next, "ctx", 1)
    out_own_swap = swapped(w_out, "ctx", 1)
    other, v_next_other, out_across_next, out_own_swap = barrier(
        (other, v_next_other, out_across_next, out_own_swap)
    )
    out_passed_next = lax.ppermute(out_across_next, "ctx", outward)
    out_near_swap, out_across_swap = swapped(out_near, "ctx", 1), swapped(out_across, "ctx", 1)
    group_rows = lax.dynamic_slice_in_dim(head_mix, GROUP * (ctx // GROUP), GROUP, 0)
    mix = lax.dynamic_index_in_dim(group_rows, ctx % GROUP, 1, keepdims=False)
    out_mine, out_theirs = attend_head(
        place, mix, weights, mine, other, (v_pair, v_next, v_pair_other, v_next_other)
    )
    out_mine, out_theirs, out_passed, out_passed_next, out_near_swap, out_across_swap = barrier(
        (out_mine, out_theirs, out_passed, out_passed_next, out_near_swap, out_across_swap)
    )
    out_parts = [w_out, out_own_swap, out_near, out_near_swap, out_across, out_across_swap]
    for part in (out_passed, out_across_next, out_passed_next):
        out_parts += [part, swapped(part, "ctx", 1)]
    summed = out_mine.astype(jnp.float32) + swapped(out_theirs, "ctx", 1).astype(jnp.float32)
    own = lax.dynamic_index_in_dim(summed, z, 0, keepdims=False)
    r1, r2, r3 = [
        swapped(
            lax.dynamic_index_in_dim(summed, z ^ s, 0, keepdims=False).astype(jnp.bfloat16),
            "ctx",
            2 * s,
        )
        for s in (1, 2, 3)
    ]
    inner = (z == 1) | (z == 2)
    out_places = jnp.stack(
        [z, z ^ 1, jnp.where(inner, z ^ 3, z ^ 2), jnp.where(inner, z ^ 2, z ^ 3), inner]
    )
    where = jnp.concatenate([place[:5], out_places.astype(jnp.int32)])
    shares = finish(where, own, r1, r2, r3, out_gain.reshape(1, -1), out_parts)
    total = shares[0].astype(jnp.float32)
    for t in (1, 2, 3):
        total = total + swapped(shares[t], "head", t).astype(jnp.float32)
    return total.astype(jnp.bfloat16)


def solution(mesh):
    one_head_each = mesh.shape["ctx"] == 8 and mesh.shape["head"] == 4
    body = per_device_one_head if one_head_each else per_device
    return jax.shard_map(
        body,
        mesh=mesh,
        in_specs=(
            P("ctx", "head"),
            P("ctx"),
            P("ctx", "head"),
            P("ctx", "head"),
            P("ctx", "head"),
            P("head", None),
            P("head", None),
            P("head"),
            P("head", "ctx"),
        ),
        out_specs=P("ctx", "head"),
        check_vma=False,
    )
```

```python
import functools
import math

import jax
import jax.numpy as jnp
from jax import lax
from jax.experimental import pallas as pl
from jax.experimental.pallas import tpu as pltpu
from jax.sharding import PartitionSpec as P

HD = 128
GROUP = 4
CQ = 6
CK = 11
KB = 512


def passed_along(value, axis, steps):
    count = lax.axis_size(axis)
    leading, last = (max(0, -steps), min(count, count - steps))
    return lax.ppermute(value, axis, [(source, source + steps) for source in range(leading, last)])


def rope(projected, positions):
    row_count = projected.shape[0]
    head_count = projected.shape[1] // HD
    shaped = projected.reshape(row_count, head_count, HD)
    half_size = HD // 2
    exponents = jnp.arange(half_size, dtype=jnp.float32) * (2.0 / HD)
    inverse = jnp.exp(-exponents * math.log(500000.0))
    angle = (positions.astype(jnp.float32) * 0.25)[:, None, None] * inverse[None, None, :]
    cosine = jnp.cos(angle)
    sine = jnp.sin(angle)
    lower_half = shaped[..., :half_size]
    upper_half = shaped[..., half_size:]
    rotated_rows = jnp.concatenate(
        [lower_half * cosine - upper_half * sine, upper_half * cosine + lower_half * sine], -1
    )
    return rotated_rows.reshape(row_count, head_count * HD)


def convolve(masked, kernel, row_count, col_count):
    summed = jnp.zeros((masked.shape[0], row_count, col_count), jnp.float32)
    for lag_q in range(CQ):
        for lag_k in range(CK):
            weight = kernel[:, lag_q * CK + lag_k][:, None, None]
            window = masked[
                :,
                CQ - 1 - lag_q : CQ - 1 - lag_q + row_count,
                CK - 1 - lag_k : CK - 1 - lag_k + col_count,
            ]
            summed = summed + weight * window
    return summed


def add_rows(left, piece):
    return jnp.dot(left, piece, preferred_element_type=jnp.float32)


def share_keys(key, value):
    return (
        lax.all_gather(key, "ctx", axis=0, tiled=True),
        lax.all_gather(value, "ctx", axis=0, tiled=True),
    )


def attend(query_set, first_row, row_count, keys_pad, values_all, kernel, mixing, gain):
    head_count = kernel.shape[0]
    ext_rows = row_count + CQ - 1
    query_heads = query_set.reshape(ext_rows, head_count, HD)
    token_total = values_all.shape[0]
    block_count = token_total // KB
    last_row = first_row + row_count - 1
    scale = 1.0 / math.sqrt(HD)
    prow = first_row - (CQ - 1) + jnp.arange(ext_rows, dtype=jnp.int32)
    irow = first_row + jnp.arange(row_count, dtype=jnp.int32)

    def logits_of(block):
        key_start = block * KB
        key_block = lax.dynamic_slice_in_dim(keys_pad, key_start, KB + CK - 1, 0).reshape(
            KB + CK - 1, head_count, HD
        )
        scores = (
            jnp.einsum("rhd,khd->hrk", query_heads, key_block, preferred_element_type=jnp.float32)
            * scale
        )
        kcol = key_start - CK // 2 + jnp.arange(KB + CK - 1, dtype=jnp.int32)
        valid = (kcol[None, :] <= prow[:, None]) & (prow[:, None] >= 0)
        masked = jnp.where(valid[None], scores, 0.0)
        conv = convolve(masked, kernel, row_count, KB)
        jcol = key_start + jnp.arange(KB, dtype=jnp.int32)
        return jnp.where((jcol[None, :] <= irow[:, None])[None], conv, -jnp.inf)

    def first_pass(block, carry_in):

        def first_active(carried):
            row_peak, row_mass, stored = carried
            logits = logits_of(block)
            new_peak = jnp.maximum(row_peak, jnp.max(logits, axis=-1))
            new_mass = row_mass * jnp.exp(row_peak - new_peak) + jnp.sum(
                jnp.exp(logits - new_peak[..., None]), axis=-1
            )
            stored = lax.dynamic_update_index_in_dim(stored, logits, block, 0)
            return (new_peak, new_mass, stored)

        return lax.cond(block * KB <= last_row, first_active, lambda carried: carried, carry_in)

    peak_start = jnp.full((head_count, row_count), -jnp.inf, jnp.float32)
    mass_start = jnp.zeros((head_count, row_count), jnp.float32)
    store_start = jnp.zeros((block_count, head_count, row_count, KB), jnp.float32)
    row_peak, row_mass, stored = lax.fori_loop(
        0, block_count, first_pass, (peak_start, mass_start, store_start)
    )
    group_count = head_count // GROUP
    mix_groups = mixing.reshape(group_count, GROUP, GROUP)

    def second_pass(block, carry_in):

        def second_active(summed):
            logits = lax.dynamic_index_in_dim(stored, block, 0, keepdims=False)
            probs = jnp.exp(logits - row_peak[..., None]) / row_mass[..., None]
            grouped = probs.reshape(group_count, GROUP, row_count, KB)
            mixed_scores = (
                jnp.einsum("gab,gbrk->gark", mix_groups, grouped)
                .reshape(head_count, row_count, KB)
                .astype(jnp.bfloat16)
            )
            value_block = lax.dynamic_slice_in_dim(values_all, block * KB, KB, 0).reshape(
                KB, head_count, HD
            )
            return summed + jnp.einsum(
                "hrk,khd->rhd", mixed_scores, value_block, preferred_element_type=jnp.float32
            )

        return lax.cond(block * KB <= last_row, second_active, lambda summed: summed, carry_in)

    summed = lax.fori_loop(
        0, block_count, second_pass, jnp.zeros((row_count, head_count, HD), jnp.float32)
    )
    rms = jnp.sqrt(jnp.mean(summed * summed, axis=-1, keepdims=True) + 1e-05)
    normed = (summed / rms * gain.reshape(head_count, HD)).astype(jnp.bfloat16)
    return normed.reshape(row_count, head_count * HD)


def per_device(
    activations, positions, w_query, w_key, w_value, conv_kernel, head_mix, out_gain, w_out
):
    row_count = activations.shape[0]
    ctx_place = lax.axis_index("ctx")
    features = lax.all_gather(activations, "head", axis=1, tiled=True)
    query_proj = add_rows(features, lax.all_gather(w_query, "ctx", axis=0, tiled=True))
    key_proj = add_rows(features, lax.all_gather(w_key, "ctx", axis=0, tiled=True))
    value_proj = add_rows(features, lax.all_gather(w_value, "ctx", axis=0, tiled=True))
    key = rope(key_proj, positions).astype(jnp.bfloat16)
    value = value_proj.astype(jnp.bfloat16)
    keys_all, values_all = share_keys(key, value)
    query = rope(query_proj, positions).astype(jnp.bfloat16)
    rim_rows = passed_along(query[row_count - (CQ - 1) :], "ctx", 1)
    query_ext = jnp.concatenate([rim_rows, query], 0)
    keys_pad = jnp.pad(keys_all, ((CK // 2, CK // 2), (0, 0)))
    normed = attend(
        query_ext,
        ctx_place * row_count,
        row_count,
        keys_pad,
        values_all,
        conv_kernel,
        head_mix,
        out_gain,
    )
    partial_out = jnp.dot(
        normed, lax.all_gather(w_out, "ctx", axis=1, tiled=True), preferred_element_type=jnp.float32
    )
    return lax.psum_scatter(
        partial_out.astype(jnp.bfloat16), "head", scatter_dimension=1, tiled=True
    )


ROWS = 256
BAND = 128
LANES = 128
SUB = 64
AHEAD = 16


def kernel_params(mebibytes):
    return pltpu.CompilerParams(vmem_limit_bytes=mebibytes * 1024 * 1024)


def whole(memory_space):
    return pl.BlockSpec(memory_space=memory_space)


def project_kernel(rows, first_col, place, *refs):
    a_own, (x0, x_rest, y0, y_rest, c_low, c_high) = refs[:4], refs[4:10]
    w_same, w_swap = refs[10:12]
    abuf, wbuf, acc, sem_a, sem_w = refs[-5:]
    turn, core = place[0], place[1]
    half = w_same.shape[1]
    width = wbuf.shape[2]

    def copies_a(t):
        if t == 0:
            pairs = [(a_own[b], 0, b * rows, rows) for b in range(4)]
        elif t < 3:
            first, others = ((x0, x_rest), (y0, y_rest))[t - 1]
            pairs = [(first, 0, 0, rows), (others, 0, rows, 3 * rows)]
        else:
            late, mid = 3 * rows, rows // 2
            pairs = [(y_rest, late, 0, mid), (x_rest, late, mid, mid)]
            pairs += [(c_low, 0, rows, 3 * mid), (c_high, 0, rows + 3 * mid, 3 * mid)]
        return [
            pltpu.make_async_copy(
                ref.at[pl.ds(source, size)], abuf.at[t, pl.ds(target, size)], sem_a.at[t, n]
            )
            for n, (ref, source, target, size) in enumerate(pairs)
        ]

    def copies_w(t):
        out = []
        for n, (ref, side) in enumerate(((w_same, core), (w_swap, 1 - core))):
            source = ref.at[lax.bitwise_xor(turn, t), :, pl.ds(first_col, width)]
            target = wbuf.at[t, pl.ds(pl.multiple_of(side * half, half), half)]
            out.append(pltpu.make_async_copy(source, target, sem_w.at[t, n]))
        return out

    for t in range(4):
        for copy in copies_w(t) + copies_a(t):
            copy.start()
    for t in range(4):
        for copy in copies_w(t) + copies_a(t):
            copy.wait()
        part = jnp.dot(abuf[t], wbuf[t], preferred_element_type=jnp.float32)
        acc[...] = part if t == 0 else acc[...] + part
    if first_col:
        v_out = refs[12]
        for b in range(4):
            v_out[place[5 + b]] = acc[b * rows : (b + 1) * rows].astype(jnp.bfloat16)
        return
    cos_ref, sin_ref, mine, theirs = refs[12:16]
    first = core == 0
    for b in range(4):
        total = acc[b * rows : (b + 1) * rows]
        cosine, sine = cos_ref[b], sin_ref[b]
        at = place[5 + b]
        for col, out in ((0, 0), (2 * HD, HD)):
            heads = []
            for start in (col, col + HD):
                x = total[:, start : start + HD]
                x = x * cosine + pltpu.roll(x, HD // 2, 1) * sine
                heads.append(x.astype(jnp.bfloat16))
            mine[at, :, out : out + HD] = jnp.where(first, heads[0], heads[1])
            theirs[at, :, out : out + HD] = jnp.where(first, heads[1], heads[0])


def project(place, a_own, a_plane, w_same, w_swap, angles=()):
    rows, depth = a_own[0].shape
    first_col, width = (0, 4 * HD) if angles else (4 * HD, 2 * HD)
    out = jax.ShapeDtypeStruct((4, rows, 2 * HD), jnp.bfloat16)
    count = 2 if angles else 1
    return pl.pallas_call(
        functools.partial(project_kernel, rows, first_col),
        out_shape=[out] * count,
        in_specs=[whole(pltpu.SMEM)]
        + [whole(pl.ANY)] * 12
        + [whole(pltpu.VMEM)] * len(angles),
        out_specs=[whole(pltpu.VMEM)] * count,
        scratch_shapes=[
            pltpu.VMEM((4, 4 * rows, depth), jnp.bfloat16),
            pltpu.VMEM((4, depth, width), jnp.bfloat16),
            pltpu.VMEM((4 * rows, width), jnp.float32),
            pltpu.SemaphoreType.DMA((4, 4)),
            pltpu.SemaphoreType.DMA((4, 2)),
        ],
        compiler_params=kernel_params(56),
        cost_estimate=pl.CostEstimate(
            flops=8 * rows * 4 * depth * width, bytes_accessed=16 * 2**20, transcendentals=0
        ),
    )(place, *a_own, *a_plane, w_same, w_swap, *angles)


def prepare(core, mine, other, key_ref, even_ref, odd_ref, q_out, k_out, corr, *scratch):
    qf, kf, lags, turned = scratch
    total = q_out.shape[0]
    qf[0:8] = jnp.zeros((8, HD), jnp.float32)
    kf[0:AHEAD] = jnp.zeros((AHEAD, HD), jnp.float32)
    kf[AHEAD + total :] = jnp.zeros((kf.shape[0] - AHEAD - total, HD), jnp.float32)
    corr[...] = jnp.zeros(corr.shape, jnp.float32)
    for i in range(total // (2 * ROWS)):
        for ref, parity in ((mine, core), (other, 1 - core)):
            start = pl.multiple_of((2 * i + parity) * ROWS, ROWS)
            block = ref[i].astype(jnp.float32)
            qf[pl.ds(8 + start, ROWS)] = block[:, :HD]
            kf[pl.ds(AHEAD + start, ROWS)] = block[:, HD:]

    ahead = lax.broadcasted_iota(jnp.int32, (SUB + 8, LANES), 1) - lax.broadcasted_iota(
        jnp.int32, (SUB + 8, LANES), 0
    )
    near = (ahead >= 1) & (ahead < CQ + CK // 2)
    steps = total // LANES
    for w in range(steps):
        base = w * LANES
        window = kf[base : base + 2 * LANES].T
        turned[base : base + LANES] = window.astype(jnp.bfloat16)
        for odd in range(2):
            at = base + odd * SUB
            qwin = qf[at : at + SUB + 8]
            kwin = kf[at + AHEAD - 8 : at + AHEAD - 8 + LANES]
            scores = lax.dot_general(
                qwin.astype(jnp.bfloat16),
                kwin.astype(jnp.bfloat16),
                (((1,), (1,)), ((), ())),
                preferred_element_type=jnp.float32,
            )
            future = jnp.where(near, scores, 0.0)
            for a in range(CQ):
                cols = slice(a * LANES, (a + 1) * LANES)
                lags[odd, w * SUB : (w + 1) * SUB, cols] = future[8 - a : 8 - a + SUB].astype(
                    jnp.bfloat16
                )
                q_out[at : at + SUB, cols] = qwin[8 - a : 8 - a + SUB].astype(jnp.bfloat16)
    for w in range(0, steps, 4):
        wide = jnp.dot(
            turned[w * LANES : (w + 4) * LANES], key_ref[...], preferred_element_type=jnp.float32
        )
        for n in range(4):
            cols = slice((w + n) * LANES, (w + n + 1) * LANES)
            for a in range(CQ):
                k_out[a * HD : (a + 1) * HD, cols] = wide[
                    n * LANES : (n + 1) * LANES, a * LANES : (a + 1) * LANES
                ].astype(jnp.bfloat16)
    for odd, taps in enumerate((even_ref, odd_ref)):
        for w in range(0, steps, 8):
            fix = jnp.dot(
                lags[odd, w * SUB : (w + 8) * SUB], taps[...], preferred_element_type=jnp.float32
            )
            for n in range(8):
                m = 2 * ((w + n) % 2) + odd
                col = LANES * ((m + 1) // 2)
                corr[(w + n) // 2, m * SUB : (m + 1) * SUB, col : col + taps.shape[1]] = fix[
                    n * SUB : (n + 1) * SUB
                ]


def fill_tables(weights, key_ref, even_ref, odd_ref):
    def fill(ref, origin, swap):
        height = ref.shape[0] if swap else ref.shape[0] // CQ
        width = ref.shape[1] // CQ if swap else ref.shape[1]
        shape = (height, width)
        tap = lax.broadcasted_iota(jnp.int32, shape, 1) - lax.broadcasted_iota(jnp.int32, shape, 0)
        for a in range(CQ):
            value = jnp.zeros(shape, jnp.float32)
            for c in range(CK):
                value = jnp.where(tap == c - origin, weights[a * CK + c], value)
            value = value.astype(jnp.bfloat16)
            if swap:
                ref[:, a * width : (a + 1) * width] = value
            else:
                ref[a * height : (a + 1) * height, :] = value

    fill(key_ref, CK // 2 + AHEAD, True)
    fill(even_ref, CK // 2 + 8 - BAND, False)
    fill(odd_ref, CK // 2 + 8 - SUB, False)


def attend_kernel(place, mix, weights, *refs):
    qk_refs, (va, vb, vc, vd), (mine, theirs) = refs[:2], refs[2:6], refs[6:8]
    v_all, q_wide, k_ref, corr = refs[8:12]
    tables, sem_v = refs[16:19], refs[19]
    side, core = place[2], place[1]
    b = pl.program_id(0)
    count = k_ref.shape[1] // (2 * ROWS)

    @pl.when(b == 0)
    def _():
        def copies_v():
            out = []
            for n, ref in enumerate((va, vb, vc, vd)):
                parity = core if n < 2 else 1 - core
                start = pl.multiple_of((side if n % 2 == 0 else 1 - side) * 2 * HD, 2 * HD)
                for i in range(count):
                    rows = pl.ds(pl.multiple_of((2 * i + parity) * ROWS, ROWS), ROWS)
                    target = v_all.at[rows, pl.ds(start, 2 * HD)]
                    out.append(pltpu.make_async_copy(ref.at[i], target, sem_v.at[n, i]))
            return out

        for copy in copies_v():
            copy.start()
        fill_tables(weights, *tables)
        prepare(core, *qk_refs, *tables, q_wide, k_ref, corr, *refs[12:16])
        for copy in copies_v():
            copy.wait()

    row = lax.broadcasted_iota(jnp.int32, (ROWS, ROWS), 0)
    col = lax.broadcasted_iota(jnp.int32, (ROWS, ROWS), 1)
    seen = col <= row
    top, low = slice(0, ROWS), slice(ROWS, 2 * ROWS)

    def fixed(part, n):
        return jnp.concatenate([part[:, :BAND], part[:, BAND:] - corr[n, :, :BAND]], 1)

    def rows_of(upper, lower):
        return jnp.concatenate([upper, lower], 0)

    def block(step):
        q_rows = q_wide[2 * step * ROWS : (2 * step + 2) * ROWS]
        parts = []
        for j in range(2 * step + 1):
            part = jnp.dot(
                q_rows,
                k_ref[:, j * ROWS : (j + 1) * ROWS],
                preferred_element_type=jnp.float32,
            )
            if j == 2 * step:
                diagonal = jnp.where(seen, part[top] - corr[2 * step, :, BAND:], -jnp.inf)
                part = rows_of(diagonal, fixed(part[low], 2 * step + 1))
            elif j == 2 * step - 1:
                part = rows_of(fixed(part[top], 2 * step), part[low])
            parts.append(part)
        start = (2 * step + 1) * ROWS
        last = jnp.dot(
            q_rows[low], k_ref[:, start : start + ROWS], preferred_element_type=jnp.float32
        )
        last = jnp.where(seen, last - corr[2 * step + 1, :, BAND:], -jnp.inf)
        peak = parts[0]
        for part in parts[1:]:
            peak = jnp.maximum(peak, part)
        peak = rows_of(peak[top], jnp.maximum(peak[low], last))
        peak = jnp.max(peak, axis=1, keepdims=True)
        mass = jnp.zeros((2 * ROWS, ROWS), jnp.float32)
        probs = []
        for part in parts:
            part = jnp.exp2(part - peak)
            mass = mass + part
            probs.append(part.astype(jnp.bfloat16))
        last = jnp.exp2(last - peak[low])
        mass = rows_of(mass[top], mass[low] + last)
        summed = jnp.dot(
            jnp.concatenate(probs, 1), v_all[:start], preferred_element_type=jnp.float32
        )
        extra = jnp.dot(
            last.astype(jnp.bfloat16),
            v_all[start : start + ROWS],
            preferred_element_type=jnp.float32,
        )
        inverse = 1.0 / jnp.sum(mass, axis=1, keepdims=True)
        halves = []
        for rows, total in ((top, summed[top]), (low, summed[low] + extra)):
            halves.append(
                jnp.concatenate(
                    [
                        total[:, g * HD : (g + 1) * HD] * (inverse[rows] * mix[g])
                        for g in range(GROUP)
                    ],
                    1,
                ).astype(jnp.bfloat16)
            )
        mine[0] = jnp.where(core == 0, halves[0], halves[1])
        theirs[0] = jnp.where(core == 0, halves[1], halves[0])

    for step in range(count):
        pl.when(b == step)(lambda step=step: block(step))


def attend_head(place, mix, weights, mine, other, values):
    total = 2 * mine.shape[0] * ROWS
    count = total // (2 * ROWS)
    depth = CQ * HD
    out = jax.ShapeDtypeStruct((count, ROWS, GROUP * HD), jnp.bfloat16)
    out_spec = pl.BlockSpec((1, ROWS, GROUP * HD), lambda b: (b, 0, 0))
    return pl.pallas_call(
        attend_kernel,
        grid=(count,),
        out_shape=(out, out),
        in_specs=[whole(pltpu.SMEM)] * 3 + [whole(pltpu.VMEM)] * 2 + [whole(pl.ANY)] * 4,
        out_specs=[out_spec, out_spec],
        scratch_shapes=[
            pltpu.VMEM((total, GROUP * HD), jnp.bfloat16),
            pltpu.VMEM((total, depth), jnp.bfloat16),
            pltpu.VMEM((depth, total), jnp.bfloat16),
            pltpu.VMEM((total // ROWS, ROWS, BAND + ROWS), jnp.float32),
            pltpu.VMEM((8 + total, HD), jnp.float32),
            pltpu.VMEM((AHEAD + total + LANES, HD), jnp.float32),
            pltpu.VMEM((2, total // 2, CQ * LANES), jnp.bfloat16),
            pltpu.VMEM((total, 2 * LANES), jnp.bfloat16),
        ]
        + [
            pltpu.VMEM(shape, jnp.bfloat16)
            for shape in ((2 * LANES, depth), (CQ * LANES, 2 * LANES), (CQ * LANES, LANES))
        ]
        + [pltpu.SemaphoreType.DMA((4, count))],
        compiler_params=kernel_params(56),
        cost_estimate=pl.CostEstimate(
            flops=total * total * (depth + GROUP * HD),
            bytes_accessed=16 * 2**20,
            transcendentals=total * total // 2,
        ),
    )(place, mix, weights, mine, other, *values)


def finish_kernel(place, own, r1, r2, r3, gain, *refs):
    w_parts, outs = refs[:12], refs[12:16]
    normed, w_buf, sem = refs[16:]
    width = w_parts[0].shape[1]
    core, head, inner = place[1], place[0], place[9]

    def copy_w(n, source):
        side = core if n % 2 == 0 else 1 - core
        cols = pl.ds(pl.multiple_of(side * width, width), width)
        target = w_buf.at[lax.bitwise_xor(place[5 + n // 2], head), :, cols]
        return pltpu.make_async_copy(w_parts[source], target, sem.at[n])

    for n in range(4):
        copy_w(n, n).start()
    for n in range(4, 8):
        straight = n if n < 6 else n + 2

        @pl.when(inner == 1)
        def _():
            copy_w(n, straight).start()

        @pl.when(inner == 0)
        def _():
            copy_w(n, straight + 2).start()

    near = own[...] + r1[...].astype(jnp.float32)
    far = r2[...].astype(jnp.float32) + r3[...].astype(jnp.float32)
    low = place[3] == 0
    for g in range(2 * GROUP):
        cols = slice((g % GROUP) * HD, (g % GROUP + 1) * HD)
        first = low if g < GROUP else jnp.logical_not(low)
        x = jnp.where(first, near[:, cols], far[:, cols])
        scale = lax.rsqrt(jnp.mean(x * x, axis=1, keepdims=True) + 1e-05)
        normed[:, g * HD : (g + 1) * HD] = (
            x * scale * gain[:, g * HD : (g + 1) * HD]
        ).astype(jnp.bfloat16)
    for n in range(8):
        copy_w(n, n).wait()
    for t in (3, 2, 1, 0):
        outs[t][...] = jnp.dot(
            normed[...], w_buf[t], preferred_element_type=jnp.float32
        ).astype(jnp.bfloat16)


def finish(place, own, r1, r2, r3, gain, w_parts):
    rows = own.shape[0]
    depth, width = w_parts[0].shape
    return pl.pallas_call(
        finish_kernel,
        in_specs=[whole(pltpu.SMEM)] + [whole(pltpu.VMEM)] * 5 + [whole(pl.ANY)] * 12,
        out_specs=[whole(pltpu.VMEM)] * 4,
        out_shape=[jax.ShapeDtypeStruct((rows, 2 * width), jnp.bfloat16)] * 4,
        scratch_shapes=[
            pltpu.VMEM((rows, depth), jnp.bfloat16),
            pltpu.VMEM((4, depth, 2 * width), jnp.bfloat16),
            pltpu.SemaphoreType.DMA((8,)),
        ],
        compiler_params=kernel_params(56),
        cost_estimate=pl.CostEstimate(
            flops=2 * rows * depth * 8 * width, bytes_accessed=11 * 2**20, transcendentals=0
        ),
    )(place, own, r1, r2, r3, gain, *w_parts)


def swapped(value, axis, mask):
    count = lax.axis_size(axis)
    return lax.ppermute(value, axis, [(i, i ^ mask) for i in range(count)])


def per_device_one_head(
    activations, positions, w_query, w_key, w_value, conv_kernel, head_mix, out_gain, w_out
):
    ctx, head = lax.axis_index("ctx"), lax.axis_index("head")
    z, core = ctx // 2, ctx % 2
    rows = activations.shape[0]
    half = rows // 2
    barrier = lax.optimization_barrier
    pair = 2 * HD

    def columns(target):
        parts = [
            lax.dynamic_slice_in_dim(w, target * pair, pair, 1) for w in (w_query, w_key, w_value)
        ]
        return jnp.concatenate(parts, 1)

    digits = jnp.stack([positions // 256, positions % 256]).astype(jnp.bfloat16)
    digits = jnp.pad(digits, ((0, 14), (0, activations.shape[1] - rows)))
    block = jnp.concatenate([activations, digits])
    w_pieces = jnp.stack([columns(target) for target in range(4)])
    far = [swapped(block, "ctx", 2 * s) for s in (1, 2, 3)]
    x0, y0 = swapped(activations, "head", 1), swapped(activations, "head", 2)
    weights = lax.dynamic_index_in_dim(conv_kernel, ctx, 0, keepdims=False)
    weights = weights * (math.log2(math.e) / math.sqrt(HD))
    place = jnp.stack([head, core, z % 2, z // 2, head, z, z ^ 1, z ^ 2, z ^ 3])
    place = place.astype(jnp.int32)
    far, x0, y0, w_pieces, weights, place, w_out = barrier(
        (far, x0, y0, w_pieces, weights, place, w_out)
    )

    same_core = [[i for i in range(8) if i % 2 == k] for k in range(2)]
    inside = [a[:rows] for a in far]
    to_x, to_y = jnp.concatenate(inside + [y0[half:]]), jnp.concatenate(inside + [x0[:half]])
    to_x, to_y, w_pieces = barrier((to_x, to_y, w_pieces))
    x_rest, y_rest = swapped(to_x, "head", 1), swapped(to_y, "head", 2)
    w_same = lax.all_to_all(w_pieces, "ctx", 0, 0, axis_index_groups=same_core)
    place_of = jnp.stack(
        [
            a[rows, :rows].astype(jnp.float32) * 256.0 + a[rows + 1, :rows].astype(jnp.float32)
            for a in [block] + far
        ]
    )
    exponents = jnp.arange(HD // 2, dtype=jnp.float32) * (2.0 / HD)
    inverse = jnp.exp(-exponents * math.log(500000.0))
    angle = (place_of * 0.25)[:, :, None] * inverse
    cosine, sine = jnp.cos(angle), jnp.sin(angle)
    cosine = jnp.concatenate([cosine, cosine], -1)
    sine = jnp.concatenate([-sine, sine], -1)
    middle = [(2, 4), (3, 5), (4, 2), (5, 3)]
    outward = [(2, 0), (3, 1), (4, 6), (5, 7)]
    out_near = swapped(w_out, "ctx", 2)
    x_rest, y_rest, cosine, sine, out_near, w_out = barrier(
        (x_rest, y_rest, cosine, sine, out_near, w_out)
    )
    c_low = swapped(x_rest[: 3 * half], "head", 2)
    c_high = swapped(y_rest[3 * half : 3 * rows], "head", 1)
    out_across = lax.ppermute(w_out, "ctx", middle)
    c_low, c_high, w_same, out_across = barrier((c_low, c_high, w_same, out_across))
    w_swap = swapped(w_same, "ctx", 1)
    sources = place, [activations] + list(far), (x0, x_rest, y0, y_rest, c_low, c_high), w_same, w_swap
    (v_pair,) = project(*sources)
    place, v_pair = barrier((place, v_pair))
    v_next = swapped(v_pair, "ctx", 2)
    v_pair_other = swapped(v_pair, "ctx", 1)
    out_across_next = lax.ppermute(out_near, "ctx", middle)
    out_passed = lax.ppermute(out_across, "ctx", outward)
    mine, theirs = project(place, *sources[1:], (cosine, sine))
    mine, theirs, v_next, v_pair_other = barrier((mine, theirs, v_next, v_pair_other))
    other = swapped(theirs, "ctx", 1)
    v_next_other = swapped(v_next, "ctx", 1)
    other, v_next_other, out_across_next, out_passed = barrier(
        (other, v_next_other, out_across_next, out_passed)
    )
    out_own_swap = swapped(w_out, "ctx", 1)
    out_passed_next = lax.ppermute(out_across_next, "ctx", outward)
    out_near_swap, out_across_swap = swapped(out_near, "ctx", 1), swapped(out_across, "ctx", 1)
    group_rows = lax.dynamic_slice_in_dim(head_mix, GROUP * (ctx // GROUP), GROUP, 0)
    mix = lax.dynamic_index_in_dim(group_rows, ctx % GROUP, 1, keepdims=False)
    out_mine, out_theirs = attend_head(
        place, mix, weights, mine, other, (v_pair, v_next, v_pair_other, v_next_other)
    )
    out_mine, out_theirs, out_passed_next, out_own_swap, out_near_swap, out_across_swap = barrier(
        (out_mine, out_theirs, out_passed_next, out_own_swap, out_near_swap, out_across_swap)
    )
    out_parts = [w_out, out_own_swap, out_near, out_near_swap, out_across, out_across_swap]
    for part in (out_passed, out_across_next, out_passed_next):
        out_parts += [part, swapped(part, "ctx", 1)]
    summed = out_mine.astype(jnp.float32) + swapped(out_theirs, "ctx", 1).astype(jnp.float32)
    own = lax.dynamic_index_in_dim(summed, z, 0, keepdims=False)
    r1, r2, r3 = [
        swapped(
            lax.dynamic_index_in_dim(summed, z ^ s, 0, keepdims=False).astype(jnp.bfloat16),
            "ctx",
            2 * s,
        )
        for s in (1, 2, 3)
    ]
    inner = (z == 1) | (z == 2)
    out_places = jnp.stack(
        [z, z ^ 1, jnp.where(inner, z ^ 3, z ^ 2), jnp.where(inner, z ^ 2, z ^ 3), inner]
    )
    where = jnp.concatenate([place[:5], out_places.astype(jnp.int32)])
    shares = finish(where, own, r1, r2, r3, out_gain.reshape(1, -1), out_parts)
    total = shares[0].astype(jnp.float32)
    for t in (1, 2, 3):
        total = total + swapped(shares[t], "head", t).astype(jnp.float32)
    return total.astype(jnp.bfloat16)


def solution(mesh):
    one_head_each = mesh.shape["ctx"] == 8 and mesh.shape["head"] == 4
    body = per_device_one_head if one_head_each else per_device
    return jax.shard_map(
        body,
        mesh=mesh,
        in_specs=(
            P("ctx", "head"),
            P("ctx"),
            P("ctx", "head"),
            P("ctx", "head"),
            P("ctx", "head"),
            P("head", None),
            P("head", None),
            P("head"),
            P("head", "ctx"),
        ),
        out_specs=P("ctx", "head"),
        check_vma=False,
    )
```

```python
import functools
import math

import jax
import jax.numpy as jnp
from jax import lax
from jax.experimental import pallas as pl
from jax.experimental.pallas import tpu as pltpu
from jax.sharding import PartitionSpec as P

HD = 128
GROUP = 4
CQ = 6
CK = 11
KB = 512


def passed_along(value, axis, steps):
    count = lax.axis_size(axis)
    leading, last = (max(0, -steps), min(count, count - steps))
    return lax.ppermute(value, axis, [(source, source + steps) for source in range(leading, last)])


def rope(projected, positions):
    row_count = projected.shape[0]
    head_count = projected.shape[1] // HD
    shaped = projected.reshape(row_count, head_count, HD)
    half_size = HD // 2
    exponents = jnp.arange(half_size, dtype=jnp.float32) * (2.0 / HD)
    inverse = jnp.exp(-exponents * math.log(500000.0))
    angle = (positions.astype(jnp.float32) * 0.25)[:, None, None] * inverse[None, None, :]
    cosine = jnp.cos(angle)
    sine = jnp.sin(angle)
    lower_half = shaped[..., :half_size]
    upper_half = shaped[..., half_size:]
    rotated_rows = jnp.concatenate(
        [lower_half * cosine - upper_half * sine, upper_half * cosine + lower_half * sine], -1
    )
    return rotated_rows.reshape(row_count, head_count * HD)


def convolve(masked, kernel, row_count, col_count):
    summed = jnp.zeros((masked.shape[0], row_count, col_count), jnp.float32)
    for lag_q in range(CQ):
        for lag_k in range(CK):
            weight = kernel[:, lag_q * CK + lag_k][:, None, None]
            window = masked[
                :,
                CQ - 1 - lag_q : CQ - 1 - lag_q + row_count,
                CK - 1 - lag_k : CK - 1 - lag_k + col_count,
            ]
            summed = summed + weight * window
    return summed


def add_rows(left, piece):
    return jnp.dot(left, piece, preferred_element_type=jnp.float32)


def share_keys(key, value):
    return (
        lax.all_gather(key, "ctx", axis=0, tiled=True),
        lax.all_gather(value, "ctx", axis=0, tiled=True),
    )


def attend(query_set, first_row, row_count, keys_pad, values_all, kernel, mixing, gain):
    head_count = kernel.shape[0]
    ext_rows = row_count + CQ - 1
    query_heads = query_set.reshape(ext_rows, head_count, HD)
    token_total = values_all.shape[0]
    block_count = token_total // KB
    last_row = first_row + row_count - 1
    scale = 1.0 / math.sqrt(HD)
    prow = first_row - (CQ - 1) + jnp.arange(ext_rows, dtype=jnp.int32)
    irow = first_row + jnp.arange(row_count, dtype=jnp.int32)

    def logits_of(block):
        key_start = block * KB
        key_block = lax.dynamic_slice_in_dim(keys_pad, key_start, KB + CK - 1, 0).reshape(
            KB + CK - 1, head_count, HD
        )
        scores = (
            jnp.einsum("rhd,khd->hrk", query_heads, key_block, preferred_element_type=jnp.float32)
            * scale
        )
        kcol = key_start - CK // 2 + jnp.arange(KB + CK - 1, dtype=jnp.int32)
        valid = (kcol[None, :] <= prow[:, None]) & (prow[:, None] >= 0)
        masked = jnp.where(valid[None], scores, 0.0)
        conv = convolve(masked, kernel, row_count, KB)
        jcol = key_start + jnp.arange(KB, dtype=jnp.int32)
        return jnp.where((jcol[None, :] <= irow[:, None])[None], conv, -jnp.inf)

    def first_pass(block, carry_in):

        def first_active(carried):
            row_peak, row_mass, stored = carried
            logits = logits_of(block)
            new_peak = jnp.maximum(row_peak, jnp.max(logits, axis=-1))
            new_mass = row_mass * jnp.exp(row_peak - new_peak) + jnp.sum(
                jnp.exp(logits - new_peak[..., None]), axis=-1
            )
            stored = lax.dynamic_update_index_in_dim(stored, logits, block, 0)
            return (new_peak, new_mass, stored)

        return lax.cond(block * KB <= last_row, first_active, lambda carried: carried, carry_in)

    peak_start = jnp.full((head_count, row_count), -jnp.inf, jnp.float32)
    mass_start = jnp.zeros((head_count, row_count), jnp.float32)
    store_start = jnp.zeros((block_count, head_count, row_count, KB), jnp.float32)
    row_peak, row_mass, stored = lax.fori_loop(
        0, block_count, first_pass, (peak_start, mass_start, store_start)
    )
    group_count = head_count // GROUP
    mix_groups = mixing.reshape(group_count, GROUP, GROUP)

    def second_pass(block, carry_in):

        def second_active(summed):
            logits = lax.dynamic_index_in_dim(stored, block, 0, keepdims=False)
            probs = jnp.exp(logits - row_peak[..., None]) / row_mass[..., None]
            grouped = probs.reshape(group_count, GROUP, row_count, KB)
            mixed_scores = (
                jnp.einsum("gab,gbrk->gark", mix_groups, grouped)
                .reshape(head_count, row_count, KB)
                .astype(jnp.bfloat16)
            )
            value_block = lax.dynamic_slice_in_dim(values_all, block * KB, KB, 0).reshape(
                KB, head_count, HD
            )
            return summed + jnp.einsum(
                "hrk,khd->rhd", mixed_scores, value_block, preferred_element_type=jnp.float32
            )

        return lax.cond(block * KB <= last_row, second_active, lambda summed: summed, carry_in)

    summed = lax.fori_loop(
        0, block_count, second_pass, jnp.zeros((row_count, head_count, HD), jnp.float32)
    )
    rms = jnp.sqrt(jnp.mean(summed * summed, axis=-1, keepdims=True) + 1e-05)
    normed = (summed / rms * gain.reshape(head_count, HD)).astype(jnp.bfloat16)
    return normed.reshape(row_count, head_count * HD)


def per_device(
    activations, positions, w_query, w_key, w_value, conv_kernel, head_mix, out_gain, w_out
):
    row_count = activations.shape[0]
    ctx_place = lax.axis_index("ctx")
    features = lax.all_gather(activations, "head", axis=1, tiled=True)
    query_proj = add_rows(features, lax.all_gather(w_query, "ctx", axis=0, tiled=True))
    key_proj = add_rows(features, lax.all_gather(w_key, "ctx", axis=0, tiled=True))
    value_proj = add_rows(features, lax.all_gather(w_value, "ctx", axis=0, tiled=True))
    key = rope(key_proj, positions).astype(jnp.bfloat16)
    value = value_proj.astype(jnp.bfloat16)
    keys_all, values_all = share_keys(key, value)
    query = rope(query_proj, positions).astype(jnp.bfloat16)
    rim_rows = passed_along(query[row_count - (CQ - 1) :], "ctx", 1)
    query_ext = jnp.concatenate([rim_rows, query], 0)
    keys_pad = jnp.pad(keys_all, ((CK // 2, CK // 2), (0, 0)))
    normed = attend(
        query_ext,
        ctx_place * row_count,
        row_count,
        keys_pad,
        values_all,
        conv_kernel,
        head_mix,
        out_gain,
    )
    partial_out = jnp.dot(
        normed, lax.all_gather(w_out, "ctx", axis=1, tiled=True), preferred_element_type=jnp.float32
    )
    return lax.psum_scatter(
        partial_out.astype(jnp.bfloat16), "head", scatter_dimension=1, tiled=True
    )


ROWS = 256
BAND = 128
LANES = 128
SUB = 64
AHEAD = 16


def kernel_params(mebibytes):
    return pltpu.CompilerParams(vmem_limit_bytes=mebibytes * 1024 * 1024)


def whole(memory_space):
    return pl.BlockSpec(memory_space=memory_space)


def project_kernel(rows, first_col, place, *refs):
    a_own, (x0, x_rest, y0, y_rest, c_low, c_high) = refs[:4], refs[4:10]
    w_same, w_swap = refs[10:12]
    abuf, wbuf, acc, sem_a, sem_w = refs[-5:]
    turn, core = place[0], place[1]
    half = w_same.shape[1]
    width = wbuf.shape[2]

    def copies_a(t):
        if t == 0:
            pairs = [(a_own[b], 0, b * rows, rows) for b in range(4)]
        elif t < 3:
            first, others = ((x0, x_rest), (y0, y_rest))[t - 1]
            pairs = [(first, 0, 0, rows), (others, 0, rows, 3 * rows)]
        else:
            late, mid = 3 * rows, rows // 2
            pairs = [(y_rest, late, 0, mid), (x_rest, late, mid, mid)]
            pairs += [(c_low, 0, rows, 3 * mid), (c_high, 0, rows + 3 * mid, 3 * mid)]
        return [
            pltpu.make_async_copy(
                ref.at[pl.ds(source, size)], abuf.at[t, pl.ds(target, size)], sem_a.at[t, n]
            )
            for n, (ref, source, target, size) in enumerate(pairs)
        ]

    def copies_w(t):
        out = []
        for n, (ref, side) in enumerate(((w_same, core), (w_swap, 1 - core))):
            source = ref.at[lax.bitwise_xor(turn, t), :, pl.ds(first_col, width)]
            target = wbuf.at[t, pl.ds(pl.multiple_of(side * half, half), half)]
            out.append(pltpu.make_async_copy(source, target, sem_w.at[t, n]))
        return out

    for t in range(4):
        for copy in copies_w(t) + copies_a(t):
            copy.start()
    for t in range(4):
        for copy in copies_w(t) + copies_a(t):
            copy.wait()
        part = jnp.dot(abuf[t], wbuf[t], preferred_element_type=jnp.float32)
        acc[...] = part if t == 0 else acc[...] + part
    if first_col:
        v_out = refs[12]
        for b in range(4):
            v_out[place[5 + b]] = acc[b * rows : (b + 1) * rows].astype(jnp.bfloat16)
        return
    cos_ref, sin_ref, mine, theirs = refs[12:16]
    first = core == 0
    for b in range(4):
        total = acc[b * rows : (b + 1) * rows]
        cosine, sine = cos_ref[b], sin_ref[b]
        at = place[5 + b]
        for col, out in ((0, 0), (2 * HD, HD)):
            heads = []
            for start in (col, col + HD):
                x = total[:, start : start + HD]
                x = x * cosine + pltpu.roll(x, HD // 2, 1) * sine
                heads.append(x.astype(jnp.bfloat16))
            mine[at, :, out : out + HD] = jnp.where(first, heads[0], heads[1])
            theirs[at, :, out : out + HD] = jnp.where(first, heads[1], heads[0])


def project(place, a_own, a_plane, w_same, w_swap, angles=()):
    rows, depth = a_own[0].shape
    first_col, width = (0, 4 * HD) if angles else (4 * HD, 2 * HD)
    out = jax.ShapeDtypeStruct((4, rows, 2 * HD), jnp.bfloat16)
    count = 2 if angles else 1
    return pl.pallas_call(
        functools.partial(project_kernel, rows, first_col),
        out_shape=[out] * count,
        in_specs=[whole(pltpu.SMEM)]
        + [whole(pl.ANY)] * 12
        + [whole(pltpu.VMEM)] * len(angles),
        out_specs=[whole(pltpu.VMEM)] * count,
        scratch_shapes=[
            pltpu.VMEM((4, 4 * rows, depth), jnp.bfloat16),
            pltpu.VMEM((4, depth, width), jnp.bfloat16),
            pltpu.VMEM((4 * rows, width), jnp.float32),
            pltpu.SemaphoreType.DMA((4, 4)),
            pltpu.SemaphoreType.DMA((4, 2)),
        ],
        compiler_params=kernel_params(56),
        cost_estimate=pl.CostEstimate(
            flops=8 * rows * 4 * depth * width, bytes_accessed=16 * 2**20, transcendentals=0
        ),
    )(place, *a_own, *a_plane, w_same, w_swap, *angles)


def prepare(core, mine, other, key_ref, even_ref, odd_ref, q_out, k_out, corr, *scratch):
    qf, kf, lags, turned = scratch
    total = q_out.shape[0]
    qf[0:8] = jnp.zeros((8, HD), jnp.float32)
    kf[0:AHEAD] = jnp.zeros((AHEAD, HD), jnp.float32)
    kf[AHEAD + total :] = jnp.zeros((kf.shape[0] - AHEAD - total, HD), jnp.float32)
    corr[...] = jnp.zeros(corr.shape, jnp.float32)
    for i in range(total // (2 * ROWS)):
        for ref, parity in ((mine, core), (other, 1 - core)):
            start = pl.multiple_of((2 * i + parity) * ROWS, ROWS)
            block = ref[i].astype(jnp.float32)
            qf[pl.ds(8 + start, ROWS)] = block[:, :HD]
            kf[pl.ds(AHEAD + start, ROWS)] = block[:, HD:]

    ahead = lax.broadcasted_iota(jnp.int32, (SUB + 8, LANES), 1) - lax.broadcasted_iota(
        jnp.int32, (SUB + 8, LANES), 0
    )
    near = (ahead >= 1) & (ahead < CQ + CK // 2)
    steps = total // LANES
    for w in range(steps):
        base = w * LANES
        window = kf[base : base + 2 * LANES].T
        turned[base : base + LANES] = window.astype(jnp.bfloat16)
        for odd in range(2):
            at = base + odd * SUB
            qwin = qf[at : at + SUB + 8]
            kwin = kf[at + AHEAD - 8 : at + AHEAD - 8 + LANES]
            scores = lax.dot_general(
                qwin.astype(jnp.bfloat16),
                kwin.astype(jnp.bfloat16),
                (((1,), (1,)), ((), ())),
                preferred_element_type=jnp.float32,
            )
            future = jnp.where(near, scores, 0.0)
            for a in range(CQ):
                cols = slice(a * LANES, (a + 1) * LANES)
                lags[odd, w * SUB : (w + 1) * SUB, cols] = future[8 - a : 8 - a + SUB].astype(
                    jnp.bfloat16
                )
                q_out[at : at + SUB, cols] = qwin[8 - a : 8 - a + SUB].astype(jnp.bfloat16)
    for w in range(0, steps, 4):
        wide = jnp.dot(
            turned[w * LANES : (w + 4) * LANES], key_ref[...], preferred_element_type=jnp.float32
        )
        for n in range(4):
            cols = slice((w + n) * LANES, (w + n + 1) * LANES)
            for a in range(CQ):
                k_out[a * HD : (a + 1) * HD, cols] = wide[
                    n * LANES : (n + 1) * LANES, a * LANES : (a + 1) * LANES
                ].astype(jnp.bfloat16)
    for odd, taps in enumerate((even_ref, odd_ref)):
        for w in range(0, steps, 8):
            fix = jnp.dot(
                lags[odd, w * SUB : (w + 8) * SUB], taps[...], preferred_element_type=jnp.float32
            )
            for n in range(8):
                m = 2 * ((w + n) % 2) + odd
                col = LANES * ((m + 1) // 2)
                corr[(w + n) // 2, m * SUB : (m + 1) * SUB, col : col + taps.shape[1]] = fix[
                    n * SUB : (n + 1) * SUB
                ]


def fill_tables(weights, key_ref, even_ref, odd_ref):
    def fill(ref, origin, swap):
        height = ref.shape[0] if swap else ref.shape[0] // CQ
        width = ref.shape[1] // CQ if swap else ref.shape[1]
        shape = (height, width)
        tap = lax.broadcasted_iota(jnp.int32, shape, 1) - lax.broadcasted_iota(jnp.int32, shape, 0)
        for a in range(CQ):
            value = jnp.zeros(shape, jnp.float32)
            for c in range(CK):
                value = jnp.where(tap == c - origin, weights[a * CK + c], value)
            value = value.astype(jnp.bfloat16)
            if swap:
                ref[:, a * width : (a + 1) * width] = value
            else:
                ref[a * height : (a + 1) * height, :] = value

    fill(key_ref, CK // 2 + AHEAD, True)
    fill(even_ref, CK // 2 + 8 - BAND, False)
    fill(odd_ref, CK // 2 + 8 - SUB, False)


def attend_kernel(place, mix, weights, *refs):
    qk_refs, (va, vb, vc, vd), (mine, theirs) = refs[:2], refs[2:6], refs[6:8]
    v_all, q_wide, k_ref, corr = refs[8:12]
    tables, sem_v = refs[16:19], refs[19]
    side, core = place[2], place[1]
    b = pl.program_id(0)
    count = k_ref.shape[1] // (2 * ROWS)

    @pl.when(b == 0)
    def _():
        def copies_v():
            out = []
            for n, ref in enumerate((va, vb, vc, vd)):
                parity = core if n < 2 else 1 - core
                start = pl.multiple_of((side if n % 2 == 0 else 1 - side) * 2 * HD, 2 * HD)
                for i in range(count):
                    rows = pl.ds(pl.multiple_of((2 * i + parity) * ROWS, ROWS), ROWS)
                    target = v_all.at[rows, pl.ds(start, 2 * HD)]
                    out.append(pltpu.make_async_copy(ref.at[i], target, sem_v.at[n, i]))
            return out

        for copy in copies_v():
            copy.start()
        fill_tables(weights, *tables)
        prepare(core, *qk_refs, *tables, q_wide, k_ref, corr, *refs[12:16])
        for copy in copies_v():
            copy.wait()

    row = lax.broadcasted_iota(jnp.int32, (ROWS, ROWS), 0)
    col = lax.broadcasted_iota(jnp.int32, (ROWS, ROWS), 1)
    seen = col <= row
    top, low = slice(0, ROWS), slice(ROWS, 2 * ROWS)

    def fixed(part, n):
        return jnp.concatenate([part[:, :BAND], part[:, BAND:] - corr[n, :, :BAND]], 1)

    def rows_of(upper, lower):
        return jnp.concatenate([upper, lower], 0)

    def block(step):
        q_rows = q_wide[2 * step * ROWS : (2 * step + 2) * ROWS]
        parts = []
        for j in range(2 * step + 1):
            part = jnp.dot(
                q_rows,
                k_ref[:, j * ROWS : (j + 1) * ROWS],
                preferred_element_type=jnp.float32,
            )
            if j == 2 * step:
                diagonal = jnp.where(seen, part[top] - corr[2 * step, :, BAND:], -jnp.inf)
                part = rows_of(diagonal, fixed(part[low], 2 * step + 1))
            elif j == 2 * step - 1:
                part = rows_of(fixed(part[top], 2 * step), part[low])
            parts.append(part)
        start = (2 * step + 1) * ROWS
        last = jnp.dot(
            q_rows[low], k_ref[:, start : start + ROWS], preferred_element_type=jnp.float32
        )
        last = jnp.where(seen, last - corr[2 * step + 1, :, BAND:], -jnp.inf)
        peak = parts[0]
        for part in parts[1:]:
            peak = jnp.maximum(peak, part)
        peak = rows_of(peak[top], jnp.maximum(peak[low], last))
        peak = jnp.max(peak, axis=1, keepdims=True)
        mass = jnp.zeros((2 * ROWS, ROWS), jnp.float32)
        probs = []
        for part in parts:
            part = jnp.exp2(part - peak)
            mass = mass + part
            probs.append(part.astype(jnp.bfloat16))
        last = jnp.exp2(last - peak[low])
        mass = rows_of(mass[top], mass[low] + last)
        summed = jnp.dot(
            jnp.concatenate(probs, 1), v_all[:start], preferred_element_type=jnp.float32
        )
        extra = jnp.dot(
            last.astype(jnp.bfloat16),
            v_all[start : start + ROWS],
            preferred_element_type=jnp.float32,
        )
        inverse = 1.0 / jnp.sum(mass, axis=1, keepdims=True)
        halves = []
        for rows, total in ((top, summed[top]), (low, summed[low] + extra)):
            halves.append(
                jnp.concatenate(
                    [
                        total[:, g * HD : (g + 1) * HD] * (inverse[rows] * mix[g])
                        for g in range(GROUP)
                    ],
                    1,
                ).astype(jnp.bfloat16)
            )
        mine[0] = jnp.where(core == 0, halves[0], halves[1])
        theirs[0] = jnp.where(core == 0, halves[1], halves[0])

    for step in range(count):
        pl.when(b == step)(lambda step=step: block(step))


def attend_head(place, mix, weights, mine, other, values):
    total = 2 * mine.shape[0] * ROWS
    count = total // (2 * ROWS)
    depth = CQ * HD
    out = jax.ShapeDtypeStruct((count, ROWS, GROUP * HD), jnp.bfloat16)
    out_spec = pl.BlockSpec((1, ROWS, GROUP * HD), lambda b: (b, 0, 0))
    return pl.pallas_call(
        attend_kernel,
        grid=(count,),
        out_shape=(out, out),
        in_specs=[whole(pltpu.SMEM)] * 3 + [whole(pltpu.VMEM)] * 2 + [whole(pl.ANY)] * 4,
        out_specs=[out_spec, out_spec],
        scratch_shapes=[
            pltpu.VMEM((total, GROUP * HD), jnp.bfloat16),
            pltpu.VMEM((total, depth), jnp.bfloat16),
            pltpu.VMEM((depth, total), jnp.bfloat16),
            pltpu.VMEM((total // ROWS, ROWS, BAND + ROWS), jnp.float32),
            pltpu.VMEM((8 + total, HD), jnp.float32),
            pltpu.VMEM((AHEAD + total + LANES, HD), jnp.float32),
            pltpu.VMEM((2, total // 2, CQ * LANES), jnp.bfloat16),
            pltpu.VMEM((total, 2 * LANES), jnp.bfloat16),
        ]
        + [
            pltpu.VMEM(shape, jnp.bfloat16)
            for shape in ((2 * LANES, depth), (CQ * LANES, 2 * LANES), (CQ * LANES, LANES))
        ]
        + [pltpu.SemaphoreType.DMA((4, count))],
        compiler_params=kernel_params(56),
        cost_estimate=pl.CostEstimate(
            flops=total * total * (depth + GROUP * HD),
            bytes_accessed=16 * 2**20,
            transcendentals=total * total // 2,
        ),
    )(place, mix, weights, mine, other, *values)


def finish_kernel(place, own, r1, r2, r3, gain, w_any, o0, o1, o2, o3, normed, w_buf, sem):
    blocks, _, width = w_buf.shape
    per = blocks // 4
    order = [(t, i) for t in (3, 2, 1, 0) for i in range(per)]

    def copy_w(n):
        t, i = order[n]
        source = per * lax.bitwise_xor(place[0], t) + i
        return pltpu.make_async_copy(w_any.at[source], w_buf.at[n], sem.at[n])

    for n in range(blocks):
        copy_w(n).start()
    near = own[...] + r1[...].astype(jnp.float32)
    far = r2[...].astype(jnp.float32) + r3[...].astype(jnp.float32)
    low = place[3] == 0
    for g in range(2 * GROUP):
        cols = slice((g % GROUP) * HD, (g % GROUP + 1) * HD)
        first = low if g < GROUP else jnp.logical_not(low)
        x = jnp.where(first, near[:, cols], far[:, cols])
        scale = lax.rsqrt(jnp.mean(x * x, axis=1, keepdims=True) + 1e-05)
        normed[:, g * HD : (g + 1) * HD] = (
            x * scale * gain[:, g * HD : (g + 1) * HD]
        ).astype(jnp.bfloat16)
    for n in range(blocks):
        t, i = order[n]
        copy_w(n).wait()
        (o0, o1, o2, o3)[t][:, i * width : (i + 1) * width] = jnp.dot(
            normed[...], w_buf[n], preferred_element_type=jnp.float32
        ).astype(jnp.bfloat16)


def finish(place, own, r1, r2, r3, gain, w_all):
    rows = own.shape[0]
    blocks, depth, width = w_all.shape
    return pl.pallas_call(
        finish_kernel,
        in_specs=[whole(pltpu.SMEM)] + [whole(pltpu.VMEM)] * 5 + [whole(pl.ANY)],
        out_specs=[whole(pltpu.VMEM)] * 4,
        out_shape=[jax.ShapeDtypeStruct((rows, blocks // 4 * width), jnp.bfloat16)] * 4,
        scratch_shapes=[
            pltpu.VMEM((rows, depth), jnp.bfloat16),
            pltpu.VMEM((blocks, depth, width), jnp.bfloat16),
            pltpu.SemaphoreType.DMA((blocks,)),
        ],
        compiler_params=kernel_params(56),
        cost_estimate=pl.CostEstimate(
            flops=2 * rows * depth * blocks * width, bytes_accessed=11 * 2**20, transcendentals=0
        ),
    )(place, own, r1, r2, r3, gain, w_all)


def swapped(value, axis, mask):
    count = lax.axis_size(axis)
    return lax.ppermute(value, axis, [(i, i ^ mask) for i in range(count)])


def per_device_one_head(
    activations, positions, w_query, w_key, w_value, conv_kernel, head_mix, out_gain, w_out
):
    ctx, head = lax.axis_index("ctx"), lax.axis_index("head")
    z, core = ctx // 2, ctx % 2
    rows = activations.shape[0]
    half = rows // 2
    barrier = lax.optimization_barrier
    pair = 2 * HD

    def columns(target):
        parts = [
            lax.dynamic_slice_in_dim(w, target * pair, pair, 1) for w in (w_query, w_key, w_value)
        ]
        return jnp.concatenate(parts, 1)

    digits = jnp.stack([positions // 256, positions % 256]).astype(jnp.bfloat16)
    digits = jnp.pad(digits, ((0, 14), (0, activations.shape[1] - rows)))
    block = jnp.concatenate([activations, digits])
    w_pieces = jnp.stack([columns(target) for target in range(4)])
    far = [swapped(block, "ctx", 2 * s) for s in (1, 2, 3)]
    x0, y0 = swapped(activations, "head", 1), swapped(activations, "head", 2)
    weights = lax.dynamic_index_in_dim(conv_kernel, ctx, 0, keepdims=False)
    weights = weights * (math.log2(math.e) / math.sqrt(HD))
    place = jnp.stack([head, core, z % 2, z // 2, head, z, z ^ 1, z ^ 2, z ^ 3])
    place = place.astype(jnp.int32)
    far, x0, y0, w_pieces, weights, place, w_out = barrier(
        (far, x0, y0, w_pieces, weights, place, w_out)
    )

    same_core = [[i for i in range(8) if i % 2 == k] for k in range(2)]
    inside = [a[:rows] for a in far]
    to_x, to_y = jnp.concatenate(inside + [y0[half:]]), jnp.concatenate(inside + [x0[:half]])
    to_x, to_y, w_pieces = barrier((to_x, to_y, w_pieces))
    x_rest, y_rest = swapped(to_x, "head", 1), swapped(to_y, "head", 2)
    w_same = lax.all_to_all(w_pieces, "ctx", 0, 0, axis_index_groups=same_core)
    place_of = jnp.stack(
        [
            a[rows, :rows].astype(jnp.float32) * 256.0 + a[rows + 1, :rows].astype(jnp.float32)
            for a in [block] + far
        ]
    )
    exponents = jnp.arange(HD // 2, dtype=jnp.float32) * (2.0 / HD)
    inverse = jnp.exp(-exponents * math.log(500000.0))
    angle = (place_of * 0.25)[:, :, None] * inverse
    cosine, sine = jnp.cos(angle), jnp.sin(angle)
    cosine = jnp.concatenate([cosine, cosine], -1)
    sine = jnp.concatenate([-sine, sine], -1)
    x_rest, y_rest, cosine, sine, w_out = barrier((x_rest, y_rest, cosine, sine, w_out))
    c_low = swapped(x_rest[: 3 * half], "head", 2)
    c_high = swapped(y_rest[3 * half : 3 * rows], "head", 1)
    c_low, c_high, w_same, w_out = barrier((c_low, c_high, w_same, w_out))
    w_all = lax.all_gather(w_out, "ctx", axis=0)
    w_swap = swapped(w_same, "ctx", 1)
    sources = place, [activations] + list(far), (x0, x_rest, y0, y_rest, c_low, c_high), w_same, w_swap
    (v_pair,) = project(*sources)
    place, v_pair = barrier((place, v_pair))
    v_next = swapped(v_pair, "ctx", 2)
    v_pair_other = swapped(v_pair, "ctx", 1)
    mine, theirs = project(place, *sources[1:], (cosine, sine))
    mine, theirs, v_next, v_pair_other = barrier((mine, theirs, v_next, v_pair_other))
    other = swapped(theirs, "ctx", 1)
    v_next_other = swapped(v_next, "ctx", 1)
    group_rows = lax.dynamic_slice_in_dim(head_mix, GROUP * (ctx // GROUP), GROUP, 0)
    mix = lax.dynamic_index_in_dim(group_rows, ctx % GROUP, 1, keepdims=False)
    out_mine, out_theirs = attend_head(
        place, mix, weights, mine, other, (v_pair, v_next, v_pair_other, v_next_other)
    )
    summed = out_mine.astype(jnp.float32) + swapped(out_theirs, "ctx", 1).astype(jnp.float32)
    own = lax.dynamic_index_in_dim(summed, z, 0, keepdims=False)
    r1, r2, r3 = [
        swapped(
            lax.dynamic_index_in_dim(summed, z ^ s, 0, keepdims=False).astype(jnp.bfloat16),
            "ctx",
            2 * s,
        )
        for s in (1, 2, 3)
    ]
    shares = finish(place, own, r1, r2, r3, out_gain.reshape(1, -1), w_all)
    total = shares[0].astype(jnp.float32)
    for t in (1, 2, 3):
        total = total + swapped(shares[t], "head", t).astype(jnp.float32)
    return total.astype(jnp.bfloat16)


def solution(mesh):
    one_head_each = mesh.shape["ctx"] == 8 and mesh.shape["head"] == 4
    body = per_device_one_head if one_head_each else per_device
    return jax.shard_map(
        body,
        mesh=mesh,
        in_specs=(
            P("ctx", "head"),
            P("ctx"),
            P("ctx", "head"),
            P("ctx", "head"),
            P("ctx", "head"),
            P("head", None),
            P("head", None),
            P("head"),
            P("head", "ctx"),
        ),
        out_specs=P("ctx", "head"),
        check_vma=False,
    )
```

```python
import functools
import math

import jax
import jax.numpy as jnp
from jax import lax
from jax.experimental import pallas as pl
from jax.experimental.pallas import tpu as pltpu
from jax.sharding import PartitionSpec as P

HD = 128
GROUP = 4
CQ = 6
CK = 11
KB = 512


def passed_along(value, axis, steps):
    count = lax.axis_size(axis)
    leading, last = (max(0, -steps), min(count, count - steps))
    return lax.ppermute(value, axis, [(source, source + steps) for source in range(leading, last)])


def rope(projected, positions):
    row_count = projected.shape[0]
    head_count = projected.shape[1] // HD
    shaped = projected.reshape(row_count, head_count, HD)
    half_size = HD // 2
    exponents = jnp.arange(half_size, dtype=jnp.float32) * (2.0 / HD)
    inverse = jnp.exp(-exponents * math.log(500000.0))
    angle = (positions.astype(jnp.float32) * 0.25)[:, None, None] * inverse[None, None, :]
    cosine = jnp.cos(angle)
    sine = jnp.sin(angle)
    lower_half = shaped[..., :half_size]
    upper_half = shaped[..., half_size:]
    rotated_rows = jnp.concatenate(
        [lower_half * cosine - upper_half * sine, upper_half * cosine + lower_half * sine], -1
    )
    return rotated_rows.reshape(row_count, head_count * HD)


def convolve(masked, kernel, row_count, col_count):
    summed = jnp.zeros((masked.shape[0], row_count, col_count), jnp.float32)
    for lag_q in range(CQ):
        for lag_k in range(CK):
            weight = kernel[:, lag_q * CK + lag_k][:, None, None]
            window = masked[
                :,
                CQ - 1 - lag_q : CQ - 1 - lag_q + row_count,
                CK - 1 - lag_k : CK - 1 - lag_k + col_count,
            ]
            summed = summed + weight * window
    return summed


def add_rows(left, piece):
    return jnp.dot(left, piece, preferred_element_type=jnp.float32)


def share_keys(key, value):
    return (
        lax.all_gather(key, "ctx", axis=0, tiled=True),
        lax.all_gather(value, "ctx", axis=0, tiled=True),
    )


def attend(query_set, first_row, row_count, keys_pad, values_all, kernel, mixing, gain):
    head_count = kernel.shape[0]
    ext_rows = row_count + CQ - 1
    query_heads = query_set.reshape(ext_rows, head_count, HD)
    token_total = values_all.shape[0]
    block_count = token_total // KB
    last_row = first_row + row_count - 1
    scale = 1.0 / math.sqrt(HD)
    prow = first_row - (CQ - 1) + jnp.arange(ext_rows, dtype=jnp.int32)
    irow = first_row + jnp.arange(row_count, dtype=jnp.int32)

    def logits_of(block):
        key_start = block * KB
        key_block = lax.dynamic_slice_in_dim(keys_pad, key_start, KB + CK - 1, 0).reshape(
            KB + CK - 1, head_count, HD
        )
        scores = (
            jnp.einsum("rhd,khd->hrk", query_heads, key_block, preferred_element_type=jnp.float32)
            * scale
        )
        kcol = key_start - CK // 2 + jnp.arange(KB + CK - 1, dtype=jnp.int32)
        valid = (kcol[None, :] <= prow[:, None]) & (prow[:, None] >= 0)
        masked = jnp.where(valid[None], scores, 0.0)
        conv = convolve(masked, kernel, row_count, KB)
        jcol = key_start + jnp.arange(KB, dtype=jnp.int32)
        return jnp.where((jcol[None, :] <= irow[:, None])[None], conv, -jnp.inf)

    def first_pass(block, carry_in):

        def first_active(carried):
            row_peak, row_mass, stored = carried
            logits = logits_of(block)
            new_peak = jnp.maximum(row_peak, jnp.max(logits, axis=-1))
            new_mass = row_mass * jnp.exp(row_peak - new_peak) + jnp.sum(
                jnp.exp(logits - new_peak[..., None]), axis=-1
            )
            stored = lax.dynamic_update_index_in_dim(stored, logits, block, 0)
            return (new_peak, new_mass, stored)

        return lax.cond(block * KB <= last_row, first_active, lambda carried: carried, carry_in)

    peak_start = jnp.full((head_count, row_count), -jnp.inf, jnp.float32)
    mass_start = jnp.zeros((head_count, row_count), jnp.float32)
    store_start = jnp.zeros((block_count, head_count, row_count, KB), jnp.float32)
    row_peak, row_mass, stored = lax.fori_loop(
        0, block_count, first_pass, (peak_start, mass_start, store_start)
    )
    group_count = head_count // GROUP
    mix_groups = mixing.reshape(group_count, GROUP, GROUP)

    def second_pass(block, carry_in):

        def second_active(summed):
            logits = lax.dynamic_index_in_dim(stored, block, 0, keepdims=False)
            probs = jnp.exp(logits - row_peak[..., None]) / row_mass[..., None]
            grouped = probs.reshape(group_count, GROUP, row_count, KB)
            mixed_scores = (
                jnp.einsum("gab,gbrk->gark", mix_groups, grouped)
                .reshape(head_count, row_count, KB)
                .astype(jnp.bfloat16)
            )
            value_block = lax.dynamic_slice_in_dim(values_all, block * KB, KB, 0).reshape(
                KB, head_count, HD
            )
            return summed + jnp.einsum(
                "hrk,khd->rhd", mixed_scores, value_block, preferred_element_type=jnp.float32
            )

        return lax.cond(block * KB <= last_row, second_active, lambda summed: summed, carry_in)

    summed = lax.fori_loop(
        0, block_count, second_pass, jnp.zeros((row_count, head_count, HD), jnp.float32)
    )
    rms = jnp.sqrt(jnp.mean(summed * summed, axis=-1, keepdims=True) + 1e-05)
    normed = (summed / rms * gain.reshape(head_count, HD)).astype(jnp.bfloat16)
    return normed.reshape(row_count, head_count * HD)


def per_device(
    activations, positions, w_query, w_key, w_value, conv_kernel, head_mix, out_gain, w_out
):
    row_count = activations.shape[0]
    ctx_place = lax.axis_index("ctx")
    features = lax.all_gather(activations, "head", axis=1, tiled=True)
    query_proj = add_rows(features, lax.all_gather(w_query, "ctx", axis=0, tiled=True))
    key_proj = add_rows(features, lax.all_gather(w_key, "ctx", axis=0, tiled=True))
    value_proj = add_rows(features, lax.all_gather(w_value, "ctx", axis=0, tiled=True))
    key = rope(key_proj, positions).astype(jnp.bfloat16)
    value = value_proj.astype(jnp.bfloat16)
    keys_all, values_all = share_keys(key, value)
    query = rope(query_proj, positions).astype(jnp.bfloat16)
    rim_rows = passed_along(query[row_count - (CQ - 1) :], "ctx", 1)
    query_ext = jnp.concatenate([rim_rows, query], 0)
    keys_pad = jnp.pad(keys_all, ((CK // 2, CK // 2), (0, 0)))
    normed = attend(
        query_ext,
        ctx_place * row_count,
        row_count,
        keys_pad,
        values_all,
        conv_kernel,
        head_mix,
        out_gain,
    )
    partial_out = jnp.dot(
        normed, lax.all_gather(w_out, "ctx", axis=1, tiled=True), preferred_element_type=jnp.float32
    )
    return lax.psum_scatter(
        partial_out.astype(jnp.bfloat16), "head", scatter_dimension=1, tiled=True
    )


ROWS = 256
BAND = 128
LANES = 128
SUB = 64
AHEAD = 16


def kernel_params(mebibytes):
    return pltpu.CompilerParams(vmem_limit_bytes=mebibytes * 1024 * 1024)


def whole(memory_space):
    return pl.BlockSpec(memory_space=memory_space)


def project_kernel(rows, first_col, place, *refs):
    a_own, a_x, a_y = refs[:4], refs[4:9], refs[9:14]
    w_same, w_swap = refs[14:16]
    abuf, wbuf, acc, sem_a, sem_w = refs[-5:]
    turn, core = place[0], place[1]
    half = w_same.shape[1]
    width = wbuf.shape[2]

    def copies_a(t):
        out = []
        for b in range(4):
            if t < 3:
                source = (a_own, a_x, a_y)[t][b].at[pl.ds(0, rows)]
                target = abuf.at[t, pl.ds(b * rows, rows)]
                out.append(pltpu.make_async_copy(source, target, sem_a.at[t, b]))
                continue
            mid = rows // 2
            late = pl.ds(rows if b < 3 else 0, mid)
            for n, part in enumerate((a_y, a_x)):
                target = abuf.at[t, pl.ds(b * rows + n * mid, mid)]
                out.append(
                    pltpu.make_async_copy(part[b + 1].at[late], target, sem_a.at[t + n, b])
                )
        return out

    def copies_w(t):
        out = []
        for n, (ref, side) in enumerate(((w_same, core), (w_swap, 1 - core))):
            source = ref.at[lax.bitwise_xor(turn, t), :, pl.ds(first_col, width)]
            target = wbuf.at[t, pl.ds(pl.multiple_of(side * half, half), half)]
            out.append(pltpu.make_async_copy(source, target, sem_w.at[t, n]))
        return out

    for t in range(4):
        for copy in copies_w(t) + copies_a(t):
            copy.start()
    for t in range(4):
        for copy in copies_w(t) + copies_a(t):
            copy.wait()
        part = jnp.dot(abuf[t], wbuf[t], preferred_element_type=jnp.float32)
        acc[...] = part if t == 0 else acc[...] + part
    if first_col:
        v_out = refs[16]
        for b in range(4):
            v_out[place[5 + b]] = acc[b * rows : (b + 1) * rows].astype(jnp.bfloat16)
        return
    cos_ref, sin_ref, mine, theirs = refs[16:20]
    first = core == 0
    for b in range(4):
        total = acc[b * rows : (b + 1) * rows]
        cosine, sine = cos_ref[b], sin_ref[b]
        at = place[5 + b]
        for col, out in ((0, 0), (2 * HD, HD)):
            heads = []
            for start in (col, col + HD):
                x = total[:, start : start + HD]
                x = x * cosine + pltpu.roll(x, HD // 2, 1) * sine
                heads.append(x.astype(jnp.bfloat16))
            mine[at, :, out : out + HD] = jnp.where(first, heads[0], heads[1])
            theirs[at, :, out : out + HD] = jnp.where(first, heads[1], heads[0])


def project(place, a_own, a_plane, w_same, w_swap, angles=()):
    rows, depth = a_own[0].shape
    first_col, width = (0, 4 * HD) if angles else (4 * HD, 2 * HD)
    out = jax.ShapeDtypeStruct((4, rows, 2 * HD), jnp.bfloat16)
    count = 2 if angles else 1
    return pl.pallas_call(
        functools.partial(project_kernel, rows, first_col),
        out_shape=[out] * count,
        in_specs=[whole(pltpu.SMEM)]
        + [whole(pl.ANY)] * 16
        + [whole(pltpu.VMEM)] * len(angles),
        out_specs=[whole(pltpu.VMEM)] * count,
        scratch_shapes=[
            pltpu.VMEM((4, 4 * rows, depth), jnp.bfloat16),
            pltpu.VMEM((4, depth, width), jnp.bfloat16),
            pltpu.VMEM((4 * rows, width), jnp.float32),
            pltpu.SemaphoreType.DMA((5, 4)),
            pltpu.SemaphoreType.DMA((4, 2)),
        ],
        compiler_params=kernel_params(56),
        cost_estimate=pl.CostEstimate(
            flops=8 * rows * 4 * depth * width, bytes_accessed=16 * 2**20, transcendentals=0
        ),
    )(place, *a_own, *a_plane, w_same, w_swap, *angles)


def prepare(core, mine, other, key_ref, even_ref, odd_ref, q_out, k_out, corr, *scratch):
    qf, kf, lags, turned = scratch
    total = q_out.shape[0]
    qf[0:8] = jnp.zeros((8, HD), jnp.float32)
    kf[0:AHEAD] = jnp.zeros((AHEAD, HD), jnp.float32)
    kf[AHEAD + total :] = jnp.zeros((kf.shape[0] - AHEAD - total, HD), jnp.float32)
    corr[...] = jnp.zeros(corr.shape, jnp.float32)
    for i in range(total // (2 * ROWS)):
        for ref, parity in ((mine, core), (other, 1 - core)):
            start = pl.multiple_of((2 * i + parity) * ROWS, ROWS)
            block = ref[i].astype(jnp.float32)
            qf[pl.ds(8 + start, ROWS)] = block[:, :HD]
            kf[pl.ds(AHEAD + start, ROWS)] = block[:, HD:]

    ahead = lax.broadcasted_iota(jnp.int32, (SUB + 8, LANES), 1) - lax.broadcasted_iota(
        jnp.int32, (SUB + 8, LANES), 0
    )
    near = (ahead >= 1) & (ahead < CQ + CK // 2)
    steps = total // LANES
    for w in range(steps):
        base = w * LANES
        window = kf[base : base + 2 * LANES].T
        turned[base : base + LANES] = window.astype(jnp.bfloat16)
        for odd in range(2):
            at = base + odd * SUB
            qwin = qf[at : at + SUB + 8]
            kwin = kf[at + AHEAD - 8 : at + AHEAD - 8 + LANES]
            scores = lax.dot_general(
                qwin.astype(jnp.bfloat16),
                kwin.astype(jnp.bfloat16),
                (((1,), (1,)), ((), ())),
                preferred_element_type=jnp.float32,
            )
            future = jnp.where(near, scores, 0.0)
            for a in range(CQ):
                cols = slice(a * LANES, (a + 1) * LANES)
                lags[odd, w * SUB : (w + 1) * SUB, cols] = future[8 - a : 8 - a + SUB].astype(
                    jnp.bfloat16
                )
                q_out[at : at + SUB, cols] = qwin[8 - a : 8 - a + SUB].astype(jnp.bfloat16)
    for w in range(0, steps, 4):
        wide = jnp.dot(
            turned[w * LANES : (w + 4) * LANES], key_ref[...], preferred_element_type=jnp.float32
        )
        for n in range(4):
            cols = slice((w + n) * LANES, (w + n + 1) * LANES)
            for a in range(CQ):
                k_out[a * HD : (a + 1) * HD, cols] = wide[
                    n * LANES : (n + 1) * LANES, a * LANES : (a + 1) * LANES
                ].astype(jnp.bfloat16)
    for odd, taps in enumerate((even_ref, odd_ref)):
        for w in range(0, steps, 8):
            fix = jnp.dot(
                lags[odd, w * SUB : (w + 8) * SUB], taps[...], preferred_element_type=jnp.float32
            )
            for n in range(8):
                m = 2 * ((w + n) % 2) + odd
                col = LANES * ((m + 1) // 2)
                corr[(w + n) // 2, m * SUB : (m + 1) * SUB, col : col + taps.shape[1]] = fix[
                    n * SUB : (n + 1) * SUB
                ]


def fill_tables(weights, key_ref, even_ref, odd_ref):
    def fill(ref, origin, swap):
        height = ref.shape[0] if swap else ref.shape[0] // CQ
        width = ref.shape[1] // CQ if swap else ref.shape[1]
        shape = (height, width)
        tap = lax.broadcasted_iota(jnp.int32, shape, 1) - lax.broadcasted_iota(jnp.int32, shape, 0)
        for a in range(CQ):
            value = jnp.zeros(shape, jnp.float32)
            for c in range(CK):
                value = jnp.where(tap == c - origin, weights[a * CK + c], value)
            value = value.astype(jnp.bfloat16)
            if swap:
                ref[:, a * width : (a + 1) * width] = value
            else:
                ref[a * height : (a + 1) * height, :] = value

    fill(key_ref, CK // 2 + AHEAD, True)
    fill(even_ref, CK // 2 + 8 - BAND, False)
    fill(odd_ref, CK // 2 + 8 - SUB, False)


def attend_kernel(place, mix, weights, *refs):
    qk_refs, (va, vb, vc, vd), (mine, theirs) = refs[:2], refs[2:6], refs[6:8]
    v_all, q_wide, k_ref, corr = refs[8:12]
    tables, sem_v = refs[16:19], refs[19]
    side, core = place[2], place[1]
    b = pl.program_id(0)
    count = k_ref.shape[1] // (2 * ROWS)

    @pl.when(b == 0)
    def _():
        def copies_v():
            out = []
            for n, ref in enumerate((va, vb, vc, vd)):
                parity = core if n < 2 else 1 - core
                start = pl.multiple_of((side if n % 2 == 0 else 1 - side) * 2 * HD, 2 * HD)
                for i in range(count):
                    rows = pl.ds(pl.multiple_of((2 * i + parity) * ROWS, ROWS), ROWS)
                    target = v_all.at[rows, pl.ds(start, 2 * HD)]
                    out.append(pltpu.make_async_copy(ref.at[i], target, sem_v.at[n, i]))
            return out

        for copy in copies_v():
            copy.start()
        fill_tables(weights, *tables)
        prepare(core, *qk_refs, *tables, q_wide, k_ref, corr, *refs[12:16])
        for copy in copies_v():
            copy.wait()

    row = lax.broadcasted_iota(jnp.int32, (ROWS, ROWS), 0)
    col = lax.broadcasted_iota(jnp.int32, (ROWS, ROWS), 1)
    seen = col <= row
    top, low = slice(0, ROWS), slice(ROWS, 2 * ROWS)

    def fixed(part, n):
        return jnp.concatenate([part[:, :BAND], part[:, BAND:] - corr[n, :, :BAND]], 1)

    def rows_of(upper, lower):
        return jnp.concatenate([upper, lower], 0)

    def block(step):
        q_rows = q_wide[2 * step * ROWS : (2 * step + 2) * ROWS]
        parts = []
        for j in range(2 * step + 1):
            part = jnp.dot(
                q_rows,
                k_ref[:, j * ROWS : (j + 1) * ROWS],
                preferred_element_type=jnp.float32,
            )
            if j == 2 * step:
                diagonal = jnp.where(seen, part[top] - corr[2 * step, :, BAND:], -jnp.inf)
                part = rows_of(diagonal, fixed(part[low], 2 * step + 1))
            elif j == 2 * step - 1:
                part = rows_of(fixed(part[top], 2 * step), part[low])
            parts.append(part)
        start = (2 * step + 1) * ROWS
        last = jnp.dot(
            q_rows[low], k_ref[:, start : start + ROWS], preferred_element_type=jnp.float32
        )
        last = jnp.where(seen, last - corr[2 * step + 1, :, BAND:], -jnp.inf)
        peak = parts[0]
        for part in parts[1:]:
            peak = jnp.maximum(peak, part)
        peak = rows_of(peak[top], jnp.maximum(peak[low], last))
        peak = jnp.max(peak, axis=1, keepdims=True)
        mass = jnp.zeros((2 * ROWS, ROWS), jnp.float32)
        probs = []
        for part in parts:
            part = jnp.exp2(part - peak)
            mass = mass + part
            probs.append(part.astype(jnp.bfloat16))
        last = jnp.exp2(last - peak[low])
        mass = rows_of(mass[top], mass[low] + last)
        summed = jnp.dot(
            jnp.concatenate(probs, 1), v_all[:start], preferred_element_type=jnp.float32
        )
        extra = jnp.dot(
            last.astype(jnp.bfloat16),
            v_all[start : start + ROWS],
            preferred_element_type=jnp.float32,
        )
        inverse = 1.0 / jnp.sum(mass, axis=1, keepdims=True)
        halves = []
        for rows, total in ((top, summed[top]), (low, summed[low] + extra)):
            halves.append(
                jnp.concatenate(
                    [
                        total[:, g * HD : (g + 1) * HD] * (inverse[rows] * mix[g])
                        for g in range(GROUP)
                    ],
                    1,
                ).astype(jnp.bfloat16)
            )
        mine[0] = jnp.where(core == 0, halves[0], halves[1])
        theirs[0] = jnp.where(core == 0, halves[1], halves[0])

    for step in range(count):
        pl.when(b == step)(lambda step=step: block(step))


def attend_head(place, mix, weights, mine, other, values):
    total = 2 * mine.shape[0] * ROWS
    count = total // (2 * ROWS)
    depth = CQ * HD
    out = jax.ShapeDtypeStruct((count, ROWS, GROUP * HD), jnp.bfloat16)
    out_spec = pl.BlockSpec((1, ROWS, GROUP * HD), lambda b: (b, 0, 0))
    return pl.pallas_call(
        attend_kernel,
        grid=(count,),
        out_shape=(out, out),
        in_specs=[whole(pltpu.SMEM)] * 3 + [whole(pltpu.VMEM)] * 2 + [whole(pl.ANY)] * 4,
        out_specs=[out_spec, out_spec],
        scratch_shapes=[
            pltpu.VMEM((total, GROUP * HD), jnp.bfloat16),
            pltpu.VMEM((total, depth), jnp.bfloat16),
            pltpu.VMEM((depth, total), jnp.bfloat16),
            pltpu.VMEM((total // ROWS, ROWS, BAND + ROWS), jnp.float32),
            pltpu.VMEM((8 + total, HD), jnp.float32),
            pltpu.VMEM((AHEAD + total + LANES, HD), jnp.float32),
            pltpu.VMEM((2, total // 2, CQ * LANES), jnp.bfloat16),
            pltpu.VMEM((total, 2 * LANES), jnp.bfloat16),
        ]
        + [
            pltpu.VMEM(shape, jnp.bfloat16)
            for shape in ((2 * LANES, depth), (CQ * LANES, 2 * LANES), (CQ * LANES, LANES))
        ]
        + [pltpu.SemaphoreType.DMA((4, count))],
        compiler_params=kernel_params(56),
        cost_estimate=pl.CostEstimate(
            flops=total * total * (depth + GROUP * HD),
            bytes_accessed=16 * 2**20,
            transcendentals=total * total // 2,
        ),
    )(place, mix, weights, mine, other, *values)


def finish_kernel(place, own, r1, r2, r3, gain, *refs):
    w_parts, outs = refs[:12], refs[12:16]
    normed, w_buf, sem = refs[16:]
    width = w_parts[0].shape[1]
    core, head, inner = place[1], place[0], place[9]

    def copy_w(n, source):
        side = core if n % 2 == 0 else 1 - core
        cols = pl.ds(pl.multiple_of(side * width, width), width)
        target = w_buf.at[lax.bitwise_xor(place[5 + n // 2], head), :, cols]
        return pltpu.make_async_copy(w_parts[source], target, sem.at[n])

    for n in range(4):
        copy_w(n, n).start()
    for n in range(4, 8):
        straight = n if n < 6 else n + 2

        @pl.when(inner == 1)
        def _():
            copy_w(n, straight).start()

        @pl.when(inner == 0)
        def _():
            copy_w(n, straight + 2).start()

    near = own[...] + r1[...].astype(jnp.float32)
    far = r2[...].astype(jnp.float32) + r3[...].astype(jnp.float32)
    low = place[3] == 0
    for g in range(2 * GROUP):
        cols = slice((g % GROUP) * HD, (g % GROUP + 1) * HD)
        first = low if g < GROUP else jnp.logical_not(low)
        x = jnp.where(first, near[:, cols], far[:, cols])
        scale = lax.rsqrt(jnp.mean(x * x, axis=1, keepdims=True) + 1e-05)
        normed[:, g * HD : (g + 1) * HD] = (
            x * scale * gain[:, g * HD : (g + 1) * HD]
        ).astype(jnp.bfloat16)
    for n in range(8):
        copy_w(n, n).wait()
    for t in (3, 2, 1, 0):
        outs[t][...] = jnp.dot(
            normed[...], w_buf[t], preferred_element_type=jnp.float32
        ).astype(jnp.bfloat16)


def finish(place, own, r1, r2, r3, gain, w_parts):
    rows = own.shape[0]
    depth, width = w_parts[0].shape
    return pl.pallas_call(
        finish_kernel,
        in_specs=[whole(pltpu.SMEM)] + [whole(pltpu.VMEM)] * 5 + [whole(pl.ANY)] * 12,
        out_specs=[whole(pltpu.VMEM)] * 4,
        out_shape=[jax.ShapeDtypeStruct((rows, 2 * width), jnp.bfloat16)] * 4,
        scratch_shapes=[
            pltpu.VMEM((rows, depth), jnp.bfloat16),
            pltpu.VMEM((4, depth, 2 * width), jnp.bfloat16),
            pltpu.SemaphoreType.DMA((8,)),
        ],
        compiler_params=kernel_params(56),
        cost_estimate=pl.CostEstimate(
            flops=2 * rows * depth * 8 * width, bytes_accessed=11 * 2**20, transcendentals=0
        ),
    )(place, own, r1, r2, r3, gain, *w_parts)


def swapped(value, axis, mask):
    count = lax.axis_size(axis)
    return lax.ppermute(value, axis, [(i, i ^ mask) for i in range(count)])


def per_device_one_head(
    activations, positions, w_query, w_key, w_value, conv_kernel, head_mix, out_gain, w_out
):
    ctx, head = lax.axis_index("ctx"), lax.axis_index("head")
    z, core = ctx // 2, ctx % 2
    rows = activations.shape[0]
    half = rows // 2
    barrier = lax.optimization_barrier
    pair = 2 * HD

    def columns(target):
        parts = [
            lax.dynamic_slice_in_dim(w, target * pair, pair, 1) for w in (w_query, w_key, w_value)
        ]
        return jnp.concatenate(parts, 1)

    digits = jnp.stack([positions // 256, positions % 256]).astype(jnp.bfloat16)
    digits = jnp.pad(digits, ((0, 14), (0, activations.shape[1] - rows)))
    block = jnp.concatenate([activations, digits])
    w_pieces = jnp.stack([columns(target) for target in range(4)])
    middle = [(2, 4), (3, 5), (4, 2), (5, 3)]
    outward = [(2, 0), (3, 1), (4, 6), (5, 7)]
    inner = (z == 1) | (z == 2)

    def plane(piece, x_before, y_before):
        to_x = jnp.concatenate([piece[:rows], y_before[half:rows]])
        to_y = jnp.concatenate([piece[:rows], x_before[:half]])
        return swapped(to_x, "head", 1), swapped(to_y, "head", 2)

    near = swapped(block, "ctx", 2)
    across = lax.ppermute(block, "ctx", middle)
    x0, y0 = swapped(activations, "head", 1), swapped(activations, "head", 2)
    weights = lax.dynamic_index_in_dim(conv_kernel, ctx, 0, keepdims=False)
    weights = weights * (math.log2(math.e) / math.sqrt(HD))
    order = [z, z ^ 1, jnp.where(inner, z ^ 3, z ^ 2), jnp.where(inner, z ^ 2, z ^ 3)]
    place = jnp.stack([head, core, z % 2, z // 2, head] + order).astype(jnp.int32)
    near, across, x0, y0, w_pieces, weights, place, w_out = barrier(
        (near, across, x0, y0, w_pieces, weights, place, w_out)
    )
    same_core = [[i for i in range(8) if i % 2 == k] for k in range(2)]
    w_same = lax.all_to_all(w_pieces, "ctx", 0, 0, axis_index_groups=same_core)
    across_next = lax.ppermute(near, "ctx", middle)
    passed = lax.ppermute(across, "ctx", outward)
    x1, y1 = plane(near, x0, y0)
    across_next, passed, x1, y1 = barrier((across_next, passed, x1, y1))
    far_a = across + passed
    passed_next = lax.ppermute(across_next, "ctx", outward)
    x2, y2 = plane(far_a, x1, y1)
    passed_next, x2, y2 = barrier((passed_next, x2, y2))
    far_b = across_next + passed_next
    x3, y3 = plane(far_b, x2, y2)
    place_of = jnp.stack(
        [
            a[rows, :rows].astype(jnp.float32) * 256.0 + a[rows + 1, :rows].astype(jnp.float32)
            for a in (block, near, far_a, far_b)
        ]
    )
    exponents = jnp.arange(HD // 2, dtype=jnp.float32) * (2.0 / HD)
    inverse = jnp.exp(-exponents * math.log(500000.0))
    angle = (place_of * 0.25)[:, :, None] * inverse
    cosine, sine = jnp.cos(angle), jnp.sin(angle)
    cosine = jnp.concatenate([cosine, cosine], -1)
    sine = jnp.concatenate([-sine, sine], -1)
    x3, y3, cosine, sine, w_out = barrier((x3, y3, cosine, sine, w_out))
    x4, y4 = swapped(y3[half:rows], "head", 1), swapped(x3[:half], "head", 2)
    out_near = swapped(w_out, "ctx", 2)
    out_across = lax.ppermute(w_out, "ctx", middle)
    x4, y4, w_same = barrier((x4, y4, w_same))
    w_swap = swapped(w_same, "ctx", 1)
    planes = (x0, x1, x2, x3, x4, y0, y1, y2, y3, y4)
    sources = place, (activations, near, far_a, far_b), planes, w_same, w_swap
    (v_pair,) = project(*sources)
    place, v_pair, out_near, out_across = barrier((place, v_pair, out_near, out_across))
    v_next = swapped(v_pair, "ctx", 2)
    v_pair_other = swapped(v_pair, "ctx", 1)
    out_across_next = lax.ppermute(out_near, "ctx", middle)
    out_passed = lax.ppermute(out_across, "ctx", outward)
    mine, theirs = project(place, *sources[1:], (cosine, sine))
    mine, theirs, v_next, v_pair_other = barrier((mine, theirs, v_next, v_pair_other))
    other = swapped(theirs, "ctx", 1)
    v_next_other = swapped(v_next, "ctx", 1)
    out_own_swap = swapped(w_out, "ctx", 1)
    other, v_next_other, out_across_next, out_own_swap = barrier(
        (other, v_next_other, out_across_next, out_own_swap)
    )
    out_passed_next = lax.ppermute(out_across_next, "ctx", outward)
    out_near_swap, out_across_swap = swapped(out_near, "ctx", 1), swapped(out_across, "ctx", 1)
    group_rows = lax.dynamic_slice_in_dim(head_mix, GROUP * (ctx // GROUP), GROUP, 0)
    mix = lax.dynamic_index_in_dim(group_rows, ctx % GROUP, 1, keepdims=False)
    out_mine, out_theirs = attend_head(
        place, mix, weights, mine, other, (v_pair, v_next, v_pair_other, v_next_other)
    )
    out_mine, out_theirs, out_passed, out_passed_next, out_near_swap, out_across_swap = barrier(
        (out_mine, out_theirs, out_passed, out_passed_next, out_near_swap, out_across_swap)
    )
    out_parts = [w_out, out_own_swap, out_near, out_near_swap, out_across, out_across_swap]
    for part in (out_passed, out_across_next, out_passed_next):
        out_parts += [part, swapped(part, "ctx", 1)]
    summed = out_mine.astype(jnp.float32) + swapped(out_theirs, "ctx", 1).astype(jnp.float32)
    own = lax.dynamic_index_in_dim(summed, z, 0, keepdims=False)
    r1, r2, r3 = [
        swapped(
            lax.dynamic_index_in_dim(summed, z ^ s, 0, keepdims=False).astype(jnp.bfloat16),
            "ctx",
            2 * s,
        )
        for s in (1, 2, 3)
    ]
    where = jnp.concatenate([place, inner.astype(jnp.int32)[None]])
    shares = finish(where, own, r1, r2, r3, out_gain.reshape(1, -1), out_parts)
    total = shares[0].astype(jnp.float32)
    for t in (1, 2, 3):
        total = total + swapped(shares[t], "head", t).astype(jnp.float32)
    return total.astype(jnp.bfloat16)


def solution(mesh):
    one_head_each = mesh.shape["ctx"] == 8 and mesh.shape["head"] == 4
    body = per_device_one_head if one_head_each else per_device
    return jax.shard_map(
        body,
        mesh=mesh,
        in_specs=(
            P("ctx", "head"),
            P("ctx"),
            P("ctx", "head"),
            P("ctx", "head"),
            P("ctx", "head"),
            P("head", None),
            P("head", None),
            P("head"),
            P("head", "ctx"),
        ),
        out_specs=P("ctx", "head"),
        check_vma=False,
    )
```

```python
import functools
import math

import jax
import jax.numpy as jnp
from jax import lax
from jax.experimental import pallas as pl
from jax.experimental.pallas import tpu as pltpu
from jax.sharding import PartitionSpec as P

HD = 128
GROUP = 4
CQ = 6
CK = 11
KB = 512


def passed_along(value, axis, steps):
    count = lax.axis_size(axis)
    leading, last = (max(0, -steps), min(count, count - steps))
    return lax.ppermute(value, axis, [(source, source + steps) for source in range(leading, last)])


def rope(projected, positions):
    row_count = projected.shape[0]
    head_count = projected.shape[1] // HD
    shaped = projected.reshape(row_count, head_count, HD)
    half_size = HD // 2
    exponents = jnp.arange(half_size, dtype=jnp.float32) * (2.0 / HD)
    inverse = jnp.exp(-exponents * math.log(500000.0))
    angle = (positions.astype(jnp.float32) * 0.25)[:, None, None] * inverse[None, None, :]
    cosine = jnp.cos(angle)
    sine = jnp.sin(angle)
    lower_half = shaped[..., :half_size]
    upper_half = shaped[..., half_size:]
    rotated_rows = jnp.concatenate(
        [lower_half * cosine - upper_half * sine, upper_half * cosine + lower_half * sine], -1
    )
    return rotated_rows.reshape(row_count, head_count * HD)


def convolve(masked, kernel, row_count, col_count):
    summed = jnp.zeros((masked.shape[0], row_count, col_count), jnp.float32)
    for lag_q in range(CQ):
        for lag_k in range(CK):
            weight = kernel[:, lag_q * CK + lag_k][:, None, None]
            window = masked[
                :,
                CQ - 1 - lag_q : CQ - 1 - lag_q + row_count,
                CK - 1 - lag_k : CK - 1 - lag_k + col_count,
            ]
            summed = summed + weight * window
    return summed


def add_rows(left, piece):
    return jnp.dot(left, piece, preferred_element_type=jnp.float32)


def share_keys(key, value):
    return (
        lax.all_gather(key, "ctx", axis=0, tiled=True),
        lax.all_gather(value, "ctx", axis=0, tiled=True),
    )


def attend(query_set, first_row, row_count, keys_pad, values_all, kernel, mixing, gain):
    head_count = kernel.shape[0]
    ext_rows = row_count + CQ - 1
    query_heads = query_set.reshape(ext_rows, head_count, HD)
    token_total = values_all.shape[0]
    block_count = token_total // KB
    last_row = first_row + row_count - 1
    scale = 1.0 / math.sqrt(HD)
    prow = first_row - (CQ - 1) + jnp.arange(ext_rows, dtype=jnp.int32)
    irow = first_row + jnp.arange(row_count, dtype=jnp.int32)

    def logits_of(block):
        key_start = block * KB
        key_block = lax.dynamic_slice_in_dim(keys_pad, key_start, KB + CK - 1, 0).reshape(
            KB + CK - 1, head_count, HD
        )
        scores = (
            jnp.einsum("rhd,khd->hrk", query_heads, key_block, preferred_element_type=jnp.float32)
            * scale
        )
        kcol = key_start - CK // 2 + jnp.arange(KB + CK - 1, dtype=jnp.int32)
        valid = (kcol[None, :] <= prow[:, None]) & (prow[:, None] >= 0)
        masked = jnp.where(valid[None], scores, 0.0)
        conv = convolve(masked, kernel, row_count, KB)
        jcol = key_start + jnp.arange(KB, dtype=jnp.int32)
        return jnp.where((jcol[None, :] <= irow[:, None])[None], conv, -jnp.inf)

    def first_pass(block, carry_in):

        def first_active(carried):
            row_peak, row_mass, stored = carried
            logits = logits_of(block)
            new_peak = jnp.maximum(row_peak, jnp.max(logits, axis=-1))
            new_mass = row_mass * jnp.exp(row_peak - new_peak) + jnp.sum(
                jnp.exp(logits - new_peak[..., None]), axis=-1
            )
            stored = lax.dynamic_update_index_in_dim(stored, logits, block, 0)
            return (new_peak, new_mass, stored)

        return lax.cond(block * KB <= last_row, first_active, lambda carried: carried, carry_in)

    peak_start = jnp.full((head_count, row_count), -jnp.inf, jnp.float32)
    mass_start = jnp.zeros((head_count, row_count), jnp.float32)
    store_start = jnp.zeros((block_count, head_count, row_count, KB), jnp.float32)
    row_peak, row_mass, stored = lax.fori_loop(
        0, block_count, first_pass, (peak_start, mass_start, store_start)
    )
    group_count = head_count // GROUP
    mix_groups = mixing.reshape(group_count, GROUP, GROUP)

    def second_pass(block, carry_in):

        def second_active(summed):
            logits = lax.dynamic_index_in_dim(stored, block, 0, keepdims=False)
            probs = jnp.exp(logits - row_peak[..., None]) / row_mass[..., None]
            grouped = probs.reshape(group_count, GROUP, row_count, KB)
            mixed_scores = (
                jnp.einsum("gab,gbrk->gark", mix_groups, grouped)
                .reshape(head_count, row_count, KB)
                .astype(jnp.bfloat16)
            )
            value_block = lax.dynamic_slice_in_dim(values_all, block * KB, KB, 0).reshape(
                KB, head_count, HD
            )
            return summed + jnp.einsum(
                "hrk,khd->rhd", mixed_scores, value_block, preferred_element_type=jnp.float32
            )

        return lax.cond(block * KB <= last_row, second_active, lambda summed: summed, carry_in)

    summed = lax.fori_loop(
        0, block_count, second_pass, jnp.zeros((row_count, head_count, HD), jnp.float32)
    )
    rms = jnp.sqrt(jnp.mean(summed * summed, axis=-1, keepdims=True) + 1e-05)
    normed = (summed / rms * gain.reshape(head_count, HD)).astype(jnp.bfloat16)
    return normed.reshape(row_count, head_count * HD)


def per_device(
    activations, positions, w_query, w_key, w_value, conv_kernel, head_mix, out_gain, w_out
):
    row_count = activations.shape[0]
    ctx_place = lax.axis_index("ctx")
    features = lax.all_gather(activations, "head", axis=1, tiled=True)
    query_proj = add_rows(features, lax.all_gather(w_query, "ctx", axis=0, tiled=True))
    key_proj = add_rows(features, lax.all_gather(w_key, "ctx", axis=0, tiled=True))
    value_proj = add_rows(features, lax.all_gather(w_value, "ctx", axis=0, tiled=True))
    key = rope(key_proj, positions).astype(jnp.bfloat16)
    value = value_proj.astype(jnp.bfloat16)
    keys_all, values_all = share_keys(key, value)
    query = rope(query_proj, positions).astype(jnp.bfloat16)
    rim_rows = passed_along(query[row_count - (CQ - 1) :], "ctx", 1)
    query_ext = jnp.concatenate([rim_rows, query], 0)
    keys_pad = jnp.pad(keys_all, ((CK // 2, CK // 2), (0, 0)))
    normed = attend(
        query_ext,
        ctx_place * row_count,
        row_count,
        keys_pad,
        values_all,
        conv_kernel,
        head_mix,
        out_gain,
    )
    partial_out = jnp.dot(
        normed, lax.all_gather(w_out, "ctx", axis=1, tiled=True), preferred_element_type=jnp.float32
    )
    return lax.psum_scatter(
        partial_out.astype(jnp.bfloat16), "head", scatter_dimension=1, tiled=True
    )


ROWS = 256
BAND = 128
LANES = 128
SUB = 64
AHEAD = 16


def kernel_params(mebibytes):
    return pltpu.CompilerParams(vmem_limit_bytes=mebibytes * 1024 * 1024)


def whole(memory_space):
    return pl.BlockSpec(memory_space=memory_space)


def project_kernel(rows, first_col, place, *refs):
    a_own, a_x, a_y = refs[:4], refs[4:9], refs[9:14]
    w_same, w_swap = refs[14:16]
    abuf, wbuf, acc, sem_a, sem_w = refs[-5:]
    turn, core = place[0], place[1]
    half = w_same.shape[1]
    width = wbuf.shape[2]

    def copies_a(t):
        out = []
        for b in range(4):
            if t < 3:
                source = (a_own, a_x, a_y)[t][b].at[pl.ds(0, rows)]
                target = abuf.at[t, pl.ds(b * rows, rows)]
                out.append(pltpu.make_async_copy(source, target, sem_a.at[t, b]))
                continue
            mid = rows // 2
            late = pl.ds(rows if b < 3 else 0, mid)
            for n, part in enumerate((a_y, a_x)):
                target = abuf.at[t, pl.ds(b * rows + n * mid, mid)]
                out.append(
                    pltpu.make_async_copy(part[b + 1].at[late], target, sem_a.at[t + n, b])
                )
        return out

    def copies_w(t):
        out = []
        for n, (ref, side) in enumerate(((w_same, core), (w_swap, 1 - core))):
            source = ref.at[lax.bitwise_xor(turn, t), :, pl.ds(first_col, width)]
            target = wbuf.at[t, pl.ds(pl.multiple_of(side * half, half), half)]
            out.append(pltpu.make_async_copy(source, target, sem_w.at[t, n]))
        return out

    for t in range(4):
        for copy in copies_w(t) + copies_a(t):
            copy.start()
    for t in range(4):
        for copy in copies_w(t) + copies_a(t):
            copy.wait()
        part = jnp.dot(abuf[t], wbuf[t], preferred_element_type=jnp.float32)
        acc[...] = part if t == 0 else acc[...] + part
    if first_col:
        v_out = refs[16]
        for b in range(4):
            v_out[place[5 + b]] = acc[b * rows : (b + 1) * rows].astype(jnp.bfloat16)
        return
    cos_ref, sin_ref, mine, theirs = refs[16:20]
    first = core == 0
    for b in range(4):
        total = acc[b * rows : (b + 1) * rows]
        cosine, sine = cos_ref[b], sin_ref[b]
        at = place[5 + b]
        for col, out in ((0, 0), (2 * HD, HD)):
            heads = []
            for start in (col, col + HD):
                x = total[:, start : start + HD]
                x = x * cosine + pltpu.roll(x, HD // 2, 1) * sine
                heads.append(x.astype(jnp.bfloat16))
            mine[at, :, out : out + HD] = jnp.where(first, heads[0], heads[1])
            theirs[at, :, out : out + HD] = jnp.where(first, heads[1], heads[0])


def project(place, a_own, a_plane, w_same, w_swap, angles=()):
    rows, depth = a_own[0].shape
    first_col, width = (0, 4 * HD) if angles else (4 * HD, 2 * HD)
    out = jax.ShapeDtypeStruct((4, rows, 2 * HD), jnp.bfloat16)
    count = 2 if angles else 1
    return pl.pallas_call(
        functools.partial(project_kernel, rows, first_col),
        out_shape=[out] * count,
        in_specs=[whole(pltpu.SMEM)]
        + [whole(pl.ANY)] * 16
        + [whole(pltpu.VMEM)] * len(angles),
        out_specs=[whole(pltpu.VMEM)] * count,
        scratch_shapes=[
            pltpu.VMEM((4, 4 * rows, depth), jnp.bfloat16),
            pltpu.VMEM((4, depth, width), jnp.bfloat16),
            pltpu.VMEM((4 * rows, width), jnp.float32),
            pltpu.SemaphoreType.DMA((5, 4)),
            pltpu.SemaphoreType.DMA((4, 2)),
        ],
        compiler_params=kernel_params(56),
        cost_estimate=pl.CostEstimate(
            flops=8 * rows * 4 * depth * width, bytes_accessed=16 * 2**20, transcendentals=0
        ),
    )(place, *a_own, *a_plane, w_same, w_swap, *angles)


def prepare(core, mine, other, key_ref, even_ref, odd_ref, q_out, k_out, corr, *scratch):
    qf, kf, lags, turned = scratch
    total = q_out.shape[0]
    qf[0:8] = jnp.zeros((8, HD), jnp.float32)
    kf[0:AHEAD] = jnp.zeros((AHEAD, HD), jnp.float32)
    kf[AHEAD + total :] = jnp.zeros((kf.shape[0] - AHEAD - total, HD), jnp.float32)
    corr[...] = jnp.zeros(corr.shape, jnp.float32)
    for i in range(total // (2 * ROWS)):
        for ref, parity in ((mine, core), (other, 1 - core)):
            start = pl.multiple_of((2 * i + parity) * ROWS, ROWS)
            block = ref[i].astype(jnp.float32)
            qf[pl.ds(8 + start, ROWS)] = block[:, :HD]
            kf[pl.ds(AHEAD + start, ROWS)] = block[:, HD:]

    ahead = lax.broadcasted_iota(jnp.int32, (SUB + 8, LANES), 1) - lax.broadcasted_iota(
        jnp.int32, (SUB + 8, LANES), 0
    )
    near = (ahead >= 1) & (ahead < CQ + CK // 2)
    steps = total // LANES
    for w in range(steps):
        base = w * LANES
        window = kf[base : base + 2 * LANES].T
        turned[base : base + LANES] = window.astype(jnp.bfloat16)
        for odd in range(2):
            at = base + odd * SUB
            qwin = qf[at : at + SUB + 8]
            kwin = kf[at + AHEAD - 8 : at + AHEAD - 8 + LANES]
            scores = lax.dot_general(
                qwin.astype(jnp.bfloat16),
                kwin.astype(jnp.bfloat16),
                (((1,), (1,)), ((), ())),
                preferred_element_type=jnp.float32,
            )
            future = jnp.where(near, scores, 0.0)
            for a in range(CQ):
                cols = slice(a * LANES, (a + 1) * LANES)
                lags[odd, w * SUB : (w + 1) * SUB, cols] = future[8 - a : 8 - a + SUB].astype(
                    jnp.bfloat16
                )
                q_out[at : at + SUB, cols] = qwin[8 - a : 8 - a + SUB].astype(jnp.bfloat16)
    for w in range(0, steps, 4):
        wide = jnp.dot(
            turned[w * LANES : (w + 4) * LANES], key_ref[...], preferred_element_type=jnp.float32
        )
        for n in range(4):
            cols = slice((w + n) * LANES, (w + n + 1) * LANES)
            for a in range(CQ):
                k_out[a * HD : (a + 1) * HD, cols] = wide[
                    n * LANES : (n + 1) * LANES, a * LANES : (a + 1) * LANES
                ].astype(jnp.bfloat16)
    for odd, taps in enumerate((even_ref, odd_ref)):
        for w in range(0, steps, 8):
            fix = jnp.dot(
                lags[odd, w * SUB : (w + 8) * SUB], taps[...], preferred_element_type=jnp.float32
            )
            for n in range(8):
                m = 2 * ((w + n) % 2) + odd
                col = LANES * ((m + 1) // 2)
                corr[(w + n) // 2, m * SUB : (m + 1) * SUB, col : col + taps.shape[1]] = fix[
                    n * SUB : (n + 1) * SUB
                ]


def fill_tables(weights, key_ref, even_ref, odd_ref):
    def fill(ref, origin, swap):
        height = ref.shape[0] if swap else ref.shape[0] // CQ
        width = ref.shape[1] // CQ if swap else ref.shape[1]
        shape = (height, width)
        tap = lax.broadcasted_iota(jnp.int32, shape, 1) - lax.broadcasted_iota(jnp.int32, shape, 0)
        for a in range(CQ):
            value = jnp.zeros(shape, jnp.float32)
            for c in range(CK):
                value = jnp.where(tap == c - origin, weights[a * CK + c], value)
            value = value.astype(jnp.bfloat16)
            if swap:
                ref[:, a * width : (a + 1) * width] = value
            else:
                ref[a * height : (a + 1) * height, :] = value

    fill(key_ref, CK // 2 + AHEAD, True)
    fill(even_ref, CK // 2 + 8 - BAND, False)
    fill(odd_ref, CK // 2 + 8 - SUB, False)


def attend_kernel(place, mix, weights, *refs):
    qk_refs, (va, vb, vc, vd), (mine, theirs) = refs[:2], refs[2:6], refs[6:8]
    v_all, q_wide, k_ref, corr = refs[8:12]
    tables, sem_v = refs[16:19], refs[19]
    side, core = place[2], place[1]
    b = pl.program_id(0)
    count = k_ref.shape[1] // (2 * ROWS)

    @pl.when(b == 0)
    def _():
        def copies_v():
            out = []
            for n, ref in enumerate((va, vb, vc, vd)):
                parity = core if n < 2 else 1 - core
                start = pl.multiple_of((side if n % 2 == 0 else 1 - side) * 2 * HD, 2 * HD)
                for i in range(count):
                    rows = pl.ds(pl.multiple_of((2 * i + parity) * ROWS, ROWS), ROWS)
                    target = v_all.at[rows, pl.ds(start, 2 * HD)]
                    out.append(pltpu.make_async_copy(ref.at[i], target, sem_v.at[n, i]))
            return out

        for copy in copies_v():
            copy.start()
        fill_tables(weights, *tables)
        prepare(core, *qk_refs, *tables, q_wide, k_ref, corr, *refs[12:16])
        for copy in copies_v():
            copy.wait()

    row = lax.broadcasted_iota(jnp.int32, (ROWS, ROWS), 0)
    col = lax.broadcasted_iota(jnp.int32, (ROWS, ROWS), 1)
    seen = col <= row
    top, low = slice(0, ROWS), slice(ROWS, 2 * ROWS)

    def fixed(part, n):
        return jnp.concatenate([part[:, :BAND], part[:, BAND:] - corr[n, :, :BAND]], 1)

    def rows_of(upper, lower):
        return jnp.concatenate([upper, lower], 0)

    def block(step):
        q_rows = q_wide[2 * step * ROWS : (2 * step + 2) * ROWS]
        parts = []
        for j in range(2 * step + 1):
            part = jnp.dot(
                q_rows,
                k_ref[:, j * ROWS : (j + 1) * ROWS],
                preferred_element_type=jnp.float32,
            )
            if j == 2 * step:
                diagonal = jnp.where(seen, part[top] - corr[2 * step, :, BAND:], -jnp.inf)
                part = rows_of(diagonal, fixed(part[low], 2 * step + 1))
            elif j == 2 * step - 1:
                part = rows_of(fixed(part[top], 2 * step), part[low])
            parts.append(part)
        start = (2 * step + 1) * ROWS
        last = jnp.dot(
            q_rows[low], k_ref[:, start : start + ROWS], preferred_element_type=jnp.float32
        )
        last = jnp.where(seen, last - corr[2 * step + 1, :, BAND:], -jnp.inf)
        peak = parts[0]
        for part in parts[1:]:
            peak = jnp.maximum(peak, part)
        peak = rows_of(peak[top], jnp.maximum(peak[low], last))
        peak = jnp.max(peak, axis=1, keepdims=True)
        mass = jnp.zeros((2 * ROWS, ROWS), jnp.float32)
        probs = []
        for part in parts:
            part = jnp.exp2(part - peak)
            mass = mass + part
            probs.append(part.astype(jnp.bfloat16))
        last = jnp.exp2(last - peak[low])
        mass = rows_of(mass[top], mass[low] + last)
        summed = jnp.dot(
            jnp.concatenate(probs, 1), v_all[:start], preferred_element_type=jnp.float32
        )
        extra = jnp.dot(
            last.astype(jnp.bfloat16),
            v_all[start : start + ROWS],
            preferred_element_type=jnp.float32,
        )
        inverse = 1.0 / jnp.sum(mass, axis=1, keepdims=True)
        halves = []
        for rows, total in ((top, summed[top]), (low, summed[low] + extra)):
            halves.append(
                jnp.concatenate(
                    [
                        total[:, g * HD : (g + 1) * HD] * (inverse[rows] * mix[g])
                        for g in range(GROUP)
                    ],
                    1,
                ).astype(jnp.bfloat16)
            )
        mine[0] = jnp.where(core == 0, halves[0], halves[1])
        theirs[0] = jnp.where(core == 0, halves[1], halves[0])

    for step in range(count):
        pl.when(b == step)(lambda step=step: block(step))


def attend_head(place, mix, weights, mine, other, values):
    total = 2 * mine.shape[0] * ROWS
    count = total // (2 * ROWS)
    depth = CQ * HD
    out = jax.ShapeDtypeStruct((count, ROWS, GROUP * HD), jnp.bfloat16)
    out_spec = pl.BlockSpec((1, ROWS, GROUP * HD), lambda b: (b, 0, 0))
    return pl.pallas_call(
        attend_kernel,
        grid=(count,),
        out_shape=(out, out),
        in_specs=[whole(pltpu.SMEM)] * 3 + [whole(pltpu.VMEM)] * 2 + [whole(pl.ANY)] * 4,
        out_specs=[out_spec, out_spec],
        scratch_shapes=[
            pltpu.VMEM((total, GROUP * HD), jnp.bfloat16),
            pltpu.VMEM((total, depth), jnp.bfloat16),
            pltpu.VMEM((depth, total), jnp.bfloat16),
            pltpu.VMEM((total // ROWS, ROWS, BAND + ROWS), jnp.float32),
            pltpu.VMEM((8 + total, HD), jnp.float32),
            pltpu.VMEM((AHEAD + total + LANES, HD), jnp.float32),
            pltpu.VMEM((2, total // 2, CQ * LANES), jnp.bfloat16),
            pltpu.VMEM((total, 2 * LANES), jnp.bfloat16),
        ]
        + [
            pltpu.VMEM(shape, jnp.bfloat16)
            for shape in ((2 * LANES, depth), (CQ * LANES, 2 * LANES), (CQ * LANES, LANES))
        ]
        + [pltpu.SemaphoreType.DMA((4, count))],
        compiler_params=kernel_params(56),
        cost_estimate=pl.CostEstimate(
            flops=total * total * (depth + GROUP * HD),
            bytes_accessed=16 * 2**20,
            transcendentals=total * total // 2,
        ),
    )(place, mix, weights, mine, other, *values)


def finish_kernel(place, own, r1, r2, r3, gain, *refs):
    w_parts, outs = refs[:12], refs[12:16]
    normed, w_buf, sem = refs[16:]
    width = w_parts[0].shape[1]
    core, head, inner = place[1], place[0], place[9]

    def copy_w(n, source):
        side = core if n % 2 == 0 else 1 - core
        cols = pl.ds(pl.multiple_of(side * width, width), width)
        target = w_buf.at[lax.bitwise_xor(place[5 + n // 2], head), :, cols]
        return pltpu.make_async_copy(w_parts[source], target, sem.at[n])

    for n in range(4):
        copy_w(n, n).start()
    for n in range(4, 8):
        straight = n if n < 6 else n + 2

        @pl.when(inner == 1)
        def _():
            copy_w(n, straight).start()

        @pl.when(inner == 0)
        def _():
            copy_w(n, straight + 2).start()

    near = own[...] + r1[...].astype(jnp.float32)
    far = r2[...].astype(jnp.float32) + r3[...].astype(jnp.float32)
    low = place[3] == 0
    for g in range(2 * GROUP):
        cols = slice((g % GROUP) * HD, (g % GROUP + 1) * HD)
        first = low if g < GROUP else jnp.logical_not(low)
        x = jnp.where(first, near[:, cols], far[:, cols])
        scale = lax.rsqrt(jnp.mean(x * x, axis=1, keepdims=True) + 1e-05)
        normed[:, g * HD : (g + 1) * HD] = (
            x * scale * gain[:, g * HD : (g + 1) * HD]
        ).astype(jnp.bfloat16)
    for n in range(8):
        copy_w(n, n).wait()
    for t in (3, 2, 1, 0):
        outs[t][...] = jnp.dot(
            normed[...], w_buf[t], preferred_element_type=jnp.float32
        ).astype(jnp.bfloat16)


def finish(place, own, r1, r2, r3, gain, w_parts):
    rows = own.shape[0]
    depth, width = w_parts[0].shape
    return pl.pallas_call(
        finish_kernel,
        in_specs=[whole(pltpu.SMEM)] + [whole(pltpu.VMEM)] * 5 + [whole(pl.ANY)] * 12,
        out_specs=[whole(pltpu.VMEM)] * 4,
        out_shape=[jax.ShapeDtypeStruct((rows, 2 * width), jnp.bfloat16)] * 4,
        scratch_shapes=[
            pltpu.VMEM((rows, depth), jnp.bfloat16),
            pltpu.VMEM((4, depth, 2 * width), jnp.bfloat16),
            pltpu.SemaphoreType.DMA((8,)),
        ],
        compiler_params=kernel_params(56),
        cost_estimate=pl.CostEstimate(
            flops=2 * rows * depth * 8 * width, bytes_accessed=11 * 2**20, transcendentals=0
        ),
    )(place, own, r1, r2, r3, gain, *w_parts)


def swapped(value, axis, mask):
    count = lax.axis_size(axis)
    return lax.ppermute(value, axis, [(i, i ^ mask) for i in range(count)])


def per_device_one_head(
    activations, positions, w_query, w_key, w_value, conv_kernel, head_mix, out_gain, w_out
):
    ctx, head = lax.axis_index("ctx"), lax.axis_index("head")
    z, core = ctx // 2, ctx % 2
    rows = activations.shape[0]
    half = rows // 2
    barrier = lax.optimization_barrier
    pair = 2 * HD

    def columns(target):
        parts = [
            lax.dynamic_slice_in_dim(w, target * pair, pair, 1) for w in (w_query, w_key, w_value)
        ]
        return jnp.concatenate(parts, 1)

    digits = jnp.stack([positions // 256, positions % 256]).astype(jnp.bfloat16)
    digits = jnp.pad(digits, ((0, 14), (0, activations.shape[1] - rows)))
    block = jnp.concatenate([activations, digits])
    w_pieces = jnp.stack([columns(target) for target in range(4)])
    middle = [(2, 4), (3, 5), (4, 2), (5, 3)]
    outward = [(2, 0), (3, 1), (4, 6), (5, 7)]
    inner = (z == 1) | (z == 2)

    def plane(piece, x_before, y_before):
        to_x = jnp.concatenate([piece[:rows], y_before[half:rows]])
        to_y = jnp.concatenate([piece[:rows], x_before[:half]])
        return swapped(to_x, "head", 1), swapped(to_y, "head", 2)

    near = swapped(block, "ctx", 2)
    across = lax.ppermute(block, "ctx", middle)
    x0, y0 = swapped(activations, "head", 1), swapped(activations, "head", 2)
    weights = lax.dynamic_index_in_dim(conv_kernel, ctx, 0, keepdims=False)
    weights = weights * (math.log2(math.e) / math.sqrt(HD))
    order = [z, z ^ 1, jnp.where(inner, z ^ 3, z ^ 2), jnp.where(inner, z ^ 2, z ^ 3)]
    place = jnp.stack([head, core, z % 2, z // 2, head] + order).astype(jnp.int32)
    near, across, x0, y0, w_pieces, weights, place, w_out = barrier(
        (near, across, x0, y0, w_pieces, weights, place, w_out)
    )
    same_core = [[i for i in range(8) if i % 2 == k] for k in range(2)]
    across_next = lax.ppermute(near, "ctx", middle)
    passed = lax.ppermute(across, "ctx", outward)
    x1, y1 = plane(near, x0, y0)
    across_next, passed, x1, y1, w_pieces = barrier((across_next, passed, x1, y1, w_pieces))
    w_same = lax.all_to_all(w_pieces, "ctx", 0, 0, axis_index_groups=same_core)
    far_a = across + passed
    passed_next = lax.ppermute(across_next, "ctx", outward)
    x2, y2 = plane(far_a, x1, y1)
    passed_next, x2, y2 = barrier((passed_next, x2, y2))
    far_b = across_next + passed_next
    x3, y3 = plane(far_b, x2, y2)
    place_of = jnp.stack(
        [
            a[rows, :rows].astype(jnp.float32) * 256.0 + a[rows + 1, :rows].astype(jnp.float32)
            for a in (block, near, far_a, far_b)
        ]
    )
    exponents = jnp.arange(HD // 2, dtype=jnp.float32) * (2.0 / HD)
    inverse = jnp.exp(-exponents * math.log(500000.0))
    angle = (place_of * 0.25)[:, :, None] * inverse
    cosine, sine = jnp.cos(angle), jnp.sin(angle)
    cosine = jnp.concatenate([cosine, cosine], -1)
    sine = jnp.concatenate([-sine, sine], -1)
    x3, y3, cosine, sine, w_out = barrier((x3, y3, cosine, sine, w_out))
    x4, y4 = swapped(y3[half:rows], "head", 1), swapped(x3[:half], "head", 2)
    out_near = swapped(w_out, "ctx", 2)
    out_across = lax.ppermute(w_out, "ctx", middle)
    x4, y4, w_same = barrier((x4, y4, w_same))
    w_swap = swapped(w_same, "ctx", 1)
    planes = (x0, x1, x2, x3, x4, y0, y1, y2, y3, y4)
    sources = place, (activations, near, far_a, far_b), planes, w_same, w_swap
    (v_pair,) = project(*sources)
    place, v_pair, out_near, out_across = barrier((place, v_pair, out_near, out_across))
    v_next = swapped(v_pair, "ctx", 2)
    v_pair_other = swapped(v_pair, "ctx", 1)
    out_across_next = lax.ppermute(out_near, "ctx", middle)
    out_passed = lax.ppermute(out_across, "ctx", outward)
    mine, theirs = project(place, *sources[1:], (cosine, sine))
    mine, theirs, v_next, v_pair_other = barrier((mine, theirs, v_next, v_pair_other))
    other = swapped(theirs, "ctx", 1)
    v_next_other = swapped(v_next, "ctx", 1)
    out_own_swap = swapped(w_out, "ctx", 1)
    other, v_next_other, out_across_next, out_own_swap = barrier(
        (other, v_next_other, out_across_next, out_own_swap)
    )
    out_passed_next = lax.ppermute(out_across_next, "ctx", outward)
    out_near_swap, out_across_swap = swapped(out_near, "ctx", 1), swapped(out_across, "ctx", 1)
    group_rows = lax.dynamic_slice_in_dim(head_mix, GROUP * (ctx // GROUP), GROUP, 0)
    mix = lax.dynamic_index_in_dim(group_rows, ctx % GROUP, 1, keepdims=False)
    out_mine, out_theirs = attend_head(
        place, mix, weights, mine, other, (v_pair, v_next, v_pair_other, v_next_other)
    )
    out_mine, out_theirs, out_passed, out_passed_next, out_near_swap, out_across_swap = barrier(
        (out_mine, out_theirs, out_passed, out_passed_next, out_near_swap, out_across_swap)
    )
    out_parts = [w_out, out_own_swap, out_near, out_near_swap, out_across, out_across_swap]
    for part in (out_passed, out_across_next, out_passed_next):
        out_parts += [part, swapped(part, "ctx", 1)]
    summed = out_mine.astype(jnp.float32) + swapped(out_theirs, "ctx", 1).astype(jnp.float32)
    own = lax.dynamic_index_in_dim(summed, z, 0, keepdims=False)
    r1, r2, r3 = [
        swapped(
            lax.dynamic_index_in_dim(summed, z ^ s, 0, keepdims=False).astype(jnp.bfloat16),
            "ctx",
            2 * s,
        )
        for s in (1, 2, 3)
    ]
    where = jnp.concatenate([place, inner.astype(jnp.int32)[None]])
    shares = finish(where, own, r1, r2, r3, out_gain.reshape(1, -1), out_parts)
    total = shares[0].astype(jnp.float32)
    for t in (1, 2, 3):
        total = total + swapped(shares[t], "head", t).astype(jnp.float32)
    return total.astype(jnp.bfloat16)


def solution(mesh):
    one_head_each = mesh.shape["ctx"] == 8 and mesh.shape["head"] == 4
    body = per_device_one_head if one_head_each else per_device
    return jax.shard_map(
        body,
        mesh=mesh,
        in_specs=(
            P("ctx", "head"),
            P("ctx"),
            P("ctx", "head"),
            P("ctx", "head"),
            P("ctx", "head"),
            P("head", None),
            P("head", None),
            P("head"),
            P("head", "ctx"),
        ),
        out_specs=P("ctx", "head"),
        check_vma=False,
    )
```

```python
import functools
import math

import jax
import jax.numpy as jnp
from jax import lax
from jax.experimental import pallas as pl
from jax.experimental.pallas import tpu as pltpu
from jax.sharding import PartitionSpec as P

HD = 128
GROUP = 4
CQ = 6
CK = 11
KB = 512


def passed_along(value, axis, steps):
    count = lax.axis_size(axis)
    leading, last = (max(0, -steps), min(count, count - steps))
    return lax.ppermute(value, axis, [(source, source + steps) for source in range(leading, last)])


def rope(projected, positions):
    row_count = projected.shape[0]
    head_count = projected.shape[1] // HD
    shaped = projected.reshape(row_count, head_count, HD)
    half_size = HD // 2
    exponents = jnp.arange(half_size, dtype=jnp.float32) * (2.0 / HD)
    inverse = jnp.exp(-exponents * math.log(500000.0))
    angle = (positions.astype(jnp.float32) * 0.25)[:, None, None] * inverse[None, None, :]
    cosine = jnp.cos(angle)
    sine = jnp.sin(angle)
    lower_half = shaped[..., :half_size]
    upper_half = shaped[..., half_size:]
    rotated_rows = jnp.concatenate(
        [lower_half * cosine - upper_half * sine, upper_half * cosine + lower_half * sine], -1
    )
    return rotated_rows.reshape(row_count, head_count * HD)


def convolve(masked, kernel, row_count, col_count):
    summed = jnp.zeros((masked.shape[0], row_count, col_count), jnp.float32)
    for lag_q in range(CQ):
        for lag_k in range(CK):
            weight = kernel[:, lag_q * CK + lag_k][:, None, None]
            window = masked[
                :,
                CQ - 1 - lag_q : CQ - 1 - lag_q + row_count,
                CK - 1 - lag_k : CK - 1 - lag_k + col_count,
            ]
            summed = summed + weight * window
    return summed


def add_rows(left, piece):
    return jnp.dot(left, piece, preferred_element_type=jnp.float32)


def share_keys(key, value):
    return (
        lax.all_gather(key, "ctx", axis=0, tiled=True),
        lax.all_gather(value, "ctx", axis=0, tiled=True),
    )


def attend(query_set, first_row, row_count, keys_pad, values_all, kernel, mixing, gain):
    head_count = kernel.shape[0]
    ext_rows = row_count + CQ - 1
    query_heads = query_set.reshape(ext_rows, head_count, HD)
    token_total = values_all.shape[0]
    block_count = token_total // KB
    last_row = first_row + row_count - 1
    scale = 1.0 / math.sqrt(HD)
    prow = first_row - (CQ - 1) + jnp.arange(ext_rows, dtype=jnp.int32)
    irow = first_row + jnp.arange(row_count, dtype=jnp.int32)

    def logits_of(block):
        key_start = block * KB
        key_block = lax.dynamic_slice_in_dim(keys_pad, key_start, KB + CK - 1, 0).reshape(
            KB + CK - 1, head_count, HD
        )
        scores = (
            jnp.einsum("rhd,khd->hrk", query_heads, key_block, preferred_element_type=jnp.float32)
            * scale
        )
        kcol = key_start - CK // 2 + jnp.arange(KB + CK - 1, dtype=jnp.int32)
        valid = (kcol[None, :] <= prow[:, None]) & (prow[:, None] >= 0)
        masked = jnp.where(valid[None], scores, 0.0)
        conv = convolve(masked, kernel, row_count, KB)
        jcol = key_start + jnp.arange(KB, dtype=jnp.int32)
        return jnp.where((jcol[None, :] <= irow[:, None])[None], conv, -jnp.inf)

    def first_pass(block, carry_in):

        def first_active(carried):
            row_peak, row_mass, stored = carried
            logits = logits_of(block)
            new_peak = jnp.maximum(row_peak, jnp.max(logits, axis=-1))
            new_mass = row_mass * jnp.exp(row_peak - new_peak) + jnp.sum(
                jnp.exp(logits - new_peak[..., None]), axis=-1
            )
            stored = lax.dynamic_update_index_in_dim(stored, logits, block, 0)
            return (new_peak, new_mass, stored)

        return lax.cond(block * KB <= last_row, first_active, lambda carried: carried, carry_in)

    peak_start = jnp.full((head_count, row_count), -jnp.inf, jnp.float32)
    mass_start = jnp.zeros((head_count, row_count), jnp.float32)
    store_start = jnp.zeros((block_count, head_count, row_count, KB), jnp.float32)
    row_peak, row_mass, stored = lax.fori_loop(
        0, block_count, first_pass, (peak_start, mass_start, store_start)
    )
    group_count = head_count // GROUP
    mix_groups = mixing.reshape(group_count, GROUP, GROUP)

    def second_pass(block, carry_in):

        def second_active(summed):
            logits = lax.dynamic_index_in_dim(stored, block, 0, keepdims=False)
            probs = jnp.exp(logits - row_peak[..., None]) / row_mass[..., None]
            grouped = probs.reshape(group_count, GROUP, row_count, KB)
            mixed_scores = (
                jnp.einsum("gab,gbrk->gark", mix_groups, grouped)
                .reshape(head_count, row_count, KB)
                .astype(jnp.bfloat16)
            )
            value_block = lax.dynamic_slice_in_dim(values_all, block * KB, KB, 0).reshape(
                KB, head_count, HD
            )
            return summed + jnp.einsum(
                "hrk,khd->rhd", mixed_scores, value_block, preferred_element_type=jnp.float32
            )

        return lax.cond(block * KB <= last_row, second_active, lambda summed: summed, carry_in)

    summed = lax.fori_loop(
        0, block_count, second_pass, jnp.zeros((row_count, head_count, HD), jnp.float32)
    )
    rms = jnp.sqrt(jnp.mean(summed * summed, axis=-1, keepdims=True) + 1e-05)
    normed = (summed / rms * gain.reshape(head_count, HD)).astype(jnp.bfloat16)
    return normed.reshape(row_count, head_count * HD)


def per_device(
    activations, positions, w_query, w_key, w_value, conv_kernel, head_mix, out_gain, w_out
):
    row_count = activations.shape[0]
    ctx_place = lax.axis_index("ctx")
    features = lax.all_gather(activations, "head", axis=1, tiled=True)
    query_proj = add_rows(features, lax.all_gather(w_query, "ctx", axis=0, tiled=True))
    key_proj = add_rows(features, lax.all_gather(w_key, "ctx", axis=0, tiled=True))
    value_proj = add_rows(features, lax.all_gather(w_value, "ctx", axis=0, tiled=True))
    key = rope(key_proj, positions).astype(jnp.bfloat16)
    value = value_proj.astype(jnp.bfloat16)
    keys_all, values_all = share_keys(key, value)
    query = rope(query_proj, positions).astype(jnp.bfloat16)
    rim_rows = passed_along(query[row_count - (CQ - 1) :], "ctx", 1)
    query_ext = jnp.concatenate([rim_rows, query], 0)
    keys_pad = jnp.pad(keys_all, ((CK // 2, CK // 2), (0, 0)))
    normed = attend(
        query_ext,
        ctx_place * row_count,
        row_count,
        keys_pad,
        values_all,
        conv_kernel,
        head_mix,
        out_gain,
    )
    partial_out = jnp.dot(
        normed, lax.all_gather(w_out, "ctx", axis=1, tiled=True), preferred_element_type=jnp.float32
    )
    return lax.psum_scatter(
        partial_out.astype(jnp.bfloat16), "head", scatter_dimension=1, tiled=True
    )


ROWS = 256
BAND = 128
LANES = 128
SUB = 64
AHEAD = 16


def kernel_params(mebibytes):
    return pltpu.CompilerParams(vmem_limit_bytes=mebibytes * 1024 * 1024)


def whole(memory_space):
    return pl.BlockSpec(memory_space=memory_space)


def project_kernel(rows, first_col, place, *refs):
    a_own, a_x, a_y, corners = refs[:4], refs[4:7], refs[7:10], refs[10:12]
    w_same, w_swap = refs[12:14]
    abuf, wbuf, acc, sem_a, sem_w = refs[-5:]
    turn, core = place[0], place[1]
    half = w_same.shape[1]
    width = wbuf.shape[2]

    def copies_a(t):
        mid = rows // 2
        if t == 0:
            pairs = [(a_own[b], 0, b * rows, rows) for b in range(4)]
        elif t < 3:
            c0, c1, c2 = (a_x, a_y)[t - 1]
            pairs = [(c0, 0, 0, rows), (c1, 0, rows, rows), (c2, 0, 2 * rows, 2 * rows)]
        else:
            pairs = [(a_y[1], rows, 0, mid), (a_x[1], rows, mid, mid)]
            pairs += [(a_y[2], 2 * rows, rows, mid), (a_x[2], 2 * rows, rows + mid, mid)]
            pairs += [(corners[0], 0, 2 * rows, rows), (corners[1], 0, 3 * rows, rows)]
        return [
            pltpu.make_async_copy(
                ref.at[pl.ds(source, size)], abuf.at[t, pl.ds(target, size)], sem_a.at[t, n]
            )
            for n, (ref, source, target, size) in enumerate(pairs)
        ]

    def copies_w(t):
        out = []
        for n, (ref, side) in enumerate(((w_same, core), (w_swap, 1 - core))):
            source = ref.at[lax.bitwise_xor(turn, t), :, pl.ds(first_col, width)]
            target = wbuf.at[t, pl.ds(pl.multiple_of(side * half, half), half)]
            out.append(pltpu.make_async_copy(source, target, sem_w.at[t, n]))
        return out

    for t in range(4):
        for copy in copies_w(t) + copies_a(t):
            copy.start()
    for t in range(4):
        for copy in copies_w(t) + copies_a(t):
            copy.wait()
        part = jnp.dot(abuf[t], wbuf[t], preferred_element_type=jnp.float32)
        acc[...] = part if t == 0 else acc[...] + part
    if first_col:
        v_out = refs[14]
        for b in range(4):
            v_out[place[5 + b]] = acc[b * rows : (b + 1) * rows].astype(jnp.bfloat16)
        return
    cos_ref, sin_ref, mine, theirs = refs[14:18]
    first = core == 0
    for b in range(4):
        total = acc[b * rows : (b + 1) * rows]
        cosine, sine = cos_ref[b], sin_ref[b]
        at = place[5 + b]
        for col, out in ((0, 0), (2 * HD, HD)):
            heads = []
            for start in (col, col + HD):
                x = total[:, start : start + HD]
                x = x * cosine + pltpu.roll(x, HD // 2, 1) * sine
                heads.append(x.astype(jnp.bfloat16))
            mine[at, :, out : out + HD] = jnp.where(first, heads[0], heads[1])
            theirs[at, :, out : out + HD] = jnp.where(first, heads[1], heads[0])


def project(place, a_own, a_plane, w_same, w_swap, angles=()):
    rows, depth = a_own[0].shape
    first_col, width = (0, 4 * HD) if angles else (4 * HD, 2 * HD)
    out = jax.ShapeDtypeStruct((4, rows, 2 * HD), jnp.bfloat16)
    count = 2 if angles else 1
    return pl.pallas_call(
        functools.partial(project_kernel, rows, first_col),
        out_shape=[out] * count,
        in_specs=[whole(pltpu.SMEM)]
        + [whole(pl.ANY)] * 14
        + [whole(pltpu.VMEM)] * len(angles),
        out_specs=[whole(pltpu.VMEM)] * count,
        scratch_shapes=[
            pltpu.VMEM((4, 4 * rows, depth), jnp.bfloat16),
            pltpu.VMEM((4, depth, width), jnp.bfloat16),
            pltpu.VMEM((4 * rows, width), jnp.float32),
            pltpu.SemaphoreType.DMA((4, 6)),
            pltpu.SemaphoreType.DMA((4, 2)),
        ],
        compiler_params=kernel_params(56),
        cost_estimate=pl.CostEstimate(
            flops=8 * rows * 4 * depth * width, bytes_accessed=16 * 2**20, transcendentals=0
        ),
    )(place, *a_own, *a_plane, w_same, w_swap, *angles)


def prepare(core, mine, other, key_ref, even_ref, odd_ref, q_out, k_out, corr, *scratch):
    qf, kf, lags, turned = scratch
    total = q_out.shape[0]
    qf[0:8] = jnp.zeros((8, HD), jnp.float32)
    kf[0:AHEAD] = jnp.zeros((AHEAD, HD), jnp.float32)
    kf[AHEAD + total :] = jnp.zeros((kf.shape[0] - AHEAD - total, HD), jnp.float32)
    corr[...] = jnp.zeros(corr.shape, jnp.float32)
    for i in range(total // (2 * ROWS)):
        for ref, parity in ((mine, core), (other, 1 - core)):
            start = pl.multiple_of((2 * i + parity) * ROWS, ROWS)
            block = ref[i].astype(jnp.float32)
            qf[pl.ds(8 + start, ROWS)] = block[:, :HD]
            kf[pl.ds(AHEAD + start, ROWS)] = block[:, HD:]

    ahead = lax.broadcasted_iota(jnp.int32, (SUB + 8, LANES), 1) - lax.broadcasted_iota(
        jnp.int32, (SUB + 8, LANES), 0
    )
    near = (ahead >= 1) & (ahead < CQ + CK // 2)
    steps = total // LANES
    for w in range(steps):
        base = w * LANES
        window = kf[base : base + 2 * LANES].T
        turned[base : base + LANES] = window.astype(jnp.bfloat16)
        for odd in range(2):
            at = base + odd * SUB
            qwin = qf[at : at + SUB + 8]
            kwin = kf[at + AHEAD - 8 : at + AHEAD - 8 + LANES]
            scores = lax.dot_general(
                qwin.astype(jnp.bfloat16),
                kwin.astype(jnp.bfloat16),
                (((1,), (1,)), ((), ())),
                preferred_element_type=jnp.float32,
            )
            future = jnp.where(near, scores, 0.0)
            for a in range(CQ):
                cols = slice(a * LANES, (a + 1) * LANES)
                lags[odd, w * SUB : (w + 1) * SUB, cols] = future[8 - a : 8 - a + SUB].astype(
                    jnp.bfloat16
                )
                q_out[at : at + SUB, cols] = qwin[8 - a : 8 - a + SUB].astype(jnp.bfloat16)
    for w in range(0, steps, 4):
        wide = jnp.dot(
            turned[w * LANES : (w + 4) * LANES], key_ref[...], preferred_element_type=jnp.float32
        )
        for n in range(4):
            cols = slice((w + n) * LANES, (w + n + 1) * LANES)
            for a in range(CQ):
                k_out[a * HD : (a + 1) * HD, cols] = wide[
                    n * LANES : (n + 1) * LANES, a * LANES : (a + 1) * LANES
                ].astype(jnp.bfloat16)
    for odd, taps in enumerate((even_ref, odd_ref)):
        for w in range(0, steps, 8):
            fix = jnp.dot(
                lags[odd, w * SUB : (w + 8) * SUB], taps[...], preferred_element_type=jnp.float32
            )
            for n in range(8):
                m = 2 * ((w + n) % 2) + odd
                col = LANES * ((m + 1) // 2)
                corr[(w + n) // 2, m * SUB : (m + 1) * SUB, col : col + taps.shape[1]] = fix[
                    n * SUB : (n + 1) * SUB
                ]


def fill_tables(weights, key_ref, even_ref, odd_ref):
    def fill(ref, origin, swap):
        height = ref.shape[0] if swap else ref.shape[0] // CQ
        width = ref.shape[1] // CQ if swap else ref.shape[1]
        shape = (height, width)
        tap = lax.broadcasted_iota(jnp.int32, shape, 1) - lax.broadcasted_iota(jnp.int32, shape, 0)
        for a in range(CQ):
            value = jnp.zeros(shape, jnp.float32)
            for c in range(CK):
                value = jnp.where(tap == c - origin, weights[a * CK + c], value)
            value = value.astype(jnp.bfloat16)
            if swap:
                ref[:, a * width : (a + 1) * width] = value
            else:
                ref[a * height : (a + 1) * height, :] = value

    fill(key_ref, CK // 2 + AHEAD, True)
    fill(even_ref, CK // 2 + 8 - BAND, False)
    fill(odd_ref, CK // 2 + 8 - SUB, False)


def attend_kernel(place, mix, weights, *refs):
    qk_refs, (va, vb, vc, vd), (mine, theirs) = refs[:2], refs[2:6], refs[6:8]
    v_all, q_wide, k_ref, corr = refs[8:12]
    tables, sem_v = refs[16:19], refs[19]
    side, core = place[2], place[1]
    b = pl.program_id(0)
    count = k_ref.shape[1] // (2 * ROWS)

    @pl.when(b == 0)
    def _():
        def copies_v():
            out = []
            for n, ref in enumerate((va, vb, vc, vd)):
                parity = core if n < 2 else 1 - core
                start = pl.multiple_of((side if n % 2 == 0 else 1 - side) * 2 * HD, 2 * HD)
                for i in range(count):
                    rows = pl.ds(pl.multiple_of((2 * i + parity) * ROWS, ROWS), ROWS)
                    target = v_all.at[rows, pl.ds(start, 2 * HD)]
                    out.append(pltpu.make_async_copy(ref.at[i], target, sem_v.at[n, i]))
            return out

        for copy in copies_v():
            copy.start()
        fill_tables(weights, *tables)
        prepare(core, *qk_refs, *tables, q_wide, k_ref, corr, *refs[12:16])
        for copy in copies_v():
            copy.wait()

    row = lax.broadcasted_iota(jnp.int32, (ROWS, ROWS), 0)
    col = lax.broadcasted_iota(jnp.int32, (ROWS, ROWS), 1)
    seen = col <= row
    top, low = slice(0, ROWS), slice(ROWS, 2 * ROWS)

    def fixed(part, n):
        return jnp.concatenate([part[:, :BAND], part[:, BAND:] - corr[n, :, :BAND]], 1)

    def rows_of(upper, lower):
        return jnp.concatenate([upper, lower], 0)

    def block(step):
        q_rows = q_wide[2 * step * ROWS : (2 * step + 2) * ROWS]
        parts = []
        for j in range(2 * step + 1):
            part = jnp.dot(
                q_rows,
                k_ref[:, j * ROWS : (j + 1) * ROWS],
                preferred_element_type=jnp.float32,
            )
            if j == 2 * step:
                diagonal = jnp.where(seen, part[top] - corr[2 * step, :, BAND:], -jnp.inf)
                part = rows_of(diagonal, fixed(part[low], 2 * step + 1))
            elif j == 2 * step - 1:
                part = rows_of(fixed(part[top], 2 * step), part[low])
            parts.append(part)
        start = (2 * step + 1) * ROWS
        last = jnp.dot(
            q_rows[low], k_ref[:, start : start + ROWS], preferred_element_type=jnp.float32
        )
        last = jnp.where(seen, last - corr[2 * step + 1, :, BAND:], -jnp.inf)
        peak = parts[0]
        for part in parts[1:]:
            peak = jnp.maximum(peak, part)
        peak = rows_of(peak[top], jnp.maximum(peak[low], last))
        peak = jnp.max(peak, axis=1, keepdims=True)
        mass = jnp.zeros((2 * ROWS, ROWS), jnp.float32)
        probs = []
        for part in parts:
            part = jnp.exp2(part - peak)
            mass = mass + part
            probs.append(part.astype(jnp.bfloat16))
        last = jnp.exp2(last - peak[low])
        mass = rows_of(mass[top], mass[low] + last)
        summed = jnp.dot(
            jnp.concatenate(probs, 1), v_all[:start], preferred_element_type=jnp.float32
        )
        extra = jnp.dot(
            last.astype(jnp.bfloat16),
            v_all[start : start + ROWS],
            preferred_element_type=jnp.float32,
        )
        inverse = 1.0 / jnp.sum(mass, axis=1, keepdims=True)
        halves = []
        for rows, total in ((top, summed[top]), (low, summed[low] + extra)):
            halves.append(
                jnp.concatenate(
                    [
                        total[:, g * HD : (g + 1) * HD] * (inverse[rows] * mix[g])
                        for g in range(GROUP)
                    ],
                    1,
                ).astype(jnp.bfloat16)
            )
        mine[0] = jnp.where(core == 0, halves[0], halves[1])
        theirs[0] = jnp.where(core == 0, halves[1], halves[0])

    for step in range(count):
        pl.when(b == step)(lambda step=step: block(step))


def attend_head(place, mix, weights, mine, other, values):
    total = 2 * mine.shape[0] * ROWS
    count = total // (2 * ROWS)
    depth = CQ * HD
    out = jax.ShapeDtypeStruct((count, ROWS, GROUP * HD), jnp.bfloat16)
    out_spec = pl.BlockSpec((1, ROWS, GROUP * HD), lambda b: (b, 0, 0))
    return pl.pallas_call(
        attend_kernel,
        grid=(count,),
        out_shape=(out, out),
        in_specs=[whole(pltpu.SMEM)] * 3 + [whole(pltpu.VMEM)] * 2 + [whole(pl.ANY)] * 4,
        out_specs=[out_spec, out_spec],
        scratch_shapes=[
            pltpu.VMEM((total, GROUP * HD), jnp.bfloat16),
            pltpu.VMEM((total, depth), jnp.bfloat16),
            pltpu.VMEM((depth, total), jnp.bfloat16),
            pltpu.VMEM((total // ROWS, ROWS, BAND + ROWS), jnp.float32),
            pltpu.VMEM((8 + total, HD), jnp.float32),
            pltpu.VMEM((AHEAD + total + LANES, HD), jnp.float32),
            pltpu.VMEM((2, total // 2, CQ * LANES), jnp.bfloat16),
            pltpu.VMEM((total, 2 * LANES), jnp.bfloat16),
        ]
        + [
            pltpu.VMEM(shape, jnp.bfloat16)
            for shape in ((2 * LANES, depth), (CQ * LANES, 2 * LANES), (CQ * LANES, LANES))
        ]
        + [pltpu.SemaphoreType.DMA((4, count))],
        compiler_params=kernel_params(56),
        cost_estimate=pl.CostEstimate(
            flops=total * total * (depth + GROUP * HD),
            bytes_accessed=16 * 2**20,
            transcendentals=total * total // 2,
        ),
    )(place, mix, weights, mine, other, *values)


def finish_kernel(place, own, r1, r2, r3, gain, *refs):
    w_parts, outs = refs[:12], refs[12:16]
    normed, w_buf, sem = refs[16:]
    width = w_parts[0].shape[1]
    core, head, inner = place[1], place[0], place[9]

    def copy_w(n, source):
        side = core if n % 2 == 0 else 1 - core
        cols = pl.ds(pl.multiple_of(side * width, width), width)
        target = w_buf.at[lax.bitwise_xor(place[5 + n // 2], head), :, cols]
        return pltpu.make_async_copy(w_parts[source], target, sem.at[n])

    for n in range(4):
        copy_w(n, n).start()
    for n in range(4, 8):
        straight = n if n < 6 else n + 2

        @pl.when(inner == 1)
        def _():
            copy_w(n, straight).start()

        @pl.when(inner == 0)
        def _():
            copy_w(n, straight + 2).start()

    near = own[...] + r1[...].astype(jnp.float32)
    far = r2[...].astype(jnp.float32) + r3[...].astype(jnp.float32)
    low = place[3] == 0
    for g in range(2 * GROUP):
        cols = slice((g % GROUP) * HD, (g % GROUP + 1) * HD)
        first = low if g < GROUP else jnp.logical_not(low)
        x = jnp.where(first, near[:, cols], far[:, cols])
        scale = lax.rsqrt(jnp.mean(x * x, axis=1, keepdims=True) + 1e-05)
        normed[:, g * HD : (g + 1) * HD] = (
            x * scale * gain[:, g * HD : (g + 1) * HD]
        ).astype(jnp.bfloat16)
    for n in range(8):
        copy_w(n, n).wait()
    for t in (3, 2, 1, 0):
        outs[t][...] = jnp.dot(
            normed[...], w_buf[t], preferred_element_type=jnp.float32
        ).astype(jnp.bfloat16)


def finish(place, own, r1, r2, r3, gain, w_parts):
    rows = own.shape[0]
    depth, width = w_parts[0].shape
    return pl.pallas_call(
        finish_kernel,
        in_specs=[whole(pltpu.SMEM)] + [whole(pltpu.VMEM)] * 5 + [whole(pl.ANY)] * 12,
        out_specs=[whole(pltpu.VMEM)] * 4,
        out_shape=[jax.ShapeDtypeStruct((rows, 2 * width), jnp.bfloat16)] * 4,
        scratch_shapes=[
            pltpu.VMEM((rows, depth), jnp.bfloat16),
            pltpu.VMEM((4, depth, 2 * width), jnp.bfloat16),
            pltpu.SemaphoreType.DMA((8,)),
        ],
        compiler_params=kernel_params(56),
        cost_estimate=pl.CostEstimate(
            flops=2 * rows * depth * 8 * width, bytes_accessed=11 * 2**20, transcendentals=0
        ),
    )(place, own, r1, r2, r3, gain, *w_parts)


def swapped(value, axis, mask):
    count = lax.axis_size(axis)
    return lax.ppermute(value, axis, [(i, i ^ mask) for i in range(count)])


def per_device_one_head(
    activations, positions, w_query, w_key, w_value, conv_kernel, head_mix, out_gain, w_out
):
    ctx, head = lax.axis_index("ctx"), lax.axis_index("head")
    z, core = ctx // 2, ctx % 2
    rows = activations.shape[0]
    half = rows // 2
    barrier = lax.optimization_barrier
    pair = 2 * HD

    def columns(target):
        parts = [
            lax.dynamic_slice_in_dim(w, target * pair, pair, 1) for w in (w_query, w_key, w_value)
        ]
        return jnp.concatenate(parts, 1)

    digits = jnp.stack([positions // 256, positions % 256]).astype(jnp.bfloat16)
    digits = jnp.pad(digits, ((0, 14), (0, activations.shape[1] - rows)))
    block = jnp.concatenate([activations, digits])
    w_pieces = jnp.stack([columns(target) for target in range(4)])
    middle = [(2, 4), (3, 5), (4, 2), (5, 3)]
    outward = [(2, 0), (3, 1), (4, 6), (5, 7)]
    inner = (z == 1) | (z == 2)

    ends = [(0, 6), (1, 7), (6, 0), (7, 1)]

    def plane(pieces, x_before, y_before):
        pieces = [piece[:rows] for piece in pieces]
        to_x = jnp.concatenate(pieces + [y_before[half:rows]])
        to_y = jnp.concatenate(pieces + [x_before[:half]])
        return swapped(to_x, "head", 1), swapped(to_y, "head", 2)

    near = swapped(block, "ctx", 2)
    across = lax.ppermute(block, "ctx", middle)
    x0, y0 = swapped(activations, "head", 1), swapped(activations, "head", 2)
    weights = lax.dynamic_index_in_dim(conv_kernel, ctx, 0, keepdims=False)
    weights = weights * (math.log2(math.e) / math.sqrt(HD))
    order = [z, z ^ 1, jnp.where(inner, z ^ 3, z ^ 2), jnp.where(inner, z ^ 2, z ^ 3)]
    place = jnp.stack([head, core, z % 2, z // 2, head] + order).astype(jnp.int32)
    near, across, x0, y0, w_pieces, weights, place, w_out = barrier(
        (near, across, x0, y0, w_pieces, weights, place, w_out)
    )
    same_core = [[i for i in range(8) if i % 2 == k] for k in range(2)]
    across_next = lax.ppermute(near, "ctx", middle)
    passed = lax.ppermute(across, "ctx", outward)
    straight = lax.ppermute(block, "ctx", ends)
    x1, y1 = plane([near], x0, y0)
    across_next, passed, straight, x1, y1, w_pieces = barrier(
        (across_next, passed, straight, x1, y1, w_pieces)
    )
    w_same = lax.all_to_all(w_pieces, "ctx", 0, 0, axis_index_groups=same_core)
    far_a, far_b = across + passed, across_next + straight
    x2, y2 = plane([far_a, far_b], x1, y1)
    place_of = jnp.stack(
        [
            a[rows, :rows].astype(jnp.float32) * 256.0 + a[rows + 1, :rows].astype(jnp.float32)
            for a in (block, near, far_a, far_b)
        ]
    )
    exponents = jnp.arange(HD // 2, dtype=jnp.float32) * (2.0 / HD)
    inverse = jnp.exp(-exponents * math.log(500000.0))
    angle = (place_of * 0.25)[:, :, None] * inverse
    cosine, sine = jnp.cos(angle), jnp.sin(angle)
    cosine = jnp.concatenate([cosine, cosine], -1)
    sine = jnp.concatenate([-sine, sine], -1)
    x2, y2, cosine, sine, w_out = barrier((x2, y2, cosine, sine, w_out))
    c_low = swapped(x2[:rows], "head", 2)
    c_high = swapped(y2[rows : 2 * rows], "head", 1)
    out_near = swapped(w_out, "ctx", 2)
    out_across = lax.ppermute(w_out, "ctx", middle)
    out_ends = lax.ppermute(w_out, "ctx", ends)
    c_low, c_high, w_same = barrier((c_low, c_high, w_same))
    w_swap = swapped(w_same, "ctx", 1)
    planes = (x0, x1, x2, y0, y1, y2, c_low, c_high)
    sources = place, (activations, near, far_a, far_b), planes, w_same, w_swap
    (v_pair,) = project(*sources)
    place, v_pair, out_near, out_across, out_ends = barrier(
        (place, v_pair, out_near, out_across, out_ends)
    )
    v_next = swapped(v_pair, "ctx", 2)
    v_pair_other = swapped(v_pair, "ctx", 1)
    out_across_next = lax.ppermute(out_near, "ctx", middle)
    out_passed = lax.ppermute(out_across, "ctx", outward)
    mine, theirs = project(place, *sources[1:], (cosine, sine))
    mine, theirs, v_next, v_pair_other = barrier((mine, theirs, v_next, v_pair_other))
    other = swapped(theirs, "ctx", 1)
    v_next_other = swapped(v_next, "ctx", 1)
    out_own_swap, out_near_swap = swapped(w_out, "ctx", 1), swapped(out_near, "ctx", 1)
    out_across_swap, out_ends_swap = swapped(out_across, "ctx", 1), swapped(out_ends, "ctx", 1)
    group_rows = lax.dynamic_slice_in_dim(head_mix, GROUP * (ctx // GROUP), GROUP, 0)
    mix = lax.dynamic_index_in_dim(group_rows, ctx % GROUP, 1, keepdims=False)
    out_mine, out_theirs = attend_head(
        place, mix, weights, mine, other, (v_pair, v_next, v_pair_other, v_next_other)
    )
    out_mine, out_theirs, out_passed, out_across_next, *swaps = barrier(
        (out_mine, out_theirs, out_passed, out_across_next)
        + (out_own_swap, out_near_swap, out_across_swap, out_ends_swap)
    )
    out_own_swap, out_near_swap, out_across_swap, out_ends_swap = swaps
    out_parts = [w_out, out_own_swap, out_near, out_near_swap, out_across, out_across_swap]
    out_parts += [p for w in (out_passed, out_across_next) for p in (w, swapped(w, "ctx", 1))]
    out_parts += [out_ends, out_ends_swap]
    summed = out_mine.astype(jnp.float32) + swapped(out_theirs, "ctx", 1).astype(jnp.float32)
    own = lax.dynamic_index_in_dim(summed, z, 0, keepdims=False)
    r1, r2, r3 = [
        swapped(
            lax.dynamic_index_in_dim(summed, z ^ s, 0, keepdims=False).astype(jnp.bfloat16),
            "ctx",
            2 * s,
        )
        for s in (1, 2, 3)
    ]
    where = jnp.concatenate([place, inner.astype(jnp.int32)[None]])
    shares = finish(where, own, r1, r2, r3, out_gain.reshape(1, -1), out_parts)
    total = shares[0].astype(jnp.float32)
    for t in (1, 2, 3):
        total = total + swapped(shares[t], "head", t).astype(jnp.float32)
    return total.astype(jnp.bfloat16)


def solution(mesh):
    one_head_each = mesh.shape["ctx"] == 8 and mesh.shape["head"] == 4
    body = per_device_one_head if one_head_each else per_device
    return jax.shard_map(
        body,
        mesh=mesh,
        in_specs=(
            P("ctx", "head"),
            P("ctx"),
            P("ctx", "head"),
            P("ctx", "head"),
            P("ctx", "head"),
            P("head", None),
            P("head", None),
            P("head"),
            P("head", "ctx"),
        ),
        out_specs=P("ctx", "head"),
        check_vma=False,
    )
```

```python
import functools
import math

import jax
import jax.numpy as jnp
from jax import lax
from jax.experimental import pallas as pl
from jax.experimental.pallas import tpu as pltpu
from jax.sharding import PartitionSpec as P

HD = 128
GROUP = 4
CQ = 6
CK = 11
KB = 512


def passed_along(value, axis, steps):
    count = lax.axis_size(axis)
    leading, last = (max(0, -steps), min(count, count - steps))
    return lax.ppermute(value, axis, [(source, source + steps) for source in range(leading, last)])


def rope(projected, positions):
    row_count = projected.shape[0]
    head_count = projected.shape[1] // HD
    shaped = projected.reshape(row_count, head_count, HD)
    half_size = HD // 2
    exponents = jnp.arange(half_size, dtype=jnp.float32) * (2.0 / HD)
    inverse = jnp.exp(-exponents * math.log(500000.0))
    angle = (positions.astype(jnp.float32) * 0.25)[:, None, None] * inverse[None, None, :]
    cosine = jnp.cos(angle)
    sine = jnp.sin(angle)
    lower_half = shaped[..., :half_size]
    upper_half = shaped[..., half_size:]
    rotated_rows = jnp.concatenate(
        [lower_half * cosine - upper_half * sine, upper_half * cosine + lower_half * sine], -1
    )
    return rotated_rows.reshape(row_count, head_count * HD)


def convolve(masked, kernel, row_count, col_count):
    summed = jnp.zeros((masked.shape[0], row_count, col_count), jnp.float32)
    for lag_q in range(CQ):
        for lag_k in range(CK):
            weight = kernel[:, lag_q * CK + lag_k][:, None, None]
            window = masked[
                :,
                CQ - 1 - lag_q : CQ - 1 - lag_q + row_count,
                CK - 1 - lag_k : CK - 1 - lag_k + col_count,
            ]
            summed = summed + weight * window
    return summed


def add_rows(left, piece):
    return jnp.dot(left, piece, preferred_element_type=jnp.float32)


def share_keys(key, value):
    return (
        lax.all_gather(key, "ctx", axis=0, tiled=True),
        lax.all_gather(value, "ctx", axis=0, tiled=True),
    )


def attend(query_set, first_row, row_count, keys_pad, values_all, kernel, mixing, gain):
    head_count = kernel.shape[0]
    ext_rows = row_count + CQ - 1
    query_heads = query_set.reshape(ext_rows, head_count, HD)
    token_total = values_all.shape[0]
    block_count = token_total // KB
    last_row = first_row + row_count - 1
    scale = 1.0 / math.sqrt(HD)
    prow = first_row - (CQ - 1) + jnp.arange(ext_rows, dtype=jnp.int32)
    irow = first_row + jnp.arange(row_count, dtype=jnp.int32)

    def logits_of(block):
        key_start = block * KB
        key_block = lax.dynamic_slice_in_dim(keys_pad, key_start, KB + CK - 1, 0).reshape(
            KB + CK - 1, head_count, HD
        )
        scores = (
            jnp.einsum("rhd,khd->hrk", query_heads, key_block, preferred_element_type=jnp.float32)
            * scale
        )
        kcol = key_start - CK // 2 + jnp.arange(KB + CK - 1, dtype=jnp.int32)
        valid = (kcol[None, :] <= prow[:, None]) & (prow[:, None] >= 0)
        masked = jnp.where(valid[None], scores, 0.0)
        conv = convolve(masked, kernel, row_count, KB)
        jcol = key_start + jnp.arange(KB, dtype=jnp.int32)
        return jnp.where((jcol[None, :] <= irow[:, None])[None], conv, -jnp.inf)

    def first_pass(block, carry_in):

        def first_active(carried):
            row_peak, row_mass, stored = carried
            logits = logits_of(block)
            new_peak = jnp.maximum(row_peak, jnp.max(logits, axis=-1))
            new_mass = row_mass * jnp.exp(row_peak - new_peak) + jnp.sum(
                jnp.exp(logits - new_peak[..., None]), axis=-1
            )
            stored = lax.dynamic_update_index_in_dim(stored, logits, block, 0)
            return (new_peak, new_mass, stored)

        return lax.cond(block * KB <= last_row, first_active, lambda carried: carried, carry_in)

    peak_start = jnp.full((head_count, row_count), -jnp.inf, jnp.float32)
    mass_start = jnp.zeros((head_count, row_count), jnp.float32)
    store_start = jnp.zeros((block_count, head_count, row_count, KB), jnp.float32)
    row_peak, row_mass, stored = lax.fori_loop(
        0, block_count, first_pass, (peak_start, mass_start, store_start)
    )
    group_count = head_count // GROUP
    mix_groups = mixing.reshape(group_count, GROUP, GROUP)

    def second_pass(block, carry_in):

        def second_active(summed):
            logits = lax.dynamic_index_in_dim(stored, block, 0, keepdims=False)
            probs = jnp.exp(logits - row_peak[..., None]) / row_mass[..., None]
            grouped = probs.reshape(group_count, GROUP, row_count, KB)
            mixed_scores = (
                jnp.einsum("gab,gbrk->gark", mix_groups, grouped)
                .reshape(head_count, row_count, KB)
                .astype(jnp.bfloat16)
            )
            value_block = lax.dynamic_slice_in_dim(values_all, block * KB, KB, 0).reshape(
                KB, head_count, HD
            )
            return summed + jnp.einsum(
                "hrk,khd->rhd", mixed_scores, value_block, preferred_element_type=jnp.float32
            )

        return lax.cond(block * KB <= last_row, second_active, lambda summed: summed, carry_in)

    summed = lax.fori_loop(
        0, block_count, second_pass, jnp.zeros((row_count, head_count, HD), jnp.float32)
    )
    rms = jnp.sqrt(jnp.mean(summed * summed, axis=-1, keepdims=True) + 1e-05)
    normed = (summed / rms * gain.reshape(head_count, HD)).astype(jnp.bfloat16)
    return normed.reshape(row_count, head_count * HD)


def per_device(
    activations, positions, w_query, w_key, w_value, conv_kernel, head_mix, out_gain, w_out
):
    row_count = activations.shape[0]
    ctx_place = lax.axis_index("ctx")
    features = lax.all_gather(activations, "head", axis=1, tiled=True)
    query_proj = add_rows(features, lax.all_gather(w_query, "ctx", axis=0, tiled=True))
    key_proj = add_rows(features, lax.all_gather(w_key, "ctx", axis=0, tiled=True))
    value_proj = add_rows(features, lax.all_gather(w_value, "ctx", axis=0, tiled=True))
    key = rope(key_proj, positions).astype(jnp.bfloat16)
    value = value_proj.astype(jnp.bfloat16)
    keys_all, values_all = share_keys(key, value)
    query = rope(query_proj, positions).astype(jnp.bfloat16)
    rim_rows = passed_along(query[row_count - (CQ - 1) :], "ctx", 1)
    query_ext = jnp.concatenate([rim_rows, query], 0)
    keys_pad = jnp.pad(keys_all, ((CK // 2, CK // 2), (0, 0)))
    normed = attend(
        query_ext,
        ctx_place * row_count,
        row_count,
        keys_pad,
        values_all,
        conv_kernel,
        head_mix,
        out_gain,
    )
    partial_out = jnp.dot(
        normed, lax.all_gather(w_out, "ctx", axis=1, tiled=True), preferred_element_type=jnp.float32
    )
    return lax.psum_scatter(
        partial_out.astype(jnp.bfloat16), "head", scatter_dimension=1, tiled=True
    )


ROWS = 256
BAND = 128
LANES = 128
SUB = 64
AHEAD = 16


def kernel_params(mebibytes):
    return pltpu.CompilerParams(vmem_limit_bytes=mebibytes * 1024 * 1024)


def whole(memory_space):
    return pl.BlockSpec(memory_space=memory_space)


def project_kernel(rows, first_col, place, *refs):
    a_own, a_x, a_y = refs[:4], refs[4:9], refs[9:14]
    w_same, w_swap = refs[14:16]
    abuf, wbuf, acc, sem_a, sem_w = refs[-5:]
    turn, core = place[0], place[1]
    half = w_same.shape[1]
    width = wbuf.shape[2]

    def copies_a(t):
        out = []
        for b in range(4):
            if t < 3:
                source = (a_own, a_x, a_y)[t][b].at[pl.ds(0, rows)]
                target = abuf.at[t, pl.ds(b * rows, rows)]
                out.append(pltpu.make_async_copy(source, target, sem_a.at[t, b]))
                continue
            mid = rows // 2
            late = pl.ds(rows if b < 3 else 0, mid)
            for n, part in enumerate((a_y, a_x)):
                target = abuf.at[t, pl.ds(b * rows + n * mid, mid)]
                out.append(
                    pltpu.make_async_copy(part[b + 1].at[late], target, sem_a.at[t + n, b])
                )
        return out

    def copies_w(t):
        out = []
        for n, (ref, side) in enumerate(((w_same, core), (w_swap, 1 - core))):
            source = ref.at[lax.bitwise_xor(turn, t), :, pl.ds(first_col, width)]
            target = wbuf.at[t, pl.ds(pl.multiple_of(side * half, half), half)]
            out.append(pltpu.make_async_copy(source, target, sem_w.at[t, n]))
        return out

    for t in range(4):
        for copy in copies_w(t) + copies_a(t):
            copy.start()
    for t in range(4):
        for copy in copies_w(t) + copies_a(t):
            copy.wait()
        part = jnp.dot(abuf[t], wbuf[t], preferred_element_type=jnp.float32)
        acc[...] = part if t == 0 else acc[...] + part
    if first_col:
        v_out = refs[16]
        for b in range(4):
            v_out[place[5 + b]] = acc[b * rows : (b + 1) * rows].astype(jnp.bfloat16)
        return
    cos_ref, sin_ref, mine, theirs = refs[16:20]
    first = core == 0
    for b in range(4):
        total = acc[b * rows : (b + 1) * rows]
        cosine, sine = cos_ref[b], sin_ref[b]
        at = place[5 + b]
        for col, out in ((0, 0), (2 * HD, HD)):
            heads = []
            for start in (col, col + HD):
                x = total[:, start : start + HD]
                x = x * cosine + pltpu.roll(x, HD // 2, 1) * sine
                heads.append(x.astype(jnp.bfloat16))
            mine[at, :, out : out + HD] = jnp.where(first, heads[0], heads[1])
            theirs[at, :, out : out + HD] = jnp.where(first, heads[1], heads[0])


def project(place, a_own, a_plane, w_same, w_swap, angles=()):
    rows, depth = a_own[0].shape
    first_col, width = (0, 4 * HD) if angles else (4 * HD, 2 * HD)
    out = jax.ShapeDtypeStruct((4, rows, 2 * HD), jnp.bfloat16)
    count = 2 if angles else 1
    return pl.pallas_call(
        functools.partial(project_kernel, rows, first_col),
        out_shape=[out] * count,
        in_specs=[whole(pltpu.SMEM)]
        + [whole(pl.ANY)] * 16
        + [whole(pltpu.VMEM)] * len(angles),
        out_specs=[whole(pltpu.VMEM)] * count,
        scratch_shapes=[
            pltpu.VMEM((4, 4 * rows, depth), jnp.bfloat16),
            pltpu.VMEM((4, depth, width), jnp.bfloat16),
            pltpu.VMEM((4 * rows, width), jnp.float32),
            pltpu.SemaphoreType.DMA((5, 4)),
            pltpu.SemaphoreType.DMA((4, 2)),
        ],
        compiler_params=kernel_params(56),
        cost_estimate=pl.CostEstimate(
            flops=8 * rows * 4 * depth * width, bytes_accessed=16 * 2**20, transcendentals=0
        ),
    )(place, *a_own, *a_plane, w_same, w_swap, *angles)


def prepare(core, mine, other, key_ref, even_ref, odd_ref, q_out, k_out, corr, *scratch):
    qf, kf, lags, turned = scratch
    total = q_out.shape[0]
    qf[0:8] = jnp.zeros((8, HD), jnp.float32)
    kf[0:AHEAD] = jnp.zeros((AHEAD, HD), jnp.float32)
    kf[AHEAD + total :] = jnp.zeros((kf.shape[0] - AHEAD - total, HD), jnp.float32)
    corr[...] = jnp.zeros(corr.shape, jnp.float32)
    for i in range(total // (2 * ROWS)):
        for ref, parity in ((mine, core), (other, 1 - core)):
            start = pl.multiple_of((2 * i + parity) * ROWS, ROWS)
            block = ref[i].astype(jnp.float32)
            qf[pl.ds(8 + start, ROWS)] = block[:, :HD]
            kf[pl.ds(AHEAD + start, ROWS)] = block[:, HD:]

    ahead = lax.broadcasted_iota(jnp.int32, (SUB + 8, LANES), 1) - lax.broadcasted_iota(
        jnp.int32, (SUB + 8, LANES), 0
    )
    near = (ahead >= 1) & (ahead < CQ + CK // 2)
    steps = total // LANES
    for w in range(steps):
        base = w * LANES
        window = kf[base : base + 2 * LANES].T
        turned[base : base + LANES] = window.astype(jnp.bfloat16)
        for odd in range(2):
            at = base + odd * SUB
            qwin = qf[at : at + SUB + 8]
            kwin = kf[at + AHEAD - 8 : at + AHEAD - 8 + LANES]
            scores = lax.dot_general(
                qwin.astype(jnp.bfloat16),
                kwin.astype(jnp.bfloat16),
                (((1,), (1,)), ((), ())),
                preferred_element_type=jnp.float32,
            )
            future = jnp.where(near, scores, 0.0)
            for a in range(CQ):
                cols = slice(a * LANES, (a + 1) * LANES)
                lags[odd, w * SUB : (w + 1) * SUB, cols] = future[8 - a : 8 - a + SUB].astype(
                    jnp.bfloat16
                )
                q_out[at : at + SUB, cols] = qwin[8 - a : 8 - a + SUB].astype(jnp.bfloat16)
    for w in range(0, steps, 4):
        wide = jnp.dot(
            turned[w * LANES : (w + 4) * LANES], key_ref[...], preferred_element_type=jnp.float32
        )
        for n in range(4):
            cols = slice((w + n) * LANES, (w + n + 1) * LANES)
            for a in range(CQ):
                k_out[a * HD : (a + 1) * HD, cols] = wide[
                    n * LANES : (n + 1) * LANES, a * LANES : (a + 1) * LANES
                ].astype(jnp.bfloat16)
    for odd, taps in enumerate((even_ref, odd_ref)):
        for w in range(0, steps, 8):
            fix = jnp.dot(
                lags[odd, w * SUB : (w + 8) * SUB], taps[...], preferred_element_type=jnp.float32
            )
            for n in range(8):
                m = 2 * ((w + n) % 2) + odd
                col = LANES * ((m + 1) // 2)
                corr[(w + n) // 2, m * SUB : (m + 1) * SUB, col : col + taps.shape[1]] = fix[
                    n * SUB : (n + 1) * SUB
                ]


def fill_tables(weights, key_ref, even_ref, odd_ref):
    def fill(ref, origin, swap):
        height = ref.shape[0] if swap else ref.shape[0] // CQ
        width = ref.shape[1] // CQ if swap else ref.shape[1]
        shape = (height, width)
        tap = lax.broadcasted_iota(jnp.int32, shape, 1) - lax.broadcasted_iota(jnp.int32, shape, 0)
        for a in range(CQ):
            value = jnp.zeros(shape, jnp.float32)
            for c in range(CK):
                value = jnp.where(tap == c - origin, weights[a * CK + c], value)
            value = value.astype(jnp.bfloat16)
            if swap:
                ref[:, a * width : (a + 1) * width] = value
            else:
                ref[a * height : (a + 1) * height, :] = value

    fill(key_ref, CK // 2 + AHEAD, True)
    fill(even_ref, CK // 2 + 8 - BAND, False)
    fill(odd_ref, CK // 2 + 8 - SUB, False)


def attend_kernel(place, mix, weights, *refs):
    qk_refs, (va, vb, vc, vd), (mine, theirs) = refs[:2], refs[2:6], refs[6:8]
    v_all, q_wide, k_ref, corr = refs[8:12]
    tables, sem_v = refs[16:19], refs[19]
    side, core = place[2], place[1]
    b = pl.program_id(0)
    count = k_ref.shape[1] // (2 * ROWS)

    @pl.when(b == 0)
    def _():
        def copies_v():
            out = []
            for n, ref in enumerate((va, vb, vc, vd)):
                parity = core if n < 2 else 1 - core
                start = pl.multiple_of((side if n % 2 == 0 else 1 - side) * 2 * HD, 2 * HD)
                for i in range(count):
                    rows = pl.ds(pl.multiple_of((2 * i + parity) * ROWS, ROWS), ROWS)
                    target = v_all.at[rows, pl.ds(start, 2 * HD)]
                    out.append(pltpu.make_async_copy(ref.at[i], target, sem_v.at[n, i]))
            return out

        for copy in copies_v():
            copy.start()
        fill_tables(weights, *tables)
        prepare(core, *qk_refs, *tables, q_wide, k_ref, corr, *refs[12:16])
        for copy in copies_v():
            copy.wait()

    row = lax.broadcasted_iota(jnp.int32, (ROWS, ROWS), 0)
    col = lax.broadcasted_iota(jnp.int32, (ROWS, ROWS), 1)
    seen = col <= row
    top, low = slice(0, ROWS), slice(ROWS, 2 * ROWS)

    def fixed(part, n):
        return jnp.concatenate([part[:, :BAND], part[:, BAND:] - corr[n, :, :BAND]], 1)

    def rows_of(upper, lower):
        return jnp.concatenate([upper, lower], 0)

    def block(step):
        q_rows = q_wide[2 * step * ROWS : (2 * step + 2) * ROWS]
        parts = []
        for j in range(2 * step + 1):
            part = jnp.dot(
                q_rows,
                k_ref[:, j * ROWS : (j + 1) * ROWS],
                preferred_element_type=jnp.float32,
            )
            if j == 2 * step:
                diagonal = jnp.where(seen, part[top] - corr[2 * step, :, BAND:], -jnp.inf)
                part = rows_of(diagonal, fixed(part[low], 2 * step + 1))
            elif j == 2 * step - 1:
                part = rows_of(fixed(part[top], 2 * step), part[low])
            parts.append(part)
        start = (2 * step + 1) * ROWS
        last = jnp.dot(
            q_rows[low], k_ref[:, start : start + ROWS], preferred_element_type=jnp.float32
        )
        last = jnp.where(seen, last - corr[2 * step + 1, :, BAND:], -jnp.inf)
        peak = parts[0]
        for part in parts[1:]:
            peak = jnp.maximum(peak, part)
        peak = rows_of(peak[top], jnp.maximum(peak[low], last))
        peak = jnp.max(peak, axis=1, keepdims=True)
        mass = jnp.zeros((2 * ROWS, ROWS), jnp.float32)
        probs = []
        for part in parts:
            part = jnp.exp2(part - peak)
            mass = mass + part
            probs.append(part.astype(jnp.bfloat16))
        last = jnp.exp2(last - peak[low])
        mass = rows_of(mass[top], mass[low] + last)
        summed = jnp.dot(
            jnp.concatenate(probs, 1), v_all[:start], preferred_element_type=jnp.float32
        )
        extra = jnp.dot(
            last.astype(jnp.bfloat16),
            v_all[start : start + ROWS],
            preferred_element_type=jnp.float32,
        )
        inverse = 1.0 / jnp.sum(mass, axis=1, keepdims=True)
        halves = []
        for rows, total in ((top, summed[top]), (low, summed[low] + extra)):
            halves.append(
                jnp.concatenate(
                    [
                        total[:, g * HD : (g + 1) * HD] * (inverse[rows] * mix[g])
                        for g in range(GROUP)
                    ],
                    1,
                ).astype(jnp.bfloat16)
            )
        mine[0] = jnp.where(core == 0, halves[0], halves[1])
        theirs[0] = jnp.where(core == 0, halves[1], halves[0])

    for step in range(count):
        pl.when(b == step)(lambda step=step: block(step))


def attend_head(place, mix, weights, mine, other, values):
    total = 2 * mine.shape[0] * ROWS
    count = total // (2 * ROWS)
    depth = CQ * HD
    out = jax.ShapeDtypeStruct((count, ROWS, GROUP * HD), jnp.bfloat16)
    out_spec = pl.BlockSpec((1, ROWS, GROUP * HD), lambda b: (b, 0, 0))
    return pl.pallas_call(
        attend_kernel,
        grid=(count,),
        out_shape=(out, out),
        in_specs=[whole(pltpu.SMEM)] * 3 + [whole(pltpu.VMEM)] * 2 + [whole(pl.ANY)] * 4,
        out_specs=[out_spec, out_spec],
        scratch_shapes=[
            pltpu.VMEM((total, GROUP * HD), jnp.bfloat16),
            pltpu.VMEM((total, depth), jnp.bfloat16),
            pltpu.VMEM((depth, total), jnp.bfloat16),
            pltpu.VMEM((total // ROWS, ROWS, BAND + ROWS), jnp.float32),
            pltpu.VMEM((8 + total, HD), jnp.float32),
            pltpu.VMEM((AHEAD + total + LANES, HD), jnp.float32),
            pltpu.VMEM((2, total // 2, CQ * LANES), jnp.bfloat16),
            pltpu.VMEM((total, 2 * LANES), jnp.bfloat16),
        ]
        + [
            pltpu.VMEM(shape, jnp.bfloat16)
            for shape in ((2 * LANES, depth), (CQ * LANES, 2 * LANES), (CQ * LANES, LANES))
        ]
        + [pltpu.SemaphoreType.DMA((4, count))],
        compiler_params=kernel_params(56),
        cost_estimate=pl.CostEstimate(
            flops=total * total * (depth + GROUP * HD),
            bytes_accessed=16 * 2**20,
            transcendentals=total * total // 2,
        ),
    )(place, mix, weights, mine, other, *values)


def finish_kernel(place, own, parts, gain, *refs):
    w_parts, outs = refs[:12], refs[12:16]
    normed, w_buf, sem = refs[16:]
    width = w_parts[0].shape[1]
    core, head, inner = place[1], place[0], place[9]

    def copy_w(n, source):
        side = core if n % 2 == 0 else 1 - core
        cols = pl.ds(pl.multiple_of(side * width, width), width)
        target = w_buf.at[lax.bitwise_xor(place[5 + n // 2], head), :, cols]
        return pltpu.make_async_copy(w_parts[source], target, sem.at[n])

    for n in range(4):
        copy_w(n, n).start()
    for n in range(4, 8):
        straight = n if n < 6 else n + 2

        @pl.when(inner == 1)
        def _():
            copy_w(n, straight).start()

        @pl.when(inner == 0)
        def _():
            copy_w(n, straight + 2).start()

    near = own[...] + parts[place[6]].astype(jnp.float32)
    far = parts[place[7]].astype(jnp.float32) + parts[place[8]].astype(jnp.float32)
    low = place[3] == 0
    for g in range(2 * GROUP):
        cols = slice((g % GROUP) * HD, (g % GROUP + 1) * HD)
        first = low if g < GROUP else jnp.logical_not(low)
        x = jnp.where(first, near[:, cols], far[:, cols])
        scale = lax.rsqrt(jnp.mean(x * x, axis=1, keepdims=True) + 1e-05)
        normed[:, g * HD : (g + 1) * HD] = (
            x * scale * gain[:, g * HD : (g + 1) * HD]
        ).astype(jnp.bfloat16)
    for n in range(8):
        copy_w(n, n).wait()
    for t in (3, 2, 1, 0):
        outs[t][...] = jnp.dot(
            normed[...], w_buf[t], preferred_element_type=jnp.float32
        ).astype(jnp.bfloat16)


def finish(place, own, parts, gain, w_parts):
    rows = own.shape[0]
    depth, width = w_parts[0].shape
    return pl.pallas_call(
        finish_kernel,
        in_specs=[whole(pltpu.SMEM)] + [whole(pltpu.VMEM)] * 3 + [whole(pl.ANY)] * 12,
        out_specs=[whole(pltpu.VMEM)] * 4,
        out_shape=[jax.ShapeDtypeStruct((rows, 2 * width), jnp.bfloat16)] * 4,
        scratch_shapes=[
            pltpu.VMEM((rows, depth), jnp.bfloat16),
            pltpu.VMEM((4, depth, 2 * width), jnp.bfloat16),
            pltpu.SemaphoreType.DMA((8,)),
        ],
        compiler_params=kernel_params(56),
        cost_estimate=pl.CostEstimate(
            flops=2 * rows * depth * 8 * width, bytes_accessed=11 * 2**20, transcendentals=0
        ),
    )(place, own, parts, gain, *w_parts)


def swapped(value, axis, mask):
    count = lax.axis_size(axis)
    return lax.ppermute(value, axis, [(i, i ^ mask) for i in range(count)])


def per_device_one_head(
    activations, positions, w_query, w_key, w_value, conv_kernel, head_mix, out_gain, w_out
):
    ctx, head = lax.axis_index("ctx"), lax.axis_index("head")
    z, core = ctx // 2, ctx % 2
    rows = activations.shape[0]
    half = rows // 2
    barrier = lax.optimization_barrier
    pair = 2 * HD

    def columns(target):
        parts = [
            lax.dynamic_slice_in_dim(w, target * pair, pair, 1) for w in (w_query, w_key, w_value)
        ]
        return jnp.concatenate(parts, 1)

    digits = jnp.stack([positions // 256, positions % 256]).astype(jnp.bfloat16)
    digits = jnp.pad(digits, ((0, 14), (0, activations.shape[1] - rows)))
    block = jnp.concatenate([activations, digits])
    w_pieces = jnp.stack([columns(target) for target in range(4)])
    middle = [(2, 4), (3, 5), (4, 2), (5, 3)]
    outward = [(2, 0), (3, 1), (4, 6), (5, 7)]
    inner = (z == 1) | (z == 2)

    def plane(piece, x_before, y_before):
        to_x = jnp.concatenate([piece[:rows], y_before[half:rows]])
        to_y = jnp.concatenate([piece[:rows], x_before[:half]])
        return swapped(to_x, "head", 1), swapped(to_y, "head", 2)

    near = swapped(block, "ctx", 2)
    across = lax.ppermute(block, "ctx", middle)
    x0, y0 = swapped(activations, "head", 1), swapped(activations, "head", 2)
    weights = lax.dynamic_index_in_dim(conv_kernel, ctx, 0, keepdims=False)
    weights = weights * (math.log2(math.e) / math.sqrt(HD))
    order = [z, z ^ 1, jnp.where(inner, z ^ 3, z ^ 2), jnp.where(inner, z ^ 2, z ^ 3)]
    place = jnp.stack([head, core, z % 2, z // 2, head] + order).astype(jnp.int32)
    near, across, x0, y0, w_pieces, weights, place, w_out = barrier(
        (near, across, x0, y0, w_pieces, weights, place, w_out)
    )
    same_core = [[i for i in range(8) if i % 2 == k] for k in range(2)]
    across_next = lax.ppermute(near, "ctx", middle)
    passed = lax.ppermute(across, "ctx", outward)
    x1, y1 = plane(near, x0, y0)
    across_next, passed, x1, y1, w_pieces = barrier((across_next, passed, x1, y1, w_pieces))
    w_same = lax.all_to_all(w_pieces, "ctx", 0, 0, axis_index_groups=same_core)
    far_a = across + passed
    passed_next = lax.ppermute(across_next, "ctx", outward)
    x2, y2 = plane(far_a, x1, y1)
    passed_next, x2, y2 = barrier((passed_next, x2, y2))
    far_b = across_next + passed_next
    x3, y3 = plane(far_b, x2, y2)
    place_of = jnp.stack(
        [
            a[rows, :rows].astype(jnp.float32) * 256.0 + a[rows + 1, :rows].astype(jnp.float32)
            for a in (block, near, far_a, far_b)
        ]
    )
    exponents = jnp.arange(HD // 2, dtype=jnp.float32) * (2.0 / HD)
    inverse = jnp.exp(-exponents * math.log(500000.0))
    angle = (place_of * 0.25)[:, :, None] * inverse
    cosine, sine = jnp.cos(angle), jnp.sin(angle)
    cosine = jnp.concatenate([cosine, cosine], -1)
    sine = jnp.concatenate([-sine, sine], -1)
    x3, y3, cosine, sine, w_out = barrier((x3, y3, cosine, sine, w_out))
    x4, y4 = swapped(y3[half:rows], "head", 1), swapped(x3[:half], "head", 2)
    out_near = swapped(w_out, "ctx", 2)
    out_across = lax.ppermute(w_out, "ctx", middle)
    x4, y4, w_same = barrier((x4, y4, w_same))
    w_swap = swapped(w_same, "ctx", 1)
    planes = (x0, x1, x2, x3, x4, y0, y1, y2, y3, y4)
    sources = place, (activations, near, far_a, far_b), planes, w_same, w_swap
    (v_pair,) = project(*sources)
    place, v_pair, out_near, out_across = barrier((place, v_pair, out_near, out_across))
    v_next = swapped(v_pair, "ctx", 2)
    v_pair_other = swapped(v_pair, "ctx", 1)
    out_across_next = lax.ppermute(out_near, "ctx", middle)
    out_passed = lax.ppermute(out_across, "ctx", outward)
    mine, theirs = project(place, *sources[1:], (cosine, sine))
    mine, theirs, v_next, v_pair_other = barrier((mine, theirs, v_next, v_pair_other))
    other = swapped(theirs, "ctx", 1)
    v_next_other = swapped(v_next, "ctx", 1)
    out_own_swap = swapped(w_out, "ctx", 1)
    other, v_next_other, out_across_next, out_own_swap = barrier(
        (other, v_next_other, out_across_next, out_own_swap)
    )
    out_passed_next = lax.ppermute(out_across_next, "ctx", outward)
    out_near_swap, out_across_swap = swapped(out_near, "ctx", 1), swapped(out_across, "ctx", 1)
    group_rows = lax.dynamic_slice_in_dim(head_mix, GROUP * (ctx // GROUP), GROUP, 0)
    mix = lax.dynamic_index_in_dim(group_rows, ctx % GROUP, 1, keepdims=False)
    out_mine, out_theirs = attend_head(
        place, mix, weights, mine, other, (v_pair, v_next, v_pair_other, v_next_other)
    )
    out_mine, out_theirs, out_passed, out_passed_next, out_near_swap, out_across_swap = barrier(
        (out_mine, out_theirs, out_passed, out_passed_next, out_near_swap, out_across_swap)
    )
    out_parts = [w_out, out_own_swap, out_near, out_near_swap, out_across, out_across_swap]
    for part in (out_passed, out_across_next, out_passed_next):
        out_parts += [part, swapped(part, "ctx", 1)]
    summed = out_mine.astype(jnp.float32) + swapped(out_theirs, "ctx", 1).astype(jnp.float32)
    own = lax.dynamic_index_in_dim(summed, z, 0, keepdims=False)
    parts = lax.all_to_all(
        summed.astype(jnp.bfloat16), "ctx", 0, 0, axis_index_groups=same_core
    )
    where = jnp.concatenate([place, inner.astype(jnp.int32)[None]])
    shares = finish(where, own, parts, out_gain.reshape(1, -1), out_parts)
    total = shares[0].astype(jnp.float32)
    for t in (1, 2, 3):
        total = total + swapped(shares[t], "head", t).astype(jnp.float32)
    return total.astype(jnp.bfloat16)


def solution(mesh):
    one_head_each = mesh.shape["ctx"] == 8 and mesh.shape["head"] == 4
    body = per_device_one_head if one_head_each else per_device
    return jax.shard_map(
        body,
        mesh=mesh,
        in_specs=(
            P("ctx", "head"),
            P("ctx"),
            P("ctx", "head"),
            P("ctx", "head"),
            P("ctx", "head"),
            P("head", None),
            P("head", None),
            P("head"),
            P("head", "ctx"),
        ),
        out_specs=P("ctx", "head"),
        check_vma=False,
    )
```
